32 devices in a mesh: dp: 8 (over z, y), tensor: 4 (over x, core).
Axes of the slice: x: 2, y: 2, z: 4, core: 2. Of those that a mesh axis runs over, the one named last changes fastest.
Arguments:
- token_ids: int32 [16, 1024], P('dp'), may hold values from 0 to 31999
- targets: int32 [16, 1024], P('dp'), may hold values from 0 to 31999
- segments: int32 [16, 1024], P('dp'), may hold values from 0 to 7, never falling along the last dimension, each value on 1 to 512 neighbouring positions
- completion: int32 [16, 1024], P('dp'), may hold values from 0 to 1
- micro_order: int32 [8, 2], P('dp'), may hold values from 0 to 1, each once within a row
- embedding: float32 [32000, 768], P('tensor', 'dp'), may hold values from -0.3 to 0.3
- attn_in: float32 [768, 2304], P('dp', 'tensor'), may hold values from -0.21875 to 0.21875
- attn_out: float32 [768, 768], P('tensor', 'dp'), may hold values from -0.625 to 0.625
- ffn_in: float32 [768, 2, 3072], P('dp', None, 'tensor'), may hold values from -0.21875 to 0.21875
- ffn_out: float32 [3072, 768], P('tensor', 'dp'), may hold values from -0.109375 to 0.109375
- head_table: float32 [768, 32000], P('dp', 'tensor'), may hold values from -2 to 2
- norm_gains: float32 [3, 768], P(None, 'dp'), may hold values from 0.25 to 3
- mean_embedding: float32 [32000, 768], P('tensor', 'dp'), may hold values from -5.74836e-07 to 5.74836e-07
- mean_attn_in: float32 [768, 2304], P('dp', 'tensor'), may hold values from -5.74836e-07 to 5.74836e-07
- mean_attn_out: float32 [768, 768], P('tensor', 'dp'), may hold values from -5.74836e-07 to 5.74836e-07
- mean_ffn_in: float32 [768, 2, 3072], P('dp', None, 'tensor'), may hold values from -5.74836e-07 to 5.74836e-07
- mean_ffn_out: float32 [3072, 768], P('tensor', 'dp'), may hold values from -5.74836e-07 to 5.74836e-07
- mean_head_table: float32 [768, 32000], P('dp', 'tensor'), may hold values from -5.74836e-07 to 5.74836e-07
- mean_norm_gains: float32 [3, 768], P(None, 'dp'), may hold values from -5.74836e-06 to 5.74836e-06
- square_embedding: float32 [32000, 768], P('tensor', 'dp'), may hold values from 8.9777666e-14 to 3.5842794e-13
- square_attn_in: float32 [768, 2304], P('dp', 'tensor'), may hold values from 8.9777666e-14 to 3.5842794e-13
- square_attn_out: float32 [768, 768], P('tensor', 'dp'), may hold values from 8.9777666e-14 to 3.5842794e-13
- square_ffn_in: float32 [768, 2, 3072], P('dp', None, 'tensor'), may hold values from 8.9777666e-14 to 3.5842794e-13
- square_ffn_out: float32 [3072, 768], P('tensor', 'dp'), may hold values from 8.9777666e-14 to 3.5842794e-13
- square_head_table: float32 [768, 32000], P('dp', 'tensor'), may hold values from 8.9777666e-14 to 3.5842794e-13
- square_norm_gains: float32 [3, 768], P(None, 'dp'), may hold values from 8.9777664e-12 to 3.5842794e-11
Outputs:
- loss_parts: float32 [2, 2], replicated
- grad_norm: float32 [], replicated
- embedding_new: float32 [32000, 768], P('tensor', 'dp')
- mean_embedding_new: float32 [32000, 768], P('tensor', 'dp')
- square_embedding_new: float32 [32000, 768], P('tensor', 'dp')
- embedding_copy: bfloat16 [32000, 768], P('tensor', 'dp')
- attn_in_new: float32 [768, 2304], P('dp', 'tensor')
- mean_attn_in_new: float32 [768, 2304], P('dp', 'tensor')
- square_attn_in_new: float32 [768, 2304], P('dp', 'tensor')
- attn_in_copy: bfloat16 [768, 2304], P('dp', 'tensor')
- attn_out_new: float32 [768, 768], P('tensor', 'dp')
- mean_attn_out_new: float32 [768, 768], P('tensor', 'dp')
- square_attn_out_new: float32 [768, 768], P('tensor', 'dp')
- attn_out_copy: bfloat16 [768, 768], P('tensor', 'dp')
- ffn_in_new: float32 [768, 2, 3072], P('dp', None, 'tensor')
- mean_ffn_in_new: float32 [768, 2, 3072], P('dp', None, 'tensor')
- square_ffn_in_new: float32 [768, 2, 3072], P('dp', None, 'tensor')
- ffn_in_copy: bfloat16 [768, 2, 3072], P('dp', None, 'tensor')
- ffn_out_new: float32 [3072, 768], P('tensor', 'dp')
- mean_ffn_out_new: float32 [3072, 768], P('tensor', 'dp')
- square_ffn_out_new: float32 [3072, 768], P('tensor', 'dp')
- ffn_out_copy: bfloat16 [3072, 768], P('tensor', 'dp')
- head_table_new: float32 [768, 32000], P('dp', 'tensor')
- mean_head_table_new: float32 [768, 32000], P('dp', 'tensor')
- square_head_table_new: float32 [768, 32000], P('dp', 'tensor')
- head_table_copy: bfloat16 [768, 32000], P('dp', 'tensor')
- norm_gains_new: float32 [3, 768], P(None, 'dp')
- mean_norm_gains_new: float32 [3, 768], P(None, 'dp')
- square_norm_gains_new: float32 [3, 768], P(None, 'dp')
- norm_gains_copy: bfloat16 [3, 768], P(None, 'dp')
The draws below stay inside these ranges and needn't reach their ends.
Inputs may be any that keep to these rules, and one draw needn't show every extreme that they name: `segments`: segment numbers never fall along a sequence. `micro_order`: each row names every micro-batch's sequence once.
All inputs are finite; a program needn't handle non-finite values.
Results may differ from the reference program's by a relative error of at most 0.015.
The reference program's roundings to bfloat16 on the way count: a program that leaves them out, or rounds other values in their place, can miss the bound.
Values may be sent and summed in bfloat16 or wider, within the bound.
A program may use at most 384 MiB of HBM per device.

```python
import math
import jax
import jax.numpy as jnp
import numpy as np
from jax import lax

D = 768
HEADS = 12
HEAD_DIM = 64
FF = 3072
VOCAB = 32000
MB = 2
SEQLEN = 1024
STEP = 10
SEQS = 16
N_DP = 8


def draw_completion(key, part):
    key = jax.random.fold_in(key, 11)
    rows = jnp.arange(SEQS, dtype=jnp.int32)[:, None]
    limit = 250 + 500 * rows // max(SEQS - 1, 1)
    return (jax.random.randint(key, (SEQS, SEQLEN), 0, 1000) < limit).astype(jnp.int32)


def draw_norm_gains(key, part):
    key = jax.random.fold_in(key, 12)
    frac = jnp.arange(D, dtype=jnp.float32) / (D - 1)
    rough = jax.random.uniform(key, (3, D), jnp.float32, 0.7, 1.3)
    return 0.6 * 3.0 ** frac[None, :] * rough


def draw_head_table(key, part):
    key = jax.random.fold_in(key, 13)
    frac = jnp.arange(VOCAB, dtype=jnp.float32) / (VOCAB - 1)
    base = jax.random.truncated_normal(key, -5.0, 5.0, (D, VOCAB), jnp.float32)
    return base * (1.0 + 2.0 * frac[None, :]) / D ** 0.5


def set_ends(entries, own_key, least, largest):
    longest = entries.shape.index(max(entries.shape))
    spots = []
    for shift in (0, 1):
        where = [jax.random.randint(jax.random.fold_in(own_key, axis), (), 0, length) for axis, length in enumerate(entries.shape)]
        where[longest] = (where[longest] + shift) % entries.shape[longest]
        spots.append(tuple(where))
    return entries.at[spots[0]].set(least).at[spots[1]].set(largest)


def block_levels(stream_key, extent, shards, smallest, high):
    loudness = 1.0
    for axis_at, parts in shards:
        heights = jax.random.uniform(jax.random.fold_in(jax.random.fold_in(stream_key, 6), axis_at), (parts,), jnp.float32, smallest / len(shards), high / len(shards))
        loudness = loudness * jnp.repeat(jnp.exp(heights), extent[axis_at] // parts).reshape((-1,) + (1,) * (len(extent) - 1 - axis_at))
    return loudness


def cumulative_ranks(number_of, slope):
    portions = [(1 << 20) // math.isqrt(grade ** slope) + 1 for grade in range(1, number_of + 1)]
    deviation = 1 + sum(portions) // (1 << 30)
    return np.cumsum(np.array([max(1, weight // deviation) for weight in portions]))


def skewed_ids(rng, dims, number_of, slope):
    listing = cumulative_ranks(number_of, slope)
    ticket = jax.random.randint(jax.random.fold_in(rng, 1), dims, 0, int(listing[number_of - 1]))
    rank = jnp.searchsorted(jnp.asarray(listing, jnp.int32), ticket, side="right")
    return jax.random.permutation(jax.random.fold_in(rng, 2), number_of)[rank].astype(jnp.int32)


def length_profile(amount, total, most, slope):
    weights = [(1 << 20) // math.isqrt(grade ** slope) + 1 for grade in range(2, amount + 1)]
    rest, holding = total - most - (amount - 1), [1] * (amount - 1)
    while rest > 0:
        free = [i for i in range(amount - 1) if holding[i] < most]
        pool, budget = sum([weights[i] for i in free]), rest
        for i in free:
            extra = min(most - holding[i], max(1, budget * weights[i] // pool), rest)
            holding[i] = holding[i] + extra
            rest = rest - extra
    return np.array([most] + holding)


def uneven_parts(own_key, number_of, total, bound, lean):
    if number_of == 2:
        one = jax.random.randint(own_key, (), max(1, total - bound), min(bound, total - 1) + 1)
        return jnp.stack([one, total - one])
    lengths = jnp.asarray(length_profile(number_of, total, bound, lean), jnp.int32)
    twos = (number_of - 1) // 2
    donor, sink = lengths[1:1 + 2 * twos:2], lengths[2:2 + 2 * twos:2]
    room = jnp.minimum(donor - 1, bound - sink)
    moved = jax.random.randint(jax.random.fold_in(own_key, 1), (twos,), 0, 1 << 20) % (room + 1)
    lengths = lengths.at[1:1 + 2 * twos:2].set(donor - moved).at[2:2 + 2 * twos:2].set(sink + moved)
    return lengths[jax.random.permutation(jax.random.fold_in(own_key, 2), number_of)]


def gaussian(own_key, shape, deviation, bound, split=(), kind=jnp.bfloat16):
    entries = jax.random.normal(own_key, shape, jnp.float32) * deviation
    if len(split) > 0:
        entries = block_levels(own_key, shape, split, -0.22, 0.18) * entries
    return jnp.clip(entries, min=-bound, max=bound).astype(kind)


def setup_inputs(seed: int = 0) -> dict:
    streams_of = jax.random.split(jax.random.key(seed), 27)
    token_ids = set_ends(skewed_ids(streams_of[0], (SEQS, SEQLEN), VOCAB, 2), jax.random.fold_in(streams_of[0], 3), 0, VOCAB - 1).astype(jnp.int32)
    targets = set_ends(skewed_ids(streams_of[1], (SEQS, SEQLEN), VOCAB, 1), jax.random.fold_in(streams_of[1], 3), 0, VOCAB - 1).astype(jnp.int32)
    segments = jax.vmap(lambda own: jnp.searchsorted(jnp.cumsum(uneven_parts(own, max(4, SEQLEN // 128), SEQLEN, SEQLEN // 2, 2)), jnp.arange(SEQLEN), side="right"))(jax.random.split(streams_of[2], SEQS)).reshape((SEQS, SEQLEN)).astype(jnp.int32)
    completion = draw_completion(jax.random.fold_in(streams_of[26], 71), 0)
    micro_order = jax.vmap(lambda own: jax.random.permutation(own, MB))(jax.random.split(streams_of[4], N_DP)).reshape((N_DP, MB)).astype(jnp.int32)
    embedding = gaussian(streams_of[5], (VOCAB, D), 0.05, 0.3, ((0, 4), (1, 8)), jnp.float32)
    attn_in = gaussian(streams_of[6], (D, 3 * D), D ** -0.5, 0.21875, ((0, 8), (1, 4)), jnp.float32)
    attn_out = gaussian(streams_of[7], (D, D), (D // 8) ** -0.5, 0.625, ((0, 4), (1, 8)), jnp.float32)
    ffn_in = gaussian(streams_of[8], (D, 2, FF), D ** -0.5, 0.21875, ((0, 8), (2, 4)), jnp.float32)
    ffn_out = gaussian(streams_of[9], (FF, D), FF ** -0.5, 0.109375, ((0, 4), (1, 8)), jnp.float32)
    head_table = draw_head_table(jax.random.fold_in(streams_of[26], 71), 0)
    norm_gains = draw_norm_gains(jax.random.fold_in(streams_of[26], 71), 0)
    mean_embedding = gaussian(streams_of[12], (VOCAB, D), (0.0011 / (2 * VOCAB * D + 4 * D * D + 3 * D * FF) ** 0.5), 5.748360081270221e-07, ((0, 4), (1, 8)), jnp.float32)
    mean_attn_in = gaussian(streams_of[13], (D, 3 * D), (0.0011 / (2 * VOCAB * D + 4 * D * D + 3 * D * FF) ** 0.5), 5.748360081270221e-07, ((0, 8), (1, 4)), jnp.float32)
    mean_attn_out = gaussian(streams_of[14], (D, D), (0.0011 / (2 * VOCAB * D + 4 * D * D + 3 * D * FF) ** 0.5), 5.748360081270221e-07, ((0, 4), (1, 8)), jnp.float32)
    mean_ffn_in = gaussian(streams_of[15], (D, 2, FF), (0.0011 / (2 * VOCAB * D + 4 * D * D + 3 * D * FF) ** 0.5), 5.748360081270221e-07, ((0, 8), (2, 4)), jnp.float32)
    mean_ffn_out = gaussian(streams_of[16], (FF, D), (0.0011 / (2 * VOCAB * D + 4 * D * D + 3 * D * FF) ** 0.5), 5.748360081270221e-07, ((0, 4), (1, 8)), jnp.float32)
    mean_head_table = gaussian(streams_of[17], (D, VOCAB), (0.0011 / (2 * VOCAB * D + 4 * D * D + 3 * D * FF) ** 0.5), 5.748360081270221e-07, ((0, 8), (1, 4)), jnp.float32)
    mean_norm_gains = gaussian(streams_of[18], (3, D), (0.011 / (2 * VOCAB * D + 4 * D * D + 3 * D * FF) ** 0.5), 5.748359853896545e-06, ((1, 8),), jnp.float32)
    square_embedding = jnp.clip(jnp.exp(math.log(3.584279411900787e-13) - 1.3843914 * jax.random.uniform(streams_of[19], (VOCAB, D), jnp.float32) ** block_levels(streams_of[19], (VOCAB, D), ((0, 4), (1, 8)), -0.2, 0.2)), 8.97776658245232e-14, 3.584279411900787e-13)
    square_attn_in = jnp.clip(jnp.exp(math.log(3.584279411900787e-13) - 1.3843914 * jax.random.uniform(streams_of[20], (D, 3 * D), jnp.float32) ** block_levels(streams_of[20], (D, 3 * D), ((0, 8), (1, 4)), -0.2, 0.2)), 8.97776658245232e-14, 3.584279411900787e-13)
    square_attn_out = jnp.clip(jnp.exp(math.log(3.584279411900787e-13) - 1.3843914 * jax.random.uniform(streams_of[21], (D, D), jnp.float32) ** block_levels(streams_of[21], (D, D), ((0, 4), (1, 8)), -0.2, 0.2)), 8.97776658245232e-14, 3.584279411900787e-13)
    square_ffn_in = jnp.clip(jnp.exp(math.log(3.584279411900787e-13) - 1.3843914 * jax.random.uniform(streams_of[22], (D, 2, FF), jnp.float32) ** block_levels(streams_of[22], (D, 2, FF), ((0, 8), (2, 4)), -0.2, 0.2)), 8.97776658245232e-14, 3.584279411900787e-13)
    square_ffn_out = jnp.clip(jnp.exp(math.log(3.584279411900787e-13) - 1.3843914 * jax.random.uniform(streams_of[23], (FF, D), jnp.float32) ** block_levels(streams_of[23], (FF, D), ((0, 4), (1, 8)), -0.2, 0.2)), 8.97776658245232e-14, 3.584279411900787e-13)
    square_head_table = jnp.clip(jnp.exp(math.log(3.584279411900787e-13) - 1.3843914 * jax.random.uniform(streams_of[24], (D, VOCAB), jnp.float32) ** block_levels(streams_of[24], (D, VOCAB), ((0, 8), (1, 4)), -0.2, 0.2)), 8.97776658245232e-14, 3.584279411900787e-13)
    square_norm_gains = jnp.clip(jnp.exp(math.log(3.584279401058765e-11) - 1.3843914 * jax.random.uniform(streams_of[25], (3, D), jnp.float32) ** block_levels(streams_of[25], (3, D), ((1, 8),), -0.2, 0.2)), 8.977766446927049e-12, 3.584279401058765e-11)
    return dict(token_ids=token_ids, targets=targets, segments=segments, completion=completion, micro_order=micro_order, embedding=embedding, attn_in=attn_in, attn_out=attn_out, ffn_in=ffn_in, ffn_out=ffn_out, head_table=head_table, norm_gains=norm_gains, mean_embedding=mean_embedding, mean_attn_in=mean_attn_in, mean_attn_out=mean_attn_out, mean_ffn_in=mean_ffn_in, mean_ffn_out=mean_ffn_out, mean_head_table=mean_head_table, mean_norm_gains=mean_norm_gains, square_embedding=square_embedding, square_attn_in=square_attn_in, square_attn_out=square_attn_out, square_ffn_in=square_ffn_in, square_ffn_out=square_ffn_out, square_head_table=square_head_table, square_norm_gains=square_norm_gains)


HIGH = lax.Precision.HIGHEST
EPS = 1e-05
CLIP = 0.01
LR = 0.03
LR_GAIN = 0.5
BETA_ONE = 0.9
BETA_TWO = 0.95
ADAM_EPS = 1e-08
DECAY = 0.1
NEG = -1e+30

@jax.custom_vjp
def low(v):
    return lax.optimization_barrier(v.astype(jnp.bfloat16)).astype(jnp.float32)

@jax.custom_vjp
def low_back(v):
    return v

def low_keep(v):
    return (low(v), None)

def low_pass(kept, grad):
    return (grad,)

def back_keep(v):
    return (v, None)

def back_low(kept, grad):
    return (low(grad),)
low.defvjp(low_keep, low_pass)
low_back.defvjp(back_keep, back_low)

def normed(values, gain):
    return values * lax.rsqrt(lax.optimization_barrier(jnp.mean(values * values, axis=-1, keepdims=True)) + EPS) * gain

def rotary(values, cosine, sine):
    half = values.shape[-1] // 2
    turned = jnp.concatenate([-values[..., half:], values[..., :half]], axis=-1)
    return values * cosine + turned * sine

def tables(length, width):
    inverse = 10000.0 ** (-jnp.arange(0, width, 2, dtype=jnp.float32) / width)
    angle = jnp.arange(length, dtype=jnp.float32)[:, None] * inverse[None, :]
    angle = jnp.concatenate([angle, angle], axis=-1)
    return (jnp.cos(angle)[:, None, :], jnp.sin(angle)[:, None, :])

def sequence_loss(lowered, seq_ids, seq_targets, seq_segments, seq_flags):
    embed, attn_in, attn_out, ffn_in, ffn_out, head_table, gains = lowered
    length = seq_ids.shape[0]
    cosine, sine = tables(length, HEAD_DIM)
    stream0 = embed[seq_ids]
    attn_norm = low(normed(stream0, gains[0]))
    qkv = low_back(jnp.dot(attn_norm, attn_in, precision=HIGH)).reshape(length, HEADS, 3, HEAD_DIM)
    query = low(rotary(qkv[:, :, 0], cosine, sine))
    key = low(rotary(qkv[:, :, 1], cosine, sine))
    value = low(qkv[:, :, 2])
    scale = HEAD_DIM ** (-0.5)
    scores = low_back(scale * jnp.einsum('qhd,khd->hqk', query, key, precision=HIGH))
    places = jnp.arange(length, dtype=jnp.int32)
    allowed = (places[:, None] >= places[None, :]) & (seq_segments[:, None] == seq_segments[None, :])
    scores = jnp.where(allowed[None], scores, NEG)
    peak = lax.optimization_barrier(jnp.max(scores, axis=-1, keepdims=True))
    expo = jnp.exp(scores - peak)
    probs = expo / lax.optimization_barrier(jnp.sum(expo, axis=-1, keepdims=True))
    attended = jnp.einsum('hqk,khd->qhd', low(probs), value, precision=HIGH)
    attended = low(low_back(attended)).reshape(length, HEADS * HEAD_DIM)
    stream1 = stream0 + low_back(jnp.dot(attended, attn_out, precision=HIGH))
    ffn_norm = low(normed(stream1, gains[1]))
    gate_up = low_back(jnp.einsum('td,dcf->tcf', ffn_norm, ffn_in, precision=HIGH))
    hidden = low(gate_up[:, 0] * jax.nn.sigmoid(gate_up[:, 0]) * gate_up[:, 1])
    stream2 = stream1 + low_back(jnp.dot(hidden, ffn_out, precision=HIGH))
    final_norm = low(normed(stream2, gains[2]))
    logits = low_back(jnp.dot(final_norm, head_table, precision=HIGH))
    top = lax.optimization_barrier(jnp.max(logits, axis=-1, keepdims=True))
    log_total = top[:, 0] + jnp.log(lax.optimization_barrier(jnp.sum(jnp.exp(logits - top), axis=-1)))
    picked = jnp.take_along_axis(logits, seq_targets[:, None], axis=1)[:, 0]
    return jnp.sum((log_total - picked) * seq_flags)

def adam(weight, grad, first, second, rate, decay):
    first = BETA_ONE * first + (1.0 - BETA_ONE) * grad
    second = BETA_TWO * second + (1.0 - BETA_TWO) * grad * grad
    first_hat = first / (1.0 - BETA_ONE ** STEP)
    second_hat = second / (1.0 - BETA_TWO ** STEP)
    weight = weight - rate * (first_hat / (jnp.sqrt(second_hat) + ADAM_EPS) + decay * weight)
    return (weight, first, second, weight.astype(jnp.bfloat16))

def reference(token_ids, targets, segments, completion, micro_order, embedding, attn_in, attn_out, ffn_in, ffn_out, head_table, norm_gains, mean_embedding, mean_attn_in, mean_attn_out, mean_ffn_in, mean_ffn_out, mean_head_table, mean_norm_gains, square_embedding, square_attn_in, square_attn_out, square_ffn_in, square_ffn_out, square_head_table, square_norm_gains):
    weights = (embedding, attn_in, attn_out, ffn_in, ffn_out, head_table, norm_gains)
    means = (mean_embedding, mean_attn_in, mean_attn_out, mean_ffn_in, mean_ffn_out, mean_head_table, mean_norm_gains)
    squares = (square_embedding, square_attn_in, square_attn_out, square_ffn_in, square_ffn_out, square_head_table, square_norm_gains)
    slots = jnp.arange(MB, dtype=jnp.int32)
    match = (micro_order[:, :, None] == slots[None, None, :]).astype(jnp.int32)
    micro_of = lax.optimization_barrier(jnp.sum(slots[None, :, None] * match, axis=1)).reshape(-1)
    flags = completion.astype(jnp.float32)
    member = (micro_of[:, None] == slots[None, :]).astype(jnp.float32)
    counts = lax.optimization_barrier(jnp.sum(lax.optimization_barrier(jnp.sum(flags, axis=1))[:, None] * member, axis=0))
    row_weight = lax.optimization_barrier(jnp.sum(member / jnp.maximum(counts, 1.0)[None, :], axis=1))

    def objective(params):
        lowered = tuple((low(param) for param in params))
        checked = jax.checkpoint(sequence_loss)

        def visit(carried, row):
            seq_loss = checked(lowered, row[0], row[1], row[2], row[3])
            return (carried + row[4] * seq_loss, seq_loss)
        carried, losses = lax.scan(visit, jnp.zeros((), jnp.float32), (token_ids, targets, segments, flags, row_weight))
        return (carried, losses)
    objective_value, pull, losses = jax.vjp(objective, weights, has_aux=True)
    grads = pull(jnp.ones((), jnp.float32))[0]
    loss_sums = lax.optimization_barrier(jnp.sum(losses[:, None] * member, axis=0))
    squared = jnp.zeros((), jnp.float32)
    for grad in grads:
        squared = squared + jnp.sum(grad * grad)
    grad_norm = jnp.sqrt(squared)
    factor = CLIP / jnp.maximum(grad_norm, CLIP)
    updated = []
    for place in range(7):
        rate = LR_GAIN if place == 6 else LR
        decay = 0.0 if place == 6 else DECAY
        updated.append(adam(weights[place], grads[place] * factor, means[place], squares[place], rate, decay))
    loss_parts = jnp.stack([loss_sums, counts])
    return (loss_parts, grad_norm, updated[0][0], updated[0][1], updated[0][2], updated[0][3], updated[1][0], updated[1][1], updated[1][2], updated[1][3], updated[2][0], updated[2][1], updated[2][2], updated[2][3], updated[3][0], updated[3][1], updated[3][2], updated[3][3], updated[4][0], updated[4][1], updated[4][2], updated[4][3], updated[5][0], updated[5][1], updated[5][2], updated[5][3], updated[6][0], updated[6][1], updated[6][2], updated[6][3])
```

```python
import functools

import jax
import jax.numpy as jnp
from jax import lax
from jax.experimental import pallas as pl
from jax.experimental.pallas import tpu as pltpu
from jax.sharding import PartitionSpec as P

HEAD_DIM = 64
STEP = 10


EPS = 1e-05
CLIP = 0.01
LR = 0.03
LR_GAIN = 0.5
BETA_ONE = 0.9
BETA_TWO = 0.95
ADAM_EPS = 1e-08
DECAY = 0.1
NEG = -1e30
FLOAT = jnp.float32
HALF = jnp.bfloat16
LANES = 128
ROWS = 1024
VMEM_LIMIT = 56 * 2**20

TURN = (0, 2, 1, 3)


def swap(value, axis, bit):
    pairs = [(i, i ^ bit) for i in range(lax.axis_size(axis))]
    return lax.ppermute(value, axis, pairs)


def normed(values, gain):
    return values * lax.rsqrt(jnp.mean(values * values, axis=-1, keepdims=True) + EPS) * gain


def rotary(values, cosine, sine):
    half = values.shape[-1] // 2
    turned = jnp.concatenate([-values[..., half:], values[..., :half]], axis=-1)
    return values * cosine + turned * sine


def unrotate(grad, cosine, sine):
    half = grad.shape[-1] // 2
    turned = grad * sine
    turned = jnp.concatenate([turned[..., half:], -turned[..., :half]], axis=-1)
    return grad * cosine + turned


def tables(places, width):
    inverse = 10000.0 ** (-jnp.arange(0, width, 2, dtype=FLOAT) / width)
    angle = places.astype(FLOAT)[:, None] * inverse[None, :]
    angle = jnp.concatenate([angle, angle], axis=-1)
    return (jnp.cos(angle)[:, None, :], jnp.sin(angle)[:, None, :])


def dp_gather(block):
    group = lax.axis_size("dp")
    if group != 8:
        own = lax.axis_index("dp")
        every = lax.all_gather(block, "dp")
        order = own ^ jnp.arange(group)
        return jnp.take(every, order, axis=0).reshape(group * block.shape[0], block.shape[1])
    parts = {0: block}
    for k in (2, 4, 6):
        parts[k] = swap(block, "dp", k)
    for k in (0, 2, 4, 6):
        parts[k + 1] = swap(parts[k], "dp", 1)
    return jnp.concatenate([parts[k] for k in range(8)], axis=0)


def dp_scatter(full):
    group = lax.axis_size("dp")
    rows = full.shape[0] // group
    blocks = [full[k * rows : (k + 1) * rows] for k in range(group)]
    if group != 8:
        own = lax.axis_index("dp")
        order = own ^ jnp.arange(group)
        placed = jnp.take(full.reshape(group, rows, -1), order, axis=0)
        return lax.psum_scatter(placed.astype(FLOAT), "dp", scatter_dimension=0, tiled=False)
    sums = {}
    for k in (2, 4, 6, 0):
        there = swap(blocks[k + 1].astype(HALF), "dp", 1)
        sums[k] = blocks[k].astype(FLOAT) + there.astype(FLOAT)
    total = sums[0]
    for k in (2, 4, 6):
        total = total + swap(sums[k].astype(HALF), "dp", k).astype(FLOAT)
    return total


def dp_turn(blocks):
    return [blocks[0]] + [swap(blocks[k], "dp", k) for k in range(1, len(blocks))]


def tensor_gather(block):
    half = jnp.concatenate([block, swap(block, "tensor", 2)], axis=0)
    return jnp.concatenate([half, swap(half, "tensor", 1)], axis=0)


def tensor_scatter(full):
    half = full.shape[0] // 2
    quarter = half // 2
    both = full[:half] + swap(full[half:], "tensor", 1)
    there = swap(both[quarter:].astype(HALF), "tensor", 2)
    return both[:quarter] + there.astype(FLOAT)


def lookup_kernel(ids, table, out, rows):
    count = rows.shape[0]

    def body(i, carry):
        for u in range(16):
            r = i * 16 + u
            rows[pl.ds(r, 1), :] = table[pl.ds(ids[0, 0, r], 1), :]
        return carry

    lax.fori_loop(0, count // 16, body, 0)
    out[...] = rows[...].astype(HALF)


def lookup(table, ids):
    count = ids.shape[0]
    return pl.pallas_call(
        lookup_kernel,
        grid=(count // ROWS,),
        in_specs=[
            pl.BlockSpec((1, 1, ROWS), lambda i: (i, 0, 0), memory_space=pltpu.SMEM),
            pl.BlockSpec(table.shape, lambda i: (0, 0), pipeline_mode=pl.Buffered(1)),
        ],
        out_specs=pl.BlockSpec((ROWS, LANES), lambda i: (i, 0)),
        out_shape=jax.ShapeDtypeStruct((count, LANES), HALF),
        scratch_shapes=[pltpu.VMEM((ROWS, LANES), FLOAT)],
        compiler_params=pltpu.CompilerParams(vmem_limit_bytes=VMEM_LIMIT),
        name="lookup",
    )(ids.reshape(count // ROWS, 1, ROWS), table)


def collect_kernel(ids, grads, out, rows, *sums):
    step = pl.program_id(0)
    count = rows.shape[0]

    @pl.when(step == 0)
    def _():
        for total in sums:
            total[...] = jnp.zeros_like(total)

    rows[...] = grads[...].astype(FLOAT)

    def body(i, carry):
        for u in range(16):
            r = i * 16 + u
            total = sums[u % len(sums)]
            place = pl.ds(ids[0, 0, r], 1)
            total[place, :] = total[place, :] + rows[pl.ds(r, 1), :]
        return carry

    lax.fori_loop(0, count // 16, body, 0)

    @pl.when(step == pl.num_programs(0) - 1)
    def _():
        total = sums[0][: out.shape[0], :]
        for other in sums[1:]:
            total = total + other[: out.shape[0], :]
        out[...] = total


def collect(grads, ids, vocab):
    count = ids.shape[0]
    return pl.pallas_call(
        collect_kernel,
        grid=(count // ROWS,),
        in_specs=[
            pl.BlockSpec((1, 1, ROWS), lambda i: (i, 0, 0), memory_space=pltpu.SMEM),
            pl.BlockSpec((ROWS, LANES), lambda i: (i, 0)),
        ],
        out_specs=pl.BlockSpec((vocab, LANES), lambda i: (0, 0)),
        out_shape=jax.ShapeDtypeStruct((vocab, LANES), FLOAT),
        scratch_shapes=[pltpu.VMEM((ROWS, LANES), FLOAT)]
        + [pltpu.VMEM((vocab + 8, LANES), FLOAT)] * 8,
        compiler_params=pltpu.CompilerParams(vmem_limit_bytes=VMEM_LIMIT),
        name="collect",
    )(ids.reshape(count // ROWS, 1, ROWS), grads)


def attention_scores(query, key, allowed):
    scale = query.shape[-1] ** (-0.5)
    raw = jnp.einsum("qhd,khd->hqk", query, key, preferred_element_type=FLOAT)
    return jnp.where(allowed[None], scale * raw, NEG)


def attention_forward(qkv, cosine, sine, allowed):
    length, head_dim = qkv.shape[0], cosine.shape[-1]
    qkv = qkv.reshape(length, -1, 3, head_dim)
    query = rotary(qkv[:, :, 0], cosine, sine).astype(HALF)
    key = rotary(qkv[:, :, 1], cosine, sine).astype(HALF)
    value = qkv[:, :, 2].astype(HALF)
    scores = attention_scores(query, key, allowed)
    peak = jnp.max(scores, axis=-1, keepdims=True)
    expo = jnp.exp(scores - peak)
    summed = jnp.sum(expo, axis=-1, keepdims=True)
    probs = (expo / summed).astype(HALF)
    log_total = peak + jnp.log(summed)
    attended = jnp.einsum("hqk,khd->qhd", probs, value, preferred_element_type=FLOAT)
    attended = attended.reshape(length, -1).astype(HALF)
    return (attended, (query, key, value, log_total))


def attention_backward(d_attended, kept, cosine, sine, allowed):
    query, key, value, log_total = kept
    length, head_dim = query.shape[0], query.shape[-1]
    scale = head_dim ** (-0.5)
    d_attended = d_attended.reshape(length, -1, head_dim)
    probs = jnp.exp(attention_scores(query, key, allowed) - log_total)
    d_value = jnp.einsum(
        "hqk,qhd->khd", probs.astype(HALF), d_attended, preferred_element_type=FLOAT
    )
    d_probs = jnp.einsum("qhd,khd->hqk", d_attended, value, preferred_element_type=FLOAT)
    centre = jnp.sum(probs * d_probs, axis=-1, keepdims=True)
    d_scores = (probs * (d_probs - centre)).astype(HALF)
    d_query = scale * jnp.einsum("hqk,khd->qhd", d_scores, key, preferred_element_type=FLOAT)
    d_key = scale * jnp.einsum("hqk,qhd->khd", d_scores, query, preferred_element_type=FLOAT)
    d_qkv = jnp.stack(
        [unrotate(d_query, cosine, sine), unrotate(d_key, cosine, sine), d_value], axis=2
    )
    return d_qkv.reshape(length, -1).astype(HALF)


def normed_backward(grad, values, gain):
    unused, pull = jax.vjp(normed, values, gain)
    return pull(grad)


def product(left, right, over_left, over_right):
    return lax.dot_general(
        left, right, (((over_left,), (over_right,)), ((), ())), preferred_element_type=FLOAT
    )


def adam(weight, grad, first, second, rate, decay):
    first = BETA_ONE * first + (1.0 - BETA_ONE) * grad
    second = BETA_TWO * second + (1.0 - BETA_TWO) * grad * grad
    first_hat = first / (1.0 - BETA_ONE**STEP)
    second_hat = second / (1.0 - BETA_TWO**STEP)
    weight = weight - rate * (first_hat / (jnp.sqrt(second_hat) + ADAM_EPS) + decay * weight)
    return (weight, first, second, weight.astype(HALF))


def shards(
    token_ids,
    targets,
    segments,
    completion,
    micro_order,
    *state,
):
    weights, means, squares = state[:7], state[7:14], state[14:21]
    embedding, attn_in, attn_out, ffn_in, ffn_out, head_table, norm_gains = weights
    group = lax.axis_size("dp")
    parts = lax.axis_size("tensor")
    own, rank = lax.axis_index("dp"), lax.axis_index("tensor")
    vocab, width = embedding.shape
    start = rank * vocab
    seqs, length = token_ids.shape
    micro = micro_order.shape[1]
    share = length // parts
    turn = jnp.array(TURN, jnp.int32)
    dp_order = own ^ jnp.arange(group, dtype=jnp.int32)
    tensor_order = rank ^ turn
    ffn = ffn_out.shape[0]
    qkv_width = attn_in.shape[1]

    attn_w = dp_gather(jnp.concatenate([attn_in, attn_out.T], axis=1).astype(HALF))
    attn_in_b, attn_out_b = attn_w[:, :qkv_width], attn_w[:, qkv_width:]
    ffn_w = dp_gather(
        jnp.concatenate([ffn_in.reshape(width, -1), ffn_out.T], axis=1).astype(HALF)
    )
    ffn_in_b, ffn_out_b = ffn_w[:, : 2 * ffn], ffn_w[:, 2 * ffn :]
    head_b = dp_gather(head_table.astype(HALF))

    flags = completion.astype(FLOAT)
    picked_rows = micro_order[0]
    local_counts = jnp.sum(completion, axis=1)[picked_rows]
    packed = jnp.concatenate([token_ids.reshape(-1), jnp.pad(local_counts, (0, LANES - micro))])
    packed = lax.all_gather(packed, "dp")
    counts = jnp.sum(packed[:, seqs * length :][:, :micro].astype(FLOAT), axis=0)
    slot = jnp.argmax(picked_rows[None, :] == jnp.arange(seqs)[:, None], axis=1)
    row_weights = (1.0 / jnp.maximum(counts, 1.0))[slot]

    gains = lax.all_gather(norm_gains.astype(HALF), "dp")
    gains = jnp.take(gains, dp_order, axis=0).transpose(1, 0, 2).reshape(3, -1).astype(FLOAT)

    every_id = packed[:, : seqs * length].reshape(group, seqs, parts, share)
    every_id = jnp.take(jnp.take(every_id, dp_order, axis=0), tensor_order, axis=2)
    every_id = every_id.transpose(2, 0, 1, 3).reshape(-1) - start
    every_id = jnp.where((every_id >= 0) & (every_id < vocab), every_id, vocab)

    def local_order(values):
        return jnp.take(values.reshape(seqs, parts, share), tensor_order, axis=1).reshape(
            seqs, length
        )

    targets, segments, flags = local_order(targets), local_order(segments), local_order(flags)
    places = (tensor_order[:, None] * share + jnp.arange(share, dtype=jnp.int32)).reshape(-1)
    cosine, sine = tables(places, HEAD_DIM)

    table = jnp.pad(embedding.astype(HALF).astype(FLOAT), ((0, 8), (0, LANES - width)))
    rows = lookup(table, every_id)[:, :width].reshape(parts, group, seqs * share, width)
    rows = rows[:2] + swap(rows[2:], "tensor", 1)
    rows = rows[0] + swap(rows[1], "tensor", 2)
    if group == 8:
        rows = dp_turn([rows[k] for k in range(group)])
    else:
        rows = jnp.take(rows, dp_order, axis=0)
        rows = lax.all_to_all(rows, "dp", 0, 0)
        rows = jnp.take(rows, dp_order, axis=0)
        rows = [rows[k] for k in range(group)]
    stream0 = jnp.concatenate(rows, axis=1).astype(FLOAT)
    stream0 = [stream0[j * share : (j + 1) * share] for j in range(seqs)]

    allowed, kept, full_norm, stream1, stream2 = [], [], [], [], []
    for j in range(seqs):
        allowed.append(
            (places[:, None] >= places[None, :])
            & (segments[j][:, None] == segments[j][None, :])
        )
    attn_norm, attended = [], []
    for j in range(seqs):
        attn_norm.append(tensor_gather(normed(stream0[j], gains[0]).astype(HALF)))
        qkv = product(attn_norm[j], attn_in_b, 1, 0)
        out, keep = attention_forward(qkv, cosine, sine, allowed[j])
        attended.append(out)
        kept.append(keep)
        stream1.append(stream0[j] + tensor_scatter(product(out, attn_out_b, 1, 1)))
    ffn_norm, gate_up, hidden = [], [], []
    for j in range(seqs):
        ffn_norm.append(tensor_gather(normed(stream1[j], gains[1]).astype(HALF)))
        gate_up.append(product(ffn_norm[j], ffn_in_b, 1, 0))
        hidden.append((jax.nn.silu(gate_up[j][:, :ffn]) * gate_up[j][:, ffn:]).astype(HALF))
        stream2.append(stream1[j] + tensor_scatter(product(hidden[j], ffn_out_b, 1, 1)))

    final_norm, d_logits, d_final, seq_loss = [], [], [], []
    columns = jnp.arange(vocab, dtype=jnp.int32) + start
    for j in range(seqs):
        final_norm.append(tensor_gather(normed(stream2[j], gains[2]).astype(HALF)))
        logits = product(final_norm[j], head_b, 1, 0)
        top = jnp.max(logits, axis=-1)
        local_total = jnp.sum(jnp.exp(logits - top[:, None]), axis=-1)
        hit = columns[None, :] == targets[j][:, None]
        picked = jnp.sum(jnp.where(hit, logits, 0.0), axis=-1)
        stats = jnp.stack([top, local_total, picked]).reshape(3, parts, share)
        stats = [stats[:, p] for p in range(parts)]
        parts_of = [jnp.stack(stats, axis=1)]
        for bit in range(1, parts):
            there = swap(parts_of[0], "tensor", bit)
            parts_of.append(
                jnp.stack([there[:, TURN.index(TURN[p] ^ bit)] for p in range(parts)], axis=1)
            )
        stacked = jnp.stack(parts_of).reshape(parts, 3, length)
        peak = jnp.max(stacked[:, 0], axis=0)
        summed = jnp.sum(stacked[:, 1] * jnp.exp(stacked[:, 0] - peak), axis=0)
        target_logit = jnp.sum(stacked[:, 2], axis=0)
        log_total = peak + jnp.log(summed)
        seq_loss.append(jnp.sum((log_total - target_logit) * flags[j]))
        d_log = (jnp.exp(logits - log_total[:, None]) - hit.astype(FLOAT)) * (
            flags[j] * row_weights[j]
        )[:, None]
        d_logits.append(d_log.astype(HALF))
        d_final.append(tensor_scatter(product(d_logits[j], head_b, 1, 1)))
    g_head = dp_scatter(
        product(final_norm[0], d_logits[0], 0, 0) + product(final_norm[1], d_logits[1], 0, 0)
    )

    g_gain = [[], [], []]
    d_gate_up, d_branch2, d_stream1 = [], [], []
    for j in range(seqs):
        d_stream2, part = normed_backward(d_final[j], stream2[j], gains[2])
        g_gain[2].append(part)
        d_branch2.append(tensor_gather(d_stream2.astype(HALF)))
        d_hidden = product(d_branch2[j], ffn_out_b, 1, 0)
        unused, pull = jax.vjp(
            lambda both: jax.nn.silu(both[:, :ffn]) * both[:, ffn:], gate_up[j]
        )
        d_gate_up.append(pull(d_hidden)[0].astype(HALF))
        d_norm = tensor_scatter(product(d_gate_up[j], ffn_in_b, 1, 1))
        d_part, part = normed_backward(d_norm, stream1[j], gains[1])
        g_gain[1].append(part)
        d_stream1.append(d_stream2 + d_part)
    g_ffn_in = product(ffn_norm[0], d_gate_up[0], 0, 0) + product(ffn_norm[1], d_gate_up[1], 0, 0)
    g_ffn_out = product(d_branch2[0], hidden[0], 0, 0) + product(d_branch2[1], hidden[1], 0, 0)
    g_ffn = dp_scatter(jnp.concatenate([g_ffn_in.astype(HALF), g_ffn_out.astype(HALF)], axis=1))
    d_branch1, d_qkv, d_stream0 = [], [], []
    for j in range(seqs):
        d_branch1.append(tensor_gather(d_stream1[j].astype(HALF)))
        d_attended = product(d_branch1[j], attn_out_b, 1, 0).astype(HALF)
        d_qkv.append(attention_backward(d_attended, kept[j], cosine, sine, allowed[j]))
        d_norm = tensor_scatter(product(d_qkv[j], attn_in_b, 1, 1))
        d_part, part = normed_backward(d_norm, stream0[j], gains[0])
        g_gain[0].append(part)
        d_stream0.append((d_stream1[j] + d_part).astype(HALF))
    g_attn_in = product(attn_norm[0], d_qkv[0], 0, 0) + product(attn_norm[1], d_qkv[1], 0, 0)
    g_attn_out = product(d_branch1[0], attended[0], 0, 0) + product(
        d_branch1[1], attended[1], 0, 0
    )
    g_attn = dp_scatter(jnp.concatenate([g_attn_in.astype(HALF), g_attn_out.astype(HALF)], axis=1))

    token_grads = jnp.concatenate(d_stream0, axis=0)
    blocks = [token_grads[:, k * width : (k + 1) * width] for k in range(group)]
    if group == 8:
        blocks = jnp.stack(dp_turn(blocks))
    else:
        blocks = jnp.take(jnp.stack(blocks), dp_order, axis=0)
        blocks = lax.all_to_all(blocks, "dp", 0, 0)
        blocks = jnp.take(blocks, dp_order, axis=0)
    blocks = tensor_gather(blocks[None]).reshape(-1, width)
    blocks = jnp.pad(blocks, ((0, 0), (0, LANES - width)))
    g_embed = collect(blocks, every_id, vocab)[:, :width]

    gain_sum = jnp.stack([sum(parts_of) for parts_of in g_gain]).reshape(3, group, width)
    gain_sum = jnp.take(gain_sum, dp_order, axis=1)
    g_gains = jnp.take(lax.psum(gain_sum, ("dp", "tensor")), own, axis=1)

    reduced = (
        g_embed,
        g_attn[:, :qkv_width],
        g_attn[:, qkv_width:].T,
        g_ffn[:, : 2 * ffn].reshape(ffn_in.shape),
        g_ffn[:, 2 * ffn :].T,
        g_head,
        g_gains,
    )
    owner = (rank == 0).astype(FLOAT)
    squared = jnp.zeros((), FLOAT)
    for place in range(6):
        squared = squared + jnp.sum(reduced[place] * reduced[place])
    squared = squared + owner * jnp.sum(reduced[6] * reduced[6])
    losses = jnp.stack(seq_loss)[picked_rows]
    squared, loss_sums = lax.psum((squared, losses * owner), ("dp", "tensor"))
    grad_norm = jnp.sqrt(squared)
    factor = CLIP / jnp.maximum(grad_norm, CLIP)
    updated = []
    for place in range(7):
        rate = LR_GAIN if place == 6 else LR
        decay = 0.0 if place == 6 else DECAY
        updated.extend(
            adam(weights[place], reduced[place] * factor, means[place], squares[place], rate, decay)
        )
    return (jnp.stack([loss_sums, counts]), grad_norm, *updated)


def solution(mesh):
    in_specs = (
        P("dp", None),
        P("dp", None),
        P("dp", None),
        P("dp", None),
        P("dp", None),
        P("tensor", "dp"),
        P("dp", "tensor"),
        P("tensor", "dp"),
        P("dp", None, "tensor"),
        P("tensor", "dp"),
        P("dp", "tensor"),
        P(None, "dp"),
        P("tensor", "dp"),
        P("dp", "tensor"),
        P("tensor", "dp"),
        P("dp", None, "tensor"),
        P("tensor", "dp"),
        P("dp", "tensor"),
        P(None, "dp"),
        P("tensor", "dp"),
        P("dp", "tensor"),
        P("tensor", "dp"),
        P("dp", None, "tensor"),
        P("tensor", "dp"),
        P("dp", "tensor"),
        P(None, "dp"),
    )
    out_specs = (
        P(),
        P(),
        P("tensor", "dp"),
        P("tensor", "dp"),
        P("tensor", "dp"),
        P("tensor", "dp"),
        P("dp", "tensor"),
        P("dp", "tensor"),
        P("dp", "tensor"),
        P("dp", "tensor"),
        P("tensor", "dp"),
        P("tensor", "dp"),
        P("tensor", "dp"),
        P("tensor", "dp"),
        P("dp", None, "tensor"),
        P("dp", None, "tensor"),
        P("dp", None, "tensor"),
        P("dp", None, "tensor"),
        P("tensor", "dp"),
        P("tensor", "dp"),
        P("tensor", "dp"),
        P("tensor", "dp"),
        P("dp", "tensor"),
        P("dp", "tensor"),
        P("dp", "tensor"),
        P("dp", "tensor"),
        P(None, "dp"),
        P(None, "dp"),
        P(None, "dp"),
        P(None, "dp"),
    )
    return jax.shard_map(shards, mesh=mesh, in_specs=in_specs, out_specs=out_specs, check_vma=False)
```

```python
import functools

import jax
import jax.numpy as jnp
from jax import lax
from jax.experimental import pallas as pl
from jax.experimental.pallas import tpu as pltpu
from jax.sharding import PartitionSpec as P

HEAD_DIM = 64
STEP = 10


EPS = 1e-05
CLIP = 0.01
LR = 0.03
LR_GAIN = 0.5
BETA_ONE = 0.9
BETA_TWO = 0.95
ADAM_EPS = 1e-08
DECAY = 0.1
NEG = -1e30
FLOAT = jnp.float32
HALF = jnp.bfloat16
LANES = 128
ROWS = 1024
HEAD_PART = 4096
VMEM_LIMIT = 56 * 2**20
TILE = 512
CHUNK = 256
MESH = pl.DeviceIdType.MESH

TURN = (0, 2, 1, 3)


def swap(value, axis, bit):
    pairs = [(i, i ^ bit) for i in range(lax.axis_size(axis))]
    return lax.ppermute(value, axis, pairs)


def normed(values, gain):
    return values * lax.rsqrt(jnp.mean(values * values, axis=-1, keepdims=True) + EPS) * gain


def rotary(values, cosine, sine):
    half = values.shape[-1] // 2
    turned = jnp.concatenate([-values[..., half:], values[..., :half]], axis=-1)
    return values * cosine + turned * sine


def unrotate(grad, cosine, sine):
    half = grad.shape[-1] // 2
    turned = grad * sine
    turned = jnp.concatenate([turned[..., half:], -turned[..., :half]], axis=-1)
    return grad * cosine + turned


def tables(places, width):
    inverse = 10000.0 ** (-jnp.arange(0, width, 2, dtype=FLOAT) / width)
    angle = places.astype(FLOAT)[:, None] * inverse[None, :]
    angle = jnp.concatenate([angle, angle], axis=-1)
    return (jnp.cos(angle)[:, None, :], jnp.sin(angle)[:, None, :])


def dp_gather(block):
    group = lax.axis_size("dp")
    if group != 8:
        return lax.all_gather(block, "dp", axis=0, tiled=True)
    parts = {0: block}
    for k in (2, 4, 6):
        parts[k] = swap(block, "dp", k)
    for k in (0, 2, 4, 6):
        parts[k + 1] = swap(parts[k], "dp", 1)
    rows = block.shape[0]
    own = lax.axis_index("dp")
    full = jnp.zeros((group * rows, block.shape[1]), block.dtype)
    for k in range(group):
        full = lax.dynamic_update_slice(full, parts[k], ((own ^ k) * rows, 0))
    return full


def dp_scatter(full):
    group = lax.axis_size("dp")
    rows = full.shape[0] // group
    if group != 8:
        return lax.psum_scatter(full.astype(FLOAT), "dp", scatter_dimension=0, tiled=True)
    own = lax.axis_index("dp")

    def block(k):
        return lax.dynamic_slice(full, ((own ^ k) * rows, 0), (rows, full.shape[1]))

    sums = {}
    for k in (2, 4, 6, 0):
        there = swap(block(k + 1), "dp", 1)
        sums[k] = block(k).astype(FLOAT) + there.astype(FLOAT)
    total = sums[0]
    for k in (2, 4, 6):
        total = total + swap(sums[k].astype(HALF), "dp", k).astype(FLOAT)
    return total


def peers_of(own, rank, bits, axis):
    if axis == "dp":
        return [(own ^ k, rank) for k in bits]
    return [(own, rank ^ k) for k in bits]


def greet(peers):
    barrier = pltpu.get_barrier_semaphore()
    for peer in peers:
        pl.semaphore_signal(barrier, inc=1, device_id=peer, device_id_type=MESH)
    pl.semaphore_wait(barrier, len(peers))


def spread_kernel(ids, gains, every_id, every_gain, send, recv):
    own, rank = lax.axis_index("dp"), lax.axis_index("tensor")
    peers = peers_of(own, rank, range(1, 8), "dp")
    greet(peers)
    every_id[0] = ids[...]
    every_gain[0] = gains[...]
    copies = []
    for k in range(1, 8):
        for n, (source, target) in enumerate(((ids, every_id), (gains, every_gain))):
            copy = pltpu.make_async_remote_copy(
                src_ref=source,
                dst_ref=target.at[k],
                send_sem=send.at[n, k],
                recv_sem=recv.at[n, k],
                device_id=peers[k - 1],
                device_id_type=MESH,
            )
            copy.start()
            copies.append(copy)
    for copy in copies:
        copy.wait()


def spread(ids, gains):
    return pl.pallas_call(
        spread_kernel,
        in_specs=[pl.BlockSpec(memory_space=pltpu.VMEM)] * 2,
        out_specs=[pl.BlockSpec(memory_space=pltpu.VMEM)] * 2,
        out_shape=[
            jax.ShapeDtypeStruct((8, *ids.shape), ids.dtype),
            jax.ShapeDtypeStruct((8, *gains.shape), gains.dtype),
        ],
        scratch_shapes=[pltpu.SemaphoreType.DMA((2, 8)), pltpu.SemaphoreType.DMA((2, 8))],
        compiler_params=pltpu.CompilerParams(collective_id=1, has_side_effects=True),
        name="spread",
    )(ids, gains)


def total_kernel(blocks, out, first, summed, second, send, recv):
    own, rank = lax.axis_index("dp"), lax.axis_index("tensor")
    near = peers_of(own, rank, range(1, 4), "tensor")
    far = peers_of(own, rank, range(1, 8), "dp")
    greet(near + far)
    copies = []
    for k in range(1, 4):
        copy = pltpu.make_async_remote_copy(
            src_ref=blocks,
            dst_ref=first.at[k - 1],
            send_sem=send.at[k - 1],
            recv_sem=recv.at[k - 1],
            device_id=near[k - 1],
            device_id_type=MESH,
        )
        copy.start()
        copies.append(copy)
    for copy in copies:
        copy.wait()
    summed[...] = (blocks[...] + first[0]) + (first[1] + first[2])
    copies = []
    for k in range(1, 8):
        copy = pltpu.make_async_remote_copy(
            src_ref=summed.at[k],
            dst_ref=second.at[k],
            send_sem=send.at[2 + k],
            recv_sem=recv.at[2 + k],
            device_id=far[k - 1],
            device_id_type=MESH,
        )
        copy.start()
        copies.append(copy)
    for copy in copies:
        copy.wait()
    second[0] = summed[0]
    pairs = [second[k] + second[k + 1] for k in (0, 2, 4, 6)]
    out[...] = (pairs[0] + pairs[1]) + (pairs[2] + pairs[3])


def total_over_devices(blocks):
    shape = blocks.shape
    return pl.pallas_call(
        total_kernel,
        in_specs=[pl.BlockSpec(memory_space=pltpu.VMEM)],
        out_specs=pl.BlockSpec(memory_space=pltpu.VMEM),
        out_shape=jax.ShapeDtypeStruct(shape[1:], FLOAT),
        scratch_shapes=[
            pltpu.VMEM((3, *shape), FLOAT),
            pltpu.VMEM(shape, FLOAT),
            pltpu.VMEM(shape, FLOAT),
            pltpu.SemaphoreType.DMA((10,)),
            pltpu.SemaphoreType.DMA((10,)),
        ],
        compiler_params=pltpu.CompilerParams(collective_id=2, has_side_effects=True),
        name="total",
    )(blocks)


def dp_turn(blocks):
    return [blocks[0]] + [swap(blocks[k], "dp", k) for k in range(1, len(blocks))]


def tensor_gather(block):
    half = jnp.concatenate([block, swap(block, "tensor", 2)], axis=0)
    return jnp.concatenate([half, swap(half, "tensor", 1)], axis=0)


def tensor_scatter(full):
    half = full.shape[0] // 2
    quarter = half // 2
    both = full[:half] + swap(full[half:], "tensor", 1)
    there = swap(both[quarter:].astype(HALF), "tensor", 2)
    return both[:quarter] + there.astype(FLOAT)


def lookup_kernel(ids, turned, out, table, corner, rows):
    count = rows.shape[0]
    width, vocab = turned.shape

    @pl.when(pl.program_id(0) == 0)
    def _():
        corner[...] = jnp.zeros_like(corner)
        for v in range(0, vocab, LANES):
            some = min(LANES, vocab - v)
            corner[:width, :some] = turned[:, v : v + some].astype(HALF).astype(FLOAT)
            if some < LANES:
                corner[:width, some:] = jnp.zeros((width, LANES - some), FLOAT)
            table[v : v + LANES, :] = corner[...].T
        if vocab % LANES == 0:
            table[vocab:, :] = jnp.zeros((LANES, LANES), FLOAT)

    def body(i, carry):
        for u in range(16):
            r = i * 16 + u
            rows[pl.ds(r, 1), :] = table[pl.ds(ids[0, 0, r], 1), :]
        return carry

    lax.fori_loop(0, count // 16, body, 0)
    out[...] = rows[:, : out.shape[1]].astype(HALF)


def lookup(turned, ids):
    count = ids.shape[0]
    width, vocab = turned.shape
    padded = (vocab // LANES + 1) * LANES
    return pl.pallas_call(
        lookup_kernel,
        grid=(count // ROWS,),
        in_specs=[
            pl.BlockSpec((1, 1, ROWS), lambda i: (i, 0, 0), memory_space=pltpu.SMEM),
            pl.BlockSpec(turned.shape, lambda i: (0, 0), pipeline_mode=pl.Buffered(1)),
        ],
        out_specs=pl.BlockSpec((ROWS, width), lambda i: (i, 0)),
        out_shape=jax.ShapeDtypeStruct((count, width), HALF),
        scratch_shapes=[
            pltpu.VMEM((padded, LANES), FLOAT),
            pltpu.VMEM((LANES, LANES), FLOAT),
            pltpu.VMEM((ROWS, LANES), FLOAT),
        ],
        compiler_params=pltpu.CompilerParams(vmem_limit_bytes=VMEM_LIMIT),
        cost_estimate=pl.CostEstimate(flops=2**34, bytes_accessed=2**24, transcendentals=0),
        name="lookup",
    )(ids.reshape(count // ROWS, 1, ROWS), turned)


def collect_kernel(ids, grads, out, rows, *sums):
    step = pl.program_id(0)
    count = rows.shape[0]
    width, vocab = out.shape

    @pl.when(step == 0)
    def _():
        rows[...] = jnp.zeros_like(rows)
        for total in sums:
            total[...] = jnp.zeros_like(total)

    rows[:, :width] = grads[...].astype(FLOAT)

    def body(i, carry):
        for u in range(16):
            r = i * 16 + u
            total = sums[u % len(sums)]
            place = pl.ds(ids[0, 0, r], 1)
            total[place, :] = total[place, :] + rows[pl.ds(r, 1), :]
        return carry

    lax.fori_loop(0, count // 16, body, 0)

    @pl.when(step == pl.num_programs(0) - 1)
    def _():
        for v in range(0, vocab, LANES):
            total = sums[0][v : v + LANES, :]
            for other in sums[1:]:
                total = total + other[v : v + LANES, :]
            some = min(LANES, vocab - v)
            out[:, v : v + some] = total.T[:width, :some]


def collect(grads, ids, vocab):
    count = ids.shape[0]
    width = grads.shape[1]
    padded = (vocab // LANES + 1) * LANES
    return pl.pallas_call(
        collect_kernel,
        grid=(count // ROWS,),
        in_specs=[
            pl.BlockSpec((1, 1, ROWS), lambda i: (i, 0, 0), memory_space=pltpu.SMEM),
            pl.BlockSpec((ROWS, width), lambda i: (i, 0)),
        ],
        out_specs=pl.BlockSpec((width, vocab), lambda i: (0, 0)),
        out_shape=jax.ShapeDtypeStruct((width, vocab), FLOAT),
        scratch_shapes=[pltpu.VMEM((ROWS, LANES), FLOAT)]
        + [pltpu.VMEM((padded, LANES), FLOAT)] * 8,
        compiler_params=pltpu.CompilerParams(vmem_limit_bytes=VMEM_LIMIT),
        cost_estimate=pl.CostEstimate(flops=2**34, bytes_accessed=2**24, transcendentals=0),
        name="collect",
    )(ids.reshape(count // ROWS, 1, ROWS), grads)


def scan_kernel(vocab, offset, norm, weight, target, logits, stats, peak, total, hit):
    step = pl.program_id(0)
    steps = pl.num_programs(0)
    tile = weight.shape[1]
    rows = norm.shape[0]

    @pl.when(step == 0)
    def _():
        peak[...] = jnp.full_like(peak, NEG)
        total[...] = jnp.zeros_like(total)
        hit[...] = jnp.zeros_like(hit)

    def work(width):
        lane = lax.broadcasted_iota(jnp.int32, (CHUNK, LANES), 1)
        for r in range(0, rows, CHUNK):
            part = pl.ds(r, CHUNK)
            value = jnp.dot(norm[part, :], weight[...], preferred_element_type=FLOAT)
            logits[part, :] = value
            aim = target[part, :] - (offset + step * tile)
            slabs, found = [], hit[part, :]
            for c in range(0, width, LANES):
                slab = value[:, c : c + LANES]
                if c + LANES > width:
                    slab = jnp.where(lane < width - c, slab, NEG)
                slabs.append(slab)
                found = found + jnp.where(lane == aim - c, slab, 0.0)
            hit[part, :] = found
            before = peak[part, :]
            top = functools.reduce(jnp.maximum, slabs, before)
            added = total[part, :] * jnp.exp(before - top)
            for slab in slabs:
                added = added + jnp.exp(slab - top)
            total[part, :] = added
            peak[part, :] = top

    last = vocab - (pl.cdiv(vocab, tile) - 1) * tile
    if last == tile:
        work(tile)
    else:
        pl.when(step < steps - 1)(lambda: work(tile))
        pl.when(step == steps - 1)(lambda: work(last))

    @pl.when(step == steps - 1)
    def _():
        top = jnp.max(peak[...], axis=1, keepdims=True)
        added = jnp.sum(total[...] * jnp.exp(peak[...] - top), axis=1, keepdims=True)
        found = jnp.sum(hit[...], axis=1, keepdims=True)
        lane = lax.broadcasted_iota(jnp.int32, (rows, LANES), 1)
        joined = jnp.where(lane == 0, top, jnp.where(lane == 1, added, jnp.where(lane == 2, found, 0.0)))
        stats[...] = joined.T[:8, :]

def head_scan(norm, weight, target, offset):
    rows, depth = norm.shape
    vocab = weight.shape[1]
    return pl.pallas_call(
        functools.partial(scan_kernel, vocab, offset),
        grid=(pl.cdiv(vocab, TILE),),
        in_specs=[
            pl.BlockSpec((rows, depth), lambda i: (0, 0)),
            pl.BlockSpec((depth, TILE), lambda i: (0, i)),
            pl.BlockSpec((rows, 1), lambda i: (0, 0)),
        ],
        out_specs=[
            pl.BlockSpec((rows, TILE), lambda i: (0, i)),
            pl.BlockSpec((8, rows), lambda i: (0, 0)),
        ],
        out_shape=[
            jax.ShapeDtypeStruct((rows, vocab), FLOAT),
            jax.ShapeDtypeStruct((8, rows), FLOAT),
        ],
        scratch_shapes=[pltpu.VMEM((rows, LANES), FLOAT)] * 3,
        compiler_params=pltpu.CompilerParams(vmem_limit_bytes=VMEM_LIMIT),
        cost_estimate=pl.CostEstimate(flops=2*rows*depth*vocab, bytes_accessed=4*rows*vocab+2*depth*vocab, transcendentals=rows*vocab),
        name="head_scan",
    )(norm, weight, target)

def grad_kernel(vocab, offset, turned, weight, target, log_total, scale, logits, before, grad, final, total, slope):
    step = pl.program_id(0)
    steps = pl.num_programs(0)
    tile = weight.shape[1]
    rows = logits.shape[0]

    @pl.when(step == 0)
    def _():
        total[...] = before[...]

    def work(width):
        lane = lax.broadcasted_iota(jnp.int32, (CHUNK, tile), 1)
        table = weight[...]
        if width < tile:
            table = jnp.where(lax.broadcasted_iota(jnp.int32, table.shape, 1) < width, table, 0.0)
        for r in range(0, rows, CHUNK):
            part = pl.ds(r, CHUNK)
            aim = target[part, :] - (offset + step * tile)
            value = jnp.exp(logits[part, :] - log_total[part, :])
            value = (value - jnp.where(lane == aim, 1.0, 0.0)) * scale[part, :]
            if width < tile:
                value = jnp.where(lane < width, value, 0.0)
            value = value.astype(HALF)
            slope[part, :] = value
            total[part, :] = total[part, :] + lax.dot_general(value, table, (((1,), (1,)), ((), ())), preferred_element_type=FLOAT)
        grad[...] = jnp.dot(turned[...], slope[...], preferred_element_type=FLOAT).astype(HALF)

    last = vocab - (pl.cdiv(vocab, tile) - 1) * tile
    if last == tile:
        work(tile)
    else:
        pl.when(step < steps - 1)(lambda: work(tile))
        pl.when(step == steps - 1)(lambda: work(last))

    @pl.when(step == steps - 1)
    def _():
        final[...] = total[...]

def head_grad(turned, weight, target, log_total, scale, logits, before, offset):
    depth, rows = turned.shape
    vocab = weight.shape[1]
    column = pl.BlockSpec((rows, 1), lambda i: (0, 0), pipeline_mode=pl.Buffered(1))
    whole = pl.BlockSpec((rows, depth), lambda i: (0, 0), pipeline_mode=pl.Buffered(1))
    return pl.pallas_call(
        functools.partial(grad_kernel, vocab, offset),
        grid=(pl.cdiv(vocab, TILE),),
        in_specs=[
            pl.BlockSpec((depth, rows), lambda i: (0, 0), pipeline_mode=pl.Buffered(1)),
            pl.BlockSpec((depth, TILE), lambda i: (0, i)),
            column, column, column,
            pl.BlockSpec((rows, TILE), lambda i: (0, i)),
            whole,
        ],
        out_specs=[
            pl.BlockSpec((depth, TILE), lambda i: (0, i)),
            whole,
        ],
        out_shape=[
            jax.ShapeDtypeStruct((depth, vocab), HALF),
            jax.ShapeDtypeStruct((rows, depth), FLOAT),
        ],
        scratch_shapes=[pltpu.VMEM((rows, depth), FLOAT), pltpu.VMEM((rows, TILE), HALF)],
        compiler_params=pltpu.CompilerParams(vmem_limit_bytes=VMEM_LIMIT),
        cost_estimate=pl.CostEstimate(flops=4*rows*depth*vocab, bytes_accessed=4*rows*vocab+4*depth*vocab, transcendentals=rows*vocab),
        name="head_grad",
    )(turned, weight, target, log_total, scale, logits, before)


def attention_scores(query, key, allowed):
    scale = query.shape[-1] ** (-0.5)
    raw = jnp.einsum("qhd,khd->hqk", query, key, preferred_element_type=FLOAT)
    return jnp.where(allowed[None], scale * raw, NEG)


def attention_forward(qkv, cosine, sine, allowed):
    length, head_dim = qkv.shape[0], cosine.shape[-1]
    qkv = qkv.reshape(length, -1, 3, head_dim)
    query = rotary(qkv[:, :, 0], cosine, sine).astype(HALF)
    key = rotary(qkv[:, :, 1], cosine, sine).astype(HALF)
    value = qkv[:, :, 2].astype(HALF)
    scores = attention_scores(query, key, allowed)
    peak = jnp.max(scores, axis=-1, keepdims=True)
    expo = jnp.exp(scores - peak)
    summed = jnp.sum(expo, axis=-1, keepdims=True)
    probs = (expo / summed).astype(HALF)
    log_total = peak + jnp.log(summed)
    attended = jnp.einsum("hqk,khd->qhd", probs, value, preferred_element_type=FLOAT)
    attended = attended.reshape(length, -1).astype(HALF)
    return (attended, (query, key, value, log_total))


def attention_backward(d_attended, kept, cosine, sine, allowed):
    query, key, value, log_total = kept
    length, head_dim = query.shape[0], query.shape[-1]
    scale = head_dim ** (-0.5)
    d_attended = d_attended.reshape(length, -1, head_dim)
    probs = jnp.exp(attention_scores(query, key, allowed) - log_total)
    d_value = jnp.einsum(
        "hqk,qhd->khd", probs.astype(HALF), d_attended, preferred_element_type=FLOAT
    )
    d_probs = jnp.einsum("qhd,khd->hqk", d_attended, value, preferred_element_type=FLOAT)
    centre = jnp.sum(probs * d_probs, axis=-1, keepdims=True)
    d_scores = (probs * (d_probs - centre)).astype(HALF)
    d_query = scale * jnp.einsum("hqk,khd->qhd", d_scores, key, preferred_element_type=FLOAT)
    d_key = scale * jnp.einsum("hqk,qhd->khd", d_scores, query, preferred_element_type=FLOAT)
    d_qkv = jnp.stack(
        [unrotate(d_query, cosine, sine), unrotate(d_key, cosine, sine), d_value], axis=2
    )
    return d_qkv.reshape(length, -1).astype(HALF)


def normed_backward(grad, values, gain):
    unused, pull = jax.vjp(normed, values, gain)
    return pull(grad)


def product(left, right, over_left, over_right):
    return lax.dot_general(
        left, right, (((over_left,), (over_right,)), ((), ())), preferred_element_type=FLOAT
    )


def adam(weight, grad, first, second, rate, decay):
    first = BETA_ONE * first + (1.0 - BETA_ONE) * grad
    second = BETA_TWO * second + (1.0 - BETA_TWO) * grad * grad
    first_hat = first / (1.0 - BETA_ONE**STEP)
    second_hat = second / (1.0 - BETA_TWO**STEP)
    weight = weight - rate * (first_hat / (jnp.sqrt(second_hat) + ADAM_EPS) + decay * weight)
    return (weight, first, second, weight.astype(HALF))


def shards(
    token_ids,
    targets,
    segments,
    completion,
    micro_order,
    *state,
):
    weights, means, squares = state[:7], state[7:14], state[14:21]
    embedding, attn_in, attn_out, ffn_in, ffn_out, head_table, norm_gains = weights
    group = lax.axis_size("dp")
    parts = lax.axis_size("tensor")
    own, rank = lax.axis_index("dp"), lax.axis_index("tensor")
    vocab, width = embedding.shape
    start = rank * vocab
    seqs, length = token_ids.shape
    micro = micro_order.shape[1]
    share = length // parts
    turn = jnp.array(TURN, jnp.int32)
    dp_order = own ^ jnp.arange(group, dtype=jnp.int32)
    tensor_order = rank ^ turn
    ffn = ffn_out.shape[0]
    qkv_width = attn_in.shape[1]

    attn_w = dp_gather(jnp.concatenate([attn_in, attn_out.T], axis=1).astype(HALF))
    attn_in_b, attn_out_b = attn_w[:, :qkv_width], attn_w[:, qkv_width:]
    ffn_w = dp_gather(
        jnp.concatenate([ffn_in.reshape(width, -1), ffn_out.T], axis=1).astype(HALF)
    )
    ffn_in_b, ffn_out_b = ffn_w[:, : 2 * ffn], ffn_w[:, 2 * ffn :]
    bounds = list(range(0, vocab, HEAD_PART)) + [vocab]
    head_half = head_table.astype(HALF)
    head_b = [
        lax.all_gather(head_half[:, low:high], "dp", axis=0, tiled=True)
        for low, high in zip(bounds, bounds[1:])
    ]

    flags = completion.astype(FLOAT)
    picked_rows = micro_order[0]
    local_counts = jnp.sum(completion, axis=1)[picked_rows]
    id_rows = seqs * length // LANES
    packed = jnp.concatenate([token_ids.reshape(-1), jnp.pad(local_counts, (0, 8 * LANES - micro))])
    packed = packed.reshape(id_rows + 8, LANES)
    gains = jnp.pad(norm_gains.astype(HALF).astype(FLOAT), ((0, 5), (0, LANES - width)))
    if group == 8 and parts == 4:
        packed, gains = spread(packed, gains)
        gains = jnp.take(gains, dp_order, axis=0)
    else:
        packed, gains = lax.all_gather(packed, "dp"), lax.all_gather(gains, "dp")
        packed = jnp.take(packed, dp_order, axis=0)
    gains = gains[:, :3, :width].transpose(1, 0, 2).reshape(3, -1)
    counts = jnp.sum(packed[:, id_rows, :micro].astype(FLOAT), axis=0)
    slot = jnp.argmax(picked_rows[None, :] == jnp.arange(seqs)[:, None], axis=1)
    row_weights = (1.0 / jnp.maximum(counts, 1.0))[slot]

    every_id = packed[:, :id_rows].reshape(group, seqs, parts, share)
    every_id = jnp.take(every_id, tensor_order, axis=2)
    every_id = every_id.transpose(2, 0, 1, 3).reshape(-1) - start
    every_id = jnp.where((every_id >= 0) & (every_id < vocab), every_id, vocab)

    def local_order(values):
        return jnp.take(values.reshape(seqs, parts, share), tensor_order, axis=1).reshape(
            seqs, length
        )

    targets, segments, flags = local_order(targets), local_order(segments), local_order(flags)
    places = (tensor_order[:, None] * share + jnp.arange(share, dtype=jnp.int32)).reshape(-1)
    cosine, sine = tables(places, HEAD_DIM)

    rows = lookup(embedding.T, every_id).reshape(parts, group, seqs * share, width)
    rows = rows[:2] + swap(rows[2:], "tensor", 1)
    rows = rows[0] + swap(rows[1], "tensor", 2)
    if group == 8:
        rows = jnp.stack(dp_turn([rows[k] for k in range(group)]))
        rows = jnp.take(rows, dp_order, axis=0)
    else:
        rows = lax.all_to_all(jnp.take(rows, dp_order, axis=0), "dp", 0, 0)
    stream0 = rows.transpose(1, 0, 2).reshape(seqs * share, -1).astype(FLOAT)
    stream0 = [stream0[j * share : (j + 1) * share] for j in range(seqs)]

    allowed, kept, full_norm, stream1, stream2 = [], [], [], [], []
    for j in range(seqs):
        allowed.append(
            (places[:, None] >= places[None, :])
            & (segments[j][:, None] == segments[j][None, :])
        )
    attn_norm, attended = [], []
    for j in range(seqs):
        attn_norm.append(tensor_gather(normed(stream0[j], gains[0]).astype(HALF)))
        qkv = product(attn_norm[j], attn_in_b, 1, 0)
        out, keep = attention_forward(qkv, cosine, sine, allowed[j])
        attended.append(out)
        kept.append(keep)
        stream1.append(stream0[j] + tensor_scatter(product(out, attn_out_b, 1, 1)))
    ffn_norm, gate_up, hidden = [], [], []
    for j in range(seqs):
        ffn_norm.append(tensor_gather(normed(stream1[j], gains[1]).astype(HALF)))
        gate_up.append(product(ffn_norm[j], ffn_in_b, 1, 0))
        hidden.append((jax.nn.silu(gate_up[j][:, :ffn]) * gate_up[j][:, ffn:]).astype(HALF))
        stream2.append(stream1[j] + tensor_scatter(product(hidden[j], ffn_out_b, 1, 1)))

    def both_order(values):
        return values.reshape(seqs, parts, share).transpose(1, 0, 2).reshape(-1)

    joint = jnp.concatenate(stream2, axis=0)
    final_norm = tensor_gather(normed(joint, gains[2]).astype(HALF))
    aims = both_order(targets) - start
    aims = jnp.where((aims >= 0) & (aims < vocab), aims, -1)[:, None]
    joint_flags = both_order(flags)
    logits, stats = [], []
    for low, table in zip(bounds, head_b):
        out, stat = head_scan(final_norm, table, aims, low)
        logits.append(out)
        stats.append(stat[:3])
    own_peak = functools.reduce(jnp.maximum, [stat[0] for stat in stats])
    own_sum = sum(stat[1] * jnp.exp(stat[0] - own_peak) for stat in stats)
    stats = jnp.stack([own_peak, own_sum, sum(stat[2] for stat in stats)])
    stats = stats.reshape(3, parts, -1)
    every = [stats.reshape(3, -1)]
    for bit in range(1, parts):
        there = swap(stats, "tensor", bit)
        order = [TURN.index(TURN[p] ^ bit) for p in range(parts)]
        every.append(jnp.concatenate([there[:, p] for p in order], axis=1))
    peak = functools.reduce(jnp.maximum, [stat[0] for stat in every])
    summed = sum(stat[1] * jnp.exp(stat[0] - peak) for stat in every)
    target_logit = sum(stat[2] for stat in every)
    log_total = peak + jnp.log(summed)
    seq_loss = jnp.sum(
        ((log_total - target_logit) * joint_flags).reshape(parts, seqs, share), axis=(0, 2)
    )
    scale = joint_flags * jnp.tile(jnp.repeat(row_weights, share), parts)
    final_turned = final_norm.T
    d_final = jnp.zeros(final_norm.shape, FLOAT)
    g_head = []
    for low, table, out in zip(bounds, head_b, logits):
        g_part, d_final = head_grad(
            final_turned, table, aims, log_total[:, None], scale[:, None], out, d_final, low
        )
        g_head.append(lax.psum_scatter(g_part, "dp", scatter_dimension=0, tiled=True))
    g_head = jnp.concatenate(g_head, axis=1).astype(FLOAT)
    d_final = tensor_scatter(d_final)
    d_final = [d_final[j * share : (j + 1) * share] for j in range(seqs)]

    g_gain = [[], [], []]
    d_gate_up, d_branch2, d_stream1 = [], [], []
    for j in range(seqs):
        d_stream2, part = normed_backward(d_final[j], stream2[j], gains[2])
        g_gain[2].append(part)
        d_branch2.append(tensor_gather(d_stream2.astype(HALF)))
        d_hidden = product(d_branch2[j], ffn_out_b, 1, 0)
        unused, pull = jax.vjp(
            lambda both: jax.nn.silu(both[:, :ffn]) * both[:, ffn:], gate_up[j]
        )
        d_gate_up.append(pull(d_hidden)[0].astype(HALF))
        d_norm = tensor_scatter(product(d_gate_up[j], ffn_in_b, 1, 1))
        d_part, part = normed_backward(d_norm, stream1[j], gains[1])
        g_gain[1].append(part)
        d_stream1.append(d_stream2 + d_part)
    g_ffn_in = product(ffn_norm[0], d_gate_up[0], 0, 0) + product(ffn_norm[1], d_gate_up[1], 0, 0)
    g_ffn_out = product(d_branch2[0], hidden[0], 0, 0) + product(d_branch2[1], hidden[1], 0, 0)
    g_ffn = dp_scatter(jnp.concatenate([g_ffn_in.astype(HALF), g_ffn_out.astype(HALF)], axis=1))
    d_branch1, d_qkv, d_stream0 = [], [], []
    for j in range(seqs):
        d_branch1.append(tensor_gather(d_stream1[j].astype(HALF)))
        d_attended = product(d_branch1[j], attn_out_b, 1, 0).astype(HALF)
        d_qkv.append(attention_backward(d_attended, kept[j], cosine, sine, allowed[j]))
        d_norm = tensor_scatter(product(d_qkv[j], attn_in_b, 1, 1))
        d_part, part = normed_backward(d_norm, stream0[j], gains[0])
        g_gain[0].append(part)
        d_stream0.append((d_stream1[j] + d_part).astype(HALF))
    g_attn_in = product(attn_norm[0], d_qkv[0], 0, 0) + product(attn_norm[1], d_qkv[1], 0, 0)
    g_attn_out = product(d_branch1[0], attended[0], 0, 0) + product(
        d_branch1[1], attended[1], 0, 0
    )
    g_attn = dp_scatter(jnp.concatenate([g_attn_in.astype(HALF), g_attn_out.astype(HALF)], axis=1))

    token_grads = jnp.concatenate(d_stream0, axis=0)
    blocks = token_grads.reshape(seqs * share, group, width).transpose(1, 0, 2)
    if group == 8:
        blocks = jnp.take(blocks, dp_order, axis=0)
        blocks = jnp.stack(dp_turn([blocks[k] for k in range(group)]))
    else:
        blocks = jnp.take(lax.all_to_all(blocks, "dp", 0, 0), dp_order, axis=0)
    blocks = tensor_gather(blocks[None]).reshape(-1, width)
    g_embed = collect(blocks, every_id, vocab).T

    gain_sum = jnp.stack([sum(parts_of) for parts_of in g_gain]).reshape(3, group, width)
    if group == 8 and parts == 4:
        gain_sum = jnp.take(gain_sum.transpose(1, 0, 2), dp_order, axis=0)
        gain_sum = jnp.pad(gain_sum, ((0, 0), (0, 5), (0, LANES - width)))
        g_gains = total_over_devices(gain_sum)[:3, :width]
    else:
        g_gains = jnp.take(lax.psum(gain_sum, ("dp", "tensor")), own, axis=1)

    reduced = (
        g_embed,
        g_attn[:, :qkv_width],
        g_attn[:, qkv_width:].T,
        g_ffn[:, : 2 * ffn].reshape(ffn_in.shape),
        g_ffn[:, 2 * ffn :].T,
        g_head,
        g_gains,
    )
    owner = (rank == 0).astype(FLOAT)
    squared = jnp.zeros((), FLOAT)
    for place in range(6):
        squared = squared + jnp.sum(reduced[place] * reduced[place])
    squared = squared + owner * jnp.sum(reduced[6] * reduced[6])
    losses = seq_loss[picked_rows] * owner
    if group == 8 and parts == 4:
        sums = jnp.pad(jnp.concatenate([squared[None], losses]), (0, 8 * LANES - 1 - micro))
        sums = total_over_devices(jnp.broadcast_to(sums.reshape(1, 8, LANES), (8, 8, LANES)))
        squared, loss_sums = sums[0, 0], sums[0, 1 : 1 + micro]
    else:
        squared, loss_sums = lax.psum((squared, losses), ("dp", "tensor"))
    grad_norm = jnp.sqrt(squared)
    factor = CLIP / jnp.maximum(grad_norm, CLIP)
    updated = []
    for place in range(7):
        rate = LR_GAIN if place == 6 else LR
        decay = 0.0 if place == 6 else DECAY
        arrays = (weights[place], reduced[place], means[place], squares[place])
        if place in (0, 2, 4):
            arrays = tuple(array.T for array in arrays)
        results = adam(arrays[0], arrays[1] * factor, arrays[2], arrays[3], rate, decay)
        updated.extend(result.T if place in (0, 2, 4) else result for result in results)
    return (jnp.stack([loss_sums, counts]), grad_norm, *updated)


def solution(mesh):
    in_specs = (
        P("dp", None),
        P("dp", None),
        P("dp", None),
        P("dp", None),
        P("dp", None),
        P("tensor", "dp"),
        P("dp", "tensor"),
        P("tensor", "dp"),
        P("dp", None, "tensor"),
        P("tensor", "dp"),
        P("dp", "tensor"),
        P(None, "dp"),
        P("tensor", "dp"),
        P("dp", "tensor"),
        P("tensor", "dp"),
        P("dp", None, "tensor"),
        P("tensor", "dp"),
        P("dp", "tensor"),
        P(None, "dp"),
        P("tensor", "dp"),
        P("dp", "tensor"),
        P("tensor", "dp"),
        P("dp", None, "tensor"),
        P("tensor", "dp"),
        P("dp", "tensor"),
        P(None, "dp"),
    )
    out_specs = (
        P(),
        P(),
        P("tensor", "dp"),
        P("tensor", "dp"),
        P("tensor", "dp"),
        P("tensor", "dp"),
        P("dp", "tensor"),
        P("dp", "tensor"),
        P("dp", "tensor"),
        P("dp", "tensor"),
        P("tensor", "dp"),
        P("tensor", "dp"),
        P("tensor", "dp"),
        P("tensor", "dp"),
        P("dp", None, "tensor"),
        P("dp", None, "tensor"),
        P("dp", None, "tensor"),
        P("dp", None, "tensor"),
        P("tensor", "dp"),
        P("tensor", "dp"),
        P("tensor", "dp"),
        P("tensor", "dp"),
        P("dp", "tensor"),
        P("dp", "tensor"),
        P("dp", "tensor"),
        P("dp", "tensor"),
        P(None, "dp"),
        P(None, "dp"),
        P(None, "dp"),
        P(None, "dp"),
    )
    return jax.shard_map(shards, mesh=mesh, in_specs=in_specs, out_specs=out_specs, check_vma=False)
```

```python
import functools

import jax
import jax.numpy as jnp
from jax import lax
from jax.experimental import pallas as pl
from jax.experimental.pallas import tpu as pltpu
from jax.sharding import PartitionSpec as P

HEAD_DIM = 64
STEP = 10


EPS = 1e-05
CLIP = 0.01
LR = 0.03
LR_GAIN = 0.5
BETA_ONE = 0.9
BETA_TWO = 0.95
ADAM_EPS = 1e-08
DECAY = 0.1
NEG = -1e30
FLOAT = jnp.float32
HALF = jnp.bfloat16
LANES = 128
ROWS = 1024
HEAD_PART = 4096
VMEM_LIMIT = 56 * 2**20
TILE = 512
CHUNK = 256
MESH = pl.DeviceIdType.MESH

TURN = (0, 2, 1, 3)


def swap(value, axis, bit):
    pairs = [(i, i ^ bit) for i in range(lax.axis_size(axis))]
    return lax.ppermute(value, axis, pairs)


def normed(values, gain):
    return values * lax.rsqrt(jnp.mean(values * values, axis=-1, keepdims=True) + EPS) * gain


def tables(length, width):
    inverse = 10000.0 ** (-jnp.arange(0, width, 2, dtype=FLOAT) / width)
    angle = inverse[:, None] * jnp.arange(length, dtype=FLOAT)[None, :]
    return jnp.cos(angle), jnp.sin(angle)


def gather_first(block):
    if lax.axis_size("dp") != 8:
        return []
    return [swap(block, "dp", k) for k in (2, 4, 6)]


def gather_last(block, parts):
    group = lax.axis_size("dp")
    if group != 8:
        return lax.all_gather(block, "dp", axis=0, tiled=True)
    parts = dict(zip((0, 2, 4, 6), [block, *parts]))
    for k in (0, 2, 4, 6):
        parts[k + 1] = swap(parts[k], "dp", 1)
    rows = block.shape[0]
    own = lax.axis_index("dp")
    full = jnp.zeros((group * rows, block.shape[1]), block.dtype)
    for k in range(group):
        full = lax.dynamic_update_slice(full, parts[k], ((own ^ k) * rows, 0))
    return full


def block_of(full, k):
    rows = full.shape[0] // lax.axis_size("dp")
    own = lax.axis_index("dp")
    return lax.dynamic_slice(full, ((own ^ k) * rows, 0), (rows, full.shape[1]))


def scatter_first(full):
    if lax.axis_size("dp") != 8:
        return []
    return [swap(block_of(full, k + 1), "dp", 1) for k in (2, 4, 6, 0)]


def scatter_last(full, parts):
    if lax.axis_size("dp") != 8:
        return lax.psum_scatter(full.astype(FLOAT), "dp", scatter_dimension=0, tiled=True)
    sums = {
        k: block_of(full, k).astype(FLOAT) + part.astype(FLOAT)
        for k, part in zip((2, 4, 6, 0), parts)
    }
    total = sums[0]
    for k in (2, 4, 6):
        total = total + swap(sums[k].astype(HALF), "dp", k).astype(FLOAT)
    return total


def peers_of(own, rank, bits, axis):
    if axis == "dp":
        return [(own ^ k, rank) for k in bits]
    return [(own, rank ^ k) for k in bits]


def greet(peers):
    barrier = pltpu.get_barrier_semaphore()
    for peer in peers:
        pl.semaphore_signal(barrier, inc=1, device_id=peer, device_id_type=MESH)
    pl.semaphore_wait(barrier, len(peers))


def spread_kernel(ids, gains, every_id, every_gain, send, recv):
    own, rank = lax.axis_index("dp"), lax.axis_index("tensor")
    peers = peers_of(own, rank, range(1, 8), "dp")
    greet(peers)
    every_id[0] = ids[...]
    every_gain[0] = gains[...]
    copies = []
    for k in range(1, 8):
        for n, (source, target) in enumerate(((ids, every_id), (gains, every_gain))):
            copy = pltpu.make_async_remote_copy(
                src_ref=source,
                dst_ref=target.at[k],
                send_sem=send.at[n, k],
                recv_sem=recv.at[n, k],
                device_id=peers[k - 1],
                device_id_type=MESH,
            )
            copy.start()
            copies.append(copy)
    for copy in copies:
        copy.wait()


def spread(ids, gains):
    return pl.pallas_call(
        spread_kernel,
        in_specs=[pl.BlockSpec(memory_space=pltpu.VMEM)] * 2,
        out_specs=[pl.BlockSpec(memory_space=pltpu.VMEM)] * 2,
        out_shape=[
            jax.ShapeDtypeStruct((8, *ids.shape), ids.dtype),
            jax.ShapeDtypeStruct((8, *gains.shape), gains.dtype),
        ],
        scratch_shapes=[pltpu.SemaphoreType.DMA((2, 8)), pltpu.SemaphoreType.DMA((2, 8))],
        compiler_params=pltpu.CompilerParams(collective_id=1, has_side_effects=True),
        name="spread",
    )(ids, gains)


def total_kernel(blocks, out, first, summed, second, send, recv):
    own, rank = lax.axis_index("dp"), lax.axis_index("tensor")
    near = peers_of(own, rank, range(1, 4), "tensor")
    far = peers_of(own, rank, range(1, 8), "dp")
    greet(near + far)
    copies = []
    for k in range(1, 4):
        copy = pltpu.make_async_remote_copy(
            src_ref=blocks,
            dst_ref=first.at[k - 1],
            send_sem=send.at[k - 1],
            recv_sem=recv.at[k - 1],
            device_id=near[k - 1],
            device_id_type=MESH,
        )
        copy.start()
        copies.append(copy)
    for copy in copies:
        copy.wait()
    summed[...] = (blocks[...] + first[0]) + (first[1] + first[2])
    copies = []
    for k in range(1, 8):
        copy = pltpu.make_async_remote_copy(
            src_ref=summed.at[k],
            dst_ref=second.at[k],
            send_sem=send.at[2 + k],
            recv_sem=recv.at[2 + k],
            device_id=far[k - 1],
            device_id_type=MESH,
        )
        copy.start()
        copies.append(copy)
    for copy in copies:
        copy.wait()
    second[0] = summed[0]
    pairs = [second[k] + second[k + 1] for k in (0, 2, 4, 6)]
    out[...] = (pairs[0] + pairs[1]) + (pairs[2] + pairs[3])


def total_over_devices(blocks):
    shape = blocks.shape
    return pl.pallas_call(
        total_kernel,
        in_specs=[pl.BlockSpec(memory_space=pltpu.VMEM)],
        out_specs=pl.BlockSpec(memory_space=pltpu.VMEM),
        out_shape=jax.ShapeDtypeStruct(shape[1:], FLOAT),
        scratch_shapes=[
            pltpu.VMEM((3, *shape), FLOAT),
            pltpu.VMEM(shape, FLOAT),
            pltpu.VMEM(shape, FLOAT),
            pltpu.SemaphoreType.DMA((10,)),
            pltpu.SemaphoreType.DMA((10,)),
        ],
        compiler_params=pltpu.CompilerParams(collective_id=2, has_side_effects=True),
        name="total",
    )(blocks)


def tensor_gather(block):
    half = jnp.concatenate([block, swap(block, "tensor", 2)], axis=0)
    return jnp.concatenate([half, swap(half, "tensor", 1)], axis=0)


def tensor_scatter(full):
    half = full.shape[0] // 2
    quarter = half // 2
    both = full[:half] + swap(full[half:], "tensor", 1)
    there = swap(both[quarter:].astype(HALF), "tensor", 2)
    return both[:quarter] + there.astype(FLOAT)


def lookup_kernel(ids, turned, out, table, corner, rows):
    count = rows.shape[0]
    width, vocab = turned.shape

    @pl.when(pl.program_id(0) == 0)
    def _():
        corner[...] = jnp.zeros_like(corner)
        for v in range(0, vocab, LANES):
            some = min(LANES, vocab - v)
            corner[:width, :some] = turned[:, v : v + some].astype(HALF).astype(FLOAT)
            if some < LANES:
                corner[:width, some:] = jnp.zeros((width, LANES - some), FLOAT)
            table[v : v + LANES, :] = corner[...].T
        if vocab % LANES == 0:
            table[vocab:, :] = jnp.zeros((LANES, LANES), FLOAT)

    def body(i, carry):
        for u in range(16):
            r = i * 16 + u
            rows[pl.ds(r, 1), :] = table[pl.ds(ids[0, 0, r], 1), :]
        return carry

    lax.fori_loop(0, count // 16, body, 0)
    out[...] = rows[:, : out.shape[1]].astype(HALF)


def lookup(turned, ids):
    count = ids.shape[0]
    width, vocab = turned.shape
    padded = (vocab // LANES + 1) * LANES
    return pl.pallas_call(
        lookup_kernel,
        grid=(count // ROWS,),
        in_specs=[
            pl.BlockSpec((1, 1, ROWS), lambda i: (i, 0, 0), memory_space=pltpu.SMEM),
            pl.BlockSpec(turned.shape, lambda i: (0, 0), pipeline_mode=pl.Buffered(1)),
        ],
        out_specs=pl.BlockSpec((ROWS, width), lambda i: (i, 0)),
        out_shape=jax.ShapeDtypeStruct((count, width), HALF),
        scratch_shapes=[
            pltpu.VMEM((padded, LANES), FLOAT),
            pltpu.VMEM((LANES, LANES), FLOAT),
            pltpu.VMEM((ROWS, LANES), FLOAT),
        ],
        compiler_params=pltpu.CompilerParams(vmem_limit_bytes=VMEM_LIMIT),
        cost_estimate=pl.CostEstimate(flops=2**34, bytes_accessed=2**24, transcendentals=0),
        name="lookup",
    )(ids.reshape(count // ROWS, 1, ROWS), turned)


def collect_kernel(waits, ids, grads, *refs):
    out, rows, *sums = refs[waits:]
    step = pl.program_id(0)
    count = rows.shape[0]
    width, vocab = out.shape

    @pl.when(step == 0)
    def _():
        rows[...] = jnp.zeros_like(rows)
        for total in sums:
            total[...] = jnp.zeros_like(total)

    rows[:, :width] = grads[...].astype(FLOAT)

    def body(i, carry):
        for u in range(16):
            r = i * 16 + u
            total = sums[u % len(sums)]
            place = pl.ds(ids[0, 0, r], 1)
            total[place, :] = total[place, :] + rows[pl.ds(r, 1), :]
        return carry

    lax.fori_loop(0, count // 16, body, 0)

    @pl.when(step == pl.num_programs(0) - 1)
    def _():
        for v in range(0, vocab, LANES):
            total = sums[0][v : v + LANES, :]
            for other in sums[1:]:
                total = total + other[v : v + LANES, :]
            some = min(LANES, vocab - v)
            out[:, v : v + some] = total.T[:width, :some]


def collect(grads, ids, vocab, before):
    count = ids.shape[0]
    width = grads.shape[1]
    padded = (vocab // LANES + 1) * LANES
    return pl.pallas_call(
        functools.partial(collect_kernel, len(before)),
        grid=(count // ROWS,),
        in_specs=[
            pl.BlockSpec((1, 1, ROWS), lambda i: (i, 0, 0), memory_space=pltpu.SMEM),
            pl.BlockSpec((ROWS, width), lambda i: (i, 0)),
        ]
        + [pl.BlockSpec(memory_space=pl.ANY)] * len(before),
        out_specs=pl.BlockSpec((width, vocab), lambda i: (0, 0)),
        out_shape=jax.ShapeDtypeStruct((width, vocab), FLOAT),
        scratch_shapes=[pltpu.VMEM((ROWS, LANES), FLOAT)]
        + [pltpu.VMEM((padded, LANES), FLOAT)] * 8,
        compiler_params=pltpu.CompilerParams(vmem_limit_bytes=VMEM_LIMIT),
        cost_estimate=pl.CostEstimate(flops=2**34, bytes_accessed=2**24, transcendentals=0),
        name="collect",
    )(ids.reshape(count // ROWS, 1, ROWS), grads, *before)


def scan_kernel(vocab, offset, norm, weight, target, logits, stats, peak, total, hit, aims):
    step = pl.program_id(0)
    steps = pl.num_programs(0)
    tile = weight.shape[1]
    rows = norm.shape[0]

    @pl.when(step == 0)
    def _():
        peak[...] = jnp.full_like(peak, NEG)
        total[...] = jnp.zeros_like(total)
        hit[...] = jnp.zeros_like(hit)
        aims[...] = jnp.concatenate([target[...]] * (LANES // 8), axis=0).T

    def work(width):
        lane = lax.broadcasted_iota(jnp.int32, (CHUNK, LANES), 1)
        for r in range(0, rows, CHUNK):
            part = pl.ds(r, CHUNK)
            value = jnp.dot(norm[part, :], weight[...], preferred_element_type=FLOAT)
            logits[part, :] = value
            aim = aims[part, 1:2].astype(jnp.int32) - (offset + step * tile)
            slabs, found = [], hit[part, :]
            for c in range(0, width, LANES):
                slab = value[:, c : c + LANES]
                if c + LANES > width:
                    slab = jnp.where(lane < width - c, slab, NEG)
                slabs.append(slab)
                found = found + jnp.where(lane == aim - c, slab, 0.0)
            hit[part, :] = found
            before = peak[part, :]
            top = functools.reduce(jnp.maximum, slabs, before)
            added = total[part, :] * jnp.exp(before - top)
            for slab in slabs:
                added = added + jnp.exp(slab - top)
            total[part, :] = added
            peak[part, :] = top

    last = vocab - (pl.cdiv(vocab, tile) - 1) * tile
    if last == tile:
        work(tile)
    else:
        pl.when(step < steps - 1)(lambda: work(tile))
        pl.when(step == steps - 1)(lambda: work(last))

    @pl.when(step == steps - 1)
    def _():
        top = jnp.max(peak[...], axis=1, keepdims=True)
        added = jnp.sum(total[...] * jnp.exp(peak[...] - top), axis=1, keepdims=True)
        found = jnp.sum(hit[...], axis=1, keepdims=True)
        lane = lax.broadcasted_iota(jnp.int32, (rows, LANES), 1)
        joined = jnp.where(lane == 0, top, jnp.where(lane == 1, added, found))
        stats[...] = joined.T[:8, :]

def head_scan(norm, weight, target, offset):
    rows, depth = norm.shape
    vocab = weight.shape[1]
    return pl.pallas_call(
        functools.partial(scan_kernel, vocab, offset),
        grid=(pl.cdiv(vocab, TILE),),
        in_specs=[
            pl.BlockSpec((rows, depth), lambda i: (0, 0)),
            pl.BlockSpec((depth, TILE), lambda i: (0, i)),
            pl.BlockSpec((8, rows), lambda i: (0, 0)),
        ],
        out_specs=[
            pl.BlockSpec((rows, TILE), lambda i: (0, i)),
            pl.BlockSpec((8, rows), lambda i: (0, 0)),
        ],
        out_shape=[
            jax.ShapeDtypeStruct((rows, vocab), FLOAT),
            jax.ShapeDtypeStruct((8, rows), FLOAT),
        ],
        scratch_shapes=[pltpu.VMEM((rows, LANES), FLOAT)] * 4,
        compiler_params=pltpu.CompilerParams(vmem_limit_bytes=VMEM_LIMIT),
        cost_estimate=pl.CostEstimate(flops=2*rows*depth*vocab, bytes_accessed=4*rows*vocab+2*depth*vocab, transcendentals=rows*vocab),
        name="head_scan",
    )(norm, weight, target)

def grad_kernel(vocab, offset, with_before, *refs):
    turned, weight, info, logits = refs[:4]
    grad, total, slope, columns = refs[4 + with_before :]
    step = pl.program_id(0)
    steps = pl.num_programs(0)
    tile = weight.shape[1]
    rows = logits.shape[0]

    @pl.when(step == 0)
    def _():
        columns[...] = jnp.concatenate([info[...]] * (LANES // 8), axis=0).T
        if with_before:
            total[...] = refs[4][...]
        else:
            total[...] = jnp.zeros_like(total)

    def work(width):
        lane = lax.broadcasted_iota(jnp.int32, (CHUNK, tile), 1)
        table = weight[...]
        if width < tile:
            table = jnp.where(lax.broadcasted_iota(jnp.int32, table.shape, 1) < width, table, 0.0)
        for r in range(0, rows, CHUNK):
            part = pl.ds(r, CHUNK)
            aim = columns[part, 3:4].astype(jnp.int32) - (offset + step * tile)
            value = jnp.exp(logits[part, :] - columns[part, 0:1])
            value = (value - jnp.where(lane == aim, 1.0, 0.0)) * columns[part, 2:3]
            if width < tile:
                value = jnp.where(lane < width, value, 0.0)
            value = value.astype(HALF)
            slope[part, :] = value
            total[part, :] = total[part, :] + lax.dot_general(
                value, table, (((1,), (1,)), ((), ())), preferred_element_type=FLOAT
            )
        grad[...] = jnp.dot(turned[...], slope[...], preferred_element_type=FLOAT).astype(HALF)

    last = vocab - (pl.cdiv(vocab, tile) - 1) * tile
    if last == tile:
        work(tile)
    else:
        pl.when(step < steps - 1)(lambda: work(tile))
        pl.when(step == steps - 1)(lambda: work(last))


def head_grad(turned, weight, info, logits, before, offset):
    depth, rows = turned.shape
    vocab = weight.shape[1]
    whole = pl.BlockSpec((rows, depth), lambda i: (0, 0), pipeline_mode=pl.Buffered(1))
    given = [] if before is None else [before]
    return pl.pallas_call(
        functools.partial(grad_kernel, vocab, offset, len(given)),
        grid=(pl.cdiv(vocab, TILE),),
        in_specs=[
            pl.BlockSpec((depth, rows), lambda i: (0, 0), pipeline_mode=pl.Buffered(1)),
            pl.BlockSpec((depth, TILE), lambda i: (0, i)),
            pl.BlockSpec((8, rows), lambda i: (0, 0)),
            pl.BlockSpec((rows, TILE), lambda i: (0, i)),
        ]
        + [whole] * len(given),
        out_specs=[pl.BlockSpec((depth, TILE), lambda i: (0, i)), whole],
        out_shape=[
            jax.ShapeDtypeStruct((depth, vocab), HALF),
            jax.ShapeDtypeStruct((rows, depth), FLOAT),
        ],
        scratch_shapes=[pltpu.VMEM((rows, TILE), HALF), pltpu.VMEM((rows, LANES), FLOAT)],
        compiler_params=pltpu.CompilerParams(vmem_limit_bytes=VMEM_LIMIT),
        cost_estimate=pl.CostEstimate(
            flops=4 * rows * depth * vocab,
            bytes_accessed=4 * rows * vocab + 4 * depth * vocab,
            transcendentals=rows * vocab,
        ),
        name="head_grad",
    )(turned, weight, info, logits, *given)


def turn_rows(low, high, cosine, sine):
    return low * cosine - high * sine, high * cosine + low * sine


def reach(block, share, longest):
    back = -(-(longest - 1) // share)
    return max(0, block - back) * share


def seen(first, low, high, place):
    keys = low + lax.broadcasted_iota(jnp.int32, (high - low, first.shape[1]), 0)
    queries = place + lax.broadcasted_iota(jnp.int32, (high - low, first.shape[1]), 1)
    return (keys >= first) & (keys <= queries)


def attend_kernel(waits, base, qkv, cosine, sine, first, *refs):
    attended, kept, log_total = refs[waits:]
    seq = pl.program_id(1)
    blocks = base.shape[0]
    length = cosine.shape[1]
    share = length // blocks
    half = HEAD_DIM // 2

    def spot(i):
        return pl.ds(pl.multiple_of(base[i] + seq * share, share), share)

    for i in range(blocks):
        at = pl.ds(i * share, share)
        turns = (cosine[:, at], sine[:, at])
        for c in (0, 1):
            top = c * HEAD_DIM
            low, high = turn_rows(
                qkv[top : top + half, spot(i)], qkv[top + half : top + HEAD_DIM, spot(i)], *turns
            )
            kept[0, top : top + half, at] = low.astype(HALF)
            kept[0, top + half : top + HEAD_DIM, at] = high.astype(HALF)
        kept[0, 2 * HEAD_DIM :, at] = qkv[2 * HEAD_DIM :, spot(i)].astype(HALF)
    key = kept[0, HEAD_DIM : 2 * HEAD_DIM, :].T
    for i in range(blocks):
        low, high = reach(i, share, length // 2), (i + 1) * share
        at = pl.ds(i * share, share)
        scores = jnp.dot(
            key[low:high, :], kept[0, :HEAD_DIM, at], preferred_element_type=FLOAT
        ) * (HEAD_DIM**-0.5)
        scores = jnp.where(seen(first[0, :, at][:1], low, high, i * share), scores, NEG)
        peak = jnp.max(scores, axis=0, keepdims=True)
        expo = jnp.exp(scores - peak)
        summed = jnp.sum(expo, axis=0, keepdims=True)
        probs = (expo * (1.0 / summed)).astype(HALF)
        value = kept[0, 2 * HEAD_DIM :, low:high]
        attended[:, spot(i)] = jnp.dot(value, probs, preferred_element_type=FLOAT).astype(HALF)
        log_total[0, 0, :, at] = jnp.broadcast_to(peak + jnp.log(summed), (8, share))


def attend(base, qkv, cosine, sine, first, before):
    seqs, length = first.shape[0], first.shape[2]
    heads = qkv.shape[0] // (3 * HEAD_DIM)
    tokens = qkv.shape[1]
    return pl.pallas_call(
        functools.partial(attend_kernel, len(before)),
        grid=(heads, seqs),
        in_specs=[
            pl.BlockSpec(memory_space=pltpu.SMEM),
            pl.BlockSpec((3 * HEAD_DIM, tokens), lambda h, j: (h, 0)),
            pl.BlockSpec(cosine.shape, lambda h, j: (0, 0)),
            pl.BlockSpec(sine.shape, lambda h, j: (0, 0)),
            pl.BlockSpec((1, 8, length), lambda h, j: (j, 0, 0)),
        ]
        + [pl.BlockSpec(memory_space=pl.ANY)] * len(before),
        out_specs=[
            pl.BlockSpec((HEAD_DIM, tokens), lambda h, j: (h, 0)),
            pl.BlockSpec((1, 3 * HEAD_DIM, length), lambda h, j: (j, h, 0)),
            pl.BlockSpec((1, 1, 8, length), lambda h, j: (j, h, 0, 0)),
        ],
        out_shape=[
            jax.ShapeDtypeStruct((heads * HEAD_DIM, tokens), HALF),
            jax.ShapeDtypeStruct((seqs, heads * 3 * HEAD_DIM, length), HALF),
            jax.ShapeDtypeStruct((seqs, heads, 8, length), FLOAT),
        ],
        compiler_params=pltpu.CompilerParams(vmem_limit_bytes=VMEM_LIMIT),
        cost_estimate=pl.CostEstimate(
            flops=4 * heads * seqs * length * length * HEAD_DIM,
            bytes_accessed=8 * qkv.size,
            transcendentals=heads * seqs * length * length,
        ),
        name="attend",
    )(base, qkv, cosine, sine, first, *before)


def attend_back_kernel(base, kept, log_total, slope, cosine, sine, first, d_qkv, d_key, d_value):
    seq = pl.program_id(1)
    blocks = base.shape[0]
    length = cosine.shape[1]
    share = length // blocks
    half = HEAD_DIM // 2
    scale = HEAD_DIM**-0.5

    def spot(i):
        return pl.ds(pl.multiple_of(base[i] + seq * share, share), share)

    def put(part, i, low, high):
        at = pl.ds(i * share, share)
        d_low, d_high = turn_rows(low, high, cosine[:, at], -sine[:, at])
        top = part * HEAD_DIM
        d_qkv[top : top + half, spot(i)] = d_low.astype(HALF)
        d_qkv[top + half : top + HEAD_DIM, spot(i)] = d_high.astype(HALF)

    query = kept[0, :HEAD_DIM, :].T
    key = kept[0, HEAD_DIM : 2 * HEAD_DIM, :].T
    value = kept[0, 2 * HEAD_DIM :, :].T
    d_key[...] = jnp.zeros_like(d_key)
    d_value[...] = jnp.zeros_like(d_value)
    for i in range(blocks):
        low, high = reach(i, share, length // 2), (i + 1) * share
        at = pl.ds(i * share, share)
        turned = slope[:, spot(i)]
        scores = jnp.dot(
            key[low:high, :], kept[0, :HEAD_DIM, at], preferred_element_type=FLOAT
        ) * scale
        scores = jnp.where(seen(first[0, :, at][:1], low, high, i * share), scores, NEG)
        probs = jnp.exp(scores - log_total[0, 0, :1, at])
        d_probs = jnp.dot(value[low:high, :], turned, preferred_element_type=FLOAT)
        centre = jnp.sum(probs * d_probs, axis=0, keepdims=True)
        d_scores = (probs * (d_probs - centre)).astype(HALF)
        d_value[low:high, :] += jnp.dot(probs.astype(HALF), turned.T, preferred_element_type=FLOAT)
        d_key[low:high, :] += jnp.dot(
            d_scores, query[i * share : (i + 1) * share, :], preferred_element_type=FLOAT
        )
        d_query = scale * jnp.dot(
            kept[0, HEAD_DIM : 2 * HEAD_DIM, low:high], d_scores, preferred_element_type=FLOAT
        )
        put(0, i, d_query[:half, :], d_query[half:, :])
    for i in range(blocks):
        rows = pl.ds(i * share, share)
        turned = scale * d_key[rows, :].T
        put(1, i, turned[:half, :], turned[half:, :])
        d_qkv[2 * HEAD_DIM :, spot(i)] = d_value[rows, :].T.astype(HALF)


def attend_back(base, kept, log_total, slope, cosine, sine, first):
    seqs, length = first.shape[0], first.shape[2]
    tokens = slope.shape[1]
    heads = slope.shape[0] // HEAD_DIM
    return pl.pallas_call(
        attend_back_kernel,
        grid=(heads, seqs),
        in_specs=[
            pl.BlockSpec(memory_space=pltpu.SMEM),
            pl.BlockSpec((1, 3 * HEAD_DIM, length), lambda h, j: (j, h, 0)),
            pl.BlockSpec((1, 1, 8, length), lambda h, j: (j, h, 0, 0)),
            pl.BlockSpec((HEAD_DIM, tokens), lambda h, j: (h, 0)),
            pl.BlockSpec(cosine.shape, lambda h, j: (0, 0)),
            pl.BlockSpec(sine.shape, lambda h, j: (0, 0)),
            pl.BlockSpec((1, 8, length), lambda h, j: (j, 0, 0)),
        ],
        out_specs=pl.BlockSpec((3 * HEAD_DIM, tokens), lambda h, j: (h, 0)),
        out_shape=jax.ShapeDtypeStruct((heads * 3 * HEAD_DIM, tokens), HALF),
        scratch_shapes=[pltpu.VMEM((length, HEAD_DIM), FLOAT)] * 2,
        compiler_params=pltpu.CompilerParams(vmem_limit_bytes=VMEM_LIMIT),
        cost_estimate=pl.CostEstimate(
            flops=10 * heads * seqs * length * length * HEAD_DIM,
            bytes_accessed=8 * slope.size,
            transcendentals=heads * seqs * length * length,
        ),
        name="attend_back",
    )(base, kept, log_total, slope, cosine, sine, first)


def near_and_far(own, rank):
    return (own, rank ^ 1), (own, rank ^ 2)


def remote(source, target, send, recv, n, peer):
    return pltpu.make_async_remote_copy(
        src_ref=source,
        dst_ref=target,
        send_sem=send.at[n],
        recv_sem=recv.at[n],
        device_id=peer,
        device_id_type=MESH,
    )


class Boundary:
    COUNT = 6

    def __init__(self, own, rank, send, recv, parts, rows):
        self.near, self.far = near_and_far(own, rank)
        self.send, self.recv, self.parts = send, recv, parts
        self.rows = [pl.ds(h * rows, rows) for h in range(parts)]
        self.copies = []

    def copy(self, source, target, n, h, peer):
        made = remote(source, target, self.send, self.recv, n * self.parts + h, peer)
        made.start()
        self.copies.append(made)
        return made

    def sums(self, partial, beside, away, come):
        later = {}
        for p in (1, 0):
            for h, at in enumerate(self.rows):
                later[p, h] = self.copy(partial.at[2 + p, at], beside.at[p, at], p, h, self.near)
        crossing = []
        for h, at in enumerate(self.rows):
            later[1, h].wait_recv()
            away[at, :] = (partial[1, at, :] + beside[1, at, :]).astype(HALF)
            crossing.append(self.copy(away.at[at], come.at[at], 2, h, self.far))
        for h, at in enumerate(self.rows):
            later[0, h].wait_recv()
            total = partial[0, at, :] + beside[0, at, :]
            crossing[h].wait_recv()
            yield h, at, total + come[at, :].astype(FLOAT)

    def give(self, full, h):
        at = self.rows[h]
        self.crossed = getattr(self, "crossed", [])
        self.crossed.append(self.copy(full.at[0, at], full.at[1, at], 3, h, self.far))
        self.beside = getattr(self, "beside", [])
        self.beside.append(self.copy(full.at[0, at], full.at[2, at], 4, h, self.near))

    def pass_on(self, full):
        arrived = []
        for h, at in enumerate(self.rows):
            self.crossed[h].wait_recv()
            arrived.append(self.copy(full.at[1, at], full.at[3, at], 5, h, self.near))
        for copy in self.beside + arrived:
            copy.wait_recv()

    def end(self):
        for copy in self.copies:
            copy.wait_send()


def forward_kernel(parts, partial, stream, gain, out, full, beside, away, come, send, recv):
    own, rank = lax.axis_index("dp"), lax.axis_index("tensor")
    greet(list(near_and_far(own, rank)))
    edge = Boundary(own, rank, send, recv, parts, stream.shape[0] // parts)
    for h, at, total in edge.sums(partial, beside, away, come):
        total = stream[at, :] + total
        out[at, :] = total
        full[0, at, :] = normed(total, gain[...]).astype(HALF)
        edge.give(full, h)
    edge.pass_on(full)
    edge.end()


def exchange_scratch(rows, depth, parts):
    return [
        pltpu.VMEM((2, rows, depth), FLOAT),
        pltpu.VMEM((rows, depth), HALF),
        pltpu.VMEM((rows, depth), HALF),
        pltpu.SemaphoreType.DMA((Boundary.COUNT * parts,)),
        pltpu.SemaphoreType.DMA((Boundary.COUNT * parts,)),
    ]


def forward_boundary(partial, stream, gain):
    rows, depth = stream.shape
    parts = 2
    vmem = pl.BlockSpec(memory_space=pltpu.VMEM)
    out, full = pl.pallas_call(
        functools.partial(forward_kernel, parts),
        in_specs=[vmem] * 3,
        out_specs=[vmem] * 2,
        out_shape=[
            jax.ShapeDtypeStruct((rows, depth), FLOAT),
            jax.ShapeDtypeStruct((4, rows, depth), HALF),
        ],
        scratch_shapes=exchange_scratch(rows, depth, parts),
        compiler_params=pltpu.CompilerParams(
            collective_id=3, has_side_effects=True, vmem_limit_bytes=VMEM_LIMIT
        ),
        cost_estimate=pl.CostEstimate(flops=2**35, bytes_accessed=2**24, transcendentals=0),
        name="forward_boundary",
    )(partial.reshape(4, rows, depth), stream, gain)
    return out, full.reshape(4 * rows, depth)


def normed_slope(grad, values, gain):
    root = lax.rsqrt(jnp.mean(values * values, axis=-1, keepdims=True) + EPS)
    unit = values * root
    inner = grad * gain
    middle = jnp.mean(inner * unit, axis=-1, keepdims=True)
    return root * (inner - unit * middle), jnp.sum(grad * unit, axis=0, keepdims=True)


def backward_kernel(parts, with_prior, *refs):
    partial, stream, gain = refs[:3]
    prior = refs[3] if with_prior else None
    out, g_gain, full, beside, away, come, send, recv = refs[3 + with_prior :]
    own, rank = lax.axis_index("dp"), lax.axis_index("tensor")
    greet(list(near_and_far(own, rank)))
    edge = Boundary(own, rank, send, recv, parts, stream.shape[0] // parts)
    g_gain[...] = jnp.zeros_like(g_gain)
    for h, at, total in edge.sums(partial, beside, away, come):
        slope, by_gain = normed_slope(total, stream[at, :], gain[...])
        if with_prior:
            slope = slope + prior[at, :]
        g_gain[:1, :] = g_gain[:1, :] + by_gain
        out[at, :] = slope
        full[0, at, :] = slope.astype(HALF)
        edge.give(full, h)
    edge.pass_on(full)
    edge.end()


def backward_boundary(partial, stream, gain, prior):
    rows, depth = stream.shape
    parts = 2
    vmem = pl.BlockSpec(memory_space=pltpu.VMEM)
    with_prior = prior is not None
    out, g_gain, full = pl.pallas_call(
        functools.partial(backward_kernel, parts, int(with_prior)),
        in_specs=[vmem] * (3 + with_prior),
        out_specs=[vmem] * 3,
        out_shape=[
            jax.ShapeDtypeStruct((rows, depth), FLOAT),
            jax.ShapeDtypeStruct((8, depth), FLOAT),
            jax.ShapeDtypeStruct((4, rows, depth), HALF),
        ],
        scratch_shapes=exchange_scratch(rows, depth, parts),
        compiler_params=pltpu.CompilerParams(
            collective_id=5 if with_prior else 4,
            has_side_effects=True,
            vmem_limit_bytes=VMEM_LIMIT,
        ),
        cost_estimate=pl.CostEstimate(flops=2**35, bytes_accessed=2**24, transcendentals=0),
        name="backward_boundary",
    )(*([partial.reshape(4, rows, depth), stream, gain] + ([prior] if with_prior else [])))
    return out, g_gain[:1], full.reshape(4 * rows, depth)


def start_kernel(waits, ids, turned, gain, *refs):
    stream, full, table, corner, rows, out, near, cross, come, send, recv = refs[waits:]
    own, rank = lax.axis_index("dp"), lax.axis_index("tensor")
    beside, across = near_and_far(own, rank)
    far = [(own ^ k, rank) for k in range(1, 8)]
    greet([beside, across] + far)
    width, vocab = turned.shape
    count = rows.shape[0]
    corner[...] = jnp.zeros_like(corner)
    for v in range(0, vocab, LANES):
        some = min(LANES, vocab - v)
        corner[:width, :some] = turned[:, v : v + some].astype(HALF).astype(FLOAT)
        if some < LANES:
            corner[:width, some:] = jnp.zeros((width, LANES - some), FLOAT)
        table[v : v + LANES, :] = corner[...].T
    if vocab % LANES == 0:
        table[vocab:, :] = jnp.zeros((LANES, LANES), FLOAT)

    def fetch(place):
        def body(i, carry):
            for u in range(16):
                r = i * 16 + u
                rows[pl.ds(r, 1), :] = table[pl.ds(ids[place * count + r], 1), :]
            return carry

        lax.fori_loop(0, count // 16, body, 0)

    copies, beside_of, across_of, far_of = [], {}, {}, {}

    def begin(source, target, n, peer):
        copy = remote(source, target, send, recv, n, peer)
        copy.start()
        copies.append(copy)
        return copy

    for p in (3, 2):
        for k in range(8):
            fetch(p * 8 + k)
            out[p, k] = rows[:, :width].astype(HALF)
            beside_of[p - 2, k] = begin(out.at[p, k], near.at[p - 2, k], (p - 2) * 8 + k, beside)
    order = (7, 6, 5, 4, 3, 2, 1, 0)
    for k in order:
        fetch(8 + k)
        beside_of[1, k].wait_recv()
        total = rows[:, :width] + near[1, k].astype(FLOAT)
        out[1, k] = total.astype(HALF)
        across_of[k] = begin(out.at[1, k], cross.at[k], 16 + k, across)
    for k in order:
        fetch(k)
        beside_of[0, k].wait_recv()
        total = rows[:, :width] + near[0, k].astype(FLOAT)
        across_of[k].wait_recv()
        out[0, k] = (total + cross[k].astype(FLOAT)).astype(HALF)
        if k:
            far_of[k] = begin(out.at[0, k], come.at[k], 24 + k, far[k - 1])
    come[0] = out[0, 0]
    for k in order[:-1]:
        far_of[k].wait_recv()
    for b in range(8):
        stream[:, b * width : (b + 1) * width] = come[own ^ b].astype(FLOAT)
    full[0] = normed(stream[...], gain[...]).astype(HALF)
    one = begin(full.at[0], full.at[1], 32, across)
    two = begin(full.at[0], full.at[2], 33, beside)
    one.wait_recv()
    three = begin(full.at[1], full.at[3], 34, beside)
    two.wait_recv()
    three.wait_recv()
    for copy in copies:
        copy.wait_send()


def start_rows(ids, turned, gain, before):
    width, vocab = turned.shape
    rows = ids.shape[0] // 32
    padded = (vocab // LANES + 1) * LANES
    vmem = pl.BlockSpec(memory_space=pltpu.VMEM)
    stream, full = pl.pallas_call(
        functools.partial(start_kernel, len(before)),
        in_specs=[pl.BlockSpec(memory_space=pltpu.SMEM), vmem, vmem]
        + [pl.BlockSpec(memory_space=pl.ANY)] * len(before),
        out_specs=[vmem] * 2,
        out_shape=[
            jax.ShapeDtypeStruct((rows, 8 * width), FLOAT),
            jax.ShapeDtypeStruct((4, rows, 8 * width), HALF),
        ],
        scratch_shapes=[
            pltpu.VMEM((padded, LANES), FLOAT),
            pltpu.VMEM((LANES, LANES), FLOAT),
            pltpu.VMEM((rows, LANES), FLOAT),
            pltpu.VMEM((4, 8, rows, width), HALF),
            pltpu.VMEM((2, 8, rows, width), HALF),
            pltpu.VMEM((8, rows, width), HALF),
            pltpu.VMEM((8, rows, width), HALF),
            pltpu.SemaphoreType.DMA((35,)),
            pltpu.SemaphoreType.DMA((35,)),
        ],
        compiler_params=pltpu.CompilerParams(
            collective_id=6, has_side_effects=True, vmem_limit_bytes=VMEM_LIMIT
        ),
        cost_estimate=pl.CostEstimate(flops=2**35, bytes_accessed=2**24, transcendentals=0),
        name="start_rows",
    )(ids, turned, gain, *before)
    return stream, full.reshape(4 * rows, 8 * width)


def end_kernel(parts, waits, partial, stream, gain, prior, *refs):
    rows, g_gain, beside, away, come, leave, send, recv = refs[waits:]
    own, rank = lax.axis_index("dp"), lax.axis_index("tensor")
    near, across = near_and_far(own, rank)
    far = [(own ^ k, rank) for k in range(1, 8)]
    greet([near, across] + far)
    edge = Boundary(own, rank, send, recv, parts, stream.shape[0] // parts)
    g_gain[...] = jnp.zeros_like(g_gain)
    width = rows.shape[3]
    for h, at, total in edge.sums(partial, beside, away, come):
        slope, by_gain = normed_slope(total, stream[at, :], gain[...])
        slope = slope + prior[at, :]
        g_gain[:1, :] = g_gain[:1, :] + by_gain
        for b in range(8):
            leave[b, at, :] = slope[:, b * width : (b + 1) * width].astype(HALF)
    base = Boundary.COUNT * parts
    far_of, last = {}, []

    def begin(source, target, n, peer):
        copy = remote(source, target, send, recv, base + n, peer)
        copy.start()
        edge.copies.append(copy)
        return copy

    order = (7, 6, 5, 4, 3, 2, 1)
    for k in order:
        far_of[k] = begin(leave.at[own ^ k], rows.at[0, k], k, far[k - 1])
    rows[0, 0] = leave[own]
    crossed = {}
    for k in (0, 1, 2, 3, 4, 5, 6, 7):
        if k:
            far_of[k].wait_recv()
        crossed[k] = begin(rows.at[0, k], rows.at[1, k], 8 + k, across)
        last.append(begin(rows.at[0, k], rows.at[2, k], 16 + k, near))
    for k in (0, 1, 2, 3, 4, 5, 6, 7):
        crossed[k].wait_recv()
        last.append(begin(rows.at[1, k], rows.at[3, k], 24 + k, near))
    for copy in last:
        copy.wait_recv()
    edge.end()


def end_rows(partial, stream, gain, prior, width, before):
    rows, depth = stream.shape
    parts = 2
    vmem = pl.BlockSpec(memory_space=pltpu.VMEM)
    semaphores = Boundary.COUNT * parts + 32
    out, g_gain = pl.pallas_call(
        functools.partial(end_kernel, parts, len(before)),
        in_specs=[vmem] * 4 + [pl.BlockSpec(memory_space=pl.ANY)] * len(before),
        out_specs=[vmem] * 2,
        out_shape=[
            jax.ShapeDtypeStruct((4, 8, rows, width), HALF),
            jax.ShapeDtypeStruct((8, depth), FLOAT),
        ],
        scratch_shapes=exchange_scratch(rows, depth, parts)[:3]
        + [
            pltpu.VMEM((8, rows, width), HALF),
            pltpu.SemaphoreType.DMA((semaphores,)),
            pltpu.SemaphoreType.DMA((semaphores,)),
        ],
        compiler_params=pltpu.CompilerParams(
            collective_id=7, has_side_effects=True, vmem_limit_bytes=VMEM_LIMIT
        ),
        cost_estimate=pl.CostEstimate(flops=2**35, bytes_accessed=2**24, transcendentals=0),
        name="end_rows",
    )(partial.reshape(4, rows, depth), stream, gain, prior, *before)
    return out.reshape(-1, width), g_gain[:1]


def merge_kernel(scans, scale, joined, mine, every, send, recv):
    own, rank = lax.axis_index("dp"), lax.axis_index("tensor")
    peers = [(own, rank ^ bit) for bit in (1, 2, 3)]
    greet(peers)
    tokens = scans.shape[2]
    share = tokens // 4
    peak = scans[0, :1]
    for n in range(1, scans.shape[0]):
        peak = jnp.maximum(peak, scans[n, :1])
    summed = sum(scans[n, 1:2] * jnp.exp(scans[n, :1] - peak) for n in range(scans.shape[0]))
    mine[...] = jnp.zeros_like(mine)
    mine[:1, :] = peak
    mine[1:2, :] = summed
    mine[2:3, :] = sum(scans[n, 2:3] for n in range(scans.shape[0]))
    copies = []
    for bit in (1, 2, 3):
        copies.append(remote(mine, every.at[bit - 1], send, recv, bit - 1, peers[bit - 1]))
        copies[-1].start()
    for copy in copies:
        copy.wait()
    for p in range(4):
        at = pl.ds(p * share, share)
        terms = [mine[:, at]]
        for bit in (1, 2, 3):
            terms.append(every[bit - 1, :, pl.ds(TURN.index(TURN[p] ^ bit) * share, share)])
        peak = functools.reduce(jnp.maximum, [term[:1] for term in terms])
        sums = [term[1:2] * jnp.exp(term[:1] - peak) for term in terms]
        joined[0:1, at] = peak + jnp.log((sums[0] + sums[1]) + (sums[2] + sums[3]))
        hits = [term[2:3] for term in terms]
        joined[1:2, at] = (hits[0] + hits[1]) + (hits[2] + hits[3])
        joined[2:4, at] = scale[:2, at]
        joined[4:, at] = jnp.zeros((4, share), FLOAT)


def merge_scans(scans, scale):
    vmem = pl.BlockSpec(memory_space=pltpu.VMEM)
    shape = scans.shape[1:]
    return pl.pallas_call(
        merge_kernel,
        in_specs=[vmem] * 2,
        out_specs=vmem,
        out_shape=jax.ShapeDtypeStruct(shape, FLOAT),
        scratch_shapes=[
            pltpu.VMEM(shape, FLOAT),
            pltpu.VMEM((3, *shape), FLOAT),
            pltpu.SemaphoreType.DMA((3,)),
            pltpu.SemaphoreType.DMA((3,)),
        ],
        compiler_params=pltpu.CompilerParams(collective_id=8, has_side_effects=True),
        name="merge_scans",
    )(scans, scale)


def product(left, right, over_left, over_right):
    return lax.dot_general(
        left, right, (((over_left,), (over_right,)), ((), ())), preferred_element_type=FLOAT
    )


def adam(weight, grad, first, second, rate, decay):
    first = BETA_ONE * first + (1.0 - BETA_ONE) * grad
    second = BETA_TWO * second + (1.0 - BETA_TWO) * grad * grad
    first_hat = first / (1.0 - BETA_ONE**STEP)
    second_hat = second / (1.0 - BETA_TWO**STEP)
    weight = weight - rate * (first_hat / (jnp.sqrt(second_hat) + ADAM_EPS) + decay * weight)
    return (weight, first, second, weight.astype(HALF))


def shards(
    token_ids,
    targets,
    segments,
    completion,
    micro_order,
    *state,
):
    weights, means, squares = state[:7], state[7:14], state[14:21]
    embedding, attn_in, attn_out, ffn_in, ffn_out, head_table, norm_gains = weights
    group = lax.axis_size("dp")
    parts = lax.axis_size("tensor")
    own, rank = lax.axis_index("dp"), lax.axis_index("tensor")
    vocab, width = embedding.shape
    start = rank * vocab
    seqs, length = token_ids.shape
    micro = micro_order.shape[1]
    share = length // parts
    turn = jnp.array(TURN, jnp.int32)
    dp_order = own ^ jnp.arange(group, dtype=jnp.int32)
    tensor_order = rank ^ turn
    tensor_order_natural = rank ^ jnp.arange(parts, dtype=jnp.int32)
    ffn = ffn_out.shape[0]
    qkv_width = attn_in.shape[1]

    attn_block = jnp.concatenate([attn_in, attn_out.T], axis=1).astype(HALF)
    ffn_block = jnp.concatenate([ffn_in.reshape(width, -1), ffn_out.T], axis=1).astype(HALF)
    attn_parts = gather_first(attn_block)
    ffn_parts = gather_first(ffn_block)
    bounds = list(range(0, vocab, HEAD_PART)) + [vocab]
    head_half = head_table.astype(HALF)
    head_b = [
        lax.all_gather(head_half[:, low:high], "dp", axis=0, tiled=True)
        for low, high in zip(bounds, bounds[1:])
    ]

    flags = completion.astype(FLOAT)
    picked_rows = micro_order[0]
    local_counts = jnp.sum(completion, axis=1)[picked_rows]
    id_rows = seqs * length // LANES
    packed = jnp.concatenate([token_ids.reshape(-1), jnp.pad(local_counts, (0, 8 * LANES - micro))])
    packed = packed.reshape(id_rows + 8, LANES)
    gains = jnp.pad(norm_gains.astype(HALF).astype(FLOAT), ((0, 5), (0, LANES - width)))
    if group == 8:
        packed, gains = spread(packed, gains)
        gains = jnp.take(gains, dp_order, axis=0)
    else:
        packed, gains = lax.all_gather(packed, "dp"), lax.all_gather(gains, "dp")
        packed = jnp.take(packed, dp_order, axis=0)
    gains = gains[:, :3, :width].transpose(1, 0, 2).reshape(3, -1)
    counts = jnp.sum(packed[:, id_rows, :micro].astype(FLOAT), axis=0)
    slot = jnp.argmax(picked_rows[None, :] == jnp.arange(seqs)[:, None], axis=1)
    row_weights = (1.0 / jnp.maximum(counts, 1.0))[slot]

    every_id = packed[:, :id_rows].reshape(group, seqs, parts, share)
    every_id = jnp.take(every_id, tensor_order, axis=2)
    every_id = every_id.transpose(2, 0, 1, 3).reshape(-1) - start
    every_id = jnp.where((every_id >= 0) & (every_id < vocab), every_id, vocab)

    def both_order(values):
        values = jnp.take(values.reshape(seqs, parts, share), tensor_order, axis=1)
        return values.transpose(1, 0, 2).reshape(-1)

    joint_flags = both_order(flags)
    aims = both_order(targets) - start
    aims = jnp.where((aims >= 0) & (aims < vocab), aims, -1).astype(FLOAT)
    scale = joint_flags * jnp.tile(jnp.repeat(row_weights, share), parts)
    extra = jnp.concatenate([scale[None], aims[None], jnp.zeros((6, seqs * length), FLOAT)])

    own_segment = segments[:, :, None] == jnp.arange(8, dtype=jnp.int32)
    sizes = jnp.sum(own_segment.astype(jnp.int32), axis=1)
    begins = jnp.cumsum(sizes, axis=1) - sizes
    first = jnp.sum(jnp.where(own_segment, begins[:, None, :], 0), axis=2)
    first = jnp.broadcast_to(first[:, None, :], (seqs, 8, length))
    base = turn[tensor_order_natural] * (seqs * share)
    cosine, sine = tables(length, HEAD_DIM)

    if group == 8:
        stream0, attn_norm = start_rows(every_id, embedding.T, gains[:1], attn_parts)
    else:
        rows = lookup(embedding.T, every_id).reshape(parts, group, seqs * share, width)
        rows = rows[:2] + swap(rows[2:], "tensor", 1)
        rows = rows[0] + swap(rows[1], "tensor", 2)
        rows = lax.all_to_all(jnp.take(rows, dp_order, axis=0), "dp", 0, 0)
        stream0 = rows.transpose(1, 0, 2).reshape(seqs * share, -1).astype(FLOAT)
        attn_norm = tensor_gather(normed(stream0, gains[0]).astype(HALF))

    attn_w = gather_last(attn_block, attn_parts)
    attn_in_b, attn_out_b = attn_w[:, :qkv_width], attn_w[:, qkv_width:]
    qkv = product(attn_in_b, attn_norm, 0, 1)
    attended, kept, log_sums = attend(base, qkv, cosine, sine, first, ffn_parts)
    stream1, ffn_norm = forward_boundary(product(attended, attn_out_b, 0, 1), stream0, gains[1:2])
    ffn_w = gather_last(ffn_block, ffn_parts)
    ffn_in_b, ffn_out_b = ffn_w[:, : 2 * ffn], ffn_w[:, 2 * ffn :]
    gate_up = product(ffn_norm, ffn_in_b, 1, 0)
    hidden = (jax.nn.silu(gate_up[:, :ffn]) * gate_up[:, ffn:]).astype(HALF)
    stream2, final_norm = forward_boundary(product(hidden, ffn_out_b, 1, 1), stream1, gains[2:])

    logits, scans = [], []
    for low, table in zip(bounds, head_b):
        out, scan = head_scan(final_norm, table, extra, low)
        logits.append(out)
        scans.append(scan)
    info = merge_scans(jnp.stack(scans), extra)
    seq_loss = jnp.sum(
        ((info[0] - info[1]) * joint_flags).reshape(parts, seqs, share), axis=(0, 2)
    )
    final_turned = final_norm.T
    d_final, g_head = None, []
    for low, table, out in zip(bounds, head_b, logits):
        g_part, d_final = head_grad(final_turned, table, info, out, d_final, low)
        g_head.append(lax.psum_scatter(g_part, "dp", scatter_dimension=0, tiled=True))
    g_head = jnp.concatenate(g_head, axis=1).astype(FLOAT)

    d_stream2, g_gain2, d_branch2 = backward_boundary(d_final, stream2, gains[2:], None)
    d_hidden = product(d_branch2, ffn_out_b, 1, 0)
    unused, pull = jax.vjp(lambda both: jax.nn.silu(both[:, :ffn]) * both[:, ffn:], gate_up)
    d_gate_up = pull(d_hidden)[0].astype(HALF)
    d_stream1, g_gain1, d_branch1 = backward_boundary(
        product(d_gate_up, ffn_in_b, 1, 1), stream1, gains[1:2], d_stream2
    )
    g_ffn_in = product(ffn_norm, d_gate_up, 0, 0).astype(HALF)
    g_ffn_out = product(d_branch2, hidden, 0, 0).astype(HALF)
    g_ffn = jnp.concatenate([g_ffn_in, g_ffn_out], axis=1)
    g_ffn_parts = scatter_first(g_ffn)
    d_attended = product(attn_out_b, d_branch1, 0, 1).astype(HALF)
    d_qkv = attend_back(base, kept, log_sums, d_attended, cosine, sine, first)
    g_attn_in = product(attn_norm, d_qkv, 0, 1).astype(HALF)
    g_attn_out = product(d_branch1, attended, 0, 1).astype(HALF)
    g_attn = jnp.concatenate([g_attn_in, g_attn_out], axis=1)
    g_attn_parts = scatter_first(g_attn)
    d_norm = product(d_qkv, attn_in_b, 0, 1)
    if group == 8:
        rows, g_gain0 = end_rows(d_norm, stream0, gains[:1], d_stream1, width, g_ffn_parts)
    else:
        d_part, g_gain0 = normed_slope(tensor_scatter(d_norm), stream0, gains[:1])
        rows = (d_stream1 + d_part).astype(HALF)
        rows = rows.reshape(seqs * share, group, width).transpose(1, 0, 2)
        rows = jnp.take(lax.all_to_all(rows, "dp", 0, 0), dp_order, axis=0)
        rows = tensor_gather(rows[None]).reshape(-1, width)
    g_embed = collect(rows, every_id, vocab, g_attn_parts).T
    g_ffn = scatter_last(g_ffn, g_ffn_parts)
    g_attn = scatter_last(g_attn, g_attn_parts)

    gain_sum = jnp.concatenate([g_gain0, g_gain1, g_gain2]).reshape(3, group, width)
    if group == 8:
        gain_sum = jnp.take(gain_sum.transpose(1, 0, 2), dp_order, axis=0)
        gain_sum = jnp.pad(gain_sum, ((0, 0), (0, 5), (0, LANES - width)))
        g_gains = total_over_devices(gain_sum)[:3, :width]
    else:
        g_gains = jnp.take(lax.psum(gain_sum, ("dp", "tensor")), own, axis=1)

    reduced = (
        g_embed,
        g_attn[:, :qkv_width],
        g_attn[:, qkv_width:].T,
        g_ffn[:, : 2 * ffn].reshape(ffn_in.shape),
        g_ffn[:, 2 * ffn :].T,
        g_head,
        g_gains,
    )
    owner = (rank == 0).astype(FLOAT)
    squared = jnp.zeros((), FLOAT)
    for place in range(6):
        squared = squared + jnp.sum(reduced[place] * reduced[place])
    squared = squared + owner * jnp.sum(reduced[6] * reduced[6])
    losses = seq_loss[picked_rows] * owner
    if group == 8:
        sums = jnp.pad(jnp.concatenate([squared[None], losses]), (0, 8 * LANES - 1 - micro))
        sums = total_over_devices(jnp.broadcast_to(sums.reshape(1, 8, LANES), (8, 8, LANES)))
        squared, loss_sums = sums[0, 0], sums[0, 1 : 1 + micro]
    else:
        squared, loss_sums = lax.psum((squared, losses), ("dp", "tensor"))
    grad_norm = jnp.sqrt(squared)
    factor = CLIP / jnp.maximum(grad_norm, CLIP)
    updated = []
    for place in range(7):
        rate = LR_GAIN if place == 6 else LR
        decay = 0.0 if place == 6 else DECAY
        arrays = (weights[place], reduced[place], means[place], squares[place])
        if place in (0, 2, 4):
            arrays = tuple(array.T for array in arrays)
        results = adam(arrays[0], arrays[1] * factor, arrays[2], arrays[3], rate, decay)
        updated.extend(result.T if place in (0, 2, 4) else result for result in results)
    return (jnp.stack([loss_sums, counts]), grad_norm, *updated)


def solution(mesh):
    in_specs = (
        P("dp", None),
        P("dp", None),
        P("dp", None),
        P("dp", None),
        P("dp", None),
        P("tensor", "dp"),
        P("dp", "tensor"),
        P("tensor", "dp"),
        P("dp", None, "tensor"),
        P("tensor", "dp"),
        P("dp", "tensor"),
        P(None, "dp"),
        P("tensor", "dp"),
        P("dp", "tensor"),
        P("tensor", "dp"),
        P("dp", None, "tensor"),
        P("tensor", "dp"),
        P("dp", "tensor"),
        P(None, "dp"),
        P("tensor", "dp"),
        P("dp", "tensor"),
        P("tensor", "dp"),
        P("dp", None, "tensor"),
        P("tensor", "dp"),
        P("dp", "tensor"),
        P(None, "dp"),
    )
    out_specs = (
        P(),
        P(),
        P("tensor", "dp"),
        P("tensor", "dp"),
        P("tensor", "dp"),
        P("tensor", "dp"),
        P("dp", "tensor"),
        P("dp", "tensor"),
        P("dp", "tensor"),
        P("dp", "tensor"),
        P("tensor", "dp"),
        P("tensor", "dp"),
        P("tensor", "dp"),
        P("tensor", "dp"),
        P("dp", None, "tensor"),
        P("dp", None, "tensor"),
        P("dp", None, "tensor"),
        P("dp", None, "tensor"),
        P("tensor", "dp"),
        P("tensor", "dp"),
        P("tensor", "dp"),
        P("tensor", "dp"),
        P("dp", "tensor"),
        P("dp", "tensor"),
        P("dp", "tensor"),
        P("dp", "tensor"),
        P(None, "dp"),
        P(None, "dp"),
        P(None, "dp"),
        P(None, "dp"),
    )
    return jax.shard_map(shards, mesh=mesh, in_specs=in_specs, out_specs=out_specs, check_vma=False)
```

```python
import functools

import jax
import jax.numpy as jnp
import numpy as np
from jax import lax
from jax.experimental import pallas as pl
from jax.experimental.pallas import tpu as pltpu
from jax.sharding import PartitionSpec as P

HEAD_DIM = 64
STEP = 10


EPS = 1e-05
CLIP = 0.01
LR = 0.03
LR_GAIN = 0.5
BETA_ONE = 0.9
BETA_TWO = 0.95
ADAM_EPS = 1e-08
DECAY = 0.1
NEG = -1e30
FLOAT = jnp.float32
HALF = jnp.bfloat16
LANES = 128
ROWS = 1024
VMEM_LIMIT = 56 * 2**20
TILE = 512
CHUNK = 256
MESH = pl.DeviceIdType.MESH
SMALL = pl.CostEstimate(flops=2**20, bytes_accessed=2**20, transcendentals=0)

TURN = (0, 2, 1, 3)


def swap(value, axis, bit):
    pairs = [(i, i ^ bit) for i in range(lax.axis_size(axis))]
    return lax.ppermute(value, axis, pairs)


def normed(values, gain):
    return values * lax.rsqrt(jnp.mean(values * values, axis=-1, keepdims=True) + EPS) * gain


def tables(length, width):
    inverse = np.float32(10000.0) ** (-np.arange(0, width, 2, dtype=np.float32) / np.float32(width))
    angle = inverse[:, None] * np.arange(length, dtype=np.float32)[None, :]
    return jnp.asarray(np.cos(angle)), jnp.asarray(np.sin(angle))


def gather_first(block):
    if lax.axis_size("dp") != 8:
        return []
    return [swap(block, "dp", k) for k in (2, 4, 6)]


def gather_last(block, parts):
    group = lax.axis_size("dp")
    if group != 8:
        return lax.all_gather(block, "dp", axis=0, tiled=True)
    parts = jnp.concatenate([block, *parts], axis=0)
    there = swap(parts, "dp", 1)
    rows = block.shape[0]
    own = lax.axis_index("dp")
    full = jnp.zeros((group * rows, block.shape[1]), block.dtype)
    for n in range(group // 2):
        at = slice(n * rows, (n + 1) * rows)
        full = lax.dynamic_update_slice(full, parts[at], ((own ^ (2 * n)) * rows, 0))
        full = lax.dynamic_update_slice(full, there[at], ((own ^ (2 * n + 1)) * rows, 0))
    return full


def block_of(full, k):
    rows = full.shape[0] // lax.axis_size("dp")
    own = lax.axis_index("dp")
    return lax.dynamic_slice(full, ((own ^ k) * rows, 0), (rows, full.shape[1]))


def scatter_first(full):
    if lax.axis_size("dp") != 8:
        return []
    leaves = jnp.concatenate([block_of(full, k + 1) for k in (0, 2, 4, 6)], axis=0)
    return [swap(leaves, "dp", 1)]


def scatter_middle(full, parts):
    if lax.axis_size("dp") != 8:
        return full, []
    rows = full.shape[0] // 8
    sums = [
        block_of(full, 2 * n).astype(FLOAT) + parts[0][n * rows : (n + 1) * rows].astype(FLOAT)
        for n in range(4)
    ]
    return sums[0], [total.astype(HALF) for total in sums[1:]]


def scatter_last(total, leaves):
    if lax.axis_size("dp") != 8:
        return lax.psum_scatter(total.astype(FLOAT), "dp", scatter_dimension=0, tiled=True)
    for n, leave in enumerate(leaves):
        total = total + swap(leave, "dp", 2 * n + 2).astype(FLOAT)
    return total


def peers_of(own, rank, bits, axis):
    if axis == "dp":
        return [(own ^ k, rank) for k in bits]
    return [(own, rank ^ k) for k in bits]


def greet(peers):
    barrier = pltpu.get_barrier_semaphore()
    for peer in peers:
        pl.semaphore_signal(barrier, inc=1, device_id=peer, device_id_type=MESH)
    pl.semaphore_wait(barrier, len(peers))


def spread_kernel(vocab, seqs, numbers, gains, every, ids, all_gains, every_gain, send, recv):
    own, rank = lax.axis_index("dp"), lax.axis_index("tensor")
    peers = peers_of(own, rank, range(1, 8), "dp")
    greet(peers)
    every[0] = numbers[...]
    every_gain[0] = gains[...]
    copies = []
    for k in range(1, 8):
        for n, (source, target) in enumerate(((numbers, every), (gains, every_gain))):
            copies.append(
                pltpu.make_async_remote_copy(
                    src_ref=source,
                    dst_ref=target.at[k],
                    send_sem=send.at[n, k],
                    recv_sem=recv.at[n, k],
                    device_id=peers[k - 1],
                    device_id_type=MESH,
                )
            )
            copies[-1].start()
    for copy in copies:
        copy.wait()
    lines = ids.shape[0] // (32 * seqs)
    for p in range(4):
        shard = rank ^ TURN[p]
        for k in range(8):
            for j in range(seqs):
                local = every[k, pl.ds((j * 4 + shard) * lines, lines), :] - rank * vocab
                local = jnp.where((local >= 0) & (local < vocab), local, vocab)
                ids[pl.ds(((p * 8 + k) * seqs + j) * lines, lines), :] = local
    width = all_gains.shape[1] // 8
    for b in range(8):
        all_gains[:, b * width : (b + 1) * width] = every_gain[own ^ b][:, :width]


def spread(numbers, gains, seqs, length, vocab, width):
    vmem = pl.BlockSpec(memory_space=pltpu.VMEM)
    return pl.pallas_call(
        functools.partial(spread_kernel, vocab, seqs),
        in_specs=[vmem] * 2,
        out_specs=[vmem] * 3,
        out_shape=[
            jax.ShapeDtypeStruct((8, *numbers.shape), numbers.dtype),
            jax.ShapeDtypeStruct((8 * seqs * length // LANES, LANES), jnp.int32),
            jax.ShapeDtypeStruct((8, 8 * width), FLOAT),
        ],
        scratch_shapes=[
            pltpu.VMEM((8, *gains.shape), FLOAT),
            pltpu.SemaphoreType.DMA((2, 8)),
            pltpu.SemaphoreType.DMA((2, 8)),
        ],
        compiler_params=pltpu.CompilerParams(collective_id=1, has_side_effects=True),
        cost_estimate=SMALL,
        name="spread",
    )(numbers, gains)


def total_kernel(blocks, out, first, summed, second, send, recv):
    own, rank = lax.axis_index("dp"), lax.axis_index("tensor")
    near = peers_of(own, rank, range(1, 4), "tensor")
    far = peers_of(own, rank, range(1, 8), "dp")
    greet(near + far)
    copies = []
    for k in range(1, 4):
        copy = pltpu.make_async_remote_copy(
            src_ref=blocks,
            dst_ref=first.at[k - 1],
            send_sem=send.at[k - 1],
            recv_sem=recv.at[k - 1],
            device_id=near[k - 1],
            device_id_type=MESH,
        )
        copy.start()
        copies.append(copy)
    for copy in copies:
        copy.wait()
    summed[...] = (blocks[...] + first[0]) + (first[1] + first[2])
    copies = []
    for k in range(1, 8):
        copy = pltpu.make_async_remote_copy(
            src_ref=summed.at[k],
            dst_ref=second.at[k],
            send_sem=send.at[2 + k],
            recv_sem=recv.at[2 + k],
            device_id=far[k - 1],
            device_id_type=MESH,
        )
        copy.start()
        copies.append(copy)
    for copy in copies:
        copy.wait()
    second[0] = summed[0]
    pairs = [second[k] + second[k + 1] for k in (0, 2, 4, 6)]
    out[...] = (pairs[0] + pairs[1]) + (pairs[2] + pairs[3])


def total_over_devices(blocks):
    shape = blocks.shape
    return pl.pallas_call(
        total_kernel,
        in_specs=[pl.BlockSpec(memory_space=pltpu.VMEM)],
        out_specs=pl.BlockSpec(memory_space=pltpu.VMEM),
        out_shape=jax.ShapeDtypeStruct(shape[1:], FLOAT),
        scratch_shapes=[
            pltpu.VMEM((3, *shape), FLOAT),
            pltpu.VMEM(shape, FLOAT),
            pltpu.VMEM(shape, FLOAT),
            pltpu.SemaphoreType.DMA((10,)),
            pltpu.SemaphoreType.DMA((10,)),
        ],
        compiler_params=pltpu.CompilerParams(collective_id=2, has_side_effects=True),
        name="total",
    )(blocks)


def tensor_gather(block):
    half = jnp.concatenate([block, swap(block, "tensor", 2)], axis=0)
    return jnp.concatenate([half, swap(half, "tensor", 1)], axis=0)


def tensor_scatter(full):
    half = full.shape[0] // 2
    quarter = half // 2
    both = full[:half] + swap(full[half:], "tensor", 1)
    there = swap(both[quarter:].astype(HALF), "tensor", 2)
    return both[:quarter] + there.astype(FLOAT)


def lookup_kernel(ids, turned, out, table, corner, rows):
    count = rows.shape[0]
    width, vocab = turned.shape

    @pl.when(pl.program_id(0) == 0)
    def _():
        corner[...] = jnp.zeros_like(corner)
        for v in range(0, vocab, LANES):
            some = min(LANES, vocab - v)
            corner[:width, :some] = turned[:, v : v + some].astype(HALF).astype(FLOAT)
            if some < LANES:
                corner[:width, some:] = jnp.zeros((width, LANES - some), FLOAT)
            table[v : v + LANES, :] = corner[...].T
        if vocab % LANES == 0:
            table[vocab:, :] = jnp.zeros((LANES, LANES), FLOAT)

    def body(i, carry):
        for u in range(16):
            r = i * 16 + u
            rows[pl.ds(r, 1), :] = table[pl.ds(ids[0, 0, r], 1), :]
        return carry

    lax.fori_loop(0, count // 16, body, 0)
    out[...] = rows[:, : out.shape[1]].astype(HALF)


def lookup(turned, ids):
    count = ids.shape[0]
    width, vocab = turned.shape
    padded = (vocab // LANES + 1) * LANES
    return pl.pallas_call(
        lookup_kernel,
        grid=(count // ROWS,),
        in_specs=[
            pl.BlockSpec((1, 1, ROWS), lambda i: (i, 0, 0), memory_space=pltpu.SMEM),
            pl.BlockSpec(turned.shape, lambda i: (0, 0), pipeline_mode=pl.Buffered(1)),
        ],
        out_specs=pl.BlockSpec((ROWS, width), lambda i: (i, 0)),
        out_shape=jax.ShapeDtypeStruct((count, width), HALF),
        scratch_shapes=[
            pltpu.VMEM((padded, LANES), FLOAT),
            pltpu.VMEM((LANES, LANES), FLOAT),
            pltpu.VMEM((ROWS, LANES), FLOAT),
        ],
        compiler_params=pltpu.CompilerParams(vmem_limit_bytes=VMEM_LIMIT),
        cost_estimate=SMALL,
        name="lookup",
    )(ids.reshape(count // ROWS, 1, ROWS), turned)


def collect_kernel(waits, ids, grads, *refs):
    out, squares, rows, *sums = refs[waits:]
    step = pl.program_id(0)
    count = rows.shape[0]
    width, vocab = out.shape

    @pl.when(step == 0)
    def _():
        rows[...] = jnp.zeros_like(rows)
        for total in sums:
            total[...] = jnp.zeros_like(total)

    rows[:, :width] = grads[...].astype(FLOAT)

    def body(i, carry):
        for u in range(16):
            r = i * 16 + u
            total = sums[u % len(sums)]
            place = pl.ds(ids[0, 0, r], 1)
            total[place, :] = total[place, :] + rows[pl.ds(r, 1), :]
        return carry

    lax.fori_loop(0, count // 16, body, 0)

    @pl.when(step == pl.num_programs(0) - 1)
    def _():
        squared = jnp.zeros((8, LANES), FLOAT)
        for v in range(0, vocab, LANES):
            some = min(LANES, vocab - v)
            total = sums[0][v : v + some, :]
            for other in sums[1:]:
                total = total + other[v : v + some, :]
            for r in range(0, some, 8):
                squared = squared + total[r : r + 8, :] * total[r : r + 8, :]
            if some < LANES:
                total = jnp.concatenate([total, jnp.zeros((LANES - some, LANES), FLOAT)], axis=0)
            out[:, v : v + some] = total.T[:width, :some]
        squares[...] = squared


def collect(grads, ids, vocab, before):
    count = ids.shape[0]
    width = grads.shape[1]
    padded = (vocab // LANES + 1) * LANES
    return pl.pallas_call(
        functools.partial(collect_kernel, len(before)),
        grid=(count // ROWS,),
        in_specs=[
            pl.BlockSpec((1, 1, ROWS), lambda i: (i, 0, 0), memory_space=pltpu.SMEM),
            pl.BlockSpec((ROWS, width), lambda i: (i, 0)),
        ]
        + [pl.BlockSpec(memory_space=pl.ANY)] * len(before),
        out_specs=[
            pl.BlockSpec((width, vocab), lambda i: (0, 0)),
            pl.BlockSpec((8, LANES), lambda i: (0, 0)),
        ],
        out_shape=[
            jax.ShapeDtypeStruct((width, vocab), FLOAT),
            jax.ShapeDtypeStruct((8, LANES), FLOAT),
        ],
        scratch_shapes=[pltpu.VMEM((ROWS, LANES), FLOAT)]
        + [pltpu.VMEM((padded, LANES), FLOAT)] * 8,
        compiler_params=pltpu.CompilerParams(vmem_limit_bytes=VMEM_LIMIT),
        cost_estimate=SMALL,
        name="collect",
    )(ids.reshape(count // ROWS, 1, ROWS), grads, *before)


def edge_of(vocab):
    return vocab - (pl.cdiv(vocab, TILE) - 1) * TILE


def each_tile(vocab, work):
    last = edge_of(vocab)
    if last == TILE:
        work(TILE)
    else:
        step, steps = pl.program_id(0), pl.num_programs(0)
        pl.when(step < steps - 1)(lambda: work(TILE))
        pl.when(step == steps - 1)(lambda: work(last))


def turned_rows(rows):
    return jnp.concatenate([rows] * (LANES // 8), axis=0).T


def scan_kernel(vocab, norm, weight, target, logits, stats, peak, total, hit, aims):
    step = pl.program_id(0)
    rows = norm.shape[0]

    @pl.when(step == 0)
    def _():
        peak[...] = jnp.full_like(peak, NEG)
        total[...] = jnp.zeros_like(total)
        hit[...] = jnp.zeros_like(hit)
        aims[...] = turned_rows(target[...])

    def work(width):
        lane = lax.broadcasted_iota(jnp.int32, (CHUNK, LANES), 1)
        for r in range(0, rows, CHUNK):
            part = pl.ds(r, CHUNK)
            value = jnp.dot(norm[part, :], weight[...], preferred_element_type=FLOAT)
            logits[part, :] = value
            aim = aims[part, 1:2].astype(jnp.int32) - step * TILE
            slabs, found = [], hit[part, :]
            for c in range(0, width, LANES):
                slab = value[:, c : c + LANES]
                if c + LANES > width:
                    slab = jnp.where(lane < width - c, slab, NEG)
                slabs.append(slab)
                found = found + jnp.where(lane == aim - c, slab, 0.0)
            hit[part, :] = found
            before = peak[part, :]
            top = functools.reduce(jnp.maximum, slabs, before)
            added = total[part, :] * jnp.exp(before - top)
            for slab in slabs:
                added = added + jnp.exp(slab - top)
            total[part, :] = added
            peak[part, :] = top

    each_tile(vocab, work)

    @pl.when(step == pl.num_programs(0) - 1)
    def _():
        top = jnp.max(peak[...], axis=1, keepdims=True)
        added = jnp.sum(total[...] * jnp.exp(peak[...] - top), axis=1, keepdims=True)
        found = jnp.sum(hit[...], axis=1, keepdims=True)
        lane = lax.broadcasted_iota(jnp.int32, (rows, LANES), 1)
        joined = jnp.where(lane == 0, top, jnp.where(lane == 1, added, found))
        stats[...] = joined.T[:8, :]


def head_scan(norm, weight, extra):
    rows, depth = norm.shape
    vocab = weight.shape[1]
    return pl.pallas_call(
        functools.partial(scan_kernel, vocab),
        grid=(pl.cdiv(vocab, TILE),),
        in_specs=[
            pl.BlockSpec((rows, depth), lambda i: (0, 0), pipeline_mode=pl.Buffered(1)),
            pl.BlockSpec((depth, TILE), lambda i: (0, i)),
            pl.BlockSpec((8, rows), lambda i: (0, 0)),
        ],
        out_specs=[
            pl.BlockSpec((rows, TILE), lambda i: (0, i)),
            pl.BlockSpec((8, rows), lambda i: (0, 0)),
        ],
        out_shape=[
            jax.ShapeDtypeStruct((rows, vocab), FLOAT),
            jax.ShapeDtypeStruct((8, rows), FLOAT),
        ],
        scratch_shapes=[pltpu.VMEM((rows, LANES), FLOAT)] * 4,
        compiler_params=pltpu.CompilerParams(vmem_limit_bytes=VMEM_LIMIT),
        cost_estimate=SMALL,
        name="head_scan",
    )(norm, weight, extra)


def grad_kernel(vocab, turned, weight, info, logits, grad, out, total, slope, columns):
    step = pl.program_id(0)
    rows = logits.shape[0]

    @pl.when(step == 0)
    def _():
        columns[...] = turned_rows(info[...])
        total[...] = jnp.zeros_like(total)

    def work(width):
        lane = lax.broadcasted_iota(jnp.int32, (CHUNK, TILE), 1)
        table = weight[...]
        if width < TILE:
            table = jnp.where(lax.broadcasted_iota(jnp.int32, table.shape, 1) < width, table, 0.0)
        for r in range(0, rows, CHUNK):
            part = pl.ds(r, CHUNK)
            aim = columns[part, 3:4].astype(jnp.int32) - step * TILE
            value = jnp.exp(logits[part, :] - columns[part, 0:1])
            value = (value - jnp.where(lane == aim, 1.0, 0.0)) * columns[part, 2:3]
            if width < TILE:
                value = jnp.where(lane < width, value, 0.0)
            value = value.astype(HALF)
            slope[part, :] = value
            total[part, :] = total[part, :] + lax.dot_general(
                value, table, (((1,), (1,)), ((), ())), preferred_element_type=FLOAT
            )
        grad[...] = jnp.dot(turned[...], slope[...], preferred_element_type=FLOAT).astype(HALF)

    each_tile(vocab, work)

    @pl.when(step == pl.num_programs(0) - 1)
    def _():
        for r in range(0, rows, CHUNK):
            out[pl.ds(r, CHUNK), :] = total[pl.ds(r, CHUNK), :].astype(HALF)


def head_grad(turned, weight, info, logits):
    depth, rows = turned.shape
    vocab = weight.shape[1]
    return pl.pallas_call(
        functools.partial(grad_kernel, vocab),
        grid=(pl.cdiv(vocab, TILE),),
        in_specs=[
            pl.BlockSpec((depth, rows), lambda i: (0, 0), pipeline_mode=pl.Buffered(1)),
            pl.BlockSpec((depth, TILE), lambda i: (0, i)),
            pl.BlockSpec((8, rows), lambda i: (0, 0)),
            pl.BlockSpec((rows, TILE), lambda i: (0, i)),
        ],
        out_specs=[
            pl.BlockSpec((depth, TILE), lambda i: (0, i)),
            pl.BlockSpec((rows, depth), lambda i: (0, 0), pipeline_mode=pl.Buffered(1)),
        ],
        out_shape=[
            jax.ShapeDtypeStruct((depth, vocab), HALF),
            jax.ShapeDtypeStruct((rows, depth), HALF),
        ],
        scratch_shapes=[
            pltpu.VMEM((rows, depth), FLOAT),
            pltpu.VMEM((rows, TILE), HALF),
            pltpu.VMEM((rows, LANES), FLOAT),
        ],
        compiler_params=pltpu.CompilerParams(vmem_limit_bytes=VMEM_LIMIT),
        cost_estimate=SMALL,
        name="head_grad",
    )(turned, weight, info, logits)


def turn_rows(low, high, cosine, sine):
    return low * cosine - high * sine, high * cosine + low * sine


def reach(block, share, longest):
    back = -(-(longest - 1) // share)
    return max(0, block - back) * share


def seen(first, low, high, place):
    keys = low + lax.broadcasted_iota(jnp.int32, (high - low, first.shape[1]), 0)
    queries = place + lax.broadcasted_iota(jnp.int32, (high - low, first.shape[1]), 1)
    return (keys >= first) & (keys <= queries)


def attend_kernel(waits, base, qkv, cosine, sine, first, *refs):
    attended, kept, log_total = refs[waits:]
    seq = pl.program_id(1)
    blocks = base.shape[0]
    length = cosine.shape[1]
    share = length // blocks
    half = HEAD_DIM // 2

    def spot(i):
        return pl.ds(pl.multiple_of(base[i] + seq * share, share), share)

    for i in range(blocks):
        at = pl.ds(i * share, share)
        turns = (cosine[:, at], sine[:, at])
        for c in (0, 1):
            top = c * HEAD_DIM
            low, high = turn_rows(
                qkv[top : top + half, spot(i)], qkv[top + half : top + HEAD_DIM, spot(i)], *turns
            )
            kept[0, top : top + half, at] = low.astype(HALF)
            kept[0, top + half : top + HEAD_DIM, at] = high.astype(HALF)
        kept[0, 2 * HEAD_DIM :, at] = qkv[2 * HEAD_DIM :, spot(i)].astype(HALF)
    key = kept[0, HEAD_DIM : 2 * HEAD_DIM, :].T
    for i in range(blocks):
        low, high = reach(i, share, length // 2), (i + 1) * share
        at = pl.ds(i * share, share)
        scores = jnp.dot(
            key[low:high, :], kept[0, :HEAD_DIM, at], preferred_element_type=FLOAT
        ) * (HEAD_DIM**-0.5)
        scores = jnp.where(seen(first[0, :, at][:1], low, high, i * share), scores, NEG)
        peak = jnp.max(scores, axis=0, keepdims=True)
        expo = jnp.exp(scores - peak)
        summed = jnp.sum(expo, axis=0, keepdims=True)
        probs = (expo * (1.0 / summed)).astype(HALF)
        value = kept[0, 2 * HEAD_DIM :, low:high]
        attended[:, spot(i)] = jnp.dot(value, probs, preferred_element_type=FLOAT).astype(HALF)
        log_total[0, 0, :, at] = jnp.broadcast_to(peak + jnp.log(summed), (8, share))


def attend(base, qkv, cosine, sine, first, before):
    seqs, length = first.shape[0], first.shape[2]
    heads = qkv.shape[0] // (3 * HEAD_DIM)
    tokens = qkv.shape[1]
    return pl.pallas_call(
        functools.partial(attend_kernel, len(before)),
        grid=(heads, seqs),
        in_specs=[
            pl.BlockSpec(memory_space=pltpu.SMEM),
            pl.BlockSpec((3 * HEAD_DIM, tokens), lambda h, j: (h, 0)),
            pl.BlockSpec(cosine.shape, lambda h, j: (0, 0)),
            pl.BlockSpec(sine.shape, lambda h, j: (0, 0)),
            pl.BlockSpec((1, 8, length), lambda h, j: (j, 0, 0)),
        ]
        + [pl.BlockSpec(memory_space=pl.ANY)] * len(before),
        out_specs=[
            pl.BlockSpec((HEAD_DIM, tokens), lambda h, j: (h, 0)),
            pl.BlockSpec((1, 3 * HEAD_DIM, length), lambda h, j: (j, h, 0)),
            pl.BlockSpec((1, 1, 8, length), lambda h, j: (j, h, 0, 0)),
        ],
        out_shape=[
            jax.ShapeDtypeStruct((heads * HEAD_DIM, tokens), HALF),
            jax.ShapeDtypeStruct((seqs, heads * 3 * HEAD_DIM, length), HALF),
            jax.ShapeDtypeStruct((seqs, heads, 8, length), FLOAT),
        ],
        compiler_params=pltpu.CompilerParams(vmem_limit_bytes=VMEM_LIMIT),
        cost_estimate=SMALL,
        name="attend",
    )(base, qkv, cosine, sine, first, *before)


def attend_back_kernel(base, kept, log_total, slope, cosine, sine, first, d_qkv, d_key, d_value):
    seq = pl.program_id(1)
    blocks = base.shape[0]
    length = cosine.shape[1]
    share = length // blocks
    half = HEAD_DIM // 2
    scale = HEAD_DIM**-0.5

    def spot(i):
        return pl.ds(pl.multiple_of(base[i] + seq * share, share), share)

    def put(part, i, low, high):
        at = pl.ds(i * share, share)
        d_low, d_high = turn_rows(low, high, cosine[:, at], -sine[:, at])
        top = part * HEAD_DIM
        d_qkv[top : top + half, spot(i)] = d_low.astype(HALF)
        d_qkv[top + half : top + HEAD_DIM, spot(i)] = d_high.astype(HALF)

    query = kept[0, :HEAD_DIM, :].T
    key = kept[0, HEAD_DIM : 2 * HEAD_DIM, :].T
    value = kept[0, 2 * HEAD_DIM :, :].T
    d_key[...] = jnp.zeros_like(d_key)
    d_value[...] = jnp.zeros_like(d_value)
    for i in range(blocks):
        low, high = reach(i, share, length // 2), (i + 1) * share
        at = pl.ds(i * share, share)
        turned = slope[:, spot(i)]
        scores = jnp.dot(
            key[low:high, :], kept[0, :HEAD_DIM, at], preferred_element_type=FLOAT
        ) * scale
        scores = jnp.where(seen(first[0, :, at][:1], low, high, i * share), scores, NEG)
        probs = jnp.exp(scores - log_total[0, 0, :1, at])
        d_probs = jnp.dot(value[low:high, :], turned, preferred_element_type=FLOAT)
        centre = jnp.sum(probs * d_probs, axis=0, keepdims=True)
        d_scores = (probs * (d_probs - centre)).astype(HALF)
        d_value[low:high, :] += jnp.dot(probs.astype(HALF), turned.T, preferred_element_type=FLOAT)
        d_key[low:high, :] += jnp.dot(
            d_scores, query[i * share : (i + 1) * share, :], preferred_element_type=FLOAT
        )
        d_query = scale * jnp.dot(
            kept[0, HEAD_DIM : 2 * HEAD_DIM, low:high], d_scores, preferred_element_type=FLOAT
        )
        put(0, i, d_query[:half, :], d_query[half:, :])
    for i in range(blocks):
        rows = pl.ds(i * share, share)
        turned = scale * d_key[rows, :].T
        put(1, i, turned[:half, :], turned[half:, :])
        d_qkv[2 * HEAD_DIM :, spot(i)] = d_value[rows, :].T.astype(HALF)


def attend_back(base, kept, log_total, slope, cosine, sine, first):
    seqs, length = first.shape[0], first.shape[2]
    tokens = slope.shape[1]
    heads = slope.shape[0] // HEAD_DIM
    return pl.pallas_call(
        attend_back_kernel,
        grid=(heads, seqs),
        in_specs=[
            pl.BlockSpec(memory_space=pltpu.SMEM),
            pl.BlockSpec((1, 3 * HEAD_DIM, length), lambda h, j: (j, h, 0)),
            pl.BlockSpec((1, 1, 8, length), lambda h, j: (j, h, 0, 0)),
            pl.BlockSpec((HEAD_DIM, tokens), lambda h, j: (h, 0)),
            pl.BlockSpec(cosine.shape, lambda h, j: (0, 0)),
            pl.BlockSpec(sine.shape, lambda h, j: (0, 0)),
            pl.BlockSpec((1, 8, length), lambda h, j: (j, 0, 0)),
        ],
        out_specs=pl.BlockSpec((3 * HEAD_DIM, tokens), lambda h, j: (h, 0)),
        out_shape=jax.ShapeDtypeStruct((heads * 3 * HEAD_DIM, tokens), HALF),
        scratch_shapes=[pltpu.VMEM((length, HEAD_DIM), FLOAT)] * 2,
        compiler_params=pltpu.CompilerParams(vmem_limit_bytes=VMEM_LIMIT),
        cost_estimate=SMALL,
        name="attend_back",
    )(base, kept, log_total, slope, cosine, sine, first)


def near_and_far(own, rank):
    return (own, rank ^ 1), (own, rank ^ 2)


def remote(source, target, send, recv, n, peer):
    return pltpu.make_async_remote_copy(
        src_ref=source,
        dst_ref=target,
        send_sem=send.at[n],
        recv_sem=recv.at[n],
        device_id=peer,
        device_id_type=MESH,
    )


class Boundary:
    COUNT = 6

    def __init__(self, own, rank, send, recv, parts, rows):
        self.near, self.far = near_and_far(own, rank)
        self.send, self.recv, self.parts = send, recv, parts
        self.rows = [pl.ds(h * rows, rows) for h in range(parts)]
        self.copies = []

    def copy(self, source, target, n, h, peer):
        made = remote(source, target, self.send, self.recv, n * self.parts + h, peer)
        made.start()
        self.copies.append(made)
        return made

    def sums(self, partial, beside, away, come):
        later = {}
        for p in (1, 0):
            for h, at in enumerate(self.rows):
                later[p, h] = self.copy(partial.at[2 + p, at], beside.at[p, at], p, h, self.near)
        crossing = []
        for h, at in enumerate(self.rows):
            later[1, h].wait_recv()
            away[at, :] = (partial[1, at, :] + beside[1, at, :]).astype(HALF)
            crossing.append(self.copy(away.at[at], come.at[at], 2, h, self.far))
        for h, at in enumerate(self.rows):
            later[0, h].wait_recv()
            total = partial[0, at, :] + beside[0, at, :]
            crossing[h].wait_recv()
            yield h, at, total + come[at, :].astype(FLOAT)

    def give(self, full, h):
        at = self.rows[h]
        self.crossed = getattr(self, "crossed", [])
        self.crossed.append(self.copy(full.at[0, at], full.at[1, at], 3, h, self.far))
        self.beside = getattr(self, "beside", [])
        self.beside.append(self.copy(full.at[0, at], full.at[2, at], 4, h, self.near))

    def pass_on(self, full):
        arrived = []
        for h, at in enumerate(self.rows):
            self.crossed[h].wait_recv()
            arrived.append(self.copy(full.at[1, at], full.at[3, at], 5, h, self.near))
        for copy in self.beside + arrived:
            copy.wait_recv()

    def end(self):
        for copy in self.copies:
            copy.wait_send()


def forward_kernel(parts, partial, stream, gain, out, full, beside, away, come, send, recv):
    own, rank = lax.axis_index("dp"), lax.axis_index("tensor")
    greet(list(near_and_far(own, rank)))
    edge = Boundary(own, rank, send, recv, parts, stream.shape[0] // parts)
    for h, at, total in edge.sums(partial, beside, away, come):
        total = stream[at, :] + total
        out[at, :] = total
        full[0, at, :] = normed(total, gain[...]).astype(HALF)
        edge.give(full, h)
    edge.pass_on(full)
    edge.end()


def wide_forward_kernel(partial, stream, gain, out, full, beside, away, come, send, recv):
    own, rank = lax.axis_index("dp"), lax.axis_index("tensor")
    near, far = near_and_far(own, rank)
    other = (own ^ 1, rank)
    greet([near, far, other])
    parts = 2
    edge = Boundary(own, rank, send, recv, parts, stream.shape[0] // parts)
    crossed, moved, last = [], [], []
    for h, at, total in edge.sums(partial, beside, away, come):
        total = stream[at, :] + total
        out[at, :] = total
        full[0, 0, at, :] = normed(total, gain[...]).astype(HALF)
        mine = full.at[0, 0, at]
        crossed.append(edge.copy(mine, full.at[0, 1, at], 3, h, far))
        moved.append(edge.copy(mine, full.at[1, 0, at], 4, h, other))
        last.append(edge.copy(mine, full.at[0, 2, at], 5, h, near))
    early, late = edge.rows
    crossed[0].wait_recv()
    one = edge.copy(full.at[0, 1, early], full.at[1, 1, early], 6, 0, other)
    last.append(edge.copy(full.at[0, 1, early], full.at[0, 3, early], 7, 0, near))
    moved[0].wait_recv()
    last.append(edge.copy(full.at[1, 0, early], full.at[1, 2, early], 8, 0, near))
    moved[1].wait_recv()
    two = edge.copy(full.at[1, 0, late], full.at[1, 1, late], 6, 1, far)
    last.append(edge.copy(full.at[1, 0, late], full.at[1, 2, late], 8, 1, near))
    crossed[1].wait_recv()
    last.append(edge.copy(full.at[0, 1, late], full.at[0, 3, late], 7, 1, near))
    one.wait_recv()
    last.append(edge.copy(full.at[1, 1, early], full.at[1, 3, early], 9, 0, near))
    two.wait_recv()
    last.append(edge.copy(full.at[1, 1, late], full.at[1, 3, late], 9, 1, near))
    for copy in last:
        copy.wait_recv()
    edge.end()


def wide_forward(partial, stream, gain):
    rows, depth = stream.shape
    vmem = pl.BlockSpec(memory_space=pltpu.VMEM)
    out, full = pl.pallas_call(
        wide_forward_kernel,
        in_specs=[vmem] * 3,
        out_specs=[vmem] * 2,
        out_shape=[
            jax.ShapeDtypeStruct((rows, depth), FLOAT),
            jax.ShapeDtypeStruct((2, 4, rows, depth), HALF),
        ],
        scratch_shapes=exchange_scratch(rows, depth, 2)[:3] + [pltpu.SemaphoreType.DMA((20,))] * 2,
        compiler_params=pltpu.CompilerParams(
            collective_id=9, has_side_effects=True, vmem_limit_bytes=VMEM_LIMIT
        ),
        cost_estimate=SMALL,
        name="wide_forward",
    )(partial.reshape(4, rows, depth), stream, gain)
    return out, full.reshape(8 * rows, depth)


def wide_backward_kernel(partial, stream, gain, out, g_gain, full, beside, leave, come, send, recv):
    own, rank = lax.axis_index("dp"), lax.axis_index("tensor")
    near, far = near_and_far(own, rank)
    other = (own ^ 1, rank)
    greet([near, far, other])
    parts = 2
    edge = Boundary(own, rank, send, recv, parts, stream.shape[0] // parts)
    early, late = edge.rows
    first = {}
    for n, (y, p) in enumerate(((1, 1), (1, 0), (0, 1), (0, 0))):
        for h, at in enumerate(edge.rows):
            first[y, p, h] = edge.copy(
                partial.at[y, 2 + p, at], beside.at[y, p, at], 5 + n, h, near
            )

    def pair(y, p, h):
        at = edge.rows[h]
        first[y, p, h].wait_recv()
        return partial[y, p, at, :].astype(FLOAT) + beside[y, p, at, :].astype(FLOAT)

    leave[1, 1, early, :] = pair(1, 1, 0).astype(HALF)
    by_other = edge.copy(leave.at[1, 1, early], come.at[1, 1, early], 9, 0, other)
    leave[1, 1, late, :] = pair(1, 1, 1).astype(HALF)
    by_far = edge.copy(leave.at[1, 1, late], come.at[1, 1, late], 9, 1, far)
    leave[1, 0, early, :] = pair(1, 0, 0).astype(HALF)
    other_early = edge.copy(leave.at[1, 0, early], come.at[1, 0, early], 0, 0, other)
    leave[0, 1, late, :] = pair(0, 1, 1).astype(HALF)
    far_late = edge.copy(leave.at[0, 1, late], come.at[0, 1, late], 1, 1, far)
    far_early_sum, other_late_sum = pair(0, 1, 0), pair(1, 0, 1)
    by_other.wait_recv()
    leave[0, 1, early, :] = (far_early_sum + come[1, 1, early, :].astype(FLOAT)).astype(HALF)
    far_early = edge.copy(leave.at[0, 1, early], come.at[0, 1, early], 1, 0, far)
    by_far.wait_recv()
    leave[1, 0, late, :] = (other_late_sum + come[1, 1, late, :].astype(FLOAT)).astype(HALF)
    other_late = edge.copy(leave.at[1, 0, late], come.at[1, 0, late], 0, 1, other)
    g_gain[...] = jnp.zeros_like(g_gain)
    for h, waits in ((0, (other_early, far_early)), (1, (far_late, other_late))):
        at = edge.rows[h]
        total = pair(0, 0, h)
        for copy in waits:
            copy.wait_recv()
        total = total + come[1, 0, at, :].astype(FLOAT) + come[0, 1, at, :].astype(FLOAT)
        slope, by_gain = normed_slope(total, stream[at, :], gain[...])
        g_gain[:1, :] = g_gain[:1, :] + by_gain
        out[at, :] = slope
        full[0, at, :] = slope.astype(HALF)
        edge.crossed = getattr(edge, "crossed", [])
        edge.crossed.append(edge.copy(full.at[0, at], full.at[1, at], 2, h, far))
        edge.beside = getattr(edge, "beside", [])
        edge.beside.append(edge.copy(full.at[0, at], full.at[2, at], 3, h, near))
    arrived = []
    for h, at in enumerate(edge.rows):
        edge.crossed[h].wait_recv()
        arrived.append(edge.copy(full.at[1, at], full.at[3, at], 4, h, near))
    for copy in edge.beside + arrived:
        copy.wait_recv()
    edge.end()


def wide_backward(partial, stream, gain):
    rows, depth = stream.shape
    vmem = pl.BlockSpec(memory_space=pltpu.VMEM)
    out, g_gain, full = pl.pallas_call(
        wide_backward_kernel,
        in_specs=[vmem] * 3,
        out_specs=[vmem] * 3,
        out_shape=[
            jax.ShapeDtypeStruct((rows, depth), FLOAT),
            jax.ShapeDtypeStruct((8, depth), FLOAT),
            jax.ShapeDtypeStruct((4, rows, depth), HALF),
        ],
        scratch_shapes=[pltpu.VMEM((2, 2, rows, depth), HALF)] * 3
        + [pltpu.SemaphoreType.DMA((20,))] * 2,
        compiler_params=pltpu.CompilerParams(
            collective_id=4, has_side_effects=True, vmem_limit_bytes=VMEM_LIMIT
        ),
        cost_estimate=SMALL,
        name="wide_backward",
    )(partial.reshape(2, 4, rows, depth), stream, gain)
    return out, g_gain[:1], full.reshape(4 * rows, depth)


def exchange_scratch(rows, depth, parts):
    return [
        pltpu.VMEM((2, rows, depth), FLOAT),
        pltpu.VMEM((rows, depth), HALF),
        pltpu.VMEM((rows, depth), HALF),
        pltpu.SemaphoreType.DMA((Boundary.COUNT * parts,)),
        pltpu.SemaphoreType.DMA((Boundary.COUNT * parts,)),
    ]


def forward_boundary(partial, stream, gain):
    rows, depth = stream.shape
    parts = 2
    vmem = pl.BlockSpec(memory_space=pltpu.VMEM)
    out, full = pl.pallas_call(
        functools.partial(forward_kernel, parts),
        in_specs=[vmem] * 3,
        out_specs=[vmem] * 2,
        out_shape=[
            jax.ShapeDtypeStruct((rows, depth), FLOAT),
            jax.ShapeDtypeStruct((4, rows, depth), HALF),
        ],
        scratch_shapes=exchange_scratch(rows, depth, parts),
        compiler_params=pltpu.CompilerParams(
            collective_id=3, has_side_effects=True, vmem_limit_bytes=VMEM_LIMIT
        ),
        cost_estimate=SMALL,
        name="forward_boundary",
    )(partial.reshape(4, rows, depth), stream, gain)
    return out, full.reshape(4 * rows, depth)


def normed_slope(grad, values, gain):
    root = lax.rsqrt(jnp.mean(values * values, axis=-1, keepdims=True) + EPS)
    unit = values * root
    inner = grad * gain
    middle = jnp.mean(inner * unit, axis=-1, keepdims=True)
    return root * (inner - unit * middle), jnp.sum(grad * unit, axis=0, keepdims=True)


def backward_kernel(parts, partial, stream, gain, prior, out, g_gain, full, beside, away, come, send, recv):
    own, rank = lax.axis_index("dp"), lax.axis_index("tensor")
    greet(list(near_and_far(own, rank)))
    edge = Boundary(own, rank, send, recv, parts, stream.shape[0] // parts)
    g_gain[...] = jnp.zeros_like(g_gain)
    for h, at, total in edge.sums(partial, beside, away, come):
        slope, by_gain = normed_slope(total, stream[at, :], gain[...])
        slope = slope + prior[at, :]
        g_gain[:1, :] = g_gain[:1, :] + by_gain
        out[at, :] = slope
        full[0, at, :] = slope.astype(HALF)
        edge.give(full, h)
    edge.pass_on(full)
    edge.end()


def backward_boundary(partial, stream, gain, prior):
    rows, depth = stream.shape
    parts = 2
    vmem = pl.BlockSpec(memory_space=pltpu.VMEM)
    out, g_gain, full = pl.pallas_call(
        functools.partial(backward_kernel, parts),
        in_specs=[vmem] * 4,
        out_specs=[vmem] * 3,
        out_shape=[
            jax.ShapeDtypeStruct((rows, depth), FLOAT),
            jax.ShapeDtypeStruct((8, depth), FLOAT),
            jax.ShapeDtypeStruct((4, rows, depth), HALF),
        ],
        scratch_shapes=exchange_scratch(rows, depth, parts),
        compiler_params=pltpu.CompilerParams(
            collective_id=5, has_side_effects=True, vmem_limit_bytes=VMEM_LIMIT
        ),
        cost_estimate=SMALL,
        name="backward_boundary",
    )(partial.reshape(4, rows, depth), stream, gain, prior)
    return out, g_gain[:1], full.reshape(4 * rows, depth)


def start_kernel(ids, turned, gain, block, stream, full, weights, table, corner, rows, out, near, cross, come, send, recv):
    own, rank = lax.axis_index("dp"), lax.axis_index("tensor")
    beside, across = near_and_far(own, rank)
    far = [(own ^ k, rank) for k in range(1, 8)]
    greet([beside, across] + far)
    width, vocab = turned.shape
    count = rows.shape[0]
    copies, beside_of, across_of, far_of = [], {}, {}, {}

    def begin(source, target, n, peer):
        copy = remote(source, target, send, recv, n, peer)
        copy.start()
        copies.append(copy)
        return copy

    def place(k):
        return pl.ds(pl.multiple_of((own ^ k) * width, width), width)

    weights_of = {}
    for k in (1, 2, 4, 6):
        weights_of[k] = begin(block, weights.at[place(0)], 35 + k, far[k - 1])
    weights[place(0), :] = block[...]
    corner[...] = jnp.zeros_like(corner)
    for v in range(0, vocab, LANES):
        some = min(LANES, vocab - v)
        corner[:width, :some] = turned[:, v : v + some].astype(HALF).astype(FLOAT)
        if some < LANES:
            corner[:width, some:] = jnp.zeros((width, LANES - some), FLOAT)
        table[v : v + LANES, :] = corner[...].T
    if vocab % LANES == 0:
        table[vocab:, :] = jnp.zeros((LANES, LANES), FLOAT)

    def fetch(place):
        def body(i, carry):
            for u in range(16):
                r = i * 16 + u
                rows[pl.ds(r, 1), :] = table[pl.ds(ids[place * count + r], 1), :]
            return carry

        lax.fori_loop(0, count // 16, body, 0)

    for p in (3, 2):
        for k in range(8):
            fetch(p * 8 + k)
            out[p, k] = rows[:, :width].astype(HALF)
            beside_of[p - 2, k] = begin(out.at[p, k], near.at[p - 2, k], (p - 2) * 8 + k, beside)
    for k in (2, 4, 6):
        weights_of[k].wait_recv()
        weights_of[k + 1] = begin(weights.at[place(k)], weights.at[place(k)], 36 + k, far[0])
    order = (7, 6, 5, 4, 3, 2, 1, 0)
    for k in order:
        fetch(8 + k)
        beside_of[1, k].wait_recv()
        total = rows[:, :width] + near[1, k].astype(FLOAT)
        out[1, k] = total.astype(HALF)
        across_of[k] = begin(out.at[1, k], cross.at[k], 16 + k, across)
    for k in order:
        fetch(k)
        beside_of[0, k].wait_recv()
        total = rows[:, :width] + near[0, k].astype(FLOAT)
        across_of[k].wait_recv()
        out[0, k] = (total + cross[k].astype(FLOAT)).astype(HALF)
        if k:
            far_of[k] = begin(out.at[0, k], come.at[k], 24 + k, far[k - 1])
    come[0] = out[0, 0]
    for k in order[:-1]:
        far_of[k].wait_recv()
    for b in range(8):
        stream[:, b * width : (b + 1) * width] = come[own ^ b].astype(FLOAT)
    full[0] = normed(stream[...], gain[...]).astype(HALF)
    one = begin(full.at[0], full.at[1], 32, across)
    two = begin(full.at[0], full.at[2], 33, beside)
    one.wait_recv()
    three = begin(full.at[1], full.at[3], 34, beside)
    two.wait_recv()
    three.wait_recv()
    for k in (1, 3, 5, 7):
        weights_of[k].wait_recv()
    for copy in copies:
        copy.wait_send()


def start_rows(ids, turned, gain, block):
    width, vocab = turned.shape
    rows = ids.shape[0] // 32
    padded = (vocab // LANES + 1) * LANES
    vmem = pl.BlockSpec(memory_space=pltpu.VMEM)
    stream, full, weights = pl.pallas_call(
        start_kernel,
        in_specs=[pl.BlockSpec(memory_space=pltpu.SMEM), vmem, vmem, vmem],
        out_specs=[vmem] * 3,
        out_shape=[
            jax.ShapeDtypeStruct((rows, 8 * width), FLOAT),
            jax.ShapeDtypeStruct((4, rows, 8 * width), HALF),
            jax.ShapeDtypeStruct((8 * width, block.shape[1]), HALF),
        ],
        scratch_shapes=[
            pltpu.VMEM((padded, LANES), FLOAT),
            pltpu.VMEM((LANES, LANES), FLOAT),
            pltpu.VMEM((rows, LANES), FLOAT),
            pltpu.VMEM((4, 8, rows, width), HALF),
            pltpu.VMEM((2, 8, rows, width), HALF),
            pltpu.VMEM((8, rows, width), HALF),
            pltpu.VMEM((8, rows, width), HALF),
            pltpu.SemaphoreType.DMA((43,)),
            pltpu.SemaphoreType.DMA((43,)),
        ],
        compiler_params=pltpu.CompilerParams(
            collective_id=6, has_side_effects=True, vmem_limit_bytes=VMEM_LIMIT
        ),
        cost_estimate=SMALL,
        name="start_rows",
    )(ids, turned, gain, block)
    return stream, full.reshape(4 * rows, 8 * width), weights


def end_kernel(parts, waits, partial, stream, gain, prior, apart, *refs):
    rows, g_gain, arrived, beside, away, come, leave, send, recv = refs[waits:]
    own, rank = lax.axis_index("dp"), lax.axis_index("tensor")
    near, across = near_and_far(own, rank)
    far = [(own ^ k, rank) for k in range(1, 8)]
    greet([near, across] + far)
    edge = Boundary(own, rank, send, recv, parts, stream.shape[0] // parts)
    aside = remote(apart, arrived, send, recv, Boundary.COUNT * parts, far[0])
    aside.start()
    edge.copies.append(aside)
    g_gain[...] = jnp.zeros_like(g_gain)
    width = rows.shape[3]
    for h, at, total in edge.sums(partial, beside, away, come):
        slope, by_gain = normed_slope(total, stream[at, :], gain[...])
        slope = slope + prior[at, :]
        g_gain[:1, :] = g_gain[:1, :] + by_gain
        for b in range(8):
            leave[b, at, :] = slope[:, b * width : (b + 1) * width].astype(HALF)
    base = Boundary.COUNT * parts
    far_of, last = {}, []

    def begin(source, target, n, peer):
        copy = remote(source, target, send, recv, base + n, peer)
        copy.start()
        edge.copies.append(copy)
        return copy

    order = (7, 6, 5, 4, 3, 2, 1)
    for k in order:
        far_of[k] = begin(leave.at[own ^ k], rows.at[0, k], k, far[k - 1])
    rows[0, 0] = leave[own]
    crossed = {}
    for k in (0, 1, 2, 3, 4, 5, 6, 7):
        if k:
            far_of[k].wait_recv()
        crossed[k] = begin(rows.at[0, k], rows.at[1, k], 8 + k, across)
        last.append(begin(rows.at[0, k], rows.at[2, k], 16 + k, near))
    for k in (0, 1, 2, 3, 4, 5, 6, 7):
        crossed[k].wait_recv()
        last.append(begin(rows.at[1, k], rows.at[3, k], 24 + k, near))
    for copy in last:
        copy.wait_recv()
    aside.wait_recv()
    edge.end()


def end_rows(partial, stream, gain, prior, apart, width, before):
    rows, depth = stream.shape
    parts = 2
    vmem = pl.BlockSpec(memory_space=pltpu.VMEM)
    semaphores = Boundary.COUNT * parts + 32
    whole = pl.BlockSpec(memory_space=pl.ANY)
    out, g_gain, arrived = pl.pallas_call(
        functools.partial(end_kernel, parts, len(before)),
        in_specs=[vmem] * 4 + [whole] * (1 + len(before)),
        out_specs=[vmem] * 2 + [whole],
        out_shape=[
            jax.ShapeDtypeStruct((4, 8, rows, width), HALF),
            jax.ShapeDtypeStruct((8, depth), FLOAT),
            jax.ShapeDtypeStruct(apart.shape, HALF),
        ],
        scratch_shapes=exchange_scratch(rows, depth, parts)[:3]
        + [
            pltpu.VMEM((8, rows, width), HALF),
            pltpu.SemaphoreType.DMA((semaphores,)),
            pltpu.SemaphoreType.DMA((semaphores,)),
        ],
        compiler_params=pltpu.CompilerParams(
            collective_id=7, has_side_effects=True, vmem_limit_bytes=VMEM_LIMIT
        ),
        cost_estimate=SMALL,
        name="end_rows",
    )(partial.reshape(4, rows, depth), stream, gain, prior, apart, *before)
    return out.reshape(-1, width), g_gain[:1], arrived


def merge_kernel(scan, extra, joined, mine, every, send, recv):
    own, rank = lax.axis_index("dp"), lax.axis_index("tensor")
    turns = [(a, b) for a in (0, 1) for b in range(4)][1:]
    peers = [(own ^ a, rank ^ b) for a, b in turns]
    greet(peers)
    tokens = scan.shape[1] // 2
    share = tokens // 4
    mine[...] = jnp.zeros_like(mine)
    mine[0:3, :] = scan[0:3, :tokens]
    mine[3:6, :] = scan[0:3, tokens:]
    copies = []
    for n, peer in enumerate(peers):
        copies.append(remote(mine, every.at[n], send, recv, n, peer))
        copies[-1].start()
    joined[...] = jnp.zeros_like(joined)
    joined[2:4, :] = extra[:2, :]
    for copy in copies:
        copy.wait()
    for y in (0, 1):
        for p in range(4):
            terms = {(0, 0): mine[3 * y : 3 * y + 3, p * share : (p + 1) * share]}
            for n, (a, b) in enumerate(turns):
                q = TURN.index(TURN[p] ^ b)
                terms[a, b] = every[n, 3 * (y ^ a) : 3 * (y ^ a) + 3, q * share : (q + 1) * share]
            peak = functools.reduce(jnp.maximum, [term[0:1] for term in terms.values()])
            sums, hits = [], []
            for a in (0, 1):
                for b in (0, 2):
                    pair = (terms[a, b], terms[a, b ^ 1])
                    sums.append(sum(term[1:2] * jnp.exp(term[0:1] - peak) for term in pair))
                    hits.append(pair[0][2:3] + pair[1][2:3])
            at = pl.ds(y * tokens + p * share, share)
            joined[0:1, at] = peak + jnp.log((sums[0] + sums[1]) + (sums[2] + sums[3]))
            joined[1:2, at] = (hits[0] + hits[1]) + (hits[2] + hits[3])


def merge_scans(scan, extra):
    vmem = pl.BlockSpec(memory_space=pltpu.VMEM)
    shape = (8, scan.shape[1] // 2)
    return pl.pallas_call(
        merge_kernel,
        in_specs=[vmem] * 2,
        out_specs=vmem,
        out_shape=jax.ShapeDtypeStruct(scan.shape, FLOAT),
        scratch_shapes=[
            pltpu.VMEM(shape, FLOAT),
            pltpu.VMEM((7, *shape), FLOAT),
            pltpu.SemaphoreType.DMA((7,)),
            pltpu.SemaphoreType.DMA((7,)),
        ],
        compiler_params=pltpu.CompilerParams(collective_id=8, has_side_effects=True),
        name="merge_scans",
    )(scan, extra)


def across(left, right):
    return lax.dot_general(left, right, (((1,), (1,)), ((), ())), preferred_element_type=FLOAT)


def feed_kernel(norm, weight, out):
    ffn = weight.shape[1] // 3
    both = jnp.dot(norm[...], weight[:, : 2 * ffn], preferred_element_type=FLOAT)
    gate, up = both[:, :ffn], both[:, ffn:]
    hidden = (gate * (1.0 / (1.0 + jnp.exp(-gate))) * up).astype(HALF)
    out[...] = across(hidden, weight[:, 2 * ffn :])


def feed(norm, weight):
    tokens, depth = norm.shape
    rows = 512
    return pl.pallas_call(
        feed_kernel,
        grid=(tokens // rows,),
        in_specs=[
            pl.BlockSpec((rows, depth), lambda i: (i, 0)),
            pl.BlockSpec(weight.shape, lambda i: (0, 0), pipeline_mode=pl.Buffered(1)),
        ],
        out_specs=pl.BlockSpec((rows, depth), lambda i: (i, 0)),
        out_shape=jax.ShapeDtypeStruct((tokens, depth), FLOAT),
        compiler_params=pltpu.CompilerParams(vmem_limit_bytes=VMEM_LIMIT),
        cost_estimate=SMALL,
        name="feed",
    )(norm, weight)


def feed_back_kernel(norm, slope, weight, out, grad, total):
    step = pl.program_id(0)
    ffn = weight.shape[1] // 3

    @pl.when(step == 0)
    def _():
        total[...] = jnp.zeros_like(total)

    both = jnp.dot(norm[...], weight[:, : 2 * ffn], preferred_element_type=FLOAT)
    d_hidden = jnp.dot(slope[...], weight[:, 2 * ffn :], preferred_element_type=FLOAT)
    gate, up = both[:, :ffn], both[:, ffn:]
    open_part = 1.0 / (1.0 + jnp.exp(-gate))
    passed = gate * open_part
    hidden = (passed * up).astype(HALF)
    d_up = (d_hidden * passed).astype(HALF)
    d_gate = (d_hidden * up * (open_part * (1.0 + gate * (1.0 - open_part)))).astype(HALF)
    out[...] = across(d_gate, weight[:, :ffn]) + across(d_up, weight[:, ffn : 2 * ffn])
    turned = norm[...].T
    total[:, :ffn] += jnp.dot(turned, d_gate, preferred_element_type=FLOAT)
    total[:, ffn : 2 * ffn] += jnp.dot(turned, d_up, preferred_element_type=FLOAT)
    total[:, 2 * ffn :] += jnp.dot(slope[...].T, hidden, preferred_element_type=FLOAT)

    @pl.when(step == pl.num_programs(0) - 1)
    def _():
        grad[...] = total[...].astype(HALF)


def feed_back(norm, slope, weight):
    tokens, depth = norm.shape
    rows = 512
    return pl.pallas_call(
        feed_back_kernel,
        grid=(tokens // rows,),
        in_specs=[
            pl.BlockSpec((rows, depth), lambda i: (i, 0)),
            pl.BlockSpec((rows, depth), lambda i: (i, 0)),
            pl.BlockSpec(weight.shape, lambda i: (0, 0), pipeline_mode=pl.Buffered(1)),
        ],
        out_specs=[
            pl.BlockSpec((rows, depth), lambda i: (i, 0)),
            pl.BlockSpec(weight.shape, lambda i: (0, 0), pipeline_mode=pl.Buffered(1)),
        ],
        out_shape=[
            jax.ShapeDtypeStruct((tokens, depth), FLOAT),
            jax.ShapeDtypeStruct(weight.shape, HALF),
        ],
        scratch_shapes=[pltpu.VMEM(weight.shape, FLOAT)],
        compiler_params=pltpu.CompilerParams(vmem_limit_bytes=VMEM_LIMIT),
        cost_estimate=SMALL,
        name="feed_back",
    )(norm, slope, weight)


def product(left, right, over_left, over_right):
    return lax.dot_general(
        left, right, (((over_left,), (over_right,)), ((), ())), preferred_element_type=FLOAT
    )


def adam(weight, grad, first, second, rate, decay):
    first = BETA_ONE * first + (1.0 - BETA_ONE) * grad
    second = BETA_TWO * second + (1.0 - BETA_TWO) * grad * grad
    first_hat = first / (1.0 - BETA_ONE**STEP)
    second_hat = second / (1.0 - BETA_TWO**STEP)
    weight = weight - rate * (first_hat / (jnp.sqrt(second_hat) + ADAM_EPS) + decay * weight)
    return (weight, first, second, weight.astype(HALF))


def update_kernel(counts, factor, *refs):
    arrays = len(counts)
    inputs, outputs = refs[: 3 * arrays + sum(counts)], refs[3 * arrays + sum(counts) :]
    grads = inputs[3 * arrays :]
    for n in range(arrays):
        weight, first, second = inputs[3 * n : 3 * n + 3]
        low = 0
        for grad in grads[: counts[n]]:
            high = low + grad.shape[-1]
            at = (Ellipsis, slice(low, high))
            results = adam(
                weight[at], grad[...].astype(FLOAT) * factor[0], first[at], second[at], LR, DECAY
            )
            for out, result in zip(outputs[4 * n : 4 * n + 4], results):
                out[at] = result
            low = high
        grads = grads[counts[n] :]


def update(arrays, factor):
    rows = arrays[0][0].shape[0]
    step = 16 if rows % 16 == 0 else rows

    def block(array):
        zeros = (0,) * (array.ndim - 1)
        return pl.BlockSpec((step, *array.shape[1:]), lambda i: (i, *zeros))

    inputs = [array for entry in arrays for array in entry[:3]]
    grads = [grad for entry in arrays for grad in entry[3]]
    outs = [
        jax.ShapeDtypeStruct(entry[0].shape, kind)
        for entry in arrays
        for kind in (FLOAT, FLOAT, FLOAT, HALF)
    ]
    results = pl.pallas_call(
        functools.partial(update_kernel, tuple(len(entry[3]) for entry in arrays)),
        grid=(rows // step,),
        in_specs=[pl.BlockSpec(memory_space=pltpu.SMEM)] + [block(a) for a in inputs + grads],
        out_specs=[block(a) for a in outs],
        out_shape=outs,
        compiler_params=pltpu.CompilerParams(vmem_limit_bytes=VMEM_LIMIT),
        cost_estimate=SMALL,
        name="update",
    )(factor.reshape(1), *inputs, *grads)
    return [results[4 * n : 4 * n + 4] for n in range(len(arrays))]


def shards(
    token_ids,
    targets,
    segments,
    completion,
    micro_order,
    *state,
):
    weights, means, squares_in = state[:7], state[7:14], state[14:21]
    embedding, attn_in, attn_out, ffn_in, ffn_out, head_table, norm_gains = weights
    group = lax.axis_size("dp")
    parts = lax.axis_size("tensor")
    own, rank = lax.axis_index("dp"), lax.axis_index("tensor")
    vocab, width = embedding.shape
    start = rank * vocab
    seqs, length = token_ids.shape
    micro = micro_order.shape[1]
    share = length // parts
    turn = jnp.array(TURN, jnp.int32)
    dp_order = own ^ jnp.arange(group, dtype=jnp.int32)
    tensor_order = rank ^ turn
    tensor_order_natural = rank ^ jnp.arange(parts, dtype=jnp.int32)
    ffn = ffn_out.shape[0]
    qkv_width = attn_in.shape[1]

    attn_block = jnp.concatenate([attn_in, attn_out.T], axis=1).astype(HALF)
    ffn_block = jnp.concatenate([ffn_in.reshape(width, -1), ffn_out.T], axis=1).astype(HALF)
    bit = own % 2
    entries = vocab // 2
    low_half, high_half = head_table[:, :entries].astype(HALF), head_table[:, entries:].astype(HALF)
    stays = jnp.where(bit == 0, low_half, high_half)
    leaves = jnp.where(bit == 0, high_half, low_half)
    lines = [[i for i in range(group) if i % 2 == odd] for odd in (0, 1)]

    flags = completion.astype(FLOAT)
    picked_rows = micro_order[0]
    local_counts = jnp.sum(completion, axis=1)[picked_rows]
    id_rows = seqs * length // LANES
    packed = jnp.concatenate(
        [
            token_ids.reshape(-1),
            targets.reshape(-1),
            completion.reshape(-1),
            jnp.pad(jnp.concatenate([local_counts, picked_rows]), (0, 8 * LANES - 2 * micro)),
        ]
    ).reshape(3 * id_rows + 8, LANES)
    gains = jnp.pad(norm_gains.astype(HALF).astype(FLOAT), ((0, 5), (0, LANES - width)))
    if group == 8:
        packed, every_id, gains = spread(packed, gains, seqs, length, vocab, width)
        every_id = every_id.reshape(-1)
    else:
        packed, gains = lax.all_gather(packed, "dp"), lax.all_gather(gains, "dp")
        packed = jnp.take(packed, dp_order, axis=0)
        every_id = packed[:, :id_rows].reshape(group, seqs, parts, share)
        every_id = jnp.take(every_id, tensor_order, axis=2)
        every_id = every_id.transpose(2, 0, 1, 3).reshape(-1) - start
        every_id = jnp.where((every_id >= 0) & (every_id < vocab), every_id, vocab)
        gains = gains.transpose(1, 0, 2)[:, :, :width].reshape(8, -1)
    packed, attn_block, ffn_block, leaves = lax.optimization_barrier(
        (packed, attn_block, ffn_block, leaves)
    )
    ffn_parts = gather_first(ffn_block)
    came = swap(leaves, "dp", 1)
    head_rows = jnp.concatenate(
        [jnp.where(bit == 0, stays, came), jnp.where(bit == 0, came, stays)], axis=0
    )
    gains = gains[:3]
    numbers = packed[:, 3 * id_rows, : 2 * micro]
    counts = jnp.sum(numbers[:, :micro].astype(FLOAT), axis=0)

    def both_order(values):
        values = jnp.take(values.reshape(seqs, parts, share), tensor_order, axis=1)
        return values.transpose(1, 0, 2).reshape(-1)

    own_segment = segments[:, :, None] == jnp.arange(8, dtype=jnp.int32)
    sizes = jnp.sum(own_segment.astype(jnp.int32), axis=1)
    begins = jnp.cumsum(sizes, axis=1) - sizes
    first = jnp.sum(jnp.where(own_segment, begins[:, None, :], 0), axis=2)
    first = jnp.broadcast_to(first[:, None, :], (seqs, 8, length))
    base = turn[tensor_order_natural] * (seqs * share)
    cosine, sine = tables(length, HEAD_DIM)

    if group == 8:
        stream0, attn_norm, attn_w = start_rows(every_id, embedding.T, gains[:1], attn_block)
    else:
        rows = lookup(embedding.T, every_id).reshape(parts, group, seqs * share, width)
        rows = rows[:2] + swap(rows[2:], "tensor", 1)
        rows = rows[0] + swap(rows[1], "tensor", 2)
        rows = lax.all_to_all(jnp.take(rows, dp_order, axis=0), "dp", 0, 0)
        stream0 = rows.transpose(1, 0, 2).reshape(seqs * share, -1).astype(FLOAT)
        attn_norm = tensor_gather(normed(stream0, gains[0]).astype(HALF))

        attn_w = lax.all_gather(attn_block, "dp", axis=0, tiled=True)
    attn_norm, head_rows = lax.optimization_barrier((attn_norm, head_rows))
    head_b = lax.all_gather(head_rows, "dp", axis=0, tiled=True, axis_index_groups=lines)
    attn_in_b, attn_out_b = attn_w[:, :qkv_width], attn_w[:, qkv_width:]
    qkv = product(attn_in_b, attn_norm, 0, 1)
    attended, kept, log_sums = attend(base, qkv, cosine, sine, first, ffn_parts)
    stream1, ffn_norm = forward_boundary(product(attended, attn_out_b, 0, 1), stream0, gains[1:2])
    ffn_w = gather_last(ffn_block, ffn_parts)
    stream2, final_norm = wide_forward(feed(ffn_norm, ffn_w), stream1, gains[2:])

    final_norm, packed = lax.optimization_barrier((final_norm, packed))
    rows_extra = []
    for k in (0, 1):
        its_flags = packed[k, 2 * id_rows : 3 * id_rows].reshape(seqs, length).astype(FLOAT)
        its_order = numbers[k, micro:]
        slot = jnp.argmax(its_order[None, :] == jnp.arange(seqs)[:, None], axis=1)
        its_scale = its_flags * (1.0 / jnp.maximum(counts, 1.0))[slot][:, None]
        aims = packed[k, id_rows : 2 * id_rows].reshape(seqs, length) - start - bit * entries
        aims = jnp.where((aims >= 0) & (aims < entries), aims, -1).astype(FLOAT)
        rows_extra.append(jnp.stack([both_order(its_scale), both_order(aims)]))
    extra = jnp.pad(jnp.concatenate(rows_extra, axis=1), ((0, 6), (0, 0)))
    joint_flags = both_order(flags)
    logits, scan = head_scan(final_norm, head_b, extra)
    info = merge_scans(scan, extra)
    tokens = seqs * length
    seq_loss = jnp.sum(
        ((info[0, :tokens] - info[1, :tokens]) * joint_flags).reshape(parts, seqs, share),
        axis=(0, 2),
    )
    g_head, d_final = head_grad(final_norm.T, head_b, info, logits)
    g_head = lax.psum_scatter(
        g_head, "dp", scatter_dimension=0, tiled=True, axis_index_groups=lines
    )
    g_stays = jnp.where(bit == 0, g_head[:width], g_head[width:])
    g_leaves = jnp.where(bit == 0, g_head[width:], g_head[:width])

    d_stream2, g_gain2, d_branch2 = wide_backward(d_final, stream2, gains[2:])
    d_norm, g_ffn = feed_back(ffn_norm, d_branch2, ffn_w)
    g_ffn_parts = scatter_first(g_ffn)
    d_stream1, g_gain1, d_branch1 = backward_boundary(d_norm, stream1, gains[1:2], d_stream2)
    d_attended = product(attn_out_b, d_branch1, 0, 1).astype(HALF)
    d_qkv = attend_back(base, kept, log_sums, d_attended, cosine, sine, first)
    g_attn_in = product(attn_norm, d_qkv, 0, 1).astype(HALF)
    g_attn_out = product(d_branch1, attended, 0, 1).astype(HALF)
    g_attn = jnp.concatenate([g_attn_in, g_attn_out], axis=1)
    g_attn_parts = scatter_first(g_attn)
    d_norm = product(d_qkv, attn_in_b, 0, 1)
    g_ffn, g_ffn_leaves = scatter_middle(g_ffn, g_ffn_parts)
    if group == 8:
        rows, g_gain0, g_came = end_rows(
            d_norm, stream0, gains[:1], d_stream1, g_leaves, width, g_ffn_leaves
        )
    else:
        d_part, g_gain0 = normed_slope(tensor_scatter(d_norm), stream0, gains[:1])
        rows = (d_stream1 + d_part).astype(HALF)
        rows = rows.reshape(seqs * share, group, width).transpose(1, 0, 2)
        rows = jnp.take(lax.all_to_all(rows, "dp", 0, 0), dp_order, axis=0)
        rows = tensor_gather(rows[None]).reshape(-1, width)
        g_came = swap(g_leaves, "dp", 1)
    g_head = [jnp.where(bit == 0, g_stays, g_came), jnp.where(bit == 0, g_came, g_stays)]
    rows, g_ffn, g_attn = lax.optimization_barrier((rows, g_ffn, g_attn))
    g_attn, g_attn_leaves = scatter_middle(g_attn, g_attn_parts)
    g_embed, squares = collect(rows, every_id, vocab, g_attn_leaves)
    squares, g_ffn, g_attn = lax.optimization_barrier((squares, g_ffn, g_attn))
    g_ffn = scatter_last(g_ffn, g_ffn_leaves)
    g_attn = scatter_last(g_attn, g_attn_leaves)

    gain_sum = jnp.concatenate([g_gain0, g_gain1, g_gain2]).reshape(3, group, width)
    if group == 8:
        gain_sum = jnp.take(gain_sum.transpose(1, 0, 2), dp_order, axis=0)
        gain_sum = jnp.pad(gain_sum, ((0, 0), (0, 5), (0, LANES - width)))
        g_gains = total_over_devices(gain_sum)[:3, :width]
    else:
        g_gains = jnp.take(lax.psum(gain_sum, ("dp", "tensor")), own, axis=1)

    owner = (rank == 0).astype(FLOAT)
    squared = jnp.sum(squares) + owner * jnp.sum(g_gains * g_gains)
    for part in (g_attn, g_ffn, *g_head):
        squared = squared + jnp.sum(part.astype(FLOAT) ** 2)
    losses = seq_loss[picked_rows] * owner
    if group == 8:
        sums = jnp.pad(jnp.concatenate([squared[None], losses]), (0, 8 * LANES - 1 - micro))
        sums = total_over_devices(jnp.broadcast_to(sums.reshape(1, 8, LANES), (8, 8, LANES)))
        squared, loss_sums = sums[0, 0], sums[0, 1 : 1 + micro]
    else:
        squared, loss_sums = lax.psum((squared, losses), ("dp", "tensor"))
    grad_norm = jnp.sqrt(squared)
    factor = CLIP / jnp.maximum(grad_norm, CLIP)
    g_parts = (
        [g_embed],
        [g_attn[:, :qkv_width]],
        [g_attn[:, qkv_width:]],
        [g_ffn[:, : 2 * ffn].reshape(ffn_in.shape)],
        [g_ffn[:, 2 * ffn :]],
        g_head,
    )
    arrays = []
    for place in range(6):
        entry = (weights[place], means[place], squares_in[place])
        if place in (0, 2, 4):
            entry = tuple(array.T for array in entry)
        arrays.append((*entry, g_parts[place]))
    updated = []
    for place, results in enumerate(update(arrays, factor)):
        updated.extend(result.T if place in (0, 2, 4) else result for result in results)
    updated.extend(adam(norm_gains, g_gains * factor, means[6], squares_in[6], LR_GAIN, 0.0))
    return (jnp.stack([loss_sums, counts]), grad_norm, *updated)


def solution(mesh):
    in_specs = (
        P("dp", None),
        P("dp", None),
        P("dp", None),
        P("dp", None),
        P("dp", None),
        P("tensor", "dp"),
        P("dp", "tensor"),
        P("tensor", "dp"),
        P("dp", None, "tensor"),
        P("tensor", "dp"),
        P("dp", "tensor"),
        P(None, "dp"),
        P("tensor", "dp"),
        P("dp", "tensor"),
        P("tensor", "dp"),
        P("dp", None, "tensor"),
        P("tensor", "dp"),
        P("dp", "tensor"),
        P(None, "dp"),
        P("tensor", "dp"),
        P("dp", "tensor"),
        P("tensor", "dp"),
        P("dp", None, "tensor"),
        P("tensor", "dp"),
        P("dp", "tensor"),
        P(None, "dp"),
    )
    out_specs = (
        P(),
        P(),
        P("tensor", "dp"),
        P("tensor", "dp"),
        P("tensor", "dp"),
        P("tensor", "dp"),
        P("dp", "tensor"),
        P("dp", "tensor"),
        P("dp", "tensor"),
        P("dp", "tensor"),
        P("tensor", "dp"),
        P("tensor", "dp"),
        P("tensor", "dp"),
        P("tensor", "dp"),
        P("dp", None, "tensor"),
        P("dp", None, "tensor"),
        P("dp", None, "tensor"),
        P("dp", None, "tensor"),
        P("tensor", "dp"),
        P("tensor", "dp"),
        P("tensor", "dp"),
        P("tensor", "dp"),
        P("dp", "tensor"),
        P("dp", "tensor"),
        P("dp", "tensor"),
        P("dp", "tensor"),
        P(None, "dp"),
        P(None, "dp"),
        P(None, "dp"),
        P(None, "dp"),
    )
    return jax.shard_map(shards, mesh=mesh, in_specs=in_specs, out_specs=out_specs, check_vma=False)
```

```python
import functools

import jax
import jax.numpy as jnp
import numpy as np
from jax import lax
from jax.experimental import pallas as pl
from jax.experimental.pallas import tpu as pltpu
from jax.sharding import PartitionSpec as P

HEAD_DIM = 64
STEP = 10


EPS = 1e-05
CLIP = 0.01
LR = 0.03
LR_GAIN = 0.5
BETA_ONE = 0.9
BETA_TWO = 0.95
ADAM_EPS = 1e-08
DECAY = 0.1
NEG = -1e30
FLOAT = jnp.float32
HALF = jnp.bfloat16
LANES = 128
ROWS = 1024
VMEM_LIMIT = 56 * 2**20
TILE = 512
CHUNK = 256
MESH = pl.DeviceIdType.MESH
SMALL = pl.CostEstimate(flops=2**20, bytes_accessed=2**20, transcendentals=0)

TURN = (0, 2, 1, 3)


def swap(value, axis, bit):
    pairs = [(i, i ^ bit) for i in range(lax.axis_size(axis))]
    return lax.ppermute(value, axis, pairs)


def normed(values, gain):
    return values * lax.rsqrt(jnp.mean(values * values, axis=-1, keepdims=True) + EPS) * gain


def tables(length, width):
    inverse = np.float32(10000.0) ** (-np.arange(0, width, 2, dtype=np.float32) / np.float32(width))
    angle = inverse[:, None] * np.arange(length, dtype=np.float32)[None, :]
    return jnp.asarray(np.cos(angle)), jnp.asarray(np.sin(angle))


def gather_first(block):
    if lax.axis_size("dp") != 8:
        return []
    return [swap(block, "dp", k) for k in (2, 4, 6)]


def gather_middle(block, parts):
    return jnp.concatenate([block, *parts], axis=0)


def gather_last(parts):
    group = lax.axis_size("dp")
    if group != 8:
        return lax.all_gather(parts, "dp", axis=0, tiled=True)
    there = swap(parts, "dp", 1)
    rows = parts.shape[0] // 4
    own = lax.axis_index("dp")
    full = jnp.zeros((group * rows, parts.shape[1]), parts.dtype)
    for n in range(group // 2):
        at = slice(n * rows, (n + 1) * rows)
        full = lax.dynamic_update_slice(full, parts[at], ((own ^ (2 * n)) * rows, 0))
        full = lax.dynamic_update_slice(full, there[at], ((own ^ (2 * n + 1)) * rows, 0))
    return full


def block_of(full, k):
    rows = full.shape[0] // lax.axis_size("dp")
    own = lax.axis_index("dp")
    return lax.dynamic_slice(full, ((own ^ k) * rows, 0), (rows, full.shape[1]))


def scatter_first(full):
    if lax.axis_size("dp") != 8:
        return []
    leaves = jnp.concatenate([block_of(full, k + 1) for k in (0, 2, 4, 6)], axis=0)
    return [swap(leaves, "dp", 1)]


def scatter_middle(full, parts):
    if lax.axis_size("dp") != 8:
        return full, []
    rows = full.shape[0] // 8
    sums = [
        block_of(full, 2 * n).astype(FLOAT) + parts[0][n * rows : (n + 1) * rows].astype(FLOAT)
        for n in range(4)
    ]
    return sums[0], [total.astype(HALF) for total in sums[1:]]


def scatter_last(total, leaves):
    if lax.axis_size("dp") != 8:
        return lax.psum_scatter(total.astype(FLOAT), "dp", scatter_dimension=0, tiled=True)
    for n, leave in enumerate(leaves):
        total = total + swap(leave, "dp", 2 * n + 2).astype(FLOAT)
    return total


def peers_of(own, rank, bits, axis):
    if axis == "dp":
        return [(own ^ k, rank) for k in bits]
    return [(own, rank ^ k) for k in bits]


def greet(peers):
    barrier = pltpu.get_barrier_semaphore()
    for peer in peers:
        pl.semaphore_signal(barrier, inc=1, device_id=peer, device_id_type=MESH)
    pl.semaphore_wait(barrier, len(peers))


def spread_kernel(vocab, seqs, numbers, gains, every, ids, all_gains, every_gain, send, recv):
    own, rank = lax.axis_index("dp"), lax.axis_index("tensor")
    peers = peers_of(own, rank, range(1, 8), "dp")
    greet(peers)
    every[0] = numbers[...]
    every_gain[0] = gains[...]
    copies = []
    for k in range(1, 8):
        for n, (source, target) in enumerate(((numbers, every), (gains, every_gain))):
            copies.append(
                pltpu.make_async_remote_copy(
                    src_ref=source,
                    dst_ref=target.at[k],
                    send_sem=send.at[n, k],
                    recv_sem=recv.at[n, k],
                    device_id=peers[k - 1],
                    device_id_type=MESH,
                )
            )
            copies[-1].start()
    for copy in copies:
        copy.wait()
    lines = ids.shape[0] // (32 * seqs)
    for p in range(4):
        shard = rank ^ TURN[p]
        for k in range(8):
            for j in range(seqs):
                local = every[k, pl.ds((j * 4 + shard) * lines, lines), :] - rank * vocab
                local = jnp.where((local >= 0) & (local < vocab), local, vocab)
                ids[pl.ds(((p * 8 + k) * seqs + j) * lines, lines), :] = local
    width = all_gains.shape[1] // 8
    for b in range(8):
        all_gains[:, b * width : (b + 1) * width] = every_gain[own ^ b][:, :width]


def spread(numbers, gains, seqs, length, vocab, width):
    vmem = pl.BlockSpec(memory_space=pltpu.VMEM)
    return pl.pallas_call(
        functools.partial(spread_kernel, vocab, seqs),
        in_specs=[vmem] * 2,
        out_specs=[vmem] * 3,
        out_shape=[
            jax.ShapeDtypeStruct((8, *numbers.shape), numbers.dtype),
            jax.ShapeDtypeStruct((8 * seqs * length // LANES, LANES), jnp.int32),
            jax.ShapeDtypeStruct((8, 8 * width), FLOAT),
        ],
        scratch_shapes=[
            pltpu.VMEM((8, *gains.shape), FLOAT),
            pltpu.SemaphoreType.DMA((2, 8)),
            pltpu.SemaphoreType.DMA((2, 8)),
        ],
        compiler_params=pltpu.CompilerParams(collective_id=1, has_side_effects=True),
        cost_estimate=SMALL,
        name="spread",
    )(numbers, gains)


def total_kernel(blocks, out, first, summed, second, send, recv):
    own, rank = lax.axis_index("dp"), lax.axis_index("tensor")
    near = peers_of(own, rank, range(1, 4), "tensor")
    far = peers_of(own, rank, range(1, 8), "dp")
    greet(near + far)
    copies = []
    for k in range(1, 4):
        copy = pltpu.make_async_remote_copy(
            src_ref=blocks,
            dst_ref=first.at[k - 1],
            send_sem=send.at[k - 1],
            recv_sem=recv.at[k - 1],
            device_id=near[k - 1],
            device_id_type=MESH,
        )
        copy.start()
        copies.append(copy)
    for copy in copies:
        copy.wait()
    summed[...] = (blocks[...] + first[0]) + (first[1] + first[2])
    copies = []
    for k in range(1, 8):
        copy = pltpu.make_async_remote_copy(
            src_ref=summed.at[k],
            dst_ref=second.at[k],
            send_sem=send.at[2 + k],
            recv_sem=recv.at[2 + k],
            device_id=far[k - 1],
            device_id_type=MESH,
        )
        copy.start()
        copies.append(copy)
    for copy in copies:
        copy.wait()
    second[0] = summed[0]
    pairs = [second[k] + second[k + 1] for k in (0, 2, 4, 6)]
    out[...] = (pairs[0] + pairs[1]) + (pairs[2] + pairs[3])


def total_over_devices(blocks):
    shape = blocks.shape
    return pl.pallas_call(
        total_kernel,
        in_specs=[pl.BlockSpec(memory_space=pltpu.VMEM)],
        out_specs=pl.BlockSpec(memory_space=pltpu.VMEM),
        out_shape=jax.ShapeDtypeStruct(shape[1:], FLOAT),
        scratch_shapes=[
            pltpu.VMEM((3, *shape), FLOAT),
            pltpu.VMEM(shape, FLOAT),
            pltpu.VMEM(shape, FLOAT),
            pltpu.SemaphoreType.DMA((10,)),
            pltpu.SemaphoreType.DMA((10,)),
        ],
        compiler_params=pltpu.CompilerParams(collective_id=2, has_side_effects=True),
        name="total",
    )(blocks)


def tensor_gather(block):
    half = jnp.concatenate([block, swap(block, "tensor", 2)], axis=0)
    return jnp.concatenate([half, swap(half, "tensor", 1)], axis=0)


def tensor_scatter(full):
    half = full.shape[0] // 2
    quarter = half // 2
    both = full[:half] + swap(full[half:], "tensor", 1)
    there = swap(both[quarter:].astype(HALF), "tensor", 2)
    return both[:quarter] + there.astype(FLOAT)


def lookup_kernel(ids, turned, out, table, corner, rows):
    count = rows.shape[0]
    width, vocab = turned.shape

    @pl.when(pl.program_id(0) == 0)
    def _():
        corner[...] = jnp.zeros_like(corner)
        for v in range(0, vocab, LANES):
            some = min(LANES, vocab - v)
            corner[:width, :some] = turned[:, v : v + some].astype(HALF).astype(FLOAT)
            if some < LANES:
                corner[:width, some:] = jnp.zeros((width, LANES - some), FLOAT)
            table[v : v + LANES, :] = corner[...].T
        if vocab % LANES == 0:
            table[vocab:, :] = jnp.zeros((LANES, LANES), FLOAT)

    def body(i, carry):
        for u in range(16):
            r = i * 16 + u
            rows[pl.ds(r, 1), :] = table[pl.ds(ids[0, 0, r], 1), :]
        return carry

    lax.fori_loop(0, count // 16, body, 0)
    out[...] = rows[:, : out.shape[1]].astype(HALF)


def lookup(turned, ids):
    count = ids.shape[0]
    width, vocab = turned.shape
    padded = (vocab // LANES + 1) * LANES
    return pl.pallas_call(
        lookup_kernel,
        grid=(count // ROWS,),
        in_specs=[
            pl.BlockSpec((1, 1, ROWS), lambda i: (i, 0, 0), memory_space=pltpu.SMEM),
            pl.BlockSpec(turned.shape, lambda i: (0, 0), pipeline_mode=pl.Buffered(1)),
        ],
        out_specs=pl.BlockSpec((ROWS, width), lambda i: (i, 0)),
        out_shape=jax.ShapeDtypeStruct((count, width), HALF),
        scratch_shapes=[
            pltpu.VMEM((padded, LANES), FLOAT),
            pltpu.VMEM((LANES, LANES), FLOAT),
            pltpu.VMEM((ROWS, LANES), FLOAT),
        ],
        compiler_params=pltpu.CompilerParams(vmem_limit_bytes=VMEM_LIMIT),
        cost_estimate=SMALL,
        name="lookup",
    )(ids.reshape(count // ROWS, 1, ROWS), turned)


def collect_kernel(waits, ids, grads, *refs):
    out, squares, rows, *sums = refs[waits:]
    step = pl.program_id(0)
    count = rows.shape[0]
    width, vocab = out.shape

    @pl.when(step == 0)
    def _():
        rows[...] = jnp.zeros_like(rows)
        for total in sums:
            total[...] = jnp.zeros_like(total)

    rows[:, :width] = grads[...].astype(FLOAT)

    def body(i, carry):
        for u in range(16):
            r = i * 16 + u
            total = sums[u % len(sums)]
            place = pl.ds(ids[0, 0, r], 1)
            total[place, :] = total[place, :] + rows[pl.ds(r, 1), :]
        return carry

    lax.fori_loop(0, count // 16, body, 0)

    @pl.when(step == pl.num_programs(0) - 1)
    def _():
        squared = jnp.zeros((8, LANES), FLOAT)
        for v in range(0, vocab, LANES):
            some = min(LANES, vocab - v)
            total = sums[0][v : v + some, :]
            for other in sums[1:]:
                total = total + other[v : v + some, :]
            for r in range(0, some, 8):
                squared = squared + total[r : r + 8, :] * total[r : r + 8, :]
            if some < LANES:
                total = jnp.concatenate([total, jnp.zeros((LANES - some, LANES), FLOAT)], axis=0)
            out[:, v : v + some] = total.T[:width, :some]
        squares[...] = squared


def collect(grads, ids, vocab, before):
    count = ids.shape[0]
    width = grads.shape[1]
    padded = (vocab // LANES + 1) * LANES
    return pl.pallas_call(
        functools.partial(collect_kernel, len(before)),
        grid=(count // ROWS,),
        in_specs=[
            pl.BlockSpec((1, 1, ROWS), lambda i: (i, 0, 0), memory_space=pltpu.SMEM),
            pl.BlockSpec((ROWS, width), lambda i: (i, 0)),
        ]
        + [pl.BlockSpec(memory_space=pl.ANY)] * len(before),
        out_specs=[
            pl.BlockSpec((width, vocab), lambda i: (0, 0)),
            pl.BlockSpec((8, LANES), lambda i: (0, 0)),
        ],
        out_shape=[
            jax.ShapeDtypeStruct((width, vocab), FLOAT),
            jax.ShapeDtypeStruct((8, LANES), FLOAT),
        ],
        scratch_shapes=[pltpu.VMEM((ROWS, LANES), FLOAT)]
        + [pltpu.VMEM((padded, LANES), FLOAT)] * 8,
        compiler_params=pltpu.CompilerParams(vmem_limit_bytes=VMEM_LIMIT),
        cost_estimate=SMALL,
        name="collect",
    )(ids.reshape(count // ROWS, 1, ROWS), grads, *before)


def edge_of(vocab):
    return vocab - (pl.cdiv(vocab, TILE) - 1) * TILE


def each_tile(vocab, work):
    last = edge_of(vocab)
    if last == TILE:
        work(TILE)
    else:
        step, steps = pl.program_id(0), pl.num_programs(0)
        pl.when(step < steps - 1)(lambda: work(TILE))
        pl.when(step == steps - 1)(lambda: work(last))


def turned_rows(rows):
    return jnp.concatenate([rows] * (LANES // 8), axis=0).T


def scan_kernel(vocab, norm, weight, target, logits, stats, turned, peak, total, hit, aims):
    step = pl.program_id(0)
    rows = norm.shape[0]

    @pl.when(step == 0)
    def _():
        peak[...] = jnp.full_like(peak, NEG)
        total[...] = jnp.zeros_like(total)
        hit[...] = jnp.zeros_like(hit)
        aims[...] = turned_rows(target[...])
        for r in range(0, rows, CHUNK):
            turned[:, r : r + CHUNK] = norm[r : r + CHUNK, :].T

    def work(width):
        lane = lax.broadcasted_iota(jnp.int32, (CHUNK, LANES), 1)
        for r in range(0, rows, CHUNK):
            part = pl.ds(r, CHUNK)
            value = jnp.dot(norm[part, :], weight[...], preferred_element_type=FLOAT)
            logits[part, :] = value
            aim = aims[part, 1:2].astype(jnp.int32) - step * TILE
            slabs, found = [], hit[part, :]
            for c in range(0, width, LANES):
                slab = value[:, c : c + LANES]
                if c + LANES > width:
                    slab = jnp.where(lane < width - c, slab, NEG)
                slabs.append(slab)
                found = found + jnp.where(lane == aim - c, slab, 0.0)
            hit[part, :] = found
            before = peak[part, :]
            top = functools.reduce(jnp.maximum, slabs, before)
            added = total[part, :] * jnp.exp(before - top)
            for slab in slabs:
                added = added + jnp.exp(slab - top)
            total[part, :] = added
            peak[part, :] = top

    each_tile(vocab, work)

    @pl.when(step == pl.num_programs(0) - 1)
    def _():
        top = jnp.max(peak[...], axis=1, keepdims=True)
        added = jnp.sum(total[...] * jnp.exp(peak[...] - top), axis=1, keepdims=True)
        found = jnp.sum(hit[...], axis=1, keepdims=True)
        lane = lax.broadcasted_iota(jnp.int32, (rows, LANES), 1)
        joined = jnp.where(lane == 0, top, jnp.where(lane == 1, added, found))
        stats[...] = joined.T[:8, :]


def head_scan(norm, weight, extra):
    rows, depth = norm.shape
    vocab = weight.shape[1]
    return pl.pallas_call(
        functools.partial(scan_kernel, vocab),
        grid=(pl.cdiv(vocab, TILE),),
        in_specs=[
            pl.BlockSpec((rows, depth), lambda i: (0, 0), pipeline_mode=pl.Buffered(1)),
            pl.BlockSpec((depth, TILE), lambda i: (0, i)),
            pl.BlockSpec((8, rows), lambda i: (0, 0)),
        ],
        out_specs=[
            pl.BlockSpec((rows, TILE), lambda i: (0, i)),
            pl.BlockSpec((8, rows), lambda i: (0, 0)),
            pl.BlockSpec((depth, rows), lambda i: (0, 0), pipeline_mode=pl.Buffered(1)),
        ],
        out_shape=[
            jax.ShapeDtypeStruct((rows, vocab), FLOAT),
            jax.ShapeDtypeStruct((8, rows), FLOAT),
            jax.ShapeDtypeStruct((depth, rows), HALF),
        ],
        scratch_shapes=[pltpu.VMEM((rows, LANES), FLOAT)] * 4,
        compiler_params=pltpu.CompilerParams(vmem_limit_bytes=VMEM_LIMIT),
        cost_estimate=SMALL,
        name="head_scan",
    )(norm, weight, extra)


def grad_kernel(vocab, turned, weight, info, logits, grad, out, total, slope, columns):
    step = pl.program_id(0)
    rows = logits.shape[0]

    @pl.when(step == 0)
    def _():
        columns[...] = turned_rows(info[...])
        total[...] = jnp.zeros_like(total)

    def work(width):
        lane = lax.broadcasted_iota(jnp.int32, (CHUNK, TILE), 1)
        table = weight[...]
        if width < TILE:
            table = jnp.where(lax.broadcasted_iota(jnp.int32, table.shape, 1) < width, table, 0.0)
        for r in range(0, rows, CHUNK):
            part = pl.ds(r, CHUNK)
            aim = columns[part, 3:4].astype(jnp.int32) - step * TILE
            value = jnp.exp(logits[part, :] - columns[part, 0:1])
            value = (value - jnp.where(lane == aim, 1.0, 0.0)) * columns[part, 2:3]
            if width < TILE:
                value = jnp.where(lane < width, value, 0.0)
            value = value.astype(HALF)
            slope[part, :] = value
            total[part, :] = total[part, :] + lax.dot_general(
                value, table, (((1,), (1,)), ((), ())), preferred_element_type=FLOAT
            )
        grad[...] = jnp.dot(turned[...], slope[...], preferred_element_type=FLOAT).astype(HALF)

    each_tile(vocab, work)

    @pl.when(step == pl.num_programs(0) - 1)
    def _():
        for r in range(0, rows, CHUNK):
            out[pl.ds(r, CHUNK), :] = total[pl.ds(r, CHUNK), :].astype(HALF)


def head_grad(turned, weight, info, logits):
    depth, rows = turned.shape
    vocab = weight.shape[1]
    return pl.pallas_call(
        functools.partial(grad_kernel, vocab),
        grid=(pl.cdiv(vocab, TILE),),
        in_specs=[
            pl.BlockSpec((depth, rows), lambda i: (0, 0), pipeline_mode=pl.Buffered(1)),
            pl.BlockSpec((depth, TILE), lambda i: (0, i)),
            pl.BlockSpec((8, rows), lambda i: (0, 0)),
            pl.BlockSpec((rows, TILE), lambda i: (0, i)),
        ],
        out_specs=[
            pl.BlockSpec((depth, TILE), lambda i: (0, i)),
            pl.BlockSpec((rows, depth), lambda i: (0, 0), pipeline_mode=pl.Buffered(1)),
        ],
        out_shape=[
            jax.ShapeDtypeStruct((depth, vocab), HALF),
            jax.ShapeDtypeStruct((rows, depth), HALF),
        ],
        scratch_shapes=[
            pltpu.VMEM((rows, depth), FLOAT),
            pltpu.VMEM((rows, TILE), HALF),
            pltpu.VMEM((rows, LANES), FLOAT),
        ],
        compiler_params=pltpu.CompilerParams(vmem_limit_bytes=VMEM_LIMIT),
        cost_estimate=SMALL,
        name="head_grad",
    )(turned, weight, info, logits)


def turn_rows(low, high, cosine, sine):
    return low * cosine - high * sine, high * cosine + low * sine


def reach(block, share, longest):
    back = -(-(longest - 1) // share)
    return max(0, block - back) * share


def seen(first, low, high, place):
    keys = low + lax.broadcasted_iota(jnp.int32, (high - low, first.shape[1]), 0)
    queries = place + lax.broadcasted_iota(jnp.int32, (high - low, first.shape[1]), 1)
    return (keys >= first) & (keys <= queries)


def attend_kernel(base, qkv, cosine, sine, first, attended, kept, log_total):
    seq = pl.program_id(1)
    blocks = base.shape[0]
    length = cosine.shape[1]
    share = length // blocks
    half = HEAD_DIM // 2

    def spot(i):
        return pl.ds(pl.multiple_of(base[i] + seq * share, share), share)

    for i in range(blocks):
        at = pl.ds(i * share, share)
        turns = (cosine[:, at], sine[:, at])
        for c in (0, 1):
            top = c * HEAD_DIM
            low, high = turn_rows(
                qkv[top : top + half, spot(i)], qkv[top + half : top + HEAD_DIM, spot(i)], *turns
            )
            kept[0, top : top + half, at] = low.astype(HALF)
            kept[0, top + half : top + HEAD_DIM, at] = high.astype(HALF)
        kept[0, 2 * HEAD_DIM :, at] = qkv[2 * HEAD_DIM :, spot(i)].astype(HALF)
    key = kept[0, HEAD_DIM : 2 * HEAD_DIM, :].T
    for i in range(blocks):
        low, high = reach(i, share, length // 2), (i + 1) * share
        at = pl.ds(i * share, share)
        scores = jnp.dot(
            key[low:high, :], kept[0, :HEAD_DIM, at], preferred_element_type=FLOAT
        ) * (HEAD_DIM**-0.5)
        scores = jnp.where(seen(first[0, :, at][:1], low, high, i * share), scores, NEG)
        peak = jnp.max(scores, axis=0, keepdims=True)
        expo = jnp.exp(scores - peak)
        summed = jnp.sum(expo, axis=0, keepdims=True)
        probs = (expo * (1.0 / summed)).astype(HALF)
        value = kept[0, 2 * HEAD_DIM :, low:high]
        attended[:, spot(i)] = jnp.dot(value, probs, preferred_element_type=FLOAT).astype(HALF)
        log_total[0, 0, :, at] = jnp.broadcast_to(peak + jnp.log(summed), (8, share))


def attend(base, qkv, cosine, sine, first):
    seqs, length = first.shape[0], first.shape[2]
    heads = qkv.shape[0] // (3 * HEAD_DIM)
    tokens = qkv.shape[1]
    return pl.pallas_call(
        attend_kernel,
        grid=(heads, seqs),
        in_specs=[
            pl.BlockSpec(memory_space=pltpu.SMEM),
            pl.BlockSpec((3 * HEAD_DIM, tokens), lambda h, j: (h, 0)),
            pl.BlockSpec(cosine.shape, lambda h, j: (0, 0)),
            pl.BlockSpec(sine.shape, lambda h, j: (0, 0)),
            pl.BlockSpec((1, 8, length), lambda h, j: (j, 0, 0)),
        ],
        out_specs=[
            pl.BlockSpec((HEAD_DIM, tokens), lambda h, j: (h, 0)),
            pl.BlockSpec((1, 3 * HEAD_DIM, length), lambda h, j: (j, h, 0)),
            pl.BlockSpec((1, 1, 8, length), lambda h, j: (j, h, 0, 0)),
        ],
        out_shape=[
            jax.ShapeDtypeStruct((heads * HEAD_DIM, tokens), HALF),
            jax.ShapeDtypeStruct((seqs, heads * 3 * HEAD_DIM, length), HALF),
            jax.ShapeDtypeStruct((seqs, heads, 8, length), FLOAT),
        ],
        compiler_params=pltpu.CompilerParams(vmem_limit_bytes=VMEM_LIMIT),
        cost_estimate=SMALL,
        name="attend",
    )(base, qkv, cosine, sine, first)


def attend_back_kernel(waits, base, kept, log_total, slope, cosine, sine, first, *refs):
    d_qkv, d_key, d_value = refs[waits:]
    seq = pl.program_id(1)
    blocks = base.shape[0]
    length = cosine.shape[1]
    share = length // blocks
    half = HEAD_DIM // 2
    scale = HEAD_DIM**-0.5

    def spot(i):
        return pl.ds(pl.multiple_of(base[i] + seq * share, share), share)

    def put(part, i, low, high):
        at = pl.ds(i * share, share)
        d_low, d_high = turn_rows(low, high, cosine[:, at], -sine[:, at])
        top = part * HEAD_DIM
        d_qkv[top : top + half, spot(i)] = d_low.astype(HALF)
        d_qkv[top + half : top + HEAD_DIM, spot(i)] = d_high.astype(HALF)

    query = kept[0, :HEAD_DIM, :].T
    key = kept[0, HEAD_DIM : 2 * HEAD_DIM, :].T
    value = kept[0, 2 * HEAD_DIM :, :].T
    d_key[...] = jnp.zeros_like(d_key)
    d_value[...] = jnp.zeros_like(d_value)
    for i in range(blocks):
        low, high = reach(i, share, length // 2), (i + 1) * share
        at = pl.ds(i * share, share)
        turned = slope[:, spot(i)]
        scores = jnp.dot(
            key[low:high, :], kept[0, :HEAD_DIM, at], preferred_element_type=FLOAT
        ) * scale
        scores = jnp.where(seen(first[0, :, at][:1], low, high, i * share), scores, NEG)
        probs = jnp.exp(scores - log_total[0, 0, :1, at])
        d_probs = jnp.dot(value[low:high, :], turned, preferred_element_type=FLOAT)
        centre = jnp.sum(probs * d_probs, axis=0, keepdims=True)
        d_scores = (probs * (d_probs - centre)).astype(HALF)
        d_value[low:high, :] += jnp.dot(probs.astype(HALF), turned.T, preferred_element_type=FLOAT)
        d_key[low:high, :] += jnp.dot(
            d_scores, query[i * share : (i + 1) * share, :], preferred_element_type=FLOAT
        )
        d_query = scale * jnp.dot(
            kept[0, HEAD_DIM : 2 * HEAD_DIM, low:high], d_scores, preferred_element_type=FLOAT
        )
        put(0, i, d_query[:half, :], d_query[half:, :])
    for i in range(blocks):
        rows = pl.ds(i * share, share)
        turned = scale * d_key[rows, :].T
        put(1, i, turned[:half, :], turned[half:, :])
        d_qkv[2 * HEAD_DIM :, spot(i)] = d_value[rows, :].T.astype(HALF)


def attend_back(base, kept, log_total, slope, cosine, sine, first, before):
    seqs, length = first.shape[0], first.shape[2]
    tokens = slope.shape[1]
    heads = slope.shape[0] // HEAD_DIM
    return pl.pallas_call(
        functools.partial(attend_back_kernel, len(before)),
        grid=(heads, seqs),
        in_specs=[
            pl.BlockSpec(memory_space=pltpu.SMEM),
            pl.BlockSpec((1, 3 * HEAD_DIM, length), lambda h, j: (j, h, 0)),
            pl.BlockSpec((1, 1, 8, length), lambda h, j: (j, h, 0, 0)),
            pl.BlockSpec((HEAD_DIM, tokens), lambda h, j: (h, 0)),
            pl.BlockSpec(cosine.shape, lambda h, j: (0, 0)),
            pl.BlockSpec(sine.shape, lambda h, j: (0, 0)),
            pl.BlockSpec((1, 8, length), lambda h, j: (j, 0, 0)),
        ]
        + [pl.BlockSpec(memory_space=pl.ANY)] * len(before),
        out_specs=pl.BlockSpec((3 * HEAD_DIM, tokens), lambda h, j: (h, 0)),
        out_shape=jax.ShapeDtypeStruct((heads * 3 * HEAD_DIM, tokens), HALF),
        scratch_shapes=[pltpu.VMEM((length, HEAD_DIM), FLOAT)] * 2,
        compiler_params=pltpu.CompilerParams(vmem_limit_bytes=VMEM_LIMIT),
        cost_estimate=SMALL,
        name="attend_back",
    )(base, kept, log_total, slope, cosine, sine, first, *before)


def near_and_far(own, rank):
    return (own, rank ^ 1), (own, rank ^ 2)


def remote(source, target, send, recv, n, peer):
    return pltpu.make_async_remote_copy(
        src_ref=source,
        dst_ref=target,
        send_sem=send.at[n],
        recv_sem=recv.at[n],
        device_id=peer,
        device_id_type=MESH,
    )


class Boundary:
    COUNT = 6

    def __init__(self, own, rank, send, recv, parts, rows):
        self.near, self.far = near_and_far(own, rank)
        self.send, self.recv, self.parts = send, recv, parts
        self.rows = [pl.ds(h * rows, rows) for h in range(parts)]
        self.copies = []

    def copy(self, source, target, n, h, peer):
        made = remote(source, target, self.send, self.recv, n * self.parts + h, peer)
        made.start()
        self.copies.append(made)
        return made

    def sums(self, partial, beside, away, come):
        later = {}
        for p in (1, 0):
            for h, at in enumerate(self.rows):
                later[p, h] = self.copy(partial.at[2 + p, at], beside.at[p, at], p, h, self.near)
        crossing = []
        for h, at in enumerate(self.rows):
            later[1, h].wait_recv()
            total = partial[1, at, :].astype(FLOAT) + beside[1, at, :].astype(FLOAT)
            away[at, :] = total.astype(HALF)
            crossing.append(self.copy(away.at[at], come.at[at], 2, h, self.far))
        for h, at in enumerate(self.rows):
            later[0, h].wait_recv()
            total = partial[0, at, :].astype(FLOAT) + beside[0, at, :].astype(FLOAT)
            crossing[h].wait_recv()
            yield h, at, total + come[at, :].astype(FLOAT)

    def give(self, full, h):
        at = self.rows[h]
        self.crossed = getattr(self, "crossed", [])
        self.crossed.append(self.copy(full.at[0, at], full.at[1, at], 3, h, self.far))
        self.beside = getattr(self, "beside", [])
        self.beside.append(self.copy(full.at[0, at], full.at[2, at], 4, h, self.near))

    def pass_on(self, full):
        arrived = []
        for h, at in enumerate(self.rows):
            self.crossed[h].wait_recv()
            arrived.append(self.copy(full.at[1, at], full.at[3, at], 5, h, self.near))
        for copy in self.beside + arrived:
            copy.wait_recv()

    def end(self):
        for copy in self.copies:
            copy.wait_send()


def forward_kernel(parts, waits, partial, stream, gain, *refs):
    out, full, beside, away, come, send, recv = refs[waits:]
    own, rank = lax.axis_index("dp"), lax.axis_index("tensor")
    greet(list(near_and_far(own, rank)))
    edge = Boundary(own, rank, send, recv, parts, stream.shape[0] // parts)
    for h, at, total in edge.sums(partial, beside, away, come):
        total = stream[at, :] + total
        out[at, :] = total
        full[0, at, :] = normed(total, gain[...]).astype(HALF)
        edge.give(full, h)
    edge.pass_on(full)
    edge.end()


def wide_forward_kernel(partial, stream, gain, out, full, beside, away, come, send, recv):
    own, rank = lax.axis_index("dp"), lax.axis_index("tensor")
    near, far = near_and_far(own, rank)
    other = (own ^ 1, rank)
    greet([near, far, other])
    parts = 2
    edge = Boundary(own, rank, send, recv, parts, stream.shape[0] // parts)
    crossed, moved, last = [], [], []
    for h, at, total in edge.sums(partial, beside, away, come):
        total = stream[at, :] + total
        out[at, :] = total
        full[0, 0, at, :] = normed(total, gain[...]).astype(HALF)
        mine = full.at[0, 0, at]
        crossed.append(edge.copy(mine, full.at[0, 1, at], 3, h, far))
        moved.append(edge.copy(mine, full.at[1, 0, at], 4, h, other))
        last.append(edge.copy(mine, full.at[0, 2, at], 5, h, near))
    early, late = edge.rows
    crossed[0].wait_recv()
    one = edge.copy(full.at[0, 1, early], full.at[1, 1, early], 6, 0, other)
    last.append(edge.copy(full.at[0, 1, early], full.at[0, 3, early], 7, 0, near))
    moved[0].wait_recv()
    last.append(edge.copy(full.at[1, 0, early], full.at[1, 2, early], 8, 0, near))
    moved[1].wait_recv()
    two = edge.copy(full.at[1, 0, late], full.at[1, 1, late], 6, 1, far)
    last.append(edge.copy(full.at[1, 0, late], full.at[1, 2, late], 8, 1, near))
    crossed[1].wait_recv()
    last.append(edge.copy(full.at[0, 1, late], full.at[0, 3, late], 7, 1, near))
    one.wait_recv()
    last.append(edge.copy(full.at[1, 1, early], full.at[1, 3, early], 9, 0, near))
    two.wait_recv()
    last.append(edge.copy(full.at[1, 1, late], full.at[1, 3, late], 9, 1, near))
    for copy in last:
        copy.wait_recv()
    edge.end()


def wide_forward(partial, stream, gain):
    rows, depth = stream.shape
    vmem = pl.BlockSpec(memory_space=pltpu.VMEM)
    out, full = pl.pallas_call(
        wide_forward_kernel,
        in_specs=[vmem] * 3,
        out_specs=[vmem] * 2,
        out_shape=[
            jax.ShapeDtypeStruct((rows, depth), FLOAT),
            jax.ShapeDtypeStruct((2, 4, rows, depth), HALF),
        ],
        scratch_shapes=exchange_scratch(rows, depth, 2)[:3] + [pltpu.SemaphoreType.DMA((20,))] * 2,
        compiler_params=pltpu.CompilerParams(
            collective_id=9, has_side_effects=True, vmem_limit_bytes=VMEM_LIMIT
        ),
        cost_estimate=SMALL,
        name="wide_forward",
    )(partial.reshape(4, rows, depth), stream, gain)
    return out, full.reshape(8 * rows, depth)


def wide_backward_kernel(partial, stream, gain, out, g_gain, full, beside, leave, come, send, recv):
    own, rank = lax.axis_index("dp"), lax.axis_index("tensor")
    near, far = near_and_far(own, rank)
    other = (own ^ 1, rank)
    greet([near, far, other])
    parts = 2
    edge = Boundary(own, rank, send, recv, parts, stream.shape[0] // parts)
    early, late = edge.rows
    first = {}
    for n, (y, p) in enumerate(((1, 1), (1, 0), (0, 1), (0, 0))):
        for h, at in enumerate(edge.rows):
            first[y, p, h] = edge.copy(
                partial.at[y, 2 + p, at], beside.at[y, p, at], 5 + n, h, near
            )

    def pair(y, p, h):
        at = edge.rows[h]
        first[y, p, h].wait_recv()
        return partial[y, p, at, :].astype(FLOAT) + beside[y, p, at, :].astype(FLOAT)

    leave[1, 1, early, :] = pair(1, 1, 0).astype(HALF)
    by_other = edge.copy(leave.at[1, 1, early], come.at[1, 1, early], 9, 0, other)
    leave[1, 1, late, :] = pair(1, 1, 1).astype(HALF)
    by_far = edge.copy(leave.at[1, 1, late], come.at[1, 1, late], 9, 1, far)
    leave[1, 0, early, :] = pair(1, 0, 0).astype(HALF)
    other_early = edge.copy(leave.at[1, 0, early], come.at[1, 0, early], 0, 0, other)
    leave[0, 1, late, :] = pair(0, 1, 1).astype(HALF)
    far_late = edge.copy(leave.at[0, 1, late], come.at[0, 1, late], 1, 1, far)
    far_early_sum, other_late_sum = pair(0, 1, 0), pair(1, 0, 1)
    by_other.wait_recv()
    leave[0, 1, early, :] = (far_early_sum + come[1, 1, early, :].astype(FLOAT)).astype(HALF)
    far_early = edge.copy(leave.at[0, 1, early], come.at[0, 1, early], 1, 0, far)
    by_far.wait_recv()
    leave[1, 0, late, :] = (other_late_sum + come[1, 1, late, :].astype(FLOAT)).astype(HALF)
    other_late = edge.copy(leave.at[1, 0, late], come.at[1, 0, late], 0, 1, other)
    g_gain[...] = jnp.zeros_like(g_gain)
    for h, waits in ((0, (other_early, far_early)), (1, (far_late, other_late))):
        at = edge.rows[h]
        total = pair(0, 0, h)
        for copy in waits:
            copy.wait_recv()
        total = total + come[1, 0, at, :].astype(FLOAT) + come[0, 1, at, :].astype(FLOAT)
        slope, by_gain = normed_slope(total, stream[at, :], gain[...])
        g_gain[:1, :] = g_gain[:1, :] + by_gain
        out[at, :] = slope
        full[0, at, :] = slope.astype(HALF)
        edge.crossed = getattr(edge, "crossed", [])
        edge.crossed.append(edge.copy(full.at[0, at], full.at[1, at], 2, h, far))
        edge.beside = getattr(edge, "beside", [])
        edge.beside.append(edge.copy(full.at[0, at], full.at[2, at], 3, h, near))
    arrived = []
    for h, at in enumerate(edge.rows):
        edge.crossed[h].wait_recv()
        arrived.append(edge.copy(full.at[1, at], full.at[3, at], 4, h, near))
    for copy in edge.beside + arrived:
        copy.wait_recv()
    edge.end()


def wide_backward(partial, stream, gain):
    rows, depth = stream.shape
    vmem = pl.BlockSpec(memory_space=pltpu.VMEM)
    out, g_gain, full = pl.pallas_call(
        wide_backward_kernel,
        in_specs=[vmem] * 3,
        out_specs=[vmem] * 3,
        out_shape=[
            jax.ShapeDtypeStruct((rows, depth), FLOAT),
            jax.ShapeDtypeStruct((8, depth), FLOAT),
            jax.ShapeDtypeStruct((4, rows, depth), HALF),
        ],
        scratch_shapes=[pltpu.VMEM((2, 2, rows, depth), HALF)] * 3
        + [pltpu.SemaphoreType.DMA((20,))] * 2,
        compiler_params=pltpu.CompilerParams(
            collective_id=4, has_side_effects=True, vmem_limit_bytes=VMEM_LIMIT
        ),
        cost_estimate=SMALL,
        name="wide_backward",
    )(partial.reshape(2, 4, rows, depth), stream, gain)
    return out, g_gain[:1], full.reshape(4 * rows, depth)


def exchange_scratch(rows, depth, parts):
    return [
        pltpu.VMEM((2, rows, depth), HALF),
        pltpu.VMEM((rows, depth), HALF),
        pltpu.VMEM((rows, depth), HALF),
        pltpu.SemaphoreType.DMA((Boundary.COUNT * parts,)),
        pltpu.SemaphoreType.DMA((Boundary.COUNT * parts,)),
    ]


def forward_boundary(partial, stream, gain, before):
    rows, depth = stream.shape
    parts = 2
    vmem = pl.BlockSpec(memory_space=pltpu.VMEM)
    out, full = pl.pallas_call(
        functools.partial(forward_kernel, parts, len(before)),
        in_specs=[vmem] * 3 + [pl.BlockSpec(memory_space=pl.ANY)] * len(before),
        out_specs=[vmem] * 2,
        out_shape=[
            jax.ShapeDtypeStruct((rows, depth), FLOAT),
            jax.ShapeDtypeStruct((4, rows, depth), HALF),
        ],
        scratch_shapes=exchange_scratch(rows, depth, parts),
        compiler_params=pltpu.CompilerParams(
            collective_id=3, has_side_effects=True, vmem_limit_bytes=VMEM_LIMIT
        ),
        cost_estimate=SMALL,
        name="forward_boundary",
    )(partial.reshape(4, rows, depth), stream, gain, *before)
    return out, full.reshape(4 * rows, depth)


def normed_slope(grad, values, gain):
    root = lax.rsqrt(jnp.mean(values * values, axis=-1, keepdims=True) + EPS)
    unit = values * root
    inner = grad * gain
    middle = jnp.mean(inner * unit, axis=-1, keepdims=True)
    return root * (inner - unit * middle), jnp.sum(grad * unit, axis=0, keepdims=True)


def backward_kernel(parts, partial, stream, gain, prior, out, g_gain, full, beside, away, come, send, recv):
    own, rank = lax.axis_index("dp"), lax.axis_index("tensor")
    greet(list(near_and_far(own, rank)))
    edge = Boundary(own, rank, send, recv, parts, stream.shape[0] // parts)
    g_gain[...] = jnp.zeros_like(g_gain)
    for h, at, total in edge.sums(partial, beside, away, come):
        slope, by_gain = normed_slope(total, stream[at, :], gain[...])
        slope = slope + prior[at, :]
        g_gain[:1, :] = g_gain[:1, :] + by_gain
        out[at, :] = slope
        full[0, at, :] = slope.astype(HALF)
        edge.give(full, h)
    edge.pass_on(full)
    edge.end()


def backward_boundary(partial, stream, gain, prior):
    rows, depth = stream.shape
    parts = 2
    vmem = pl.BlockSpec(memory_space=pltpu.VMEM)
    out, g_gain, full = pl.pallas_call(
        functools.partial(backward_kernel, parts),
        in_specs=[vmem] * 4,
        out_specs=[vmem] * 3,
        out_shape=[
            jax.ShapeDtypeStruct((rows, depth), FLOAT),
            jax.ShapeDtypeStruct((8, depth), FLOAT),
            jax.ShapeDtypeStruct((4, rows, depth), HALF),
        ],
        scratch_shapes=exchange_scratch(rows, depth, parts),
        compiler_params=pltpu.CompilerParams(
            collective_id=5, has_side_effects=True, vmem_limit_bytes=VMEM_LIMIT
        ),
        cost_estimate=SMALL,
        name="backward_boundary",
    )(partial.reshape(4, rows, depth), stream, gain, prior)
    return out, g_gain[:1], full.reshape(4 * rows, depth)


def start_kernel(ids, turned, gain, block, stays, leaves, stream, full, weights, pair, *refs):
    table, corner, rows, out, near, cross, come, send, recv, local = refs
    own, rank = lax.axis_index("dp"), lax.axis_index("tensor")
    beside, across = near_and_far(own, rank)
    far = [(own ^ k, rank) for k in range(1, 8)]
    greet([beside, across] + far)
    width, vocab = turned.shape
    count = rows.shape[0]
    copies, beside_of, across_of, far_of = [], {}, {}, {}

    def begin(source, target, n, peer):
        copy = remote(source, target, send, recv, n, peer)
        copy.start()
        copies.append(copy)
        return copy

    def place(k):
        return pl.ds(pl.multiple_of((own ^ k) * width, width), width)

    weights_of = {}
    for k in (1, 2, 4, 6):
        weights_of[k] = begin(block, weights.at[place(0)], 35 + k, far[k - 1])
    weights[place(0), :] = block[...]
    bit = own % 2
    line = pl.ds(pl.multiple_of(bit * width, width), width)
    aside = begin(leaves, pair.at[line], 43, far[0])
    own_line = pltpu.make_async_copy(stays, pair.at[line], local)
    own_line.start()
    corner[...] = jnp.zeros_like(corner)
    for v in range(0, vocab, LANES):
        some = min(LANES, vocab - v)
        corner[:width, :some] = turned[:, v : v + some].astype(HALF).astype(FLOAT)
        if some < LANES:
            corner[:width, some:] = jnp.zeros((width, LANES - some), FLOAT)
        table[v : v + LANES, :] = corner[...].T
    if vocab % LANES == 0:
        table[vocab:, :] = jnp.zeros((LANES, LANES), FLOAT)

    def fetch(place):
        def body(i, carry):
            for u in range(16):
                r = i * 16 + u
                rows[pl.ds(r, 1), :] = table[pl.ds(ids[place * count + r], 1), :]
            return carry

        lax.fori_loop(0, count // 16, body, 0)

    for p in (3, 2):
        for k in range(8):
            fetch(p * 8 + k)
            out[p, k] = rows[:, :width].astype(HALF)
            beside_of[p - 2, k] = begin(out.at[p, k], near.at[p - 2, k], (p - 2) * 8 + k, beside)
    for k in (2, 4, 6):
        weights_of[k].wait_recv()
        weights_of[k + 1] = begin(weights.at[place(k)], weights.at[place(k)], 36 + k, far[0])
    order = (7, 6, 5, 4, 3, 2, 1, 0)
    for k in order:
        fetch(8 + k)
        beside_of[1, k].wait_recv()
        total = rows[:, :width] + near[1, k].astype(FLOAT)
        out[1, k] = total.astype(HALF)
        across_of[k] = begin(out.at[1, k], cross.at[k], 16 + k, across)
    for k in order:
        fetch(k)
        beside_of[0, k].wait_recv()
        total = rows[:, :width] + near[0, k].astype(FLOAT)
        across_of[k].wait_recv()
        out[0, k] = (total + cross[k].astype(FLOAT)).astype(HALF)
        if k:
            far_of[k] = begin(out.at[0, k], come.at[k], 24 + k, far[k - 1])
    come[0] = out[0, 0]
    for k in order[:-1]:
        far_of[k].wait_recv()
    for b in range(8):
        stream[:, b * width : (b + 1) * width] = come[own ^ b].astype(FLOAT)
    full[0] = normed(stream[...], gain[...]).astype(HALF)
    one = begin(full.at[0], full.at[1], 32, across)
    two = begin(full.at[0], full.at[2], 33, beside)
    one.wait_recv()
    three = begin(full.at[1], full.at[3], 34, beside)
    two.wait_recv()
    three.wait_recv()
    for k in (1, 3, 5, 7):
        weights_of[k].wait_recv()
    aside.wait_recv()
    own_line.wait()
    for copy in copies:
        copy.wait_send()


def start_rows(ids, turned, gain, block, stays, leaves):
    width, vocab = turned.shape
    rows = ids.shape[0] // 32
    padded = (vocab // LANES + 1) * LANES
    vmem = pl.BlockSpec(memory_space=pltpu.VMEM)
    whole = pl.BlockSpec(memory_space=pl.ANY)
    stream, full, weights, pair = pl.pallas_call(
        start_kernel,
        in_specs=[pl.BlockSpec(memory_space=pltpu.SMEM), vmem, vmem, vmem, whole, whole],
        out_specs=[vmem] * 3 + [whole],
        out_shape=[
            jax.ShapeDtypeStruct((rows, 8 * width), FLOAT),
            jax.ShapeDtypeStruct((4, rows, 8 * width), HALF),
            jax.ShapeDtypeStruct((8 * width, block.shape[1]), HALF),
            jax.ShapeDtypeStruct((2 * width, stays.shape[1]), HALF),
        ],
        scratch_shapes=[
            pltpu.VMEM((padded, LANES), FLOAT),
            pltpu.VMEM((LANES, LANES), FLOAT),
            pltpu.VMEM((rows, LANES), FLOAT),
            pltpu.VMEM((4, 8, rows, width), HALF),
            pltpu.VMEM((2, 8, rows, width), HALF),
            pltpu.VMEM((8, rows, width), HALF),
            pltpu.VMEM((8, rows, width), HALF),
            pltpu.SemaphoreType.DMA((44,)),
            pltpu.SemaphoreType.DMA((44,)),
            pltpu.SemaphoreType.DMA,
        ],
        compiler_params=pltpu.CompilerParams(
            collective_id=6, has_side_effects=True, vmem_limit_bytes=VMEM_LIMIT
        ),
        cost_estimate=SMALL,
        name="start_rows",
    )(ids, turned, gain, block, stays, leaves)
    return stream, full.reshape(4 * rows, 8 * width), weights, pair


def end_kernel(parts, waits, partial, stream, gain, prior, gain_one, gain_two, apart, *refs):
    rows, g_gain, arrived, beside, away, come, leave, mine, summed, first, second, send, recv = refs[waits:]
    own, rank = lax.axis_index("dp"), lax.axis_index("tensor")
    near, across = near_and_far(own, rank)
    far = [(own ^ k, rank) for k in range(1, 8)]
    greet([near, across, (own, rank ^ 3)] + far)
    edge = Boundary(own, rank, send, recv, parts, stream.shape[0] // parts)
    aside = remote(apart, arrived, send, recv, Boundary.COUNT * parts, far[0])
    aside.start()
    edge.copies.append(aside)
    width = rows.shape[3]
    gain_zero = jnp.zeros_like(gain[...])
    mine[...] = jnp.zeros_like(mine)
    for h, at, total in edge.sums(partial, beside, away, come):
        slope, by_gain = normed_slope(total, stream[at, :], gain[...])
        slope = slope + prior[at, :]
        gain_zero = gain_zero + by_gain
        for b in range(8):
            leave[b, at, :] = slope[:, b * width : (b + 1) * width].astype(HALF)
    base = Boundary.COUNT * parts
    far_of, last = {}, []

    def begin(source, target, n, peer):
        copy = remote(source, target, send, recv, base + n, peer)
        copy.start()
        edge.copies.append(copy)
        return copy

    order = (7, 6, 5, 4, 3, 2, 1)
    for k in order:
        far_of[k] = begin(leave.at[own ^ k], rows.at[0, k], k, far[k - 1])
    rows[0, 0] = leave[own]
    for b in range(8):
        for n, line in enumerate((gain_zero, gain_one[...], gain_two[...])):
            mine[own ^ b, n : n + 1, :width] = line[:, b * width : (b + 1) * width]
    gains_of = [
        begin(mine, first.at[n - 1], 31 + n, (own, rank ^ n)) for n in (1, 2, 3)
    ]
    crossed = {}
    for k in (0, 1, 2, 3, 4, 5, 6, 7):
        if k:
            far_of[k].wait_recv()
        crossed[k] = begin(rows.at[0, k], rows.at[1, k], 8 + k, across)
        last.append(begin(rows.at[0, k], rows.at[2, k], 16 + k, near))
    for copy in gains_of:
        copy.wait_recv()
    summed[...] = (mine[...] + first[0]) + (first[1] + first[2])
    gains_of = [begin(summed.at[k], second.at[k], 34 + k, far[k - 1]) for k in range(1, 8)]
    for k in (0, 1, 2, 3, 4, 5, 6, 7):
        crossed[k].wait_recv()
        last.append(begin(rows.at[1, k], rows.at[3, k], 24 + k, near))
    for copy in last + gains_of:
        copy.wait_recv()
    second[0] = summed[0]
    pairs = [second[k] + second[k + 1] for k in (0, 2, 4, 6)]
    g_gain[...] = (pairs[0] + pairs[1]) + (pairs[2] + pairs[3])
    aside.wait_recv()
    edge.end()


def end_rows(partial, stream, gain, prior, gain_one, gain_two, apart, width, before):
    rows, depth = stream.shape
    parts = 2
    vmem = pl.BlockSpec(memory_space=pltpu.VMEM)
    semaphores = Boundary.COUNT * parts + 42
    whole = pl.BlockSpec(memory_space=pl.ANY)
    out, g_gain, arrived = pl.pallas_call(
        functools.partial(end_kernel, parts, len(before)),
        in_specs=[vmem] * 6 + [whole] * (1 + len(before)),
        out_specs=[vmem] * 2 + [whole],
        out_shape=[
            jax.ShapeDtypeStruct((4, 8, rows, width), HALF),
            jax.ShapeDtypeStruct((8, LANES), FLOAT),
            jax.ShapeDtypeStruct(apart.shape, HALF),
        ],
        scratch_shapes=exchange_scratch(rows, depth, parts)[:3]
        + [
            pltpu.VMEM((8, rows, width), HALF),
            pltpu.VMEM((8, 8, LANES), FLOAT),
            pltpu.VMEM((8, 8, LANES), FLOAT),
            pltpu.VMEM((3, 8, 8, LANES), FLOAT),
            pltpu.VMEM((8, 8, LANES), FLOAT),
            pltpu.SemaphoreType.DMA((semaphores,)),
            pltpu.SemaphoreType.DMA((semaphores,)),
        ],
        compiler_params=pltpu.CompilerParams(
            collective_id=7, has_side_effects=True, vmem_limit_bytes=VMEM_LIMIT
        ),
        cost_estimate=SMALL,
        name="end_rows",
    )(
        partial.reshape(4, rows, depth), stream, gain, prior, gain_one, gain_two, apart, *before
    )
    return out.reshape(-1, width), g_gain[:3, :width], arrived


def merge_kernel(scan, extra, joined, mine, every, send, recv):
    own, rank = lax.axis_index("dp"), lax.axis_index("tensor")
    turns = [(a, b) for a in (0, 1) for b in range(4)][1:]
    peers = [(own ^ a, rank ^ b) for a, b in turns]
    greet(peers)
    tokens = scan.shape[1] // 2
    share = tokens // 4
    mine[...] = jnp.zeros_like(mine)
    mine[0:3, :] = scan[0:3, :tokens]
    mine[3:6, :] = scan[0:3, tokens:]
    copies = []
    for n, peer in enumerate(peers):
        copies.append(remote(mine, every.at[n], send, recv, n, peer))
        copies[-1].start()
    joined[...] = jnp.zeros_like(joined)
    joined[2:4, :] = extra[:2, :]
    for copy in copies:
        copy.wait()
    for y in (0, 1):
        for p in range(4):
            terms = {(0, 0): mine[3 * y : 3 * y + 3, p * share : (p + 1) * share]}
            for n, (a, b) in enumerate(turns):
                q = TURN.index(TURN[p] ^ b)
                terms[a, b] = every[n, 3 * (y ^ a) : 3 * (y ^ a) + 3, q * share : (q + 1) * share]
            peak = functools.reduce(jnp.maximum, [term[0:1] for term in terms.values()])
            sums, hits = [], []
            for a in (0, 1):
                for b in (0, 2):
                    pair = (terms[a, b], terms[a, b ^ 1])
                    sums.append(sum(term[1:2] * jnp.exp(term[0:1] - peak) for term in pair))
                    hits.append(pair[0][2:3] + pair[1][2:3])
            at = pl.ds(y * tokens + p * share, share)
            joined[0:1, at] = peak + jnp.log((sums[0] + sums[1]) + (sums[2] + sums[3]))
            joined[1:2, at] = (hits[0] + hits[1]) + (hits[2] + hits[3])


def merge_scans(scan, extra):
    vmem = pl.BlockSpec(memory_space=pltpu.VMEM)
    shape = (8, scan.shape[1] // 2)
    return pl.pallas_call(
        merge_kernel,
        in_specs=[vmem] * 2,
        out_specs=vmem,
        out_shape=jax.ShapeDtypeStruct(scan.shape, FLOAT),
        scratch_shapes=[
            pltpu.VMEM(shape, FLOAT),
            pltpu.VMEM((7, *shape), FLOAT),
            pltpu.SemaphoreType.DMA((7,)),
            pltpu.SemaphoreType.DMA((7,)),
        ],
        compiler_params=pltpu.CompilerParams(collective_id=8, has_side_effects=True),
        name="merge_scans",
    )(scan, extra)


def across(left, right):
    return lax.dot_general(left, right, (((1,), (1,)), ((), ())), preferred_element_type=FLOAT)


def feed_kernel(norm, weight, out):
    ffn = weight.shape[1] // 3
    both = jnp.dot(norm[...], weight[:, : 2 * ffn], preferred_element_type=FLOAT)
    gate, up = both[:, :ffn], both[:, ffn:]
    hidden = (gate * (1.0 / (1.0 + jnp.exp(-gate))) * up).astype(HALF)
    out[...] = across(hidden, weight[:, 2 * ffn :]).astype(HALF)


def feed(norm, weight):
    tokens, depth = norm.shape
    rows = 512
    return pl.pallas_call(
        feed_kernel,
        grid=(tokens // rows,),
        in_specs=[
            pl.BlockSpec((rows, depth), lambda i: (i, 0)),
            pl.BlockSpec(weight.shape, lambda i: (0, 0), pipeline_mode=pl.Buffered(1)),
        ],
        out_specs=pl.BlockSpec((rows, depth), lambda i: (i, 0)),
        out_shape=jax.ShapeDtypeStruct((tokens, depth), HALF),
        compiler_params=pltpu.CompilerParams(vmem_limit_bytes=VMEM_LIMIT),
        cost_estimate=SMALL,
        name="feed",
    )(norm, weight)


def feed_back_kernel(norm, slope, weight, out, grad, total):
    step = pl.program_id(0)
    ffn = weight.shape[1] // 3

    @pl.when(step == 0)
    def _():
        total[...] = jnp.zeros_like(total)

    both = jnp.dot(norm[...], weight[:, : 2 * ffn], preferred_element_type=FLOAT)
    d_hidden = jnp.dot(slope[...], weight[:, 2 * ffn :], preferred_element_type=FLOAT)
    gate, up = both[:, :ffn], both[:, ffn:]
    open_part = 1.0 / (1.0 + jnp.exp(-gate))
    passed = gate * open_part
    hidden = (passed * up).astype(HALF)
    d_up = (d_hidden * passed).astype(HALF)
    d_gate = (d_hidden * up * (open_part * (1.0 + gate * (1.0 - open_part)))).astype(HALF)
    by_norm = across(d_gate, weight[:, :ffn]) + across(d_up, weight[:, ffn : 2 * ffn])
    out[...] = by_norm.astype(HALF)
    turned = norm[...].T
    total[:, :ffn] += jnp.dot(turned, d_gate, preferred_element_type=FLOAT)
    total[:, ffn : 2 * ffn] += jnp.dot(turned, d_up, preferred_element_type=FLOAT)
    total[:, 2 * ffn :] += jnp.dot(slope[...].T, hidden, preferred_element_type=FLOAT)

    @pl.when(step == pl.num_programs(0) - 1)
    def _():
        grad[...] = total[...].astype(HALF)


def feed_back(norm, slope, weight):
    tokens, depth = norm.shape
    rows = 512
    return pl.pallas_call(
        feed_back_kernel,
        grid=(tokens // rows,),
        in_specs=[
            pl.BlockSpec((rows, depth), lambda i: (i, 0)),
            pl.BlockSpec((rows, depth), lambda i: (i, 0)),
            pl.BlockSpec(weight.shape, lambda i: (0, 0), pipeline_mode=pl.Buffered(1)),
        ],
        out_specs=[
            pl.BlockSpec((rows, depth), lambda i: (i, 0)),
            pl.BlockSpec(weight.shape, lambda i: (0, 0), pipeline_mode=pl.Buffered(1)),
        ],
        out_shape=[
            jax.ShapeDtypeStruct((tokens, depth), HALF),
            jax.ShapeDtypeStruct(weight.shape, HALF),
        ],
        scratch_shapes=[pltpu.VMEM(weight.shape, FLOAT)],
        compiler_params=pltpu.CompilerParams(vmem_limit_bytes=VMEM_LIMIT),
        cost_estimate=SMALL,
        name="feed_back",
    )(norm, slope, weight)


def product(left, right, over_left, over_right):
    return lax.dot_general(
        left, right, (((over_left,), (over_right,)), ((), ())), preferred_element_type=FLOAT
    )


def adam(weight, grad, first, second, rate, decay):
    first = BETA_ONE * first + (1.0 - BETA_ONE) * grad
    second = BETA_TWO * second + (1.0 - BETA_TWO) * grad * grad
    first_hat = first / (1.0 - BETA_ONE**STEP)
    second_hat = second / (1.0 - BETA_TWO**STEP)
    weight = weight - rate * (first_hat / (jnp.sqrt(second_hat) + ADAM_EPS) + decay * weight)
    return (weight, first, second, weight.astype(HALF))


def update_kernel(counts, factor, *refs):
    arrays = len(counts)
    inputs, outputs = refs[: 3 * arrays + sum(counts)], refs[3 * arrays + sum(counts) :]
    grads = inputs[3 * arrays :]
    for n in range(arrays):
        weight, first, second = inputs[3 * n : 3 * n + 3]
        low = 0
        for grad in grads[: counts[n]]:
            high = low + grad.shape[-1]
            at = (Ellipsis, slice(low, high))
            results = adam(
                weight[at], grad[...].astype(FLOAT) * factor[0], first[at], second[at], LR, DECAY
            )
            for out, result in zip(outputs[4 * n : 4 * n + 4], results):
                out[at] = result
            low = high
        grads = grads[counts[n] :]


def update(arrays, factor):
    rows = arrays[0][0].shape[0]
    steps = rows // 16 if rows % 16 == 0 else 1

    def block(array):
        zeros = (0,) * (array.ndim - 1)
        return pl.BlockSpec((array.shape[0] // steps, *array.shape[1:]), lambda i: (i, *zeros))

    inputs = [array for entry in arrays for array in entry[:3]]
    grads = [grad for entry in arrays for grad in entry[3]]
    outs = [
        jax.ShapeDtypeStruct(entry[0].shape, kind)
        for entry in arrays
        for kind in (FLOAT, FLOAT, FLOAT, HALF)
    ]
    results = pl.pallas_call(
        functools.partial(update_kernel, tuple(len(entry[3]) for entry in arrays)),
        grid=(steps,),
        in_specs=[pl.BlockSpec(memory_space=pltpu.SMEM)] + [block(a) for a in inputs + grads],
        out_specs=[block(a) for a in outs],
        out_shape=outs,
        compiler_params=pltpu.CompilerParams(vmem_limit_bytes=VMEM_LIMIT),
        cost_estimate=SMALL,
        name="update",
    )(factor.reshape(1), *inputs, *grads)
    return [results[4 * n : 4 * n + 4] for n in range(len(arrays))]


def shards(
    token_ids,
    targets,
    segments,
    completion,
    micro_order,
    *state,
):
    weights, means, squares_in = state[:7], state[7:14], state[14:21]
    embedding, attn_in, attn_out, ffn_in, ffn_out, head_table, norm_gains = weights
    group = lax.axis_size("dp")
    parts = lax.axis_size("tensor")
    own, rank = lax.axis_index("dp"), lax.axis_index("tensor")
    vocab, width = embedding.shape
    start = rank * vocab
    seqs, length = token_ids.shape
    micro = micro_order.shape[1]
    share = length // parts
    turn = jnp.array(TURN, jnp.int32)
    dp_order = own ^ jnp.arange(group, dtype=jnp.int32)
    tensor_order = rank ^ turn
    tensor_order_natural = rank ^ jnp.arange(parts, dtype=jnp.int32)
    ffn = ffn_out.shape[0]
    qkv_width = attn_in.shape[1]

    attn_block = jnp.concatenate([attn_in, attn_out.T], axis=1).astype(HALF)
    ffn_block = jnp.concatenate([ffn_in.reshape(width, -1), ffn_out.T], axis=1).astype(HALF)
    bit = own % 2
    entries = vocab // 2
    low_half, high_half = head_table[:, :entries].astype(HALF), head_table[:, entries:].astype(HALF)
    stays = jnp.where(bit == 0, low_half, high_half)
    leaves = jnp.where(bit == 0, high_half, low_half)
    lines = [[i for i in range(group) if i % 2 == odd] for odd in (0, 1)]

    flags = completion.astype(FLOAT)
    picked_rows = micro_order[0]
    local_counts = jnp.sum(completion, axis=1)[picked_rows]
    id_rows = seqs * length // LANES
    packed = jnp.concatenate(
        [
            token_ids.reshape(-1),
            targets.reshape(-1),
            completion.reshape(-1),
            jnp.pad(jnp.concatenate([local_counts, picked_rows]), (0, 8 * LANES - 2 * micro)),
        ]
    ).reshape(3 * id_rows + 8, LANES)
    gains = jnp.pad(norm_gains.astype(HALF).astype(FLOAT), ((0, 5), (0, LANES - width)))
    if group == 8:
        packed, every_id, gains = spread(packed, gains, seqs, length, vocab, width)
        every_id = every_id.reshape(-1)
    else:
        packed, gains = lax.all_gather(packed, "dp"), lax.all_gather(gains, "dp")
        packed = jnp.take(packed, dp_order, axis=0)
        every_id = packed[:, :id_rows].reshape(group, seqs, parts, share)
        every_id = jnp.take(every_id, tensor_order, axis=2)
        every_id = every_id.transpose(2, 0, 1, 3).reshape(-1) - start
        every_id = jnp.where((every_id >= 0) & (every_id < vocab), every_id, vocab)
        gains = gains.transpose(1, 0, 2)[:, :, :width].reshape(8, -1)
    packed, leaves = lax.optimization_barrier((packed, leaves))
    gains = gains[:3]
    numbers = packed[:, 3 * id_rows, : 2 * micro]
    counts = jnp.sum(numbers[:, :micro].astype(FLOAT), axis=0)

    def both_order(values):
        values = jnp.take(values.reshape(seqs, parts, share), tensor_order, axis=1)
        return values.transpose(1, 0, 2).reshape(-1)

    own_segment = segments[:, :, None] == jnp.arange(8, dtype=jnp.int32)
    sizes = jnp.sum(own_segment.astype(jnp.int32), axis=1)
    begins = jnp.cumsum(sizes, axis=1) - sizes
    first = jnp.sum(jnp.where(own_segment, begins[:, None, :], 0), axis=2)
    first = jnp.broadcast_to(first[:, None, :], (seqs, 8, length))
    base = turn[tensor_order_natural] * (seqs * share)
    cosine, sine = tables(length, HEAD_DIM)

    if group == 8:
        stream0, attn_norm, attn_w, head_rows = start_rows(
            every_id, embedding.T, gains[:1], attn_block, stays, leaves
        )
    else:
        rows = lookup(embedding.T, every_id).reshape(parts, group, seqs * share, width)
        rows = rows[:2] + swap(rows[2:], "tensor", 1)
        rows = rows[0] + swap(rows[1], "tensor", 2)
        rows = lax.all_to_all(jnp.take(rows, dp_order, axis=0), "dp", 0, 0)
        stream0 = rows.transpose(1, 0, 2).reshape(seqs * share, -1).astype(FLOAT)
        attn_norm = tensor_gather(normed(stream0, gains[0]).astype(HALF))

        attn_w = lax.all_gather(attn_block, "dp", axis=0, tiled=True)
        came = swap(leaves, "dp", 1)
        head_rows = jnp.concatenate(
            [jnp.where(bit == 0, stays, came), jnp.where(bit == 0, came, stays)], axis=0
        )
    attn_norm, ffn_block = lax.optimization_barrier((attn_norm, ffn_block))
    ffn_parts = gather_first(ffn_block)
    head_b = lax.all_gather(head_rows, "dp", axis=0, tiled=True, axis_index_groups=lines)
    attn_in_b, attn_out_b = attn_w[:, :qkv_width], attn_w[:, qkv_width:]
    qkv = product(attn_in_b, attn_norm, 0, 1)
    attended, kept, log_sums = attend(base, qkv, cosine, sine, first)
    attended, ffn_block = lax.optimization_barrier((attended, ffn_block))
    ffn_parts = gather_middle(ffn_block, ffn_parts)
    stream1, ffn_norm = forward_boundary(
        product(attended, attn_out_b, 0, 1).astype(HALF), stream0, gains[1:2], [ffn_parts]
    )
    ffn_w = gather_last(ffn_parts)
    stream2, final_norm = wide_forward(feed(ffn_norm, ffn_w), stream1, gains[2:])

    final_norm, packed = lax.optimization_barrier((final_norm, packed))
    rows_extra = []
    for k in (0, 1):
        its_flags = packed[k, 2 * id_rows : 3 * id_rows].reshape(seqs, length).astype(FLOAT)
        its_order = numbers[k, micro:]
        slot = jnp.argmax(its_order[None, :] == jnp.arange(seqs)[:, None], axis=1)
        its_scale = its_flags * (1.0 / jnp.maximum(counts, 1.0))[slot][:, None]
        aims = packed[k, id_rows : 2 * id_rows].reshape(seqs, length) - start - bit * entries
        aims = jnp.where((aims >= 0) & (aims < entries), aims, -1).astype(FLOAT)
        rows_extra.append(jnp.stack([both_order(its_scale), both_order(aims)]))
    extra = jnp.pad(jnp.concatenate(rows_extra, axis=1), ((0, 6), (0, 0)))
    joint_flags = both_order(flags)
    logits, scan, final_turned = head_scan(final_norm, head_b, extra)
    info = merge_scans(scan, extra)
    tokens = seqs * length
    seq_loss = jnp.sum(
        ((info[0, :tokens] - info[1, :tokens]) * joint_flags).reshape(parts, seqs, share),
        axis=(0, 2),
    )
    g_head, d_final = head_grad(final_turned, head_b, info, logits)
    g_head = lax.psum_scatter(
        g_head, "dp", scatter_dimension=0, tiled=True, axis_index_groups=lines
    )
    g_stays = jnp.where(bit == 0, g_head[:width], g_head[width:])
    g_leaves = jnp.where(bit == 0, g_head[width:], g_head[:width])

    d_stream2, g_gain2, d_branch2 = wide_backward(d_final, stream2, gains[2:])
    d_norm, g_ffn = feed_back(ffn_norm, d_branch2, ffn_w)
    g_ffn_parts = scatter_first(g_ffn)
    d_stream1, g_gain1, d_branch1 = backward_boundary(d_norm, stream1, gains[1:2], d_stream2)
    d_attended = product(attn_out_b, d_branch1, 0, 1).astype(HALF)
    g_ffn, g_ffn_leaves = scatter_middle(g_ffn, g_ffn_parts)
    d_qkv = attend_back(base, kept, log_sums, d_attended, cosine, sine, first, g_ffn_leaves)
    g_attn_in = product(attn_norm, d_qkv, 0, 1).astype(HALF)
    g_attn_out = product(d_branch1, attended, 0, 1).astype(HALF)
    g_attn = jnp.concatenate([g_attn_in, g_attn_out], axis=1)
    g_attn_parts = scatter_first(g_attn)
    d_norm = product(d_qkv, attn_in_b, 0, 1).astype(HALF)
    if group == 8:
        rows, g_gains, g_came = end_rows(
            d_norm, stream0, gains[:1], d_stream1, g_gain1, g_gain2, g_leaves, width, []
        )
    else:
        d_part, g_gain0 = normed_slope(tensor_scatter(d_norm.astype(FLOAT)), stream0, gains[:1])
        rows = (d_stream1 + d_part).astype(HALF)
        rows = rows.reshape(seqs * share, group, width).transpose(1, 0, 2)
        rows = jnp.take(lax.all_to_all(rows, "dp", 0, 0), dp_order, axis=0)
        rows = tensor_gather(rows[None]).reshape(-1, width)
        g_came = swap(g_leaves, "dp", 1)
        gain_sum = jnp.concatenate([g_gain0, g_gain1, g_gain2]).reshape(3, group, width)
        g_gains = jnp.take(lax.psum(gain_sum, ("dp", "tensor")), own, axis=1)
    g_head = [jnp.where(bit == 0, g_stays, g_came), jnp.where(bit == 0, g_came, g_stays)]
    rows, g_ffn, g_attn = lax.optimization_barrier((rows, g_ffn, g_attn))
    g_ffn = scatter_last(g_ffn, g_ffn_leaves)
    g_attn, g_attn_leaves = scatter_middle(g_attn, g_attn_parts)
    g_embed, squares = collect(rows, every_id, vocab, [g_ffn, *g_attn_leaves])
    squares, g_attn = lax.optimization_barrier((squares, g_attn))
    g_attn = scatter_last(g_attn, g_attn_leaves)

    owner = (rank == 0).astype(FLOAT)
    squared = jnp.sum(squares) + owner * jnp.sum(g_gains * g_gains)
    for part in (g_attn, g_ffn, *g_head):
        squared = squared + jnp.sum(part.astype(FLOAT) ** 2)
    losses = seq_loss[picked_rows] * owner
    if group == 8:
        sums = jnp.pad(jnp.concatenate([squared[None], losses]), (0, 8 * LANES - 1 - micro))
        sums = total_over_devices(jnp.broadcast_to(sums.reshape(1, 8, LANES), (8, 8, LANES)))
        squared, loss_sums = sums[0, 0], sums[0, 1 : 1 + micro]
    else:
        squared, loss_sums = lax.psum((squared, losses), ("dp", "tensor"))
    grad_norm = jnp.sqrt(squared)
    factor = CLIP / jnp.maximum(grad_norm, CLIP)
    g_parts = (
        [g_embed],
        [g_attn[:, :qkv_width]],
        [g_attn[:, qkv_width:].T],
        [g_ffn[:, : 2 * ffn].reshape(ffn_in.shape)],
        [g_ffn[:, 2 * ffn :]],
        g_head,
    )
    arrays = []
    for place in range(6):
        entry = (weights[place], means[place], squares_in[place])
        if place in (0, 4):
            entry = tuple(array.T for array in entry)
        arrays.append((*entry, g_parts[place]))
    updated = []
    for place, results in enumerate(update(arrays, factor)):
        updated.extend(result.T if place in (0, 4) else result for result in results)
    updated.extend(adam(norm_gains, g_gains * factor, means[6], squares_in[6], LR_GAIN, 0.0))
    return (jnp.stack([loss_sums, counts]), grad_norm, *updated)


def solution(mesh):
    in_specs = (
        P("dp", None),
        P("dp", None),
        P("dp", None),
        P("dp", None),
        P("dp", None),
        P("tensor", "dp"),
        P("dp", "tensor"),
        P("tensor", "dp"),
        P("dp", None, "tensor"),
        P("tensor", "dp"),
        P("dp", "tensor"),
        P(None, "dp"),
        P("tensor", "dp"),
        P("dp", "tensor"),
        P("tensor", "dp"),
        P("dp", None, "tensor"),
        P("tensor", "dp"),
        P("dp", "tensor"),
        P(None, "dp"),
        P("tensor", "dp"),
        P("dp", "tensor"),
        P("tensor", "dp"),
        P("dp", None, "tensor"),
        P("tensor", "dp"),
        P("dp", "tensor"),
        P(None, "dp"),
    )
    out_specs = (
        P(),
        P(),
        P("tensor", "dp"),
        P("tensor", "dp"),
        P("tensor", "dp"),
        P("tensor", "dp"),
        P("dp", "tensor"),
        P("dp", "tensor"),
        P("dp", "tensor"),
        P("dp", "tensor"),
        P("tensor", "dp"),
        P("tensor", "dp"),
        P("tensor", "dp"),
        P("tensor", "dp"),
        P("dp", None, "tensor"),
        P("dp", None, "tensor"),
        P("dp", None, "tensor"),
        P("dp", None, "tensor"),
        P("tensor", "dp"),
        P("tensor", "dp"),
        P("tensor", "dp"),
        P("tensor", "dp"),
        P("dp", "tensor"),
        P("dp", "tensor"),
        P("dp", "tensor"),
        P("dp", "tensor"),
        P(None, "dp"),
        P(None, "dp"),
        P(None, "dp"),
        P(None, "dp"),
    )
    return jax.shard_map(shards, mesh=mesh, in_specs=in_specs, out_specs=out_specs, check_vma=False)
```

```python
import functools

import jax
import jax.numpy as jnp
import numpy as np
from jax import lax
from jax.experimental import pallas as pl
from jax.experimental.pallas import tpu as pltpu
from jax.sharding import PartitionSpec as P

HEAD_DIM = 64
STEP = 10


EPS = 1e-05
CLIP = 0.01
LR = 0.03
LR_GAIN = 0.5
BETA_ONE = 0.9
BETA_TWO = 0.95
ADAM_EPS = 1e-08
DECAY = 0.1
NEG = -1e30
FLOAT = jnp.float32
HALF = jnp.bfloat16
LANES = 128
ROWS = 1024
VMEM_LIMIT = 56 * 2**20
TILE = 512
CHUNK = 256
MESH = pl.DeviceIdType.MESH
SMALL = pl.CostEstimate(flops=2**20, bytes_accessed=2**20, transcendentals=0)

TURN = (0, 2, 1, 3)


def swap(value, axis, bit):
    pairs = [(i, i ^ bit) for i in range(lax.axis_size(axis))]
    return lax.ppermute(value, axis, pairs)


def normed(values, gain):
    return values * lax.rsqrt(jnp.mean(values * values, axis=-1, keepdims=True) + EPS) * gain


def tables(length, width):
    inverse = np.float32(10000.0) ** (-np.arange(0, width, 2, dtype=np.float32) / np.float32(width))
    angle = inverse[:, None] * np.arange(length, dtype=np.float32)[None, :]
    return jnp.asarray(np.cos(angle)), jnp.asarray(np.sin(angle))


def gather_first(block):
    if lax.axis_size("dp") != 8:
        return []
    return [swap(block, "dp", k) for k in (2, 4, 6)]


def gather_middle(block, parts):
    return jnp.concatenate([block, *parts], axis=0)


def gather_last(parts):
    group = lax.axis_size("dp")
    if group != 8:
        return lax.all_gather(parts, "dp", axis=0, tiled=True)
    there = swap(parts, "dp", 1)
    rows = parts.shape[0] // 4
    own = lax.axis_index("dp")
    full = jnp.zeros((group * rows, parts.shape[1]), parts.dtype)
    for n in range(group // 2):
        at = slice(n * rows, (n + 1) * rows)
        full = lax.dynamic_update_slice(full, parts[at], ((own ^ (2 * n)) * rows, 0))
        full = lax.dynamic_update_slice(full, there[at], ((own ^ (2 * n + 1)) * rows, 0))
    return full


def block_of(full, k):
    rows = full.shape[0] // lax.axis_size("dp")
    own = lax.axis_index("dp")
    return lax.dynamic_slice(full, ((own ^ k) * rows, 0), (rows, full.shape[1]))


def scatter_first(full):
    if lax.axis_size("dp") != 8:
        return []
    leaves = jnp.concatenate([block_of(full, k + 1) for k in (0, 2, 4, 6)], axis=0)
    return [swap(leaves, "dp", 1)]


def scatter_middle(full, parts):
    if lax.axis_size("dp") != 8:
        return full, []
    rows = full.shape[0] // 8
    sums = [
        block_of(full, 2 * n).astype(FLOAT) + parts[0][n * rows : (n + 1) * rows].astype(FLOAT)
        for n in range(4)
    ]
    return sums[0], [total.astype(HALF) for total in sums[1:]]


def scatter_last(total, leaves):
    if lax.axis_size("dp") != 8:
        return lax.psum_scatter(total.astype(FLOAT), "dp", scatter_dimension=0, tiled=True)
    for n, leave in enumerate(leaves):
        total = total + swap(leave, "dp", 2 * n + 2).astype(FLOAT)
    return total


def peers_of(own, rank, bits, axis):
    if axis == "dp":
        return [(own ^ k, rank) for k in bits]
    return [(own, rank ^ k) for k in bits]


def greet(peers):
    barrier = pltpu.get_barrier_semaphore()
    for peer in peers:
        pl.semaphore_signal(barrier, inc=1, device_id=peer, device_id_type=MESH)
    pl.semaphore_wait(barrier, len(peers))


def spread_kernel(vocab, seqs, numbers, gains, every, ids, all_gains, every_gain, send, recv):
    own, rank = lax.axis_index("dp"), lax.axis_index("tensor")
    peers = peers_of(own, rank, range(1, 8), "dp")
    greet(peers)
    every[0] = numbers[...]
    every_gain[0] = gains[...]
    copies = []
    for k in range(1, 8):
        for n, (source, target) in enumerate(((numbers, every), (gains, every_gain))):
            copies.append(
                pltpu.make_async_remote_copy(
                    src_ref=source,
                    dst_ref=target.at[k],
                    send_sem=send.at[n, k],
                    recv_sem=recv.at[n, k],
                    device_id=peers[k - 1],
                    device_id_type=MESH,
                )
            )
            copies[-1].start()
    for copy in copies:
        copy.wait()
    lines = ids.shape[0] // (32 * seqs)
    for p in range(4):
        shard = rank ^ TURN[p]
        for k in range(8):
            for j in range(seqs):
                local = every[k, pl.ds((j * 4 + shard) * lines, lines), :] - rank * vocab
                local = jnp.where((local >= 0) & (local < vocab), local, vocab)
                ids[pl.ds(((p * 8 + k) * seqs + j) * lines, lines), :] = local
    width = all_gains.shape[1] // 8
    for b in range(8):
        all_gains[:, b * width : (b + 1) * width] = every_gain[own ^ b][:, :width]


def spread(numbers, gains, seqs, length, vocab, width):
    vmem = pl.BlockSpec(memory_space=pltpu.VMEM)
    return pl.pallas_call(
        functools.partial(spread_kernel, vocab, seqs),
        in_specs=[vmem] * 2,
        out_specs=[vmem] * 3,
        out_shape=[
            jax.ShapeDtypeStruct((8, *numbers.shape), numbers.dtype),
            jax.ShapeDtypeStruct((8 * seqs * length // LANES, LANES), jnp.int32),
            jax.ShapeDtypeStruct((8, 8 * width), FLOAT),
        ],
        scratch_shapes=[
            pltpu.VMEM((8, *gains.shape), FLOAT),
            pltpu.SemaphoreType.DMA((2, 8)),
            pltpu.SemaphoreType.DMA((2, 8)),
        ],
        compiler_params=pltpu.CompilerParams(collective_id=1, has_side_effects=True),
        cost_estimate=SMALL,
        name="spread",
    )(numbers, gains)


def total_kernel(blocks, out, first, summed, second, send, recv):
    own, rank = lax.axis_index("dp"), lax.axis_index("tensor")
    near = peers_of(own, rank, range(1, 4), "tensor")
    far = peers_of(own, rank, range(1, 8), "dp")
    greet(near + far)
    copies = []
    for k in range(1, 4):
        copy = pltpu.make_async_remote_copy(
            src_ref=blocks,
            dst_ref=first.at[k - 1],
            send_sem=send.at[k - 1],
            recv_sem=recv.at[k - 1],
            device_id=near[k - 1],
            device_id_type=MESH,
        )
        copy.start()
        copies.append(copy)
    for copy in copies:
        copy.wait()
    summed[...] = (blocks[...] + first[0]) + (first[1] + first[2])
    copies = []
    for k in range(1, 8):
        copy = pltpu.make_async_remote_copy(
            src_ref=summed.at[k],
            dst_ref=second.at[k],
            send_sem=send.at[2 + k],
            recv_sem=recv.at[2 + k],
            device_id=far[k - 1],
            device_id_type=MESH,
        )
        copy.start()
        copies.append(copy)
    for copy in copies:
        copy.wait()
    second[0] = summed[0]
    pairs = [second[k] + second[k + 1] for k in (0, 2, 4, 6)]
    out[...] = (pairs[0] + pairs[1]) + (pairs[2] + pairs[3])


def total_over_devices(blocks):
    shape = blocks.shape
    return pl.pallas_call(
        total_kernel,
        in_specs=[pl.BlockSpec(memory_space=pltpu.VMEM)],
        out_specs=pl.BlockSpec(memory_space=pltpu.VMEM),
        out_shape=jax.ShapeDtypeStruct(shape[1:], FLOAT),
        scratch_shapes=[
            pltpu.VMEM((3, *shape), FLOAT),
            pltpu.VMEM(shape, FLOAT),
            pltpu.VMEM(shape, FLOAT),
            pltpu.SemaphoreType.DMA((10,)),
            pltpu.SemaphoreType.DMA((10,)),
        ],
        compiler_params=pltpu.CompilerParams(collective_id=2, has_side_effects=True),
        name="total",
    )(blocks)


def tensor_gather(block):
    half = jnp.concatenate([block, swap(block, "tensor", 2)], axis=0)
    return jnp.concatenate([half, swap(half, "tensor", 1)], axis=0)


def tensor_scatter(full):
    half = full.shape[0] // 2
    quarter = half // 2
    both = full[:half] + swap(full[half:], "tensor", 1)
    there = swap(both[quarter:].astype(HALF), "tensor", 2)
    return both[:quarter] + there.astype(FLOAT)


def lookup_kernel(ids, turned, out, table, corner, rows):
    count = rows.shape[0]
    width, vocab = turned.shape

    @pl.when(pl.program_id(0) == 0)
    def _():
        corner[...] = jnp.zeros_like(corner)
        for v in range(0, vocab, LANES):
            some = min(LANES, vocab - v)
            corner[:width, :some] = turned[:, v : v + some].astype(HALF).astype(FLOAT)
            if some < LANES:
                corner[:width, some:] = jnp.zeros((width, LANES - some), FLOAT)
            table[v : v + LANES, :] = corner[...].T
        if vocab % LANES == 0:
            table[vocab:, :] = jnp.zeros((LANES, LANES), FLOAT)

    def body(i, carry):
        for u in range(16):
            r = i * 16 + u
            rows[pl.ds(r, 1), :] = table[pl.ds(ids[0, 0, r], 1), :]
        return carry

    lax.fori_loop(0, count // 16, body, 0)
    out[...] = rows[:, : out.shape[1]].astype(HALF)


def lookup(turned, ids):
    count = ids.shape[0]
    width, vocab = turned.shape
    padded = (vocab // LANES + 1) * LANES
    return pl.pallas_call(
        lookup_kernel,
        grid=(count // ROWS,),
        in_specs=[
            pl.BlockSpec((1, 1, ROWS), lambda i: (i, 0, 0), memory_space=pltpu.SMEM),
            pl.BlockSpec(turned.shape, lambda i: (0, 0), pipeline_mode=pl.Buffered(1)),
        ],
        out_specs=pl.BlockSpec((ROWS, width), lambda i: (i, 0)),
        out_shape=jax.ShapeDtypeStruct((count, width), HALF),
        scratch_shapes=[
            pltpu.VMEM((padded, LANES), FLOAT),
            pltpu.VMEM((LANES, LANES), FLOAT),
            pltpu.VMEM((ROWS, LANES), FLOAT),
        ],
        compiler_params=pltpu.CompilerParams(vmem_limit_bytes=VMEM_LIMIT),
        cost_estimate=SMALL,
        name="lookup",
    )(ids.reshape(count // ROWS, 1, ROWS), turned)


def collect_kernel(waits, ids, grads, *refs):
    out, squares, rows, *sums = refs[waits:]
    step = pl.program_id(0)
    count = rows.shape[0]
    width, vocab = out.shape

    @pl.when(step == 0)
    def _():
        rows[...] = jnp.zeros_like(rows)
        for total in sums:
            total[...] = jnp.zeros_like(total)

    rows[:, :width] = grads[...].astype(FLOAT)

    def body(i, carry):
        for u in range(16):
            r = i * 16 + u
            total = sums[u % len(sums)]
            place = pl.ds(ids[0, 0, r], 1)
            total[place, :] = total[place, :] + rows[pl.ds(r, 1), :]
        return carry

    lax.fori_loop(0, count // 16, body, 0)

    @pl.when(step == pl.num_programs(0) - 1)
    def _():
        squared = jnp.zeros((8, LANES), FLOAT)
        for v in range(0, vocab, LANES):
            some = min(LANES, vocab - v)
            total = sums[0][v : v + some, :]
            for other in sums[1:]:
                total = total + other[v : v + some, :]
            for r in range(0, some, 8):
                squared = squared + total[r : r + 8, :] * total[r : r + 8, :]
            if some < LANES:
                total = jnp.concatenate([total, jnp.zeros((LANES - some, LANES), FLOAT)], axis=0)
            out[:, v : v + some] = total.T[:width, :some]
        squares[...] = squared


def collect(grads, ids, vocab, before):
    count = ids.shape[0]
    width = grads.shape[1]
    padded = (vocab // LANES + 1) * LANES
    return pl.pallas_call(
        functools.partial(collect_kernel, len(before)),
        grid=(count // ROWS,),
        in_specs=[
            pl.BlockSpec((1, 1, ROWS), lambda i: (i, 0, 0), memory_space=pltpu.SMEM),
            pl.BlockSpec((ROWS, width), lambda i: (i, 0)),
        ]
        + [pl.BlockSpec(memory_space=pl.ANY)] * len(before),
        out_specs=[
            pl.BlockSpec((width, vocab), lambda i: (0, 0)),
            pl.BlockSpec((8, LANES), lambda i: (0, 0)),
        ],
        out_shape=[
            jax.ShapeDtypeStruct((width, vocab), FLOAT),
            jax.ShapeDtypeStruct((8, LANES), FLOAT),
        ],
        scratch_shapes=[pltpu.VMEM((ROWS, LANES), FLOAT)]
        + [pltpu.VMEM((padded, LANES), FLOAT)] * 8,
        compiler_params=pltpu.CompilerParams(vmem_limit_bytes=VMEM_LIMIT),
        cost_estimate=SMALL,
        name="collect",
    )(ids.reshape(count // ROWS, 1, ROWS), grads, *before)


def edge_of(vocab):
    return vocab - (pl.cdiv(vocab, TILE) - 1) * TILE


def each_tile(vocab, work):
    last = edge_of(vocab)
    if last == TILE:
        work(TILE)
    else:
        step, steps = pl.program_id(0), pl.num_programs(0)
        pl.when(step < steps - 1)(lambda: work(TILE))
        pl.when(step == steps - 1)(lambda: work(last))


def turned_rows(rows):
    return jnp.concatenate([rows] * (LANES // 8), axis=0).T


def scan_kernel(vocab, norm, weight, target, logits, stats, turned, peak, total, hit, aims):
    step = pl.program_id(0)
    rows = norm.shape[0]

    @pl.when(step == 0)
    def _():
        peak[...] = jnp.full_like(peak, NEG)
        total[...] = jnp.zeros_like(total)
        hit[...] = jnp.zeros_like(hit)
        aims[...] = turned_rows(target[...])
        for r in range(0, rows, CHUNK):
            turned[:, r : r + CHUNK] = norm[r : r + CHUNK, :].T

    def work(width):
        lane = lax.broadcasted_iota(jnp.int32, (CHUNK, LANES), 1)
        for r in range(0, rows, CHUNK):
            part = pl.ds(r, CHUNK)
            value = jnp.dot(norm[part, :], weight[...], preferred_element_type=FLOAT)
            logits[part, :] = value
            aim = aims[part, 1:2].astype(jnp.int32) - step * TILE
            slabs, found = [], hit[part, :]
            for c in range(0, width, LANES):
                slab = value[:, c : c + LANES]
                if c + LANES > width:
                    slab = jnp.where(lane < width - c, slab, NEG)
                slabs.append(slab)
                found = found + jnp.where(lane == aim - c, slab, 0.0)
            hit[part, :] = found
            before = peak[part, :]
            top = functools.reduce(jnp.maximum, slabs, before)
            added = total[part, :] * jnp.exp(before - top)
            for slab in slabs:
                added = added + jnp.exp(slab - top)
            total[part, :] = added
            peak[part, :] = top

    each_tile(vocab, work)

    @pl.when(step == pl.num_programs(0) - 1)
    def _():
        top = jnp.max(peak[...], axis=1, keepdims=True)
        added = jnp.sum(total[...] * jnp.exp(peak[...] - top), axis=1, keepdims=True)
        found = jnp.sum(hit[...], axis=1, keepdims=True)
        lane = lax.broadcasted_iota(jnp.int32, (rows, LANES), 1)
        joined = jnp.where(lane == 0, top, jnp.where(lane == 1, added, found))
        stats[...] = joined.T[:8, :]


def head_scan(norm, weight, extra):
    rows, depth = norm.shape
    vocab = weight.shape[1]
    return pl.pallas_call(
        functools.partial(scan_kernel, vocab),
        grid=(pl.cdiv(vocab, TILE),),
        in_specs=[
            pl.BlockSpec((rows, depth), lambda i: (0, 0), pipeline_mode=pl.Buffered(1)),
            pl.BlockSpec((depth, TILE), lambda i: (0, i)),
            pl.BlockSpec((8, rows), lambda i: (0, 0)),
        ],
        out_specs=[
            pl.BlockSpec((rows, TILE), lambda i: (0, i)),
            pl.BlockSpec((8, rows), lambda i: (0, 0)),
            pl.BlockSpec((depth, rows), lambda i: (0, 0), pipeline_mode=pl.Buffered(1)),
        ],
        out_shape=[
            jax.ShapeDtypeStruct((rows, vocab), FLOAT),
            jax.ShapeDtypeStruct((8, rows), FLOAT),
            jax.ShapeDtypeStruct((depth, rows), HALF),
        ],
        scratch_shapes=[pltpu.VMEM((rows, LANES), FLOAT)] * 4,
        compiler_params=pltpu.CompilerParams(vmem_limit_bytes=VMEM_LIMIT),
        cost_estimate=SMALL,
        name="head_scan",
    )(norm, weight, extra)


def grad_kernel(vocab, turned, weight, info, logits, grad, out, total, slope, columns):
    step = pl.program_id(0)
    rows = logits.shape[0]

    @pl.when(step == 0)
    def _():
        columns[...] = turned_rows(info[...])
        total[...] = jnp.zeros_like(total)

    def work(width):
        lane = lax.broadcasted_iota(jnp.int32, (CHUNK, TILE), 1)
        table = weight[...]
        if width < TILE:
            table = jnp.where(lax.broadcasted_iota(jnp.int32, table.shape, 1) < width, table, 0.0)
        for r in range(0, rows, CHUNK):
            part = pl.ds(r, CHUNK)
            aim = columns[part, 3:4].astype(jnp.int32) - step * TILE
            value = jnp.exp(logits[part, :] - columns[part, 0:1])
            value = (value - jnp.where(lane == aim, 1.0, 0.0)) * columns[part, 2:3]
            if width < TILE:
                value = jnp.where(lane < width, value, 0.0)
            value = value.astype(HALF)
            slope[part, :] = value
            total[part, :] = total[part, :] + lax.dot_general(
                value, table, (((1,), (1,)), ((), ())), preferred_element_type=FLOAT
            )
        grad[...] = jnp.dot(turned[...], slope[...], preferred_element_type=FLOAT).astype(HALF)

    each_tile(vocab, work)

    @pl.when(step == pl.num_programs(0) - 1)
    def _():
        for r in range(0, rows, CHUNK):
            out[pl.ds(r, CHUNK), :] = total[pl.ds(r, CHUNK), :].astype(HALF)


def head_grad(turned, weight, info, logits):
    depth, rows = turned.shape
    vocab = weight.shape[1]
    return pl.pallas_call(
        functools.partial(grad_kernel, vocab),
        grid=(pl.cdiv(vocab, TILE),),
        in_specs=[
            pl.BlockSpec((depth, rows), lambda i: (0, 0), pipeline_mode=pl.Buffered(1)),
            pl.BlockSpec((depth, TILE), lambda i: (0, i)),
            pl.BlockSpec((8, rows), lambda i: (0, 0)),
            pl.BlockSpec((rows, TILE), lambda i: (0, i)),
        ],
        out_specs=[
            pl.BlockSpec((depth, TILE), lambda i: (0, i)),
            pl.BlockSpec((rows, depth), lambda i: (0, 0), pipeline_mode=pl.Buffered(1)),
        ],
        out_shape=[
            jax.ShapeDtypeStruct((depth, vocab), HALF),
            jax.ShapeDtypeStruct((rows, depth), HALF),
        ],
        scratch_shapes=[
            pltpu.VMEM((rows, depth), FLOAT),
            pltpu.VMEM((rows, TILE), HALF),
            pltpu.VMEM((rows, LANES), FLOAT),
        ],
        compiler_params=pltpu.CompilerParams(vmem_limit_bytes=VMEM_LIMIT),
        cost_estimate=SMALL,
        name="head_grad",
    )(turned, weight, info, logits)


def turn_rows(low, high, cosine, sine):
    return low * cosine - high * sine, high * cosine + low * sine


def reach(block, share, longest):
    back = -(-(longest - 1) // share)
    return max(0, block - back) * share


def seen(first, low, high, place):
    keys = low + lax.broadcasted_iota(jnp.int32, (high - low, first.shape[1]), 0)
    queries = place + lax.broadcasted_iota(jnp.int32, (high - low, first.shape[1]), 1)
    return (keys >= first) & (keys <= queries)


def attend_kernel(base, qkv, cosine, sine, first, attended, kept, log_total):
    seq = pl.program_id(1)
    blocks = base.shape[0]
    length = cosine.shape[1]
    share = length // blocks
    half = HEAD_DIM // 2

    def spot(i):
        return pl.ds(pl.multiple_of(base[i] + seq * share, share), share)

    for i in range(blocks):
        at = pl.ds(i * share, share)
        turns = (cosine[:, at], sine[:, at])
        for c in (0, 1):
            top = c * HEAD_DIM
            low, high = turn_rows(
                qkv[top : top + half, spot(i)], qkv[top + half : top + HEAD_DIM, spot(i)], *turns
            )
            kept[0, top : top + half, at] = low.astype(HALF)
            kept[0, top + half : top + HEAD_DIM, at] = high.astype(HALF)
        kept[0, 2 * HEAD_DIM :, at] = qkv[2 * HEAD_DIM :, spot(i)].astype(HALF)
    key = kept[0, HEAD_DIM : 2 * HEAD_DIM, :].T
    for i in range(blocks):
        low, high = reach(i, share, length // 2), (i + 1) * share
        at = pl.ds(i * share, share)
        scores = jnp.dot(
            key[low:high, :], kept[0, :HEAD_DIM, at], preferred_element_type=FLOAT
        ) * (HEAD_DIM**-0.5)
        scores = jnp.where(seen(first[0, :, at][:1], low, high, i * share), scores, NEG)
        peak = jnp.max(scores, axis=0, keepdims=True)
        expo = jnp.exp(scores - peak)
        summed = jnp.sum(expo, axis=0, keepdims=True)
        probs = (expo * (1.0 / summed)).astype(HALF)
        value = kept[0, 2 * HEAD_DIM :, low:high]
        attended[:, spot(i)] = jnp.dot(value, probs, preferred_element_type=FLOAT).astype(HALF)
        log_total[0, 0, :, at] = jnp.broadcast_to(peak + jnp.log(summed), (8, share))


def attend(base, qkv, cosine, sine, first):
    seqs, length = first.shape[0], first.shape[2]
    heads = qkv.shape[0] // (3 * HEAD_DIM)
    tokens = qkv.shape[1]
    return pl.pallas_call(
        attend_kernel,
        grid=(heads, seqs),
        in_specs=[
            pl.BlockSpec(memory_space=pltpu.SMEM),
            pl.BlockSpec((3 * HEAD_DIM, tokens), lambda h, j: (h, 0)),
            pl.BlockSpec(cosine.shape, lambda h, j: (0, 0)),
            pl.BlockSpec(sine.shape, lambda h, j: (0, 0)),
            pl.BlockSpec((1, 8, length), lambda h, j: (j, 0, 0)),
        ],
        out_specs=[
            pl.BlockSpec((HEAD_DIM, tokens), lambda h, j: (h, 0)),
            pl.BlockSpec((1, 3 * HEAD_DIM, length), lambda h, j: (j, h, 0)),
            pl.BlockSpec((1, 1, 8, length), lambda h, j: (j, h, 0, 0)),
        ],
        out_shape=[
            jax.ShapeDtypeStruct((heads * HEAD_DIM, tokens), HALF),
            jax.ShapeDtypeStruct((seqs, heads * 3 * HEAD_DIM, length), HALF),
            jax.ShapeDtypeStruct((seqs, heads, 8, length), FLOAT),
        ],
        compiler_params=pltpu.CompilerParams(vmem_limit_bytes=VMEM_LIMIT),
        cost_estimate=SMALL,
        name="attend",
    )(base, qkv, cosine, sine, first)


def attend_back_kernel(waits, base, kept, log_total, slope, cosine, sine, first, *refs):
    d_qkv, d_key, d_value = refs[waits:]
    seq = pl.program_id(1)
    blocks = base.shape[0]
    length = cosine.shape[1]
    share = length // blocks
    half = HEAD_DIM // 2
    scale = HEAD_DIM**-0.5

    def spot(i):
        return pl.ds(pl.multiple_of(base[i] + seq * share, share), share)

    def put(part, i, low, high):
        at = pl.ds(i * share, share)
        d_low, d_high = turn_rows(low, high, cosine[:, at], -sine[:, at])
        top = part * HEAD_DIM
        d_qkv[top : top + half, spot(i)] = d_low.astype(HALF)
        d_qkv[top + half : top + HEAD_DIM, spot(i)] = d_high.astype(HALF)

    query = kept[0, :HEAD_DIM, :].T
    key = kept[0, HEAD_DIM : 2 * HEAD_DIM, :].T
    value = kept[0, 2 * HEAD_DIM :, :].T
    d_key[...] = jnp.zeros_like(d_key)
    d_value[...] = jnp.zeros_like(d_value)
    for i in range(blocks):
        low, high = reach(i, share, length // 2), (i + 1) * share
        at = pl.ds(i * share, share)
        turned = slope[:, spot(i)]
        scores = jnp.dot(
            key[low:high, :], kept[0, :HEAD_DIM, at], preferred_element_type=FLOAT
        ) * scale
        scores = jnp.where(seen(first[0, :, at][:1], low, high, i * share), scores, NEG)
        probs = jnp.exp(scores - log_total[0, 0, :1, at])
        d_probs = jnp.dot(value[low:high, :], turned, preferred_element_type=FLOAT)
        centre = jnp.sum(probs * d_probs, axis=0, keepdims=True)
        d_scores = (probs * (d_probs - centre)).astype(HALF)
        d_value[low:high, :] += jnp.dot(probs.astype(HALF), turned.T, preferred_element_type=FLOAT)
        d_key[low:high, :] += jnp.dot(
            d_scores, query[i * share : (i + 1) * share, :], preferred_element_type=FLOAT
        )
        d_query = scale * jnp.dot(
            kept[0, HEAD_DIM : 2 * HEAD_DIM, low:high], d_scores, preferred_element_type=FLOAT
        )
        put(0, i, d_query[:half, :], d_query[half:, :])
    for i in range(blocks):
        rows = pl.ds(i * share, share)
        turned = scale * d_key[rows, :].T
        put(1, i, turned[:half, :], turned[half:, :])
        d_qkv[2 * HEAD_DIM :, spot(i)] = d_value[rows, :].T.astype(HALF)


def attend_back(base, kept, log_total, slope, cosine, sine, first, before):
    seqs, length = first.shape[0], first.shape[2]
    tokens = slope.shape[1]
    heads = slope.shape[0] // HEAD_DIM
    return pl.pallas_call(
        functools.partial(attend_back_kernel, len(before)),
        grid=(heads, seqs),
        in_specs=[
            pl.BlockSpec(memory_space=pltpu.SMEM),
            pl.BlockSpec((1, 3 * HEAD_DIM, length), lambda h, j: (j, h, 0)),
            pl.BlockSpec((1, 1, 8, length), lambda h, j: (j, h, 0, 0)),
            pl.BlockSpec((HEAD_DIM, tokens), lambda h, j: (h, 0)),
            pl.BlockSpec(cosine.shape, lambda h, j: (0, 0)),
            pl.BlockSpec(sine.shape, lambda h, j: (0, 0)),
            pl.BlockSpec((1, 8, length), lambda h, j: (j, 0, 0)),
        ]
        + [pl.BlockSpec(memory_space=pl.ANY)] * len(before),
        out_specs=pl.BlockSpec((3 * HEAD_DIM, tokens), lambda h, j: (h, 0)),
        out_shape=jax.ShapeDtypeStruct((heads * 3 * HEAD_DIM, tokens), HALF),
        scratch_shapes=[pltpu.VMEM((length, HEAD_DIM), FLOAT)] * 2,
        compiler_params=pltpu.CompilerParams(vmem_limit_bytes=VMEM_LIMIT),
        cost_estimate=SMALL,
        name="attend_back",
    )(base, kept, log_total, slope, cosine, sine, first, *before)


def near_and_far(own, rank):
    return (own, rank ^ 1), (own, rank ^ 2)


def remote(source, target, send, recv, n, peer):
    return pltpu.make_async_remote_copy(
        src_ref=source,
        dst_ref=target,
        send_sem=send.at[n],
        recv_sem=recv.at[n],
        device_id=peer,
        device_id_type=MESH,
    )


class Boundary:
    COUNT = 6

    def __init__(self, own, rank, send, recv, parts, rows):
        self.near, self.far = near_and_far(own, rank)
        self.send, self.recv, self.parts = send, recv, parts
        self.rows = [pl.ds(h * rows, rows) for h in range(parts)]
        self.copies = []

    def copy(self, source, target, n, h, peer):
        made = remote(source, target, self.send, self.recv, n * self.parts + h, peer)
        made.start()
        self.copies.append(made)
        return made

    def sums(self, make, partial, beside, away, come):
        later, crossing = {}, []

        def part(p, h):
            partial[p, self.rows[h], :] = make(p, h).astype(HALF)

        def leave(p, h):
            part(2 + p, h)
            at = self.rows[h]
            later[p, h] = self.copy(partial.at[2 + p, at], beside.at[p, at], p, h, self.near)

        def pair(p, h):
            at = self.rows[h]
            later[p, h].wait_recv()
            return partial[p, at, :].astype(FLOAT) + beside[p, at, :].astype(FLOAT)

        for h, at in enumerate(self.rows):
            leave(1, h)
            part(1, h)
            away[at, :] = pair(1, h).astype(HALF)
            crossing.append(self.copy(away.at[at], come.at[at], 2, h, self.far))
        for h in range(self.parts):
            leave(0, h)
        for h in range(self.parts):
            part(0, h)
        for h, at in enumerate(self.rows):
            total = pair(0, h)
            crossing[h].wait_recv()
            yield h, at, total + come[at, :].astype(FLOAT)

    def give(self, full, h):
        at = self.rows[h]
        self.crossed = getattr(self, "crossed", [])
        self.crossed.append(self.copy(full.at[0, at], full.at[1, at], 3, h, self.far))
        self.beside = getattr(self, "beside", [])
        self.beside.append(self.copy(full.at[0, at], full.at[2, at], 4, h, self.near))

    def pass_on(self, full):
        arrived = []
        for h, at in enumerate(self.rows):
            self.crossed[h].wait_recv()
            arrived.append(self.copy(full.at[1, at], full.at[3, at], 5, h, self.near))
        for copy in self.beside + arrived:
            copy.wait_recv()

    def end(self):
        for copy in self.copies:
            copy.wait_send()


def turned_product(left, right):
    return lax.dot_general(left, right, (((0,), (1,)), ((), ())), preferred_element_type=FLOAT)


def columns_of(array, p, h, parts):
    step = array.shape[1] // (4 * parts)
    return array[:, (p * parts + h) * step : (p * parts + h + 1) * step]


def forward_kernel(parts, waits, attended, weight, stream, gain, *refs):
    out, full, partial, beside, away, come, send, recv = refs[waits:]
    own, rank = lax.axis_index("dp"), lax.axis_index("tensor")
    greet(list(near_and_far(own, rank)))
    edge = Boundary(own, rank, send, recv, parts, stream.shape[0] // parts)

    def make(p, h):
        return turned_product(columns_of(attended, p, h, parts), weight[...])

    for h, at, total in edge.sums(make, partial, beside, away, come):
        total = stream[at, :] + total
        out[at, :] = total
        full[0, at, :] = normed(total, gain[...]).astype(HALF)
        edge.give(full, h)
    edge.pass_on(full)
    edge.end()


def forward_boundary(attended, weight, stream, gain, before):
    rows, depth = stream.shape
    parts = 2
    vmem = pl.BlockSpec(memory_space=pltpu.VMEM)
    out, full = pl.pallas_call(
        functools.partial(forward_kernel, parts, len(before)),
        in_specs=[vmem] * 4 + [pl.BlockSpec(memory_space=pl.ANY)] * len(before),
        out_specs=[vmem] * 2,
        out_shape=[
            jax.ShapeDtypeStruct((rows, depth), FLOAT),
            jax.ShapeDtypeStruct((4, rows, depth), HALF),
        ],
        scratch_shapes=exchange_scratch(rows, depth, parts),
        compiler_params=pltpu.CompilerParams(
            collective_id=3, has_side_effects=True, vmem_limit_bytes=VMEM_LIMIT
        ),
        cost_estimate=SMALL,
        name="forward_boundary",
    )(attended, weight, stream, gain, *before)
    return out, full.reshape(4 * rows, depth)


def normed_slope(grad, values, gain):
    root = lax.rsqrt(jnp.mean(values * values, axis=-1, keepdims=True) + EPS)
    unit = values * root
    inner = grad * gain
    middle = jnp.mean(inner * unit, axis=-1, keepdims=True)
    return root * (inner - unit * middle), jnp.sum(grad * unit, axis=0, keepdims=True)


def wide_forward_kernel(
    norm, weight, stream, gain, out, full, partial, beside, away, come, send, recv
):
    own, rank = lax.axis_index("dp"), lax.axis_index("tensor")
    near, far = near_and_far(own, rank)
    other = (own ^ 1, rank)
    greet([near, far, other])
    parts = 2
    edge = Boundary(own, rank, send, recv, parts, stream.shape[0] // parts)
    crossed, moved, last = [], [], []
    ffn = weight.shape[1] // 3

    def make(p, h):
        both = jnp.dot(
            norm[p, edge.rows[h], :], weight[:, : 2 * ffn], preferred_element_type=FLOAT
        )
        gate, up = both[:, :ffn], both[:, ffn:]
        hidden = (gate * (1.0 / (1.0 + jnp.exp(-gate))) * up).astype(HALF)
        return across(hidden, weight[:, 2 * ffn :])

    for h, at, total in edge.sums(make, partial, beside, away, come):
        total = stream[at, :] + total
        out[at, :] = total
        full[0, 0, at, :] = normed(total, gain[...]).astype(HALF)
        mine = full.at[0, 0, at]
        crossed.append(edge.copy(mine, full.at[0, 1, at], 3, h, far))
        moved.append(edge.copy(mine, full.at[1, 0, at], 4, h, other))
        last.append(edge.copy(mine, full.at[0, 2, at], 5, h, near))
    early, late = edge.rows
    crossed[0].wait_recv()
    one = edge.copy(full.at[0, 1, early], full.at[1, 1, early], 6, 0, other)
    last.append(edge.copy(full.at[0, 1, early], full.at[0, 3, early], 7, 0, near))
    moved[0].wait_recv()
    last.append(edge.copy(full.at[1, 0, early], full.at[1, 2, early], 8, 0, near))
    moved[1].wait_recv()
    two = edge.copy(full.at[1, 0, late], full.at[1, 1, late], 6, 1, far)
    last.append(edge.copy(full.at[1, 0, late], full.at[1, 2, late], 8, 1, near))
    crossed[1].wait_recv()
    last.append(edge.copy(full.at[0, 1, late], full.at[0, 3, late], 7, 1, near))
    one.wait_recv()
    last.append(edge.copy(full.at[1, 1, early], full.at[1, 3, early], 9, 0, near))
    two.wait_recv()
    last.append(edge.copy(full.at[1, 1, late], full.at[1, 3, late], 9, 1, near))
    for copy in last:
        copy.wait_recv()
    edge.end()


def wide_forward(norm, weight, stream, gain):
    rows, depth = stream.shape
    vmem = pl.BlockSpec(memory_space=pltpu.VMEM)
    out, full = pl.pallas_call(
        wide_forward_kernel,
        in_specs=[vmem] * 4,
        out_specs=[vmem] * 2,
        out_shape=[
            jax.ShapeDtypeStruct((rows, depth), FLOAT),
            jax.ShapeDtypeStruct((2, 4, rows, depth), HALF),
        ],
        scratch_shapes=exchange_scratch(rows, depth, 2)[:4] + [pltpu.SemaphoreType.DMA((20,))] * 2,
        compiler_params=pltpu.CompilerParams(
            collective_id=9, has_side_effects=True, vmem_limit_bytes=VMEM_LIMIT
        ),
        cost_estimate=SMALL,
        name="wide_forward",
    )(norm.reshape(4, rows, depth), weight, stream, gain)
    return out, full.reshape(8 * rows, depth)


def wide_backward_kernel(partial, stream, gain, out, g_gain, full, beside, leave, come, send, recv):
    own, rank = lax.axis_index("dp"), lax.axis_index("tensor")
    near, far = near_and_far(own, rank)
    other = (own ^ 1, rank)
    greet([near, far, other])
    parts = 2
    edge = Boundary(own, rank, send, recv, parts, stream.shape[0] // parts)
    early, late = edge.rows
    first = {}
    for n, (y, p) in enumerate(((1, 1), (1, 0), (0, 1), (0, 0))):
        for h, at in enumerate(edge.rows):
            first[y, p, h] = edge.copy(
                partial.at[y, 2 + p, at], beside.at[y, p, at], 5 + n, h, near
            )

    def pair(y, p, h):
        at = edge.rows[h]
        first[y, p, h].wait_recv()
        return partial[y, p, at, :].astype(FLOAT) + beside[y, p, at, :].astype(FLOAT)

    leave[1, 1, early, :] = pair(1, 1, 0).astype(HALF)
    by_other = edge.copy(leave.at[1, 1, early], come.at[1, 1, early], 9, 0, other)
    leave[1, 1, late, :] = pair(1, 1, 1).astype(HALF)
    by_far = edge.copy(leave.at[1, 1, late], come.at[1, 1, late], 9, 1, far)
    leave[1, 0, early, :] = pair(1, 0, 0).astype(HALF)
    other_early = edge.copy(leave.at[1, 0, early], come.at[1, 0, early], 0, 0, other)
    leave[0, 1, late, :] = pair(0, 1, 1).astype(HALF)
    far_late = edge.copy(leave.at[0, 1, late], come.at[0, 1, late], 1, 1, far)
    far_early_sum, other_late_sum = pair(0, 1, 0), pair(1, 0, 1)
    by_other.wait_recv()
    leave[0, 1, early, :] = (far_early_sum + come[1, 1, early, :].astype(FLOAT)).astype(HALF)
    far_early = edge.copy(leave.at[0, 1, early], come.at[0, 1, early], 1, 0, far)
    by_far.wait_recv()
    leave[1, 0, late, :] = (other_late_sum + come[1, 1, late, :].astype(FLOAT)).astype(HALF)
    other_late = edge.copy(leave.at[1, 0, late], come.at[1, 0, late], 0, 1, other)
    g_gain[...] = jnp.zeros_like(g_gain)
    for h, waits in ((0, (other_early, far_early)), (1, (far_late, other_late))):
        at = edge.rows[h]
        total = pair(0, 0, h)
        for copy in waits:
            copy.wait_recv()
        total = total + come[1, 0, at, :].astype(FLOAT) + come[0, 1, at, :].astype(FLOAT)
        slope, by_gain = normed_slope(total, stream[at, :], gain[...])
        g_gain[:1, :] = g_gain[:1, :] + by_gain
        out[at, :] = slope
        full[0, at, :] = slope.astype(HALF)
        edge.crossed = getattr(edge, "crossed", [])
        edge.crossed.append(edge.copy(full.at[0, at], full.at[1, at], 2, h, far))
        edge.beside = getattr(edge, "beside", [])
        edge.beside.append(edge.copy(full.at[0, at], full.at[2, at], 3, h, near))
    arrived = []
    for h, at in enumerate(edge.rows):
        edge.crossed[h].wait_recv()
        arrived.append(edge.copy(full.at[1, at], full.at[3, at], 4, h, near))
    for copy in edge.beside + arrived:
        copy.wait_recv()
    edge.end()


def wide_backward(partial, stream, gain):
    rows, depth = stream.shape
    vmem = pl.BlockSpec(memory_space=pltpu.VMEM)
    out, g_gain, full = pl.pallas_call(
        wide_backward_kernel,
        in_specs=[vmem] * 3,
        out_specs=[vmem] * 3,
        out_shape=[
            jax.ShapeDtypeStruct((rows, depth), FLOAT),
            jax.ShapeDtypeStruct((8, depth), FLOAT),
            jax.ShapeDtypeStruct((4, rows, depth), HALF),
        ],
        scratch_shapes=[pltpu.VMEM((2, 2, rows, depth), HALF)] * 3
        + [pltpu.SemaphoreType.DMA((20,))] * 2,
        compiler_params=pltpu.CompilerParams(
            collective_id=4, has_side_effects=True, vmem_limit_bytes=VMEM_LIMIT
        ),
        cost_estimate=SMALL,
        name="wide_backward",
    )(partial.reshape(2, 4, rows, depth), stream, gain)
    return out, g_gain[:1], full.reshape(4 * rows, depth)


def exchange_scratch(rows, depth, parts):
    return [
        pltpu.VMEM((4, rows, depth), HALF),
        pltpu.VMEM((2, rows, depth), HALF),
        pltpu.VMEM((rows, depth), HALF),
        pltpu.VMEM((rows, depth), HALF),
        pltpu.SemaphoreType.DMA((Boundary.COUNT * parts,)),
        pltpu.SemaphoreType.DMA((Boundary.COUNT * parts,)),
    ]


def backward_kernel(
    parts, norm, later, weight, stream, gain, prior, out, g_gain, full, grad, partial, beside, away, come, kept, send, recv
):
    own, rank = lax.axis_index("dp"), lax.axis_index("tensor")
    greet(list(near_and_far(own, rank)))
    edge = Boundary(own, rank, send, recv, parts, stream.shape[0] // parts)
    ffn = weight.shape[1] // 3

    def make(p, h):
        at = edge.rows[h]
        both = jnp.dot(norm[p, at, :], weight[:, : 2 * ffn], preferred_element_type=FLOAT)
        d_hidden = jnp.dot(later[p, at, :], weight[:, 2 * ffn :], preferred_element_type=FLOAT)
        gate, up = both[:, :ffn], both[:, ffn:]
        open_part = 1.0 / (1.0 + jnp.exp(-gate))
        passed = gate * open_part
        d_gate = (d_hidden * up * (open_part * (1.0 + gate * (1.0 - open_part)))).astype(HALF)
        d_up = (d_hidden * passed).astype(HALF)
        kept[p, at, :ffn] = d_gate
        kept[p, at, ffn : 2 * ffn] = d_up
        kept[p, at, 2 * ffn :] = (passed * up).astype(HALF)
        return across(d_gate, weight[:, :ffn]) + across(d_up, weight[:, ffn : 2 * ffn])

    g_gain[...] = jnp.zeros_like(g_gain)
    for h, at, total in edge.sums(make, partial, beside, away, come):
        slope, by_gain = normed_slope(total, stream[at, :], gain[...])
        slope = slope + prior[at, :]
        g_gain[:1, :] = g_gain[:1, :] + by_gain
        out[at, :] = slope
        full[0, at, :] = slope.astype(HALF)
        edge.give(full, h)
    for left, low, high in ((norm, 0, 2 * ffn), (later, 2 * ffn, 3 * ffn)):
        turned = [left[p].T for p in range(4)]
        for c in range(low, high, CHUNK):
            total = jnp.dot(turned[0], kept[0, :, c : c + CHUNK], preferred_element_type=FLOAT)
            for p in (1, 2, 3):
                total = total + jnp.dot(
                    turned[p], kept[p, :, c : c + CHUNK], preferred_element_type=FLOAT
                )
            grad[:, c : c + CHUNK] = total.astype(HALF)
    edge.pass_on(full)
    edge.end()


def backward_boundary(norm, later, weight, stream, gain, prior):
    rows, depth = stream.shape
    parts = 2
    vmem = pl.BlockSpec(memory_space=pltpu.VMEM)
    scratch = exchange_scratch(rows, depth, parts)
    out, g_gain, full, grad = pl.pallas_call(
        functools.partial(backward_kernel, parts),
        in_specs=[vmem] * 6,
        out_specs=[vmem] * 4,
        out_shape=[
            jax.ShapeDtypeStruct((rows, depth), FLOAT),
            jax.ShapeDtypeStruct((8, depth), FLOAT),
            jax.ShapeDtypeStruct((4, rows, depth), HALF),
            jax.ShapeDtypeStruct(weight.shape, HALF),
        ],
        scratch_shapes=scratch[:4] + [pltpu.VMEM((4, rows, weight.shape[1]), HALF)] + scratch[4:],
        compiler_params=pltpu.CompilerParams(
            collective_id=5, has_side_effects=True, vmem_limit_bytes=VMEM_LIMIT
        ),
        cost_estimate=SMALL,
        name="backward_boundary",
    )(norm.reshape(4, rows, depth), later.reshape(4, rows, depth), weight, stream, gain, prior)
    return out, g_gain[:1], full.reshape(4 * rows, depth), grad


def start_kernel(ids, turned, gain, block, stays, leaves, stream, full, weights, pair, *refs):
    table, corner, rows, out, near, cross, come, send, recv, local = refs
    own, rank = lax.axis_index("dp"), lax.axis_index("tensor")
    beside, across = near_and_far(own, rank)
    far = [(own ^ k, rank) for k in range(1, 8)]
    greet([beside, across] + far)
    width, vocab = turned.shape
    count = rows.shape[0]
    copies, beside_of, across_of, far_of = [], {}, {}, {}

    def begin(source, target, n, peer):
        copy = remote(source, target, send, recv, n, peer)
        copy.start()
        copies.append(copy)
        return copy

    def place(k):
        return pl.ds(pl.multiple_of((own ^ k) * width, width), width)

    weights_of = {}
    for k in (1, 2, 4, 6):
        weights_of[k] = begin(block, weights.at[place(0)], 35 + k, far[k - 1])
    weights[place(0), :] = block[...]
    bit = own % 2
    line = pl.ds(pl.multiple_of(bit * width, width), width)
    aside = begin(leaves, pair.at[line], 43, far[0])
    own_line = pltpu.make_async_copy(stays, pair.at[line], local)
    own_line.start()
    corner[...] = jnp.zeros_like(corner)
    for v in range(0, vocab, LANES):
        some = min(LANES, vocab - v)
        corner[:width, :some] = turned[:, v : v + some].astype(HALF).astype(FLOAT)
        if some < LANES:
            corner[:width, some:] = jnp.zeros((width, LANES - some), FLOAT)
        table[v : v + LANES, :] = corner[...].T
    if vocab % LANES == 0:
        table[vocab:, :] = jnp.zeros((LANES, LANES), FLOAT)

    def fetch(place):
        def body(i, carry):
            for u in range(16):
                r = i * 16 + u
                rows[pl.ds(r, 1), :] = table[pl.ds(ids[place * count + r], 1), :]
            return carry

        lax.fori_loop(0, count // 16, body, 0)

    for p in (3, 2):
        for k in range(8):
            fetch(p * 8 + k)
            out[p, k] = rows[:, :width].astype(HALF)
            beside_of[p - 2, k] = begin(out.at[p, k], near.at[p - 2, k], (p - 2) * 8 + k, beside)
    for k in (2, 4, 6):
        weights_of[k].wait_recv()
        weights_of[k + 1] = begin(weights.at[place(k)], weights.at[place(k)], 36 + k, far[0])
    order = (7, 6, 5, 4, 3, 2, 1, 0)
    for k in order:
        fetch(8 + k)
        beside_of[1, k].wait_recv()
        total = rows[:, :width] + near[1, k].astype(FLOAT)
        out[1, k] = total.astype(HALF)
        across_of[k] = begin(out.at[1, k], cross.at[k], 16 + k, across)
    for k in order:
        fetch(k)
        beside_of[0, k].wait_recv()
        total = rows[:, :width] + near[0, k].astype(FLOAT)
        across_of[k].wait_recv()
        out[0, k] = (total + cross[k].astype(FLOAT)).astype(HALF)
        if k:
            far_of[k] = begin(out.at[0, k], come.at[k], 24 + k, far[k - 1])
    come[0] = out[0, 0]
    for k in order[:-1]:
        far_of[k].wait_recv()
    for b in range(8):
        stream[:, b * width : (b + 1) * width] = come[own ^ b].astype(FLOAT)
    full[0] = normed(stream[...], gain[...]).astype(HALF)
    one = begin(full.at[0], full.at[1], 32, across)
    two = begin(full.at[0], full.at[2], 33, beside)
    one.wait_recv()
    three = begin(full.at[1], full.at[3], 34, beside)
    two.wait_recv()
    three.wait_recv()
    for k in (1, 3, 5, 7):
        weights_of[k].wait_recv()
    aside.wait_recv()
    own_line.wait()
    for copy in copies:
        copy.wait_send()


def start_rows(ids, turned, gain, block, stays, leaves):
    width, vocab = turned.shape
    rows = ids.shape[0] // 32
    padded = (vocab // LANES + 1) * LANES
    vmem = pl.BlockSpec(memory_space=pltpu.VMEM)
    whole = pl.BlockSpec(memory_space=pl.ANY)
    stream, full, weights, pair = pl.pallas_call(
        start_kernel,
        in_specs=[pl.BlockSpec(memory_space=pltpu.SMEM), vmem, vmem, vmem, whole, whole],
        out_specs=[vmem] * 3 + [whole],
        out_shape=[
            jax.ShapeDtypeStruct((rows, 8 * width), FLOAT),
            jax.ShapeDtypeStruct((4, rows, 8 * width), HALF),
            jax.ShapeDtypeStruct((8 * width, block.shape[1]), HALF),
            jax.ShapeDtypeStruct((2 * width, stays.shape[1]), HALF),
        ],
        scratch_shapes=[
            pltpu.VMEM((padded, LANES), FLOAT),
            pltpu.VMEM((LANES, LANES), FLOAT),
            pltpu.VMEM((rows, LANES), FLOAT),
            pltpu.VMEM((4, 8, rows, width), HALF),
            pltpu.VMEM((2, 8, rows, width), HALF),
            pltpu.VMEM((8, rows, width), HALF),
            pltpu.VMEM((8, rows, width), HALF),
            pltpu.SemaphoreType.DMA((44,)),
            pltpu.SemaphoreType.DMA((44,)),
            pltpu.SemaphoreType.DMA,
        ],
        compiler_params=pltpu.CompilerParams(
            collective_id=6, has_side_effects=True, vmem_limit_bytes=VMEM_LIMIT
        ),
        cost_estimate=SMALL,
        name="start_rows",
    )(ids, turned, gain, block, stays, leaves)
    return stream, full.reshape(4 * rows, 8 * width), weights, pair


def end_kernel(parts, waits, d_qkv, weight, stream, gain, prior, gain_one, gain_two, apart, *refs):
    rows, g_gain, arrived, partial, beside, away, come, leave, mine, summed, first, second, send, recv = refs[waits:]
    own, rank = lax.axis_index("dp"), lax.axis_index("tensor")
    near, across = near_and_far(own, rank)
    far = [(own ^ k, rank) for k in range(1, 8)]
    greet([near, across, (own, rank ^ 3)] + far)
    edge = Boundary(own, rank, send, recv, parts, stream.shape[0] // parts)
    aside = remote(apart, arrived, send, recv, Boundary.COUNT * parts, far[0])
    aside.start()
    edge.copies.append(aside)
    width = rows.shape[3]
    gain_zero = jnp.zeros_like(gain[...])
    mine[...] = jnp.zeros_like(mine)

    def make(p, h):
        return turned_product(columns_of(d_qkv, p, h, parts), weight[...])

    for h, at, total in edge.sums(make, partial, beside, away, come):
        slope, by_gain = normed_slope(total, stream[at, :], gain[...])
        slope = slope + prior[at, :]
        gain_zero = gain_zero + by_gain
        for b in range(8):
            leave[b, at, :] = slope[:, b * width : (b + 1) * width].astype(HALF)
    base = Boundary.COUNT * parts
    far_of, last = {}, []

    def begin(source, target, n, peer):
        copy = remote(source, target, send, recv, base + n, peer)
        copy.start()
        edge.copies.append(copy)
        return copy

    order = (7, 6, 5, 4, 3, 2, 1)
    for k in order:
        far_of[k] = begin(leave.at[own ^ k], rows.at[0, k], k, far[k - 1])
    rows[0, 0] = leave[own]
    for b in range(8):
        for n, line in enumerate((gain_zero, gain_one[...], gain_two[...])):
            mine[own ^ b, n : n + 1, :width] = line[:, b * width : (b + 1) * width]
    gains_of = [
        begin(mine, first.at[n - 1], 31 + n, (own, rank ^ n)) for n in (1, 2, 3)
    ]
    crossed = {}
    for k in (0, 1, 2, 3, 4, 5, 6, 7):
        if k:
            far_of[k].wait_recv()
        crossed[k] = begin(rows.at[0, k], rows.at[1, k], 8 + k, across)
        last.append(begin(rows.at[0, k], rows.at[2, k], 16 + k, near))
    for copy in gains_of:
        copy.wait_recv()
    summed[...] = (mine[...] + first[0]) + (first[1] + first[2])
    gains_of = [begin(summed.at[k], second.at[k], 34 + k, far[k - 1]) for k in range(1, 8)]
    for k in (0, 1, 2, 3, 4, 5, 6, 7):
        crossed[k].wait_recv()
        last.append(begin(rows.at[1, k], rows.at[3, k], 24 + k, near))
    for copy in last + gains_of:
        copy.wait_recv()
    second[0] = summed[0]
    pairs = [second[k] + second[k + 1] for k in (0, 2, 4, 6)]
    g_gain[...] = (pairs[0] + pairs[1]) + (pairs[2] + pairs[3])
    aside.wait_recv()
    edge.end()


def end_rows(d_qkv, weight, stream, gain, prior, gain_one, gain_two, apart, width, before):
    rows, depth = stream.shape
    parts = 2
    vmem = pl.BlockSpec(memory_space=pltpu.VMEM)
    semaphores = Boundary.COUNT * parts + 42
    whole = pl.BlockSpec(memory_space=pl.ANY)
    out, g_gain, arrived = pl.pallas_call(
        functools.partial(end_kernel, parts, len(before)),
        in_specs=[vmem] * 7 + [whole] * (1 + len(before)),
        out_specs=[vmem] * 2 + [whole],
        out_shape=[
            jax.ShapeDtypeStruct((4, 8, rows, width), HALF),
            jax.ShapeDtypeStruct((8, LANES), FLOAT),
            jax.ShapeDtypeStruct(apart.shape, HALF),
        ],
        scratch_shapes=exchange_scratch(rows, depth, parts)[:4]
        + [
            pltpu.VMEM((8, rows, width), HALF),
            pltpu.VMEM((8, 8, LANES), FLOAT),
            pltpu.VMEM((8, 8, LANES), FLOAT),
            pltpu.VMEM((3, 8, 8, LANES), FLOAT),
            pltpu.VMEM((8, 8, LANES), FLOAT),
            pltpu.SemaphoreType.DMA((semaphores,)),
            pltpu.SemaphoreType.DMA((semaphores,)),
        ],
        compiler_params=pltpu.CompilerParams(
            collective_id=7, has_side_effects=True, vmem_limit_bytes=VMEM_LIMIT
        ),
        cost_estimate=SMALL,
        name="end_rows",
    )(d_qkv, weight, stream, gain, prior, gain_one, gain_two, apart, *before)
    return out.reshape(-1, width), g_gain[:3, :width], arrived


def merge_kernel(scan, extra, joined, mine, every, send, recv):
    own, rank = lax.axis_index("dp"), lax.axis_index("tensor")
    turns = [(a, b) for a in (0, 1) for b in range(4)][1:]
    peers = [(own ^ a, rank ^ b) for a, b in turns]
    greet(peers)
    tokens = scan.shape[1] // 2
    share = tokens // 4
    mine[...] = jnp.zeros_like(mine)
    mine[0:3, :] = scan[0:3, :tokens]
    mine[3:6, :] = scan[0:3, tokens:]
    copies = []
    for n, peer in enumerate(peers):
        copies.append(remote(mine, every.at[n], send, recv, n, peer))
        copies[-1].start()
    joined[...] = jnp.zeros_like(joined)
    joined[2:4, :] = extra[:2, :]
    for copy in copies:
        copy.wait()
    for y in (0, 1):
        for p in range(4):
            terms = {(0, 0): mine[3 * y : 3 * y + 3, p * share : (p + 1) * share]}
            for n, (a, b) in enumerate(turns):
                q = TURN.index(TURN[p] ^ b)
                terms[a, b] = every[n, 3 * (y ^ a) : 3 * (y ^ a) + 3, q * share : (q + 1) * share]
            peak = functools.reduce(jnp.maximum, [term[0:1] for term in terms.values()])
            sums, hits = [], []
            for a in (0, 1):
                for b in (0, 2):
                    pair = (terms[a, b], terms[a, b ^ 1])
                    sums.append(sum(term[1:2] * jnp.exp(term[0:1] - peak) for term in pair))
                    hits.append(pair[0][2:3] + pair[1][2:3])
            at = pl.ds(y * tokens + p * share, share)
            joined[0:1, at] = peak + jnp.log((sums[0] + sums[1]) + (sums[2] + sums[3]))
            joined[1:2, at] = (hits[0] + hits[1]) + (hits[2] + hits[3])


def merge_scans(scan, extra):
    vmem = pl.BlockSpec(memory_space=pltpu.VMEM)
    shape = (8, scan.shape[1] // 2)
    return pl.pallas_call(
        merge_kernel,
        in_specs=[vmem] * 2,
        out_specs=vmem,
        out_shape=jax.ShapeDtypeStruct(scan.shape, FLOAT),
        scratch_shapes=[
            pltpu.VMEM(shape, FLOAT),
            pltpu.VMEM((7, *shape), FLOAT),
            pltpu.SemaphoreType.DMA((7,)),
            pltpu.SemaphoreType.DMA((7,)),
        ],
        compiler_params=pltpu.CompilerParams(collective_id=8, has_side_effects=True),
        name="merge_scans",
    )(scan, extra)


def across(left, right):
    return lax.dot_general(left, right, (((1,), (1,)), ((), ())), preferred_element_type=FLOAT)


def product(left, right, over_left, over_right):
    return lax.dot_general(
        left, right, (((over_left,), (over_right,)), ((), ())), preferred_element_type=FLOAT
    )


def adam(weight, grad, first, second, rate, decay):
    first = BETA_ONE * first + (1.0 - BETA_ONE) * grad
    second = BETA_TWO * second + (1.0 - BETA_TWO) * grad * grad
    first_hat = first / (1.0 - BETA_ONE**STEP)
    second_hat = second / (1.0 - BETA_TWO**STEP)
    weight = weight - rate * (first_hat / (jnp.sqrt(second_hat) + ADAM_EPS) + decay * weight)
    return (weight, first, second, weight.astype(HALF))


def update_kernel(counts, factor, *refs):
    arrays = len(counts)
    inputs, outputs = refs[: 3 * arrays + sum(counts)], refs[3 * arrays + sum(counts) :]
    grads = inputs[3 * arrays :]
    for n in range(arrays):
        weight, first, second = inputs[3 * n : 3 * n + 3]
        low = 0
        for grad in grads[: counts[n]]:
            high = low + grad.shape[-1]
            at = (Ellipsis, slice(low, high))
            results = adam(
                weight[at], grad[...].astype(FLOAT) * factor[0], first[at], second[at], LR, DECAY
            )
            for out, result in zip(outputs[4 * n : 4 * n + 4], results):
                out[at] = result
            low = high
        grads = grads[counts[n] :]


def update(arrays, factor):
    rows = arrays[0][0].shape[0]
    steps = rows // 16 if rows % 16 == 0 else 1

    def block(array):
        zeros = (0,) * (array.ndim - 1)
        return pl.BlockSpec((array.shape[0] // steps, *array.shape[1:]), lambda i: (i, *zeros))

    inputs = [array for entry in arrays for array in entry[:3]]
    grads = [grad for entry in arrays for grad in entry[3]]
    outs = [
        jax.ShapeDtypeStruct(entry[0].shape, kind)
        for entry in arrays
        for kind in (FLOAT, FLOAT, FLOAT, HALF)
    ]
    results = pl.pallas_call(
        functools.partial(update_kernel, tuple(len(entry[3]) for entry in arrays)),
        grid=(steps,),
        in_specs=[pl.BlockSpec(memory_space=pltpu.SMEM)] + [block(a) for a in inputs + grads],
        out_specs=[block(a) for a in outs],
        out_shape=outs,
        compiler_params=pltpu.CompilerParams(vmem_limit_bytes=VMEM_LIMIT),
        cost_estimate=SMALL,
        name="update",
    )(factor.reshape(1), *inputs, *grads)
    return [results[4 * n : 4 * n + 4] for n in range(len(arrays))]


def shards(
    token_ids,
    targets,
    segments,
    completion,
    micro_order,
    *state,
):
    weights, means, squares_in = state[:7], state[7:14], state[14:21]
    embedding, attn_in, attn_out, ffn_in, ffn_out, head_table, norm_gains = weights
    group = lax.axis_size("dp")
    parts = lax.axis_size("tensor")
    own, rank = lax.axis_index("dp"), lax.axis_index("tensor")
    vocab, width = embedding.shape
    start = rank * vocab
    seqs, length = token_ids.shape
    micro = micro_order.shape[1]
    share = length // parts
    turn = jnp.array(TURN, jnp.int32)
    dp_order = own ^ jnp.arange(group, dtype=jnp.int32)
    tensor_order = rank ^ turn
    tensor_order_natural = rank ^ jnp.arange(parts, dtype=jnp.int32)
    ffn = ffn_out.shape[0]
    qkv_width = attn_in.shape[1]

    attn_block = jnp.concatenate([attn_in, attn_out.T], axis=1).astype(HALF)
    ffn_block = jnp.concatenate([ffn_in.reshape(width, -1), ffn_out.T], axis=1).astype(HALF)
    bit = own % 2
    entries = vocab // 2
    low_half, high_half = head_table[:, :entries].astype(HALF), head_table[:, entries:].astype(HALF)
    stays = jnp.where(bit == 0, low_half, high_half)
    leaves = jnp.where(bit == 0, high_half, low_half)
    lines = [[i for i in range(group) if i % 2 == odd] for odd in (0, 1)]

    flags = completion.astype(FLOAT)
    picked_rows = micro_order[0]
    local_counts = jnp.sum(completion, axis=1)[picked_rows]
    id_rows = seqs * length // LANES
    packed = jnp.concatenate(
        [
            token_ids.reshape(-1),
            targets.reshape(-1),
            completion.reshape(-1),
            jnp.pad(jnp.concatenate([local_counts, picked_rows]), (0, 8 * LANES - 2 * micro)),
        ]
    ).reshape(3 * id_rows + 8, LANES)
    gains = jnp.pad(norm_gains.astype(HALF).astype(FLOAT), ((0, 5), (0, LANES - width)))
    if group == 8:
        packed, every_id, gains = spread(packed, gains, seqs, length, vocab, width)
        every_id = every_id.reshape(-1)
    else:
        packed, gains = lax.all_gather(packed, "dp"), lax.all_gather(gains, "dp")
        packed = jnp.take(packed, dp_order, axis=0)
        every_id = packed[:, :id_rows].reshape(group, seqs, parts, share)
        every_id = jnp.take(every_id, tensor_order, axis=2)
        every_id = every_id.transpose(2, 0, 1, 3).reshape(-1) - start
        every_id = jnp.where((every_id >= 0) & (every_id < vocab), every_id, vocab)
        gains = gains.transpose(1, 0, 2)[:, :, :width].reshape(8, -1)
    packed, leaves = lax.optimization_barrier((packed, leaves))
    gains = gains[:3]
    numbers = packed[:, 3 * id_rows, : 2 * micro]
    counts = jnp.sum(numbers[:, :micro].astype(FLOAT), axis=0)

    def both_order(values):
        values = jnp.take(values.reshape(seqs, parts, share), tensor_order, axis=1)
        return values.transpose(1, 0, 2).reshape(-1)

    own_segment = segments[:, :, None] == jnp.arange(8, dtype=jnp.int32)
    sizes = jnp.sum(own_segment.astype(jnp.int32), axis=1)
    begins = jnp.cumsum(sizes, axis=1) - sizes
    first = jnp.sum(jnp.where(own_segment, begins[:, None, :], 0), axis=2)
    first = jnp.broadcast_to(first[:, None, :], (seqs, 8, length))
    base = turn[tensor_order_natural] * (seqs * share)
    cosine, sine = tables(length, HEAD_DIM)

    if group == 8:
        stream0, attn_norm, attn_w, head_rows = start_rows(
            every_id, embedding.T, gains[:1], attn_block, stays, leaves
        )
    else:
        rows = lookup(embedding.T, every_id).reshape(parts, group, seqs * share, width)
        rows = rows[:2] + swap(rows[2:], "tensor", 1)
        rows = rows[0] + swap(rows[1], "tensor", 2)
        rows = lax.all_to_all(jnp.take(rows, dp_order, axis=0), "dp", 0, 0)
        stream0 = rows.transpose(1, 0, 2).reshape(seqs * share, -1).astype(FLOAT)
        attn_norm = tensor_gather(normed(stream0, gains[0]).astype(HALF))

        attn_w = lax.all_gather(attn_block, "dp", axis=0, tiled=True)
        came = swap(leaves, "dp", 1)
        head_rows = jnp.concatenate(
            [jnp.where(bit == 0, stays, came), jnp.where(bit == 0, came, stays)], axis=0
        )
    attn_norm, ffn_block = lax.optimization_barrier((attn_norm, ffn_block))
    ffn_parts = gather_first(ffn_block)
    attn_in_b, attn_out_b = attn_w[:, :qkv_width], attn_w[:, qkv_width:]
    qkv = product(attn_in_b, attn_norm, 0, 1)
    attended, kept, log_sums = attend(base, qkv, cosine, sine, first)
    attended, ffn_block, head_rows = lax.optimization_barrier((attended, ffn_block, head_rows))
    head_b = lax.all_gather(head_rows, "dp", axis=0, tiled=True, axis_index_groups=lines)
    ffn_parts = gather_middle(ffn_block, ffn_parts)
    stream1, ffn_norm = forward_boundary(
        attended, attn_out_b, stream0, gains[1:2], [ffn_parts]
    )
    ffn_w = gather_last(ffn_parts)
    stream2, final_norm = wide_forward(ffn_norm, ffn_w, stream1, gains[2:])

    final_norm, packed = lax.optimization_barrier((final_norm, packed))
    rows_extra = []
    for k in (0, 1):
        its_flags = packed[k, 2 * id_rows : 3 * id_rows].reshape(seqs, length).astype(FLOAT)
        its_order = numbers[k, micro:]
        slot = jnp.argmax(its_order[None, :] == jnp.arange(seqs)[:, None], axis=1)
        its_scale = its_flags * (1.0 / jnp.maximum(counts, 1.0))[slot][:, None]
        aims = packed[k, id_rows : 2 * id_rows].reshape(seqs, length) - start - bit * entries
        aims = jnp.where((aims >= 0) & (aims < entries), aims, -1).astype(FLOAT)
        rows_extra.append(jnp.stack([both_order(its_scale), both_order(aims)]))
    extra = jnp.pad(jnp.concatenate(rows_extra, axis=1), ((0, 6), (0, 0)))
    joint_flags = both_order(flags)
    logits, scan, final_turned = head_scan(final_norm, head_b, extra)
    info = merge_scans(scan, extra)
    tokens = seqs * length
    seq_loss = jnp.sum(
        ((info[0, :tokens] - info[1, :tokens]) * joint_flags).reshape(parts, seqs, share),
        axis=(0, 2),
    )
    g_head, d_final = head_grad(final_turned, head_b, info, logits)
    g_head = lax.psum_scatter(
        g_head, "dp", scatter_dimension=0, tiled=True, axis_index_groups=lines
    )
    g_stays = jnp.where(bit == 0, g_head[:width], g_head[width:])
    g_leaves = jnp.where(bit == 0, g_head[width:], g_head[:width])

    d_stream2, g_gain2, d_branch2 = wide_backward(d_final, stream2, gains[2:])
    d_stream1, g_gain1, d_branch1, g_ffn = backward_boundary(
        ffn_norm, d_branch2, ffn_w, stream1, gains[1:2], d_stream2
    )
    g_ffn_parts = scatter_first(g_ffn)
    d_attended = product(attn_out_b, d_branch1, 0, 1).astype(HALF)
    d_qkv = attend_back(base, kept, log_sums, d_attended, cosine, sine, first, [])
    g_attn_in = product(attn_norm, d_qkv, 0, 1).astype(HALF)
    g_attn_out = product(d_branch1, attended, 0, 1).astype(HALF)
    g_attn = jnp.concatenate([g_attn_in, g_attn_out], axis=1)
    g_attn_parts = scatter_first(g_attn)
    d_qkv, g_ffn = lax.optimization_barrier((d_qkv, g_ffn))
    g_ffn, g_ffn_leaves = scatter_middle(g_ffn, g_ffn_parts)
    if group == 8:
        rows, g_gains, g_came = end_rows(
            d_qkv,
            attn_in_b,
            stream0,
            gains[:1],
            d_stream1,
            g_gain1,
            g_gain2,
            g_leaves,
            width,
            g_ffn_leaves,
        )
    else:
        d_norm = tensor_scatter(product(d_qkv, attn_in_b, 0, 1))
        d_part, g_gain0 = normed_slope(d_norm, stream0, gains[:1])
        rows = (d_stream1 + d_part).astype(HALF)
        rows = rows.reshape(seqs * share, group, width).transpose(1, 0, 2)
        rows = jnp.take(lax.all_to_all(rows, "dp", 0, 0), dp_order, axis=0)
        rows = tensor_gather(rows[None]).reshape(-1, width)
        g_came = swap(g_leaves, "dp", 1)
        gain_sum = jnp.concatenate([g_gain0, g_gain1, g_gain2]).reshape(3, group, width)
        g_gains = jnp.take(lax.psum(gain_sum, ("dp", "tensor")), own, axis=1)
    g_head = [jnp.where(bit == 0, g_stays, g_came), jnp.where(bit == 0, g_came, g_stays)]
    rows, g_ffn, g_attn = lax.optimization_barrier((rows, g_ffn, g_attn))
    g_ffn = scatter_last(g_ffn, g_ffn_leaves)
    g_attn, g_attn_leaves = scatter_middle(g_attn, g_attn_parts)
    g_embed, squares = collect(rows, every_id, vocab, [g_ffn, *g_attn_leaves])
    squares, g_attn = lax.optimization_barrier((squares, g_attn))
    g_attn = scatter_last(g_attn, g_attn_leaves)

    owner = (rank == 0).astype(FLOAT)
    squared = jnp.sum(squares) + owner * jnp.sum(g_gains * g_gains)
    for part in (g_attn, g_ffn, *g_head):
        squared = squared + jnp.sum(part.astype(FLOAT) ** 2)
    losses = seq_loss[picked_rows] * owner
    if group == 8:
        sums = jnp.pad(jnp.concatenate([squared[None], losses]), (0, 8 * LANES - 1 - micro))
        sums = total_over_devices(jnp.broadcast_to(sums.reshape(1, 8, LANES), (8, 8, LANES)))
        squared, loss_sums = sums[0, 0], sums[0, 1 : 1 + micro]
    else:
        squared, loss_sums = lax.psum((squared, losses), ("dp", "tensor"))
    grad_norm = jnp.sqrt(squared)
    factor = CLIP / jnp.maximum(grad_norm, CLIP)
    g_parts = (
        [g_embed],
        [g_attn[:, :qkv_width]],
        [g_attn[:, qkv_width:].T],
        [g_ffn[:, : 2 * ffn].reshape(ffn_in.shape)],
        [g_ffn[:, 2 * ffn :]],
        g_head,
    )
    arrays = []
    for place in range(6):
        entry = (weights[place], means[place], squares_in[place])
        if place in (0, 4):
            entry = tuple(array.T for array in entry)
        arrays.append((*entry, g_parts[place]))
    updated = []
    for place, results in enumerate(update(arrays, factor)):
        updated.extend(result.T if place in (0, 4) else result for result in results)
    updated.extend(adam(norm_gains, g_gains * factor, means[6], squares_in[6], LR_GAIN, 0.0))
    return (jnp.stack([loss_sums, counts]), grad_norm, *updated)


def solution(mesh):
    in_specs = (
        P("dp", None),
        P("dp", None),
        P("dp", None),
        P("dp", None),
        P("dp", None),
        P("tensor", "dp"),
        P("dp", "tensor"),
        P("tensor", "dp"),
        P("dp", None, "tensor"),
        P("tensor", "dp"),
        P("dp", "tensor"),
        P(None, "dp"),
        P("tensor", "dp"),
        P("dp", "tensor"),
        P("tensor", "dp"),
        P("dp", None, "tensor"),
        P("tensor", "dp"),
        P("dp", "tensor"),
        P(None, "dp"),
        P("tensor", "dp"),
        P("dp", "tensor"),
        P("tensor", "dp"),
        P("dp", None, "tensor"),
        P("tensor", "dp"),
        P("dp", "tensor"),
        P(None, "dp"),
    )
    out_specs = (
        P(),
        P(),
        P("tensor", "dp"),
        P("tensor", "dp"),
        P("tensor", "dp"),
        P("tensor", "dp"),
        P("dp", "tensor"),
        P("dp", "tensor"),
        P("dp", "tensor"),
        P("dp", "tensor"),
        P("tensor", "dp"),
        P("tensor", "dp"),
        P("tensor", "dp"),
        P("tensor", "dp"),
        P("dp", None, "tensor"),
        P("dp", None, "tensor"),
        P("dp", None, "tensor"),
        P("dp", None, "tensor"),
        P("tensor", "dp"),
        P("tensor", "dp"),
        P("tensor", "dp"),
        P("tensor", "dp"),
        P("dp", "tensor"),
        P("dp", "tensor"),
        P("dp", "tensor"),
        P("dp", "tensor"),
        P(None, "dp"),
        P(None, "dp"),
        P(None, "dp"),
        P(None, "dp"),
    )
    return jax.shard_map(shards, mesh=mesh, in_specs=in_specs, out_specs=out_specs, check_vma=False)
```

```python
import functools

import jax
import jax.numpy as jnp
import numpy as np
from jax import lax
from jax.experimental import pallas as pl
from jax.experimental.pallas import tpu as pltpu
from jax.sharding import PartitionSpec as P

HEAD_DIM = 64
STEP = 10


EPS = 1e-05
CLIP = 0.01
LR = 0.03
LR_GAIN = 0.5
BETA_ONE = 0.9
BETA_TWO = 0.95
ADAM_EPS = 1e-08
DECAY = 0.1
NEG = -1e30
FLOAT = jnp.float32
HALF = jnp.bfloat16
LANES = 128
ROWS = 1024
VMEM_LIMIT = 56 * 2**20
TILE = 512
CHUNK = 256
MESH = pl.DeviceIdType.MESH
SMALL = pl.CostEstimate(flops=2**20, bytes_accessed=2**20, transcendentals=0)

TURN = (0, 2, 1, 3)


def swap(value, axis, bit):
    pairs = [(i, i ^ bit) for i in range(lax.axis_size(axis))]
    return lax.ppermute(value, axis, pairs)


def normed(values, gain):
    return values * lax.rsqrt(jnp.mean(values * values, axis=-1, keepdims=True) + EPS) * gain


def tables(length, width):
    inverse = np.float32(10000.0) ** (-np.arange(0, width, 2, dtype=np.float32) / np.float32(width))
    angle = inverse[:, None] * np.arange(length, dtype=np.float32)[None, :]
    return jnp.asarray(np.cos(angle)), jnp.asarray(np.sin(angle))


def block_of(full, k):
    rows = full.shape[0] // lax.axis_size("dp")
    own = lax.axis_index("dp")
    return lax.dynamic_slice(full, ((own ^ k) * rows, 0), (rows, full.shape[1]))


def scatter_first(full):
    if lax.axis_size("dp") != 8:
        return []
    leaves = jnp.concatenate([block_of(full, k + 1) for k in (0, 2, 4, 6)], axis=0)
    return [swap(leaves, "dp", 1)]


def scatter_middle(full, parts):
    if lax.axis_size("dp") != 8:
        return full, []
    rows = full.shape[0] // 8
    sums = [
        block_of(full, 2 * n).astype(FLOAT) + parts[0][n * rows : (n + 1) * rows].astype(FLOAT)
        for n in range(4)
    ]
    return sums[0], [total.astype(HALF) for total in sums[1:]]


def scatter_last(total, leaves):
    if lax.axis_size("dp") != 8:
        return lax.psum_scatter(total.astype(FLOAT), "dp", scatter_dimension=0, tiled=True)
    for n, leave in enumerate(leaves):
        total = total + swap(leave, "dp", 2 * n + 2).astype(FLOAT)
    return total


def peers_of(own, rank, bits, axis):
    if axis == "dp":
        return [(own ^ k, rank) for k in bits]
    return [(own, rank ^ k) for k in bits]


def greet(peers):
    barrier = pltpu.get_barrier_semaphore()
    for peer in peers:
        pl.semaphore_signal(barrier, inc=1, device_id=peer, device_id_type=MESH)
    pl.semaphore_wait(barrier, len(peers))


def spread_kernel(vocab, seqs, numbers, gains, every, ids, all_gains, every_gain, send, recv):
    own, rank = lax.axis_index("dp"), lax.axis_index("tensor")
    peers = peers_of(own, rank, range(1, 8), "dp")
    greet(peers)
    every[0] = numbers[...]
    every_gain[0] = gains[...]
    copies = []
    for k in range(1, 8):
        for n, (source, target) in enumerate(((numbers, every), (gains, every_gain))):
            copies.append(
                pltpu.make_async_remote_copy(
                    src_ref=source,
                    dst_ref=target.at[k],
                    send_sem=send.at[n, k],
                    recv_sem=recv.at[n, k],
                    device_id=peers[k - 1],
                    device_id_type=MESH,
                )
            )
            copies[-1].start()
    for copy in copies:
        copy.wait()
    lines = ids.shape[0] // (32 * seqs)
    for p in range(4):
        shard = rank ^ TURN[p]
        for k in range(8):
            for j in range(seqs):
                local = every[k, pl.ds((j * 4 + shard) * lines, lines), :] - rank * vocab
                local = jnp.where((local >= 0) & (local < vocab), local, vocab)
                ids[pl.ds(((p * 8 + k) * seqs + j) * lines, lines), :] = local
    width = all_gains.shape[1] // 8
    for b in range(8):
        all_gains[:, b * width : (b + 1) * width] = every_gain[own ^ b][:, :width]


def spread(numbers, gains, seqs, length, vocab, width):
    vmem = pl.BlockSpec(memory_space=pltpu.VMEM)
    return pl.pallas_call(
        functools.partial(spread_kernel, vocab, seqs),
        in_specs=[vmem] * 2,
        out_specs=[vmem] * 3,
        out_shape=[
            jax.ShapeDtypeStruct((8, *numbers.shape), numbers.dtype),
            jax.ShapeDtypeStruct((8 * seqs * length // LANES, LANES), jnp.int32),
            jax.ShapeDtypeStruct((8, 8 * width), FLOAT),
        ],
        scratch_shapes=[
            pltpu.VMEM((8, *gains.shape), FLOAT),
            pltpu.SemaphoreType.DMA((2, 8)),
            pltpu.SemaphoreType.DMA((2, 8)),
        ],
        compiler_params=pltpu.CompilerParams(collective_id=1, has_side_effects=True),
        cost_estimate=SMALL,
        name="spread",
    )(numbers, gains)


def total_kernel(blocks, out, first, summed, second, send, recv):
    own, rank = lax.axis_index("dp"), lax.axis_index("tensor")
    near = peers_of(own, rank, range(1, 4), "tensor")
    far = peers_of(own, rank, range(1, 8), "dp")
    greet(near + far)
    copies = []
    for k in range(1, 4):
        copy = pltpu.make_async_remote_copy(
            src_ref=blocks,
            dst_ref=first.at[k - 1],
            send_sem=send.at[k - 1],
            recv_sem=recv.at[k - 1],
            device_id=near[k - 1],
            device_id_type=MESH,
        )
        copy.start()
        copies.append(copy)
    for copy in copies:
        copy.wait()
    summed[...] = (blocks[...] + first[0]) + (first[1] + first[2])
    copies = []
    for k in range(1, 8):
        copy = pltpu.make_async_remote_copy(
            src_ref=summed.at[k],
            dst_ref=second.at[k],
            send_sem=send.at[2 + k],
            recv_sem=recv.at[2 + k],
            device_id=far[k - 1],
            device_id_type=MESH,
        )
        copy.start()
        copies.append(copy)
    for copy in copies:
        copy.wait()
    second[0] = summed[0]
    pairs = [second[k] + second[k + 1] for k in (0, 2, 4, 6)]
    out[...] = (pairs[0] + pairs[1]) + (pairs[2] + pairs[3])


def total_over_devices(blocks):
    shape = blocks.shape
    return pl.pallas_call(
        total_kernel,
        in_specs=[pl.BlockSpec(memory_space=pltpu.VMEM)],
        out_specs=pl.BlockSpec(memory_space=pltpu.VMEM),
        out_shape=jax.ShapeDtypeStruct(shape[1:], FLOAT),
        scratch_shapes=[
            pltpu.VMEM((3, *shape), FLOAT),
            pltpu.VMEM(shape, FLOAT),
            pltpu.VMEM(shape, FLOAT),
            pltpu.SemaphoreType.DMA((10,)),
            pltpu.SemaphoreType.DMA((10,)),
        ],
        compiler_params=pltpu.CompilerParams(collective_id=2, has_side_effects=True),
        name="total",
    )(blocks)


def tensor_gather(block):
    half = jnp.concatenate([block, swap(block, "tensor", 2)], axis=0)
    return jnp.concatenate([half, swap(half, "tensor", 1)], axis=0)


def tensor_scatter(full):
    half = full.shape[0] // 2
    quarter = half // 2
    both = full[:half] + swap(full[half:], "tensor", 1)
    there = swap(both[quarter:].astype(HALF), "tensor", 2)
    return both[:quarter] + there.astype(FLOAT)


def lookup_kernel(ids, turned, out, table, corner, rows):
    count = rows.shape[0]
    width, vocab = turned.shape

    @pl.when(pl.program_id(0) == 0)
    def _():
        corner[...] = jnp.zeros_like(corner)
        for v in range(0, vocab, LANES):
            some = min(LANES, vocab - v)
            corner[:width, :some] = turned[:, v : v + some].astype(HALF).astype(FLOAT)
            if some < LANES:
                corner[:width, some:] = jnp.zeros((width, LANES - some), FLOAT)
            table[v : v + LANES, :] = corner[...].T
        if vocab % LANES == 0:
            table[vocab:, :] = jnp.zeros((LANES, LANES), FLOAT)

    def body(i, carry):
        for u in range(16):
            r = i * 16 + u
            rows[pl.ds(r, 1), :] = table[pl.ds(ids[0, 0, r], 1), :]
        return carry

    lax.fori_loop(0, count // 16, body, 0)
    out[...] = rows[:, : out.shape[1]].astype(HALF)


def lookup(turned, ids):
    count = ids.shape[0]
    width, vocab = turned.shape
    padded = (vocab // LANES + 1) * LANES
    return pl.pallas_call(
        lookup_kernel,
        grid=(count // ROWS,),
        in_specs=[
            pl.BlockSpec((1, 1, ROWS), lambda i: (i, 0, 0), memory_space=pltpu.SMEM),
            pl.BlockSpec(turned.shape, lambda i: (0, 0), pipeline_mode=pl.Buffered(1)),
        ],
        out_specs=pl.BlockSpec((ROWS, width), lambda i: (i, 0)),
        out_shape=jax.ShapeDtypeStruct((count, width), HALF),
        scratch_shapes=[
            pltpu.VMEM((padded, LANES), FLOAT),
            pltpu.VMEM((LANES, LANES), FLOAT),
            pltpu.VMEM((ROWS, LANES), FLOAT),
        ],
        compiler_params=pltpu.CompilerParams(vmem_limit_bytes=VMEM_LIMIT),
        cost_estimate=SMALL,
        name="lookup",
    )(ids.reshape(count // ROWS, 1, ROWS), turned)


def collect_kernel(waits, ids, grads, *refs):
    out, squares, rows, *sums = refs[waits:]
    step = pl.program_id(0)
    count = rows.shape[0]
    width, vocab = out.shape

    @pl.when(step == 0)
    def _():
        rows[...] = jnp.zeros_like(rows)
        for total in sums:
            total[...] = jnp.zeros_like(total)

    rows[:, :width] = grads[...].astype(FLOAT)

    def body(i, carry):
        for u in range(16):
            r = i * 16 + u
            total = sums[u % len(sums)]
            place = pl.ds(ids[0, 0, r], 1)
            total[place, :] = total[place, :] + rows[pl.ds(r, 1), :]
        return carry

    lax.fori_loop(0, count // 16, body, 0)

    @pl.when(step == pl.num_programs(0) - 1)
    def _():
        squared = jnp.zeros((8, LANES), FLOAT)
        for v in range(0, vocab, LANES):
            some = min(LANES, vocab - v)
            total = sums[0][v : v + some, :]
            for other in sums[1:]:
                total = total + other[v : v + some, :]
            for r in range(0, some, 8):
                squared = squared + total[r : r + 8, :] * total[r : r + 8, :]
            if some < LANES:
                total = jnp.concatenate([total, jnp.zeros((LANES - some, LANES), FLOAT)], axis=0)
            out[:, v : v + some] = total.T[:width, :some]
        squares[...] = squared


def collect(grads, ids, vocab, before):
    count = ids.shape[0]
    width = grads.shape[1]
    padded = (vocab // LANES + 1) * LANES
    return pl.pallas_call(
        functools.partial(collect_kernel, len(before)),
        grid=(count // ROWS,),
        in_specs=[
            pl.BlockSpec((1, 1, ROWS), lambda i: (i, 0, 0), memory_space=pltpu.SMEM),
            pl.BlockSpec((ROWS, width), lambda i: (i, 0)),
        ]
        + [pl.BlockSpec(memory_space=pl.ANY)] * len(before),
        out_specs=[
            pl.BlockSpec((width, vocab), lambda i: (0, 0)),
            pl.BlockSpec((8, LANES), lambda i: (0, 0)),
        ],
        out_shape=[
            jax.ShapeDtypeStruct((width, vocab), FLOAT),
            jax.ShapeDtypeStruct((8, LANES), FLOAT),
        ],
        scratch_shapes=[pltpu.VMEM((ROWS, LANES), FLOAT)]
        + [pltpu.VMEM((padded, LANES), FLOAT)] * 8,
        compiler_params=pltpu.CompilerParams(vmem_limit_bytes=VMEM_LIMIT),
        cost_estimate=SMALL,
        name="collect",
    )(ids.reshape(count // ROWS, 1, ROWS), grads, *before)


def edge_of(vocab):
    return vocab - (pl.cdiv(vocab, TILE) - 1) * TILE


def each_tile(vocab, work):
    last = edge_of(vocab)
    if last == TILE:
        work(TILE)
    else:
        step, steps = pl.program_id(0), pl.num_programs(0)
        pl.when(step < steps - 1)(lambda: work(TILE))
        pl.when(step == steps - 1)(lambda: work(last))


def turned_rows(rows):
    return jnp.concatenate([rows] * (LANES // 8), axis=0).T


def scan_kernel(vocab, norm, weight, target, logits, stats, turned, peak, total, hit, aims):
    step = pl.program_id(0)
    rows = norm.shape[0]

    @pl.when(step == 0)
    def _():
        peak[...] = jnp.full_like(peak, NEG)
        total[...] = jnp.zeros_like(total)
        hit[...] = jnp.zeros_like(hit)
        aims[...] = turned_rows(target[...])
        for r in range(0, rows, CHUNK):
            turned[:, r : r + CHUNK] = norm[r : r + CHUNK, :].T

    def work(width):
        lane = lax.broadcasted_iota(jnp.int32, (CHUNK, LANES), 1)
        for r in range(0, rows, CHUNK):
            part = pl.ds(r, CHUNK)
            value = jnp.dot(norm[part, :], weight[...], preferred_element_type=FLOAT)
            logits[part, :] = value
            aim = aims[part, 1:2].astype(jnp.int32) - step * TILE
            slabs, found = [], hit[part, :]
            for c in range(0, width, LANES):
                slab = value[:, c : c + LANES]
                if c + LANES > width:
                    slab = jnp.where(lane < width - c, slab, NEG)
                slabs.append(slab)
                found = found + jnp.where(lane == aim - c, slab, 0.0)
            hit[part, :] = found
            before = peak[part, :]
            top = functools.reduce(jnp.maximum, slabs, before)
            added = total[part, :] * jnp.exp(before - top)
            for slab in slabs:
                added = added + jnp.exp(slab - top)
            total[part, :] = added
            peak[part, :] = top

    each_tile(vocab, work)

    @pl.when(step == pl.num_programs(0) - 1)
    def _():
        top = jnp.max(peak[...], axis=1, keepdims=True)
        added = jnp.sum(total[...] * jnp.exp(peak[...] - top), axis=1, keepdims=True)
        found = jnp.sum(hit[...], axis=1, keepdims=True)
        lane = lax.broadcasted_iota(jnp.int32, (rows, LANES), 1)
        joined = jnp.where(lane == 0, top, jnp.where(lane == 1, added, found))
        stats[...] = joined.T[:8, :]


def head_scan(norm, weight, extra):
    rows, depth = norm.shape
    vocab = weight.shape[1]
    return pl.pallas_call(
        functools.partial(scan_kernel, vocab),
        grid=(pl.cdiv(vocab, TILE),),
        in_specs=[
            pl.BlockSpec((rows, depth), lambda i: (0, 0), pipeline_mode=pl.Buffered(1)),
            pl.BlockSpec((depth, TILE), lambda i: (0, i)),
            pl.BlockSpec((8, rows), lambda i: (0, 0)),
        ],
        out_specs=[
            pl.BlockSpec((rows, TILE), lambda i: (0, i)),
            pl.BlockSpec((8, rows), lambda i: (0, 0)),
            pl.BlockSpec((depth, rows), lambda i: (0, 0), pipeline_mode=pl.Buffered(1)),
        ],
        out_shape=[
            jax.ShapeDtypeStruct((rows, vocab), FLOAT),
            jax.ShapeDtypeStruct((8, rows), FLOAT),
            jax.ShapeDtypeStruct((depth, rows), HALF),
        ],
        scratch_shapes=[pltpu.VMEM((rows, LANES), FLOAT)] * 4,
        compiler_params=pltpu.CompilerParams(vmem_limit_bytes=VMEM_LIMIT),
        cost_estimate=SMALL,
        name="head_scan",
    )(norm, weight, extra)


def grad_kernel(vocab, turned, weight, info, logits, grad, out, total, slope, columns):
    step = pl.program_id(0)
    rows = logits.shape[0]

    @pl.when(step == 0)
    def _():
        columns[...] = turned_rows(info[...])
        total[...] = jnp.zeros_like(total)

    def work(width):
        lane = lax.broadcasted_iota(jnp.int32, (CHUNK, TILE), 1)
        table = weight[...]
        if width < TILE:
            table = jnp.where(lax.broadcasted_iota(jnp.int32, table.shape, 1) < width, table, 0.0)
        for r in range(0, rows, CHUNK):
            part = pl.ds(r, CHUNK)
            aim = columns[part, 3:4].astype(jnp.int32) - step * TILE
            value = jnp.exp(logits[part, :] - columns[part, 0:1])
            value = (value - jnp.where(lane == aim, 1.0, 0.0)) * columns[part, 2:3]
            if width < TILE:
                value = jnp.where(lane < width, value, 0.0)
            value = value.astype(HALF)
            slope[part, :] = value
            total[part, :] = total[part, :] + lax.dot_general(
                value, table, (((1,), (1,)), ((), ())), preferred_element_type=FLOAT
            )
        grad[...] = jnp.dot(turned[...], slope[...], preferred_element_type=FLOAT).astype(HALF)

    each_tile(vocab, work)

    @pl.when(step == pl.num_programs(0) - 1)
    def _():
        for r in range(0, rows, CHUNK):
            out[pl.ds(r, CHUNK), :] = total[pl.ds(r, CHUNK), :].astype(HALF)


def head_grad(turned, weight, info, logits):
    depth, rows = turned.shape
    vocab = weight.shape[1]
    return pl.pallas_call(
        functools.partial(grad_kernel, vocab),
        grid=(pl.cdiv(vocab, TILE),),
        in_specs=[
            pl.BlockSpec((depth, rows), lambda i: (0, 0), pipeline_mode=pl.Buffered(1)),
            pl.BlockSpec((depth, TILE), lambda i: (0, i)),
            pl.BlockSpec((8, rows), lambda i: (0, 0)),
            pl.BlockSpec((rows, TILE), lambda i: (0, i)),
        ],
        out_specs=[
            pl.BlockSpec((depth, TILE), lambda i: (0, i)),
            pl.BlockSpec((rows, depth), lambda i: (0, 0), pipeline_mode=pl.Buffered(1)),
        ],
        out_shape=[
            jax.ShapeDtypeStruct((depth, vocab), HALF),
            jax.ShapeDtypeStruct((rows, depth), HALF),
        ],
        scratch_shapes=[
            pltpu.VMEM((rows, depth), FLOAT),
            pltpu.VMEM((rows, TILE), HALF),
            pltpu.VMEM((rows, LANES), FLOAT),
        ],
        compiler_params=pltpu.CompilerParams(vmem_limit_bytes=VMEM_LIMIT),
        cost_estimate=SMALL,
        name="head_grad",
    )(turned, weight, info, logits)


def turn_rows(low, high, cosine, sine):
    return low * cosine - high * sine, high * cosine + low * sine


def reach(block, share, longest):
    back = -(-(longest - 1) // share)
    return max(0, block - back) * share


def seen(first, low, high, place):
    keys = low + lax.broadcasted_iota(jnp.int32, (high - low, first.shape[1]), 0)
    queries = place + lax.broadcasted_iota(jnp.int32, (high - low, first.shape[1]), 1)
    return (keys >= first) & (keys <= queries)


def attend_kernel(base, qkv, cosine, sine, first, attended, kept, log_total):
    seq = pl.program_id(1)
    blocks = base.shape[0]
    length = cosine.shape[1]
    share = length // blocks
    half = HEAD_DIM // 2

    def spot(i):
        return pl.ds(pl.multiple_of(base[i] + seq * share, share), share)

    for i in range(blocks):
        at = pl.ds(i * share, share)
        turns = (cosine[:, at], sine[:, at])
        for c in (0, 1):
            top = c * HEAD_DIM
            low, high = turn_rows(
                qkv[top : top + half, spot(i)], qkv[top + half : top + HEAD_DIM, spot(i)], *turns
            )
            kept[0, top : top + half, at] = low.astype(HALF)
            kept[0, top + half : top + HEAD_DIM, at] = high.astype(HALF)
        kept[0, 2 * HEAD_DIM :, at] = qkv[2 * HEAD_DIM :, spot(i)].astype(HALF)
    key = kept[0, HEAD_DIM : 2 * HEAD_DIM, :].T
    for i in range(blocks):
        low, high = reach(i, share, length // 2), (i + 1) * share
        at = pl.ds(i * share, share)
        scores = jnp.dot(
            key[low:high, :], kept[0, :HEAD_DIM, at], preferred_element_type=FLOAT
        ) * (HEAD_DIM**-0.5)
        scores = jnp.where(seen(first[0, :, at][:1], low, high, i * share), scores, NEG)
        peak = jnp.max(scores, axis=0, keepdims=True)
        expo = jnp.exp(scores - peak)
        summed = jnp.sum(expo, axis=0, keepdims=True)
        probs = (expo * (1.0 / summed)).astype(HALF)
        value = kept[0, 2 * HEAD_DIM :, low:high]
        attended[:, spot(i)] = jnp.dot(value, probs, preferred_element_type=FLOAT).astype(HALF)
        log_total[0, 0, :, at] = jnp.broadcast_to(peak + jnp.log(summed), (8, share))


def attend(base, qkv, cosine, sine, first):
    seqs, length = first.shape[0], first.shape[2]
    heads = qkv.shape[0] // (3 * HEAD_DIM)
    tokens = qkv.shape[1]
    return pl.pallas_call(
        attend_kernel,
        grid=(heads, seqs),
        in_specs=[
            pl.BlockSpec(memory_space=pltpu.SMEM),
            pl.BlockSpec((3 * HEAD_DIM, tokens), lambda h, j: (h, 0)),
            pl.BlockSpec(cosine.shape, lambda h, j: (0, 0)),
            pl.BlockSpec(sine.shape, lambda h, j: (0, 0)),
            pl.BlockSpec((1, 8, length), lambda h, j: (j, 0, 0)),
        ],
        out_specs=[
            pl.BlockSpec((HEAD_DIM, tokens), lambda h, j: (h, 0)),
            pl.BlockSpec((1, 3 * HEAD_DIM, length), lambda h, j: (j, h, 0)),
            pl.BlockSpec((1, 1, 8, length), lambda h, j: (j, h, 0, 0)),
        ],
        out_shape=[
            jax.ShapeDtypeStruct((heads * HEAD_DIM, tokens), HALF),
            jax.ShapeDtypeStruct((seqs, heads * 3 * HEAD_DIM, length), HALF),
            jax.ShapeDtypeStruct((seqs, heads, 8, length), FLOAT),
        ],
        compiler_params=pltpu.CompilerParams(vmem_limit_bytes=VMEM_LIMIT),
        cost_estimate=SMALL,
        name="attend",
    )(base, qkv, cosine, sine, first)


def attend_back_kernel(waits, base, kept, log_total, slope, cosine, sine, first, *refs):
    d_qkv, d_key, d_value = refs[waits:]
    seq = pl.program_id(1)
    blocks = base.shape[0]
    length = cosine.shape[1]
    share = length // blocks
    half = HEAD_DIM // 2
    scale = HEAD_DIM**-0.5

    def spot(i):
        return pl.ds(pl.multiple_of(base[i] + seq * share, share), share)

    def put(part, i, low, high):
        at = pl.ds(i * share, share)
        d_low, d_high = turn_rows(low, high, cosine[:, at], -sine[:, at])
        top = part * HEAD_DIM
        d_qkv[top : top + half, spot(i)] = d_low.astype(HALF)
        d_qkv[top + half : top + HEAD_DIM, spot(i)] = d_high.astype(HALF)

    query = kept[0, :HEAD_DIM, :].T
    key = kept[0, HEAD_DIM : 2 * HEAD_DIM, :].T
    value = kept[0, 2 * HEAD_DIM :, :].T
    d_key[...] = jnp.zeros_like(d_key)
    d_value[...] = jnp.zeros_like(d_value)
    for i in range(blocks):
        low, high = reach(i, share, length // 2), (i + 1) * share
        at = pl.ds(i * share, share)
        turned = slope[:, spot(i)]
        scores = jnp.dot(
            key[low:high, :], kept[0, :HEAD_DIM, at], preferred_element_type=FLOAT
        ) * scale
        scores = jnp.where(seen(first[0, :, at][:1], low, high, i * share), scores, NEG)
        probs = jnp.exp(scores - log_total[0, 0, :1, at])
        d_probs = jnp.dot(value[low:high, :], turned, preferred_element_type=FLOAT)
        centre = jnp.sum(probs * d_probs, axis=0, keepdims=True)
        d_scores = (probs * (d_probs - centre)).astype(HALF)
        d_value[low:high, :] += jnp.dot(probs.astype(HALF), turned.T, preferred_element_type=FLOAT)
        d_key[low:high, :] += jnp.dot(
            d_scores, query[i * share : (i + 1) * share, :], preferred_element_type=FLOAT
        )
        d_query = scale * jnp.dot(
            kept[0, HEAD_DIM : 2 * HEAD_DIM, low:high], d_scores, preferred_element_type=FLOAT
        )
        put(0, i, d_query[:half, :], d_query[half:, :])
    for i in range(blocks):
        rows = pl.ds(i * share, share)
        turned = scale * d_key[rows, :].T
        put(1, i, turned[:half, :], turned[half:, :])
        d_qkv[2 * HEAD_DIM :, spot(i)] = d_value[rows, :].T.astype(HALF)


def attend_back(base, kept, log_total, slope, cosine, sine, first, before):
    seqs, length = first.shape[0], first.shape[2]
    tokens = slope.shape[1]
    heads = slope.shape[0] // HEAD_DIM
    return pl.pallas_call(
        functools.partial(attend_back_kernel, len(before)),
        grid=(heads, seqs),
        in_specs=[
            pl.BlockSpec(memory_space=pltpu.SMEM),
            pl.BlockSpec((1, 3 * HEAD_DIM, length), lambda h, j: (j, h, 0)),
            pl.BlockSpec((1, 1, 8, length), lambda h, j: (j, h, 0, 0)),
            pl.BlockSpec((HEAD_DIM, tokens), lambda h, j: (h, 0)),
            pl.BlockSpec(cosine.shape, lambda h, j: (0, 0)),
            pl.BlockSpec(sine.shape, lambda h, j: (0, 0)),
            pl.BlockSpec((1, 8, length), lambda h, j: (j, 0, 0)),
        ]
        + [pl.BlockSpec(memory_space=pl.ANY)] * len(before),
        out_specs=pl.BlockSpec((3 * HEAD_DIM, tokens), lambda h, j: (h, 0)),
        out_shape=jax.ShapeDtypeStruct((heads * 3 * HEAD_DIM, tokens), HALF),
        scratch_shapes=[pltpu.VMEM((length, HEAD_DIM), FLOAT)] * 2,
        compiler_params=pltpu.CompilerParams(vmem_limit_bytes=VMEM_LIMIT),
        cost_estimate=SMALL,
        name="attend_back",
    )(base, kept, log_total, slope, cosine, sine, first, *before)


def near_and_far(own, rank):
    return (own, rank ^ 1), (own, rank ^ 2)


def remote(source, target, send, recv, n, peer):
    return pltpu.make_async_remote_copy(
        src_ref=source,
        dst_ref=target,
        send_sem=send.at[n],
        recv_sem=recv.at[n],
        device_id=peer,
        device_id_type=MESH,
    )


class Boundary:
    COUNT = 6

    def __init__(self, own, rank, send, recv, parts, rows):
        self.near, self.far = near_and_far(own, rank)
        self.send, self.recv, self.parts = send, recv, parts
        self.rows = [pl.ds(h * rows, rows) for h in range(parts)]
        self.copies = []

    def copy(self, source, target, n, h, peer):
        made = remote(source, target, self.send, self.recv, n * self.parts + h, peer)
        made.start()
        self.copies.append(made)
        return made

    def sums(self, make, partial, beside, away, come):
        later, crossing = {}, []

        def part(p, h):
            partial[p, self.rows[h], :] = make(p, h).astype(HALF)

        def leave(p, h):
            part(2 + p, h)
            at = self.rows[h]
            later[p, h] = self.copy(partial.at[2 + p, at], beside.at[p, at], p, h, self.near)

        def pair(p, h):
            at = self.rows[h]
            later[p, h].wait_recv()
            return partial[p, at, :].astype(FLOAT) + beside[p, at, :].astype(FLOAT)

        for h, at in enumerate(self.rows):
            leave(1, h)
            part(1, h)
            away[at, :] = pair(1, h).astype(HALF)
            crossing.append(self.copy(away.at[at], come.at[at], 2, h, self.far))
        for h in range(self.parts):
            leave(0, h)
        for h in range(self.parts):
            part(0, h)
        for h, at in enumerate(self.rows):
            total = pair(0, h)
            crossing[h].wait_recv()
            yield h, at, total + come[at, :].astype(FLOAT)

    def give(self, full, h):
        at = self.rows[h]
        self.crossed = getattr(self, "crossed", [])
        self.crossed.append(self.copy(full.at[0, at], full.at[1, at], 3, h, self.far))
        self.beside = getattr(self, "beside", [])
        self.beside.append(self.copy(full.at[0, at], full.at[2, at], 4, h, self.near))

    def pass_on(self, full):
        arrived = []
        for h, at in enumerate(self.rows):
            self.crossed[h].wait_recv()
            arrived.append(self.copy(full.at[1, at], full.at[3, at], 5, h, self.near))
        for copy in self.beside + arrived:
            copy.wait_recv()

    def end(self):
        for copy in self.copies:
            copy.wait_send()


def turned_product(left, right):
    return lax.dot_general(left, right, (((0,), (1,)), ((), ())), preferred_element_type=FLOAT)


def columns_of(array, p, h, parts):
    step = array.shape[1] // (4 * parts)
    return array[:, (p * parts + h) * step : (p * parts + h + 1) * step]


def rows_of(index, width):
    return pl.ds(pl.multiple_of(index * width, width), width)


def forward_kernel(parts, gathers, attended, both, stream, gain, *refs):
    blocks, refs = refs[:gathers], refs[gathers:]
    if gathers:
        out, full, feed_w, weight, partial, beside, away, come, send, recv = refs
    else:
        out, full, weight, partial, beside, away, come, send, recv = refs
    own, rank = lax.axis_index("dp"), lax.axis_index("tensor")
    near, far = near_and_far(own, rank)
    others = {k: (own ^ k, rank) for k in (1, 2, 6)} if gathers else {}
    greet([near, far, *others.values()])
    edge = Boundary(own, rank, send, recv, parts, stream.shape[0] // parts)
    moved = {}

    def move(source, k, n, peer):
        copy = remote(source, feed_w.at[rows_of(own ^ k, width)], send, recv, n, peer)
        copy.start()
        edge.copies.append(copy)
        return copy

    if gathers:
        mine, four = blocks
        width, base = mine.shape[0], Boundary.COUNT * parts
        for n, k in enumerate((2, 6)):
            moved[k] = move(mine, 0, base + n, others[k])
        moved[1] = move(mine, 0, base + 2, others[1])
        moved[5] = move(four, 4, base + 3, others[1])
        feed_w[rows_of(own, width), :] = mine[...]
        feed_w[rows_of(own ^ 4, width), :] = four[...]
    weight[...] = both[:, both.shape[1] - weight.shape[1] :]

    def make(p, h):
        return turned_product(columns_of(attended, p, h, parts), weight[...])

    for h, at, total in edge.sums(make, partial, beside, away, come):
        total = stream[at, :] + total
        out[at, :] = total
        full[0, at, :] = normed(total, gain[...]).astype(HALF)
        edge.give(full, h)
    if gathers:
        for n, k in enumerate((2, 6)):
            moved[k].wait_recv()
            moved[k + 1] = move(feed_w.at[rows_of(own ^ k, width)], k, base + 4 + n, others[1])
    edge.pass_on(full)
    for k in (1, 5, 3, 7) if gathers else ():
        moved[k].wait_recv()
    edge.end()


def forward_boundary(attended, both, stream, gain, blocks):
    rows, depth = stream.shape
    parts = 2
    vmem = pl.BlockSpec(memory_space=pltpu.VMEM)
    scratch = exchange_scratch(rows, depth, parts)[:4]
    semaphores = Boundary.COUNT * parts + 6
    results = pl.pallas_call(
        functools.partial(forward_kernel, parts, len(blocks)),
        in_specs=[vmem] * (4 + len(blocks)),
        out_specs=[vmem] * (3 if blocks else 2),
        out_shape=[
            jax.ShapeDtypeStruct((rows, depth), FLOAT),
            jax.ShapeDtypeStruct((4, rows, depth), HALF),
        ]
        + [jax.ShapeDtypeStruct((8 * b.shape[0], b.shape[1]), HALF) for b in blocks[:1]],
        scratch_shapes=[pltpu.VMEM((depth, attended.shape[0]), HALF)]
        + scratch
        + [pltpu.SemaphoreType.DMA((semaphores,))] * 2,
        compiler_params=pltpu.CompilerParams(
            collective_id=3, has_side_effects=True, vmem_limit_bytes=VMEM_LIMIT
        ),
        cost_estimate=SMALL,
        name="forward_boundary",
    )(attended, both, stream, gain, *blocks)
    return (results[0], results[1].reshape(4 * rows, depth), *results[2:])


def normed_slope(grad, values, gain):
    root = lax.rsqrt(jnp.mean(values * values, axis=-1, keepdims=True) + EPS)
    unit = values * root
    inner = grad * gain
    middle = jnp.mean(inner * unit, axis=-1, keepdims=True)
    return root * (inner - unit * middle), jnp.sum(grad * unit, axis=0, keepdims=True)


def wide_forward_kernel(
    norm, weight, stream, gain, out, full, partial, beside, away, come, send, recv
):
    own, rank = lax.axis_index("dp"), lax.axis_index("tensor")
    near, far = near_and_far(own, rank)
    other = (own ^ 1, rank)
    greet([near, far, other])
    parts = 2
    edge = Boundary(own, rank, send, recv, parts, stream.shape[0] // parts)
    crossed, moved, last = [], [], []
    ffn = weight.shape[1] // 3

    def make(p, h):
        both = jnp.dot(
            norm[p, edge.rows[h], :], weight[:, : 2 * ffn], preferred_element_type=FLOAT
        )
        gate, up = both[:, :ffn], both[:, ffn:]
        hidden = (gate * (1.0 / (1.0 + jnp.exp(-gate))) * up).astype(HALF)
        return across(hidden, weight[:, 2 * ffn :])

    for h, at, total in edge.sums(make, partial, beside, away, come):
        total = stream[at, :] + total
        out[at, :] = total
        full[0, 0, at, :] = normed(total, gain[...]).astype(HALF)
        mine = full.at[0, 0, at]
        crossed.append(edge.copy(mine, full.at[0, 1, at], 3, h, far))
        moved.append(edge.copy(mine, full.at[1, 0, at], 4, h, other))
        last.append(edge.copy(mine, full.at[0, 2, at], 5, h, near))
    early, late = edge.rows
    crossed[0].wait_recv()
    one = edge.copy(full.at[0, 1, early], full.at[1, 1, early], 6, 0, other)
    last.append(edge.copy(full.at[0, 1, early], full.at[0, 3, early], 7, 0, near))
    moved[0].wait_recv()
    last.append(edge.copy(full.at[1, 0, early], full.at[1, 2, early], 8, 0, near))
    moved[1].wait_recv()
    two = edge.copy(full.at[1, 0, late], full.at[1, 1, late], 6, 1, far)
    last.append(edge.copy(full.at[1, 0, late], full.at[1, 2, late], 8, 1, near))
    crossed[1].wait_recv()
    last.append(edge.copy(full.at[0, 1, late], full.at[0, 3, late], 7, 1, near))
    one.wait_recv()
    last.append(edge.copy(full.at[1, 1, early], full.at[1, 3, early], 9, 0, near))
    two.wait_recv()
    last.append(edge.copy(full.at[1, 1, late], full.at[1, 3, late], 9, 1, near))
    for copy in last:
        copy.wait_recv()
    edge.end()


def wide_forward(norm, weight, stream, gain):
    rows, depth = stream.shape
    vmem = pl.BlockSpec(memory_space=pltpu.VMEM)
    out, full = pl.pallas_call(
        wide_forward_kernel,
        in_specs=[vmem] * 4,
        out_specs=[vmem] * 2,
        out_shape=[
            jax.ShapeDtypeStruct((rows, depth), FLOAT),
            jax.ShapeDtypeStruct((2, 4, rows, depth), HALF),
        ],
        scratch_shapes=exchange_scratch(rows, depth, 2)[:4] + [pltpu.SemaphoreType.DMA((20,))] * 2,
        compiler_params=pltpu.CompilerParams(
            collective_id=9, has_side_effects=True, vmem_limit_bytes=VMEM_LIMIT
        ),
        cost_estimate=SMALL,
        name="wide_forward",
    )(norm.reshape(4, rows, depth), weight, stream, gain)
    return out, full.reshape(8 * rows, depth)


def wide_backward_kernel(partial, stream, gain, out, g_gain, full, beside, leave, come, send, recv):
    own, rank = lax.axis_index("dp"), lax.axis_index("tensor")
    near, far = near_and_far(own, rank)
    other = (own ^ 1, rank)
    greet([near, far, other])
    parts = 2
    edge = Boundary(own, rank, send, recv, parts, stream.shape[0] // parts)
    early, late = edge.rows
    first = {}
    for n, (y, p) in enumerate(((1, 1), (1, 0), (0, 1), (0, 0))):
        for h, at in enumerate(edge.rows):
            first[y, p, h] = edge.copy(
                partial.at[y, 2 + p, at], beside.at[y, p, at], 5 + n, h, near
            )

    def pair(y, p, h):
        at = edge.rows[h]
        first[y, p, h].wait_recv()
        return partial[y, p, at, :].astype(FLOAT) + beside[y, p, at, :].astype(FLOAT)

    leave[1, 1, early, :] = pair(1, 1, 0).astype(HALF)
    by_other = edge.copy(leave.at[1, 1, early], come.at[1, 1, early], 9, 0, other)
    leave[1, 1, late, :] = pair(1, 1, 1).astype(HALF)
    by_far = edge.copy(leave.at[1, 1, late], come.at[1, 1, late], 9, 1, far)
    leave[1, 0, early, :] = pair(1, 0, 0).astype(HALF)
    other_early = edge.copy(leave.at[1, 0, early], come.at[1, 0, early], 0, 0, other)
    leave[0, 1, late, :] = pair(0, 1, 1).astype(HALF)
    far_late = edge.copy(leave.at[0, 1, late], come.at[0, 1, late], 1, 1, far)
    far_early_sum, other_late_sum = pair(0, 1, 0), pair(1, 0, 1)
    by_other.wait_recv()
    leave[0, 1, early, :] = (far_early_sum + come[1, 1, early, :].astype(FLOAT)).astype(HALF)
    far_early = edge.copy(leave.at[0, 1, early], come.at[0, 1, early], 1, 0, far)
    by_far.wait_recv()
    leave[1, 0, late, :] = (other_late_sum + come[1, 1, late, :].astype(FLOAT)).astype(HALF)
    other_late = edge.copy(leave.at[1, 0, late], come.at[1, 0, late], 0, 1, other)
    g_gain[...] = jnp.zeros_like(g_gain)
    for h, waits in ((0, (other_early, far_early)), (1, (far_late, other_late))):
        at = edge.rows[h]
        total = pair(0, 0, h)
        for copy in waits:
            copy.wait_recv()
        total = total + come[1, 0, at, :].astype(FLOAT) + come[0, 1, at, :].astype(FLOAT)
        slope, by_gain = normed_slope(total, stream[at, :], gain[...])
        g_gain[:1, :] = g_gain[:1, :] + by_gain
        out[at, :] = slope
        full[0, at, :] = slope.astype(HALF)
        edge.crossed = getattr(edge, "crossed", [])
        edge.crossed.append(edge.copy(full.at[0, at], full.at[1, at], 2, h, far))
        edge.beside = getattr(edge, "beside", [])
        edge.beside.append(edge.copy(full.at[0, at], full.at[2, at], 3, h, near))
    arrived = []
    for h, at in enumerate(edge.rows):
        edge.crossed[h].wait_recv()
        arrived.append(edge.copy(full.at[1, at], full.at[3, at], 4, h, near))
    for copy in edge.beside + arrived:
        copy.wait_recv()
    edge.end()


def wide_backward(partial, stream, gain):
    rows, depth = stream.shape
    vmem = pl.BlockSpec(memory_space=pltpu.VMEM)
    out, g_gain, full = pl.pallas_call(
        wide_backward_kernel,
        in_specs=[vmem] * 3,
        out_specs=[vmem] * 3,
        out_shape=[
            jax.ShapeDtypeStruct((rows, depth), FLOAT),
            jax.ShapeDtypeStruct((8, depth), FLOAT),
            jax.ShapeDtypeStruct((4, rows, depth), HALF),
        ],
        scratch_shapes=[pltpu.VMEM((2, 2, rows, depth), HALF)] * 3
        + [pltpu.SemaphoreType.DMA((20,))] * 2,
        compiler_params=pltpu.CompilerParams(
            collective_id=4, has_side_effects=True, vmem_limit_bytes=VMEM_LIMIT
        ),
        cost_estimate=SMALL,
        name="wide_backward",
    )(partial.reshape(2, 4, rows, depth), stream, gain)
    return out, g_gain[:1], full.reshape(4 * rows, depth)


def exchange_scratch(rows, depth, parts):
    return [
        pltpu.VMEM((4, rows, depth), HALF),
        pltpu.VMEM((2, rows, depth), HALF),
        pltpu.VMEM((rows, depth), HALF),
        pltpu.VMEM((rows, depth), HALF),
        pltpu.SemaphoreType.DMA((Boundary.COUNT * parts,)),
        pltpu.SemaphoreType.DMA((Boundary.COUNT * parts,)),
    ]


def backward_kernel(
    parts, norm, later, weight, stream, gain, prior, out, g_gain, full, grad, partial, beside, away, come, kept, send, recv
):
    own, rank = lax.axis_index("dp"), lax.axis_index("tensor")
    greet(list(near_and_far(own, rank)))
    edge = Boundary(own, rank, send, recv, parts, stream.shape[0] // parts)
    ffn = weight.shape[1] // 3

    def make(p, h):
        at = edge.rows[h]
        both = jnp.dot(norm[p, at, :], weight[:, : 2 * ffn], preferred_element_type=FLOAT)
        d_hidden = jnp.dot(later[p, at, :], weight[:, 2 * ffn :], preferred_element_type=FLOAT)
        gate, up = both[:, :ffn], both[:, ffn:]
        open_part = 1.0 / (1.0 + jnp.exp(-gate))
        passed = gate * open_part
        d_gate = (d_hidden * up * (open_part * (1.0 + gate * (1.0 - open_part)))).astype(HALF)
        d_up = (d_hidden * passed).astype(HALF)
        kept[p, at, :ffn] = d_gate
        kept[p, at, ffn : 2 * ffn] = d_up
        kept[p, at, 2 * ffn :] = (passed * up).astype(HALF)
        return across(d_gate, weight[:, :ffn]) + across(d_up, weight[:, ffn : 2 * ffn])

    g_gain[...] = jnp.zeros_like(g_gain)
    for h, at, total in edge.sums(make, partial, beside, away, come):
        slope, by_gain = normed_slope(total, stream[at, :], gain[...])
        slope = slope + prior[at, :]
        g_gain[:1, :] = g_gain[:1, :] + by_gain
        out[at, :] = slope
        full[0, at, :] = slope.astype(HALF)
        edge.give(full, h)
    for left, low, high in ((norm, 0, 2 * ffn), (later, 2 * ffn, 3 * ffn)):
        turned = [left[p].T for p in range(4)]
        for c in range(low, high, CHUNK):
            total = jnp.dot(turned[0], kept[0, :, c : c + CHUNK], preferred_element_type=FLOAT)
            for p in (1, 2, 3):
                total = total + jnp.dot(
                    turned[p], kept[p, :, c : c + CHUNK], preferred_element_type=FLOAT
                )
            grad[:, c : c + CHUNK] = total.astype(HALF)
    edge.pass_on(full)
    edge.end()


def backward_boundary(norm, later, weight, stream, gain, prior):
    rows, depth = stream.shape
    parts = 2
    vmem = pl.BlockSpec(memory_space=pltpu.VMEM)
    scratch = exchange_scratch(rows, depth, parts)
    out, g_gain, full, grad = pl.pallas_call(
        functools.partial(backward_kernel, parts),
        in_specs=[vmem] * 6,
        out_specs=[vmem] * 4,
        out_shape=[
            jax.ShapeDtypeStruct((rows, depth), FLOAT),
            jax.ShapeDtypeStruct((8, depth), FLOAT),
            jax.ShapeDtypeStruct((4, rows, depth), HALF),
            jax.ShapeDtypeStruct(weight.shape, HALF),
        ],
        scratch_shapes=scratch[:4] + [pltpu.VMEM((4, rows, weight.shape[1]), HALF)] + scratch[4:],
        compiler_params=pltpu.CompilerParams(
            collective_id=5, has_side_effects=True, vmem_limit_bytes=VMEM_LIMIT
        ),
        cost_estimate=SMALL,
        name="backward_boundary",
    )(norm.reshape(4, rows, depth), later.reshape(4, rows, depth), weight, stream, gain, prior)
    return out, g_gain[:1], full.reshape(4 * rows, depth), grad


def start_kernel(
    ids, turned, gain, block, feed, stays, leaves, stream, full, weights, four, pair, *refs
):
    table, corner, rows, out, near, cross, come, send, recv, local = refs
    own, rank = lax.axis_index("dp"), lax.axis_index("tensor")
    beside, across = near_and_far(own, rank)
    far = [(own ^ k, rank) for k in range(1, 8)]
    greet([beside, across] + far)
    width, vocab = turned.shape
    count = rows.shape[0]
    copies, beside_of, across_of, far_of = [], {}, {}, {}

    def begin(source, target, n, peer):
        copy = remote(source, target, send, recv, n, peer)
        copy.start()
        copies.append(copy)
        return copy

    def place(k):
        return pl.ds(pl.multiple_of((own ^ k) * width, width), width)

    weights_of = {}
    for k in (1, 2, 4, 6):
        weights_of[k] = begin(block, weights.at[place(0)], 35 + k, far[k - 1])
    weights[place(0), :] = block[...]
    bit = own % 2
    line = pl.ds(pl.multiple_of(bit * width, width), width)
    aside = begin(leaves, pair.at[line], 43, far[0])
    own_line = pltpu.make_async_copy(stays, pair.at[line], local)
    own_line.start()
    corner[...] = jnp.zeros_like(corner)
    for v in range(0, vocab, LANES):
        some = min(LANES, vocab - v)
        corner[:width, :some] = turned[:, v : v + some].astype(HALF).astype(FLOAT)
        if some < LANES:
            corner[:width, some:] = jnp.zeros((width, LANES - some), FLOAT)
        table[v : v + LANES, :] = corner[...].T
    if vocab % LANES == 0:
        table[vocab:, :] = jnp.zeros((LANES, LANES), FLOAT)

    def fetch(place):
        def body(i, carry):
            for u in range(16):
                r = i * 16 + u
                rows[pl.ds(r, 1), :] = table[pl.ds(ids[place * count + r], 1), :]
            return carry

        lax.fori_loop(0, count // 16, body, 0)

    for p in (3, 2):
        for k in range(8):
            fetch(p * 8 + k)
            out[p, k] = rows[:, :width].astype(HALF)
            beside_of[p - 2, k] = begin(out.at[p, k], near.at[p - 2, k], (p - 2) * 8 + k, beside)
    for k in (2, 4, 6):
        weights_of[k].wait_recv()
        weights_of[k + 1] = begin(weights.at[place(k)], weights.at[place(k)], 36 + k, far[0])
    order = (7, 6, 5, 4, 3, 2, 1, 0)
    for k in order:
        fetch(8 + k)
        beside_of[1, k].wait_recv()
        total = rows[:, :width] + near[1, k].astype(FLOAT)
        out[1, k] = total.astype(HALF)
        across_of[k] = begin(out.at[1, k], cross.at[k], 16 + k, across)
    for k in order:
        fetch(k)
        beside_of[0, k].wait_recv()
        total = rows[:, :width] + near[0, k].astype(FLOAT)
        across_of[k].wait_recv()
        out[0, k] = (total + cross[k].astype(FLOAT)).astype(HALF)
        if k:
            far_of[k] = begin(out.at[0, k], come.at[k], 24 + k, far[k - 1])
    fourth = begin(feed, four, 44, far[3])
    come[0] = out[0, 0]
    for k in order[:-1]:
        far_of[k].wait_recv()
    for b in range(8):
        stream[:, b * width : (b + 1) * width] = come[own ^ b].astype(FLOAT)
    full[0] = normed(stream[...], gain[...]).astype(HALF)
    one = begin(full.at[0], full.at[1], 32, across)
    two = begin(full.at[0], full.at[2], 33, beside)
    one.wait_recv()
    three = begin(full.at[1], full.at[3], 34, beside)
    two.wait_recv()
    three.wait_recv()
    for k in (1, 3, 5, 7):
        weights_of[k].wait_recv()
    aside.wait_recv()
    fourth.wait_recv()
    own_line.wait()
    for copy in copies:
        copy.wait_send()


def start_rows(ids, turned, gain, block, feed, stays, leaves):
    width, vocab = turned.shape
    rows = ids.shape[0] // 32
    padded = (vocab // LANES + 1) * LANES
    vmem = pl.BlockSpec(memory_space=pltpu.VMEM)
    whole = pl.BlockSpec(memory_space=pl.ANY)
    stream, full, weights, four, pair = pl.pallas_call(
        start_kernel,
        in_specs=[pl.BlockSpec(memory_space=pltpu.SMEM), vmem, vmem, vmem, vmem, whole, whole],
        out_specs=[vmem] * 4 + [whole],
        out_shape=[
            jax.ShapeDtypeStruct((rows, 8 * width), FLOAT),
            jax.ShapeDtypeStruct((4, rows, 8 * width), HALF),
            jax.ShapeDtypeStruct((8 * width, block.shape[1]), HALF),
            jax.ShapeDtypeStruct(feed.shape, HALF),
            jax.ShapeDtypeStruct((2 * width, stays.shape[1]), HALF),
        ],
        scratch_shapes=[
            pltpu.VMEM((padded, LANES), FLOAT),
            pltpu.VMEM((LANES, LANES), FLOAT),
            pltpu.VMEM((rows, LANES), FLOAT),
            pltpu.VMEM((4, 8, rows, width), HALF),
            pltpu.VMEM((2, 8, rows, width), HALF),
            pltpu.VMEM((8, rows, width), HALF),
            pltpu.VMEM((8, rows, width), HALF),
            pltpu.SemaphoreType.DMA((45,)),
            pltpu.SemaphoreType.DMA((45,)),
            pltpu.SemaphoreType.DMA,
        ],
        compiler_params=pltpu.CompilerParams(
            collective_id=6, has_side_effects=True, vmem_limit_bytes=VMEM_LIMIT
        ),
        cost_estimate=SMALL,
        name="start_rows",
    )(ids, turned, gain, block, feed, stays, leaves)
    return stream, full.reshape(4 * rows, 8 * width), weights, four, pair


def end_kernel(parts, waits, d_qkv, weight, stream, gain, prior, gain_one, gain_two, apart, *refs):
    rows, g_gain, arrived, partial, beside, away, come, leave, mine, summed, first, second, send, recv = refs[waits:]
    own, rank = lax.axis_index("dp"), lax.axis_index("tensor")
    near, across = near_and_far(own, rank)
    far = [(own ^ k, rank) for k in range(1, 8)]
    greet([near, across, (own, rank ^ 3)] + far)
    edge = Boundary(own, rank, send, recv, parts, stream.shape[0] // parts)
    aside = remote(apart, arrived, send, recv, Boundary.COUNT * parts, far[0])
    aside.start()
    edge.copies.append(aside)
    width = rows.shape[3]
    gain_zero = jnp.zeros_like(gain[...])
    mine[...] = jnp.zeros_like(mine)

    def make(p, h):
        return turned_product(columns_of(d_qkv, p, h, parts), weight[:, : d_qkv.shape[0]])

    for h, at, total in edge.sums(make, partial, beside, away, come):
        slope, by_gain = normed_slope(total, stream[at, :], gain[...])
        slope = slope + prior[at, :]
        gain_zero = gain_zero + by_gain
        for b in range(8):
            leave[b, at, :] = slope[:, b * width : (b + 1) * width].astype(HALF)
    base = Boundary.COUNT * parts
    far_of, last = {}, []

    def begin(source, target, n, peer):
        copy = remote(source, target, send, recv, base + n, peer)
        copy.start()
        edge.copies.append(copy)
        return copy

    order = (7, 6, 5, 4, 3, 2, 1)
    for k in order:
        far_of[k] = begin(leave.at[own ^ k], rows.at[0, k], k, far[k - 1])
    rows[0, 0] = leave[own]
    for b in range(8):
        for n, line in enumerate((gain_zero, gain_one[...], gain_two[...])):
            mine[own ^ b, n : n + 1, :width] = line[:, b * width : (b + 1) * width]
    gains_of = [
        begin(mine, first.at[n - 1], 31 + n, (own, rank ^ n)) for n in (1, 2, 3)
    ]
    crossed = {}
    for k in (0, 1, 2, 3, 4, 5, 6, 7):
        if k:
            far_of[k].wait_recv()
        crossed[k] = begin(rows.at[0, k], rows.at[1, k], 8 + k, across)
        last.append(begin(rows.at[0, k], rows.at[2, k], 16 + k, near))
    for copy in gains_of:
        copy.wait_recv()
    summed[...] = (mine[...] + first[0]) + (first[1] + first[2])
    gains_of = [begin(summed.at[k], second.at[k], 34 + k, far[k - 1]) for k in range(1, 8)]
    for k in (0, 1, 2, 3, 4, 5, 6, 7):
        crossed[k].wait_recv()
        last.append(begin(rows.at[1, k], rows.at[3, k], 24 + k, near))
    for copy in last + gains_of:
        copy.wait_recv()
    second[0] = summed[0]
    pairs = [second[k] + second[k + 1] for k in (0, 2, 4, 6)]
    g_gain[...] = (pairs[0] + pairs[1]) + (pairs[2] + pairs[3])
    aside.wait_recv()
    edge.end()


def end_rows(d_qkv, weight, stream, gain, prior, gain_one, gain_two, apart, width, before):
    rows, depth = stream.shape
    parts = 2
    vmem = pl.BlockSpec(memory_space=pltpu.VMEM)
    semaphores = Boundary.COUNT * parts + 42
    whole = pl.BlockSpec(memory_space=pl.ANY)
    out, g_gain, arrived = pl.pallas_call(
        functools.partial(end_kernel, parts, len(before)),
        in_specs=[vmem] * 7 + [whole] * (1 + len(before)),
        out_specs=[vmem] * 2 + [whole],
        out_shape=[
            jax.ShapeDtypeStruct((4, 8, rows, width), HALF),
            jax.ShapeDtypeStruct((8, LANES), FLOAT),
            jax.ShapeDtypeStruct(apart.shape, HALF),
        ],
        scratch_shapes=exchange_scratch(rows, depth, parts)[:4]
        + [
            pltpu.VMEM((8, rows, width), HALF),
            pltpu.VMEM((8, 8, LANES), FLOAT),
            pltpu.VMEM((8, 8, LANES), FLOAT),
            pltpu.VMEM((3, 8, 8, LANES), FLOAT),
            pltpu.VMEM((8, 8, LANES), FLOAT),
            pltpu.SemaphoreType.DMA((semaphores,)),
            pltpu.SemaphoreType.DMA((semaphores,)),
        ],
        compiler_params=pltpu.CompilerParams(
            collective_id=7, has_side_effects=True, vmem_limit_bytes=VMEM_LIMIT
        ),
        cost_estimate=SMALL,
        name="end_rows",
    )(d_qkv, weight, stream, gain, prior, gain_one, gain_two, apart, *before)
    return out.reshape(-1, width), g_gain[:3, :width], arrived


def merge_kernel(scan, extra, joined, mine, every, send, recv):
    own, rank = lax.axis_index("dp"), lax.axis_index("tensor")
    turns = [(a, b) for a in (0, 1) for b in range(4)][1:]
    peers = [(own ^ a, rank ^ b) for a, b in turns]
    greet(peers)
    tokens = scan.shape[1] // 2
    share = tokens // 4
    mine[...] = jnp.zeros_like(mine)
    mine[0:3, :] = scan[0:3, :tokens]
    mine[3:6, :] = scan[0:3, tokens:]
    copies = []
    for n, peer in enumerate(peers):
        copies.append(remote(mine, every.at[n], send, recv, n, peer))
        copies[-1].start()
    joined[...] = jnp.zeros_like(joined)
    joined[2:4, :] = extra[:2, :]
    for copy in copies:
        copy.wait()
    for y in (0, 1):
        for p in range(4):
            terms = {(0, 0): mine[3 * y : 3 * y + 3, p * share : (p + 1) * share]}
            for n, (a, b) in enumerate(turns):
                q = TURN.index(TURN[p] ^ b)
                terms[a, b] = every[n, 3 * (y ^ a) : 3 * (y ^ a) + 3, q * share : (q + 1) * share]
            peak = functools.reduce(jnp.maximum, [term[0:1] for term in terms.values()])
            sums, hits = [], []
            for a in (0, 1):
                for b in (0, 2):
                    pair = (terms[a, b], terms[a, b ^ 1])
                    sums.append(sum(term[1:2] * jnp.exp(term[0:1] - peak) for term in pair))
                    hits.append(pair[0][2:3] + pair[1][2:3])
            at = pl.ds(y * tokens + p * share, share)
            joined[0:1, at] = peak + jnp.log((sums[0] + sums[1]) + (sums[2] + sums[3]))
            joined[1:2, at] = (hits[0] + hits[1]) + (hits[2] + hits[3])


def merge_scans(scan, extra):
    vmem = pl.BlockSpec(memory_space=pltpu.VMEM)
    shape = (8, scan.shape[1] // 2)
    return pl.pallas_call(
        merge_kernel,
        in_specs=[vmem] * 2,
        out_specs=vmem,
        out_shape=jax.ShapeDtypeStruct(scan.shape, FLOAT),
        scratch_shapes=[
            pltpu.VMEM(shape, FLOAT),
            pltpu.VMEM((7, *shape), FLOAT),
            pltpu.SemaphoreType.DMA((7,)),
            pltpu.SemaphoreType.DMA((7,)),
        ],
        compiler_params=pltpu.CompilerParams(collective_id=8, has_side_effects=True),
        name="merge_scans",
    )(scan, extra)


def across(left, right):
    return lax.dot_general(left, right, (((1,), (1,)), ((), ())), preferred_element_type=FLOAT)


def product(left, right, over_left, over_right):
    return lax.dot_general(
        left, right, (((over_left,), (over_right,)), ((), ())), preferred_element_type=FLOAT
    )


def adam(weight, grad, first, second, rate, decay):
    first = BETA_ONE * first + (1.0 - BETA_ONE) * grad
    second = BETA_TWO * second + (1.0 - BETA_TWO) * grad * grad
    first_hat = first / (1.0 - BETA_ONE**STEP)
    second_hat = second / (1.0 - BETA_TWO**STEP)
    weight = weight - rate * (first_hat / (jnp.sqrt(second_hat) + ADAM_EPS) + decay * weight)
    return (weight, first, second, weight.astype(HALF))


def update_kernel(counts, factor, *refs):
    arrays = len(counts)
    inputs, outputs = refs[: 3 * arrays + sum(counts)], refs[3 * arrays + sum(counts) :]
    grads = inputs[3 * arrays :]
    for n in range(arrays):
        weight, first, second = inputs[3 * n : 3 * n + 3]
        low = 0
        for grad in grads[: counts[n]]:
            high = low + grad.shape[-1]
            at = (Ellipsis, slice(low, high))
            results = adam(
                weight[at], grad[...].astype(FLOAT) * factor[0], first[at], second[at], LR, DECAY
            )
            for out, result in zip(outputs[4 * n : 4 * n + 4], results):
                out[at] = result
            low = high
        grads = grads[counts[n] :]


def update(arrays, factor):
    rows = arrays[0][0].shape[0]
    steps = rows // 16 if rows % 16 == 0 else 1

    def block(array):
        zeros = (0,) * (array.ndim - 1)
        return pl.BlockSpec((array.shape[0] // steps, *array.shape[1:]), lambda i: (i, *zeros))

    inputs = [array for entry in arrays for array in entry[:3]]
    grads = [grad for entry in arrays for grad in entry[3]]
    outs = [
        jax.ShapeDtypeStruct(entry[0].shape, kind)
        for entry in arrays
        for kind in (FLOAT, FLOAT, FLOAT, HALF)
    ]
    results = pl.pallas_call(
        functools.partial(update_kernel, tuple(len(entry[3]) for entry in arrays)),
        grid=(steps,),
        in_specs=[pl.BlockSpec(memory_space=pltpu.SMEM)] + [block(a) for a in inputs + grads],
        out_specs=[block(a) for a in outs],
        out_shape=outs,
        compiler_params=pltpu.CompilerParams(vmem_limit_bytes=VMEM_LIMIT),
        cost_estimate=SMALL,
        name="update",
    )(factor.reshape(1), *inputs, *grads)
    return [results[4 * n : 4 * n + 4] for n in range(len(arrays))]


def shards(
    token_ids,
    targets,
    segments,
    completion,
    micro_order,
    *state,
):
    weights, means, squares_in = state[:7], state[7:14], state[14:21]
    embedding, attn_in, attn_out, ffn_in, ffn_out, head_table, norm_gains = weights
    group = lax.axis_size("dp")
    parts = lax.axis_size("tensor")
    own, rank = lax.axis_index("dp"), lax.axis_index("tensor")
    vocab, width = embedding.shape
    start = rank * vocab
    seqs, length = token_ids.shape
    micro = micro_order.shape[1]
    share = length // parts
    turn = jnp.array(TURN, jnp.int32)
    dp_order = own ^ jnp.arange(group, dtype=jnp.int32)
    tensor_order = rank ^ turn
    tensor_order_natural = rank ^ jnp.arange(parts, dtype=jnp.int32)
    ffn = ffn_out.shape[0]
    qkv_width = attn_in.shape[1]

    attn_block = jnp.concatenate([attn_in, attn_out.T], axis=1).astype(HALF)
    ffn_block = jnp.concatenate([ffn_in.reshape(width, -1), ffn_out.T], axis=1).astype(HALF)
    bit = own % 2
    entries = vocab // 2
    low_half, high_half = head_table[:, :entries].astype(HALF), head_table[:, entries:].astype(HALF)
    stays = jnp.where(bit == 0, low_half, high_half)
    leaves = jnp.where(bit == 0, high_half, low_half)
    lines = [[i for i in range(group) if i % 2 == odd] for odd in (0, 1)]

    flags = completion.astype(FLOAT)
    picked_rows = micro_order[0]
    takes_seq = picked_rows[:, None] == jnp.arange(seqs)[None, :]
    local_counts = jnp.sum(jnp.where(takes_seq, jnp.sum(completion, axis=1)[None, :], 0), axis=1)
    id_rows = seqs * length // LANES
    packed = jnp.concatenate(
        [
            token_ids.reshape(-1),
            targets.reshape(-1),
            completion.reshape(-1),
            jnp.pad(jnp.concatenate([local_counts, picked_rows]), (0, 8 * LANES - 2 * micro)),
        ]
    ).reshape(3 * id_rows + 8, LANES)
    gains = jnp.pad(norm_gains.astype(HALF).astype(FLOAT), ((0, 5), (0, LANES - width)))
    if group == 8:
        packed, every_id, gains = spread(packed, gains, seqs, length, vocab, width)
        every_id = every_id.reshape(-1)
    else:
        packed, gains = lax.all_gather(packed, "dp"), lax.all_gather(gains, "dp")
        packed = jnp.take(packed, dp_order, axis=0)
        every_id = packed[:, :id_rows].reshape(group, seqs, parts, share)
        every_id = jnp.take(every_id, tensor_order, axis=2)
        every_id = every_id.transpose(2, 0, 1, 3).reshape(-1) - start
        every_id = jnp.where((every_id >= 0) & (every_id < vocab), every_id, vocab)
        gains = gains.transpose(1, 0, 2)[:, :, :width].reshape(8, -1)
    packed, leaves = lax.optimization_barrier((packed, leaves))
    gains = gains[:3]
    numbers = packed[:, 3 * id_rows, : 2 * micro]
    counts = jnp.sum(numbers[:, :micro].astype(FLOAT), axis=0)

    def both_order(values):
        values = values.reshape(seqs, parts, share)
        values = jnp.where(rank % 2 == 1, values[:, [1, 0, 3, 2]], values)
        values = jnp.where(rank // 2 == 1, values[:, [2, 3, 0, 1]], values)
        return values[:, list(TURN)].transpose(1, 0, 2).reshape(-1)

    own_segment = segments[:, :, None] == jnp.arange(8, dtype=jnp.int32)
    sizes = jnp.sum(own_segment.astype(jnp.int32), axis=1)
    begins = jnp.cumsum(sizes, axis=1) - sizes
    first = jnp.sum(jnp.where(own_segment, begins[:, None, :], 0), axis=2)
    first = jnp.broadcast_to(first[:, None, :], (seqs, 8, length))
    base = turn[tensor_order_natural] * (seqs * share)
    cosine, sine = tables(length, HEAD_DIM)

    if group == 8:
        stream0, attn_norm, attn_w, ffn_four, head_rows = start_rows(
            every_id, embedding.T, gains[:1], attn_block, ffn_block, stays, leaves
        )
        ffn_blocks = [ffn_block, ffn_four]
    else:
        rows = lookup(embedding.T, every_id).reshape(parts, group, seqs * share, width)
        rows = rows[:2] + swap(rows[2:], "tensor", 1)
        rows = rows[0] + swap(rows[1], "tensor", 2)
        rows = lax.all_to_all(jnp.take(rows, dp_order, axis=0), "dp", 0, 0)
        stream0 = rows.transpose(1, 0, 2).reshape(seqs * share, -1).astype(FLOAT)
        attn_norm = tensor_gather(normed(stream0, gains[0]).astype(HALF))

        attn_w = lax.all_gather(attn_block, "dp", axis=0, tiled=True)
        came = swap(leaves, "dp", 1)
        head_rows = jnp.concatenate(
            [jnp.where(bit == 0, stays, came), jnp.where(bit == 0, came, stays)], axis=0
        )
        ffn_blocks = []
    head_b = lax.all_gather(head_rows, "dp", axis=0, tiled=True, axis_index_groups=lines)
    attn_in_b, attn_out_b = attn_w[:, :qkv_width], attn_w[:, qkv_width:]
    qkv = product(attn_in_b, attn_norm, 0, 1)
    attended, kept, log_sums = attend(base, qkv, cosine, sine, first)
    stream1, ffn_norm, *ffn_w = forward_boundary(
        attended, attn_w, stream0, gains[1:2], ffn_blocks
    )
    ffn_w = ffn_w[0] if ffn_w else lax.all_gather(ffn_block, "dp", axis=0, tiled=True)
    stream2, final_norm = wide_forward(ffn_norm, ffn_w, stream1, gains[2:])

    final_norm, packed = lax.optimization_barrier((final_norm, packed))
    rows_extra = []
    for k in (0, 1):
        its_flags = packed[k, 2 * id_rows : 3 * id_rows].reshape(seqs, length).astype(FLOAT)
        its_order = numbers[k, micro:]
        takes = (its_order[None, :] == jnp.arange(seqs)[:, None]).astype(FLOAT)
        its_scale = its_flags * jnp.sum(takes / jnp.maximum(counts, 1.0), axis=1)[:, None]
        aims = packed[k, id_rows : 2 * id_rows].reshape(seqs, length) - start - bit * entries
        aims = jnp.where((aims >= 0) & (aims < entries), aims, -1).astype(FLOAT)
        rows_extra.append(jnp.stack([both_order(its_scale), both_order(aims)]))
    extra = jnp.pad(jnp.concatenate(rows_extra, axis=1), ((0, 6), (0, 0)))
    joint_flags = both_order(flags)
    logits, scan, final_turned = head_scan(final_norm, head_b, extra)
    info = merge_scans(scan, extra)
    tokens = seqs * length
    seq_loss = jnp.sum(
        ((info[0, :tokens] - info[1, :tokens]) * joint_flags).reshape(parts, seqs, share),
        axis=(0, 2),
    )
    g_head, d_final = head_grad(final_turned, head_b, info, logits)
    g_head = lax.psum_scatter(
        g_head, "dp", scatter_dimension=0, tiled=True, axis_index_groups=lines
    )
    g_stays = jnp.where(bit == 0, g_head[:width], g_head[width:])
    g_leaves = jnp.where(bit == 0, g_head[width:], g_head[:width])

    d_stream2, g_gain2, d_branch2 = wide_backward(d_final, stream2, gains[2:])
    d_stream1, g_gain1, d_branch1, g_ffn = backward_boundary(
        ffn_norm, d_branch2, ffn_w, stream1, gains[1:2], d_stream2
    )
    g_ffn_parts = scatter_first(g_ffn)
    d_attended = product(attn_out_b, d_branch1, 0, 1).astype(HALF)
    d_qkv = attend_back(base, kept, log_sums, d_attended, cosine, sine, first, [])
    g_attn_in = product(attn_norm, d_qkv, 0, 1).astype(HALF)
    g_attn_out = product(d_branch1, attended, 0, 1).astype(HALF)
    g_attn = jnp.concatenate([g_attn_in, g_attn_out], axis=1)
    g_attn_parts = scatter_first(g_attn)
    d_qkv, g_ffn = lax.optimization_barrier((d_qkv, g_ffn))
    g_ffn, g_ffn_leaves = scatter_middle(g_ffn, g_ffn_parts)
    if group == 8:
        rows, g_gains, g_came = end_rows(
            d_qkv,
            attn_w,
            stream0,
            gains[:1],
            d_stream1,
            g_gain1,
            g_gain2,
            g_leaves,
            width,
            g_ffn_leaves,
        )
    else:
        d_norm = tensor_scatter(product(d_qkv, attn_in_b, 0, 1))
        d_part, g_gain0 = normed_slope(d_norm, stream0, gains[:1])
        rows = (d_stream1 + d_part).astype(HALF)
        rows = rows.reshape(seqs * share, group, width).transpose(1, 0, 2)
        rows = jnp.take(lax.all_to_all(rows, "dp", 0, 0), dp_order, axis=0)
        rows = tensor_gather(rows[None]).reshape(-1, width)
        g_came = swap(g_leaves, "dp", 1)
        gain_sum = jnp.concatenate([g_gain0, g_gain1, g_gain2]).reshape(3, group, width)
        g_gains = jnp.take(lax.psum(gain_sum, ("dp", "tensor")), own, axis=1)
    g_head = [jnp.where(bit == 0, g_stays, g_came), jnp.where(bit == 0, g_came, g_stays)]
    rows, g_ffn, g_attn = lax.optimization_barrier((rows, g_ffn, g_attn))
    g_ffn = scatter_last(g_ffn, g_ffn_leaves)
    g_attn, g_attn_leaves = scatter_middle(g_attn, g_attn_parts)
    g_embed, squares = collect(rows, every_id, vocab, [g_ffn, *g_attn_leaves])
    squares, g_attn = lax.optimization_barrier((squares, g_attn))
    g_attn = scatter_last(g_attn, g_attn_leaves)

    owner = (rank == 0).astype(FLOAT)
    squared = jnp.sum(squares) + owner * jnp.sum(g_gains * g_gains)
    for part in (g_attn, g_ffn, *g_head):
        squared = squared + jnp.sum(part.astype(FLOAT) ** 2)
    losses = jnp.sum(jnp.where(takes_seq, seq_loss[None, :], 0.0), axis=1) * owner
    if group == 8:
        sums = jnp.pad(jnp.concatenate([squared[None], losses]), (0, 8 * LANES - 1 - micro))
        sums = total_over_devices(jnp.broadcast_to(sums.reshape(1, 8, LANES), (8, 8, LANES)))
        squared, loss_sums = sums[0, 0], sums[0, 1 : 1 + micro]
    else:
        squared, loss_sums = lax.psum((squared, losses), ("dp", "tensor"))
    grad_norm = jnp.sqrt(squared)
    factor = CLIP / jnp.maximum(grad_norm, CLIP)
    g_parts = (
        [g_embed],
        [g_attn[:, :qkv_width]],
        [g_attn[:, qkv_width:].T],
        [g_ffn[:, : 2 * ffn].reshape(ffn_in.shape)],
        [g_ffn[:, 2 * ffn :]],
        g_head,
    )
    arrays = []
    for place in range(6):
        entry = (weights[place], means[place], squares_in[place])
        if place in (0, 4):
            entry = tuple(array.T for array in entry)
        arrays.append((*entry, g_parts[place]))
    updated = []
    for place, results in enumerate(update(arrays, factor)):
        updated.extend(result.T if place in (0, 4) else result for result in results)
    updated.extend(adam(norm_gains, g_gains * factor, means[6], squares_in[6], LR_GAIN, 0.0))
    return (jnp.stack([loss_sums, counts]), grad_norm, *updated)


def solution(mesh):
    in_specs = (
        P("dp", None),
        P("dp", None),
        P("dp", None),
        P("dp", None),
        P("dp", None),
        P("tensor", "dp"),
        P("dp", "tensor"),
        P("tensor", "dp"),
        P("dp", None, "tensor"),
        P("tensor", "dp"),
        P("dp", "tensor"),
        P(None, "dp"),
        P("tensor", "dp"),
        P("dp", "tensor"),
        P("tensor", "dp"),
        P("dp", None, "tensor"),
        P("tensor", "dp"),
        P("dp", "tensor"),
        P(None, "dp"),
        P("tensor", "dp"),
        P("dp", "tensor"),
        P("tensor", "dp"),
        P("dp", None, "tensor"),
        P("tensor", "dp"),
        P("dp", "tensor"),
        P(None, "dp"),
    )
    out_specs = (
        P(),
        P(),
        P("tensor", "dp"),
        P("tensor", "dp"),
        P("tensor", "dp"),
        P("tensor", "dp"),
        P("dp", "tensor"),
        P("dp", "tensor"),
        P("dp", "tensor"),
        P("dp", "tensor"),
        P("tensor", "dp"),
        P("tensor", "dp"),
        P("tensor", "dp"),
        P("tensor", "dp"),
        P("dp", None, "tensor"),
        P("dp", None, "tensor"),
        P("dp", None, "tensor"),
        P("dp", None, "tensor"),
        P("tensor", "dp"),
        P("tensor", "dp"),
        P("tensor", "dp"),
        P("tensor", "dp"),
        P("dp", "tensor"),
        P("dp", "tensor"),
        P("dp", "tensor"),
        P("dp", "tensor"),
        P(None, "dp"),
        P(None, "dp"),
        P(None, "dp"),
        P(None, "dp"),
    )
    return jax.shard_map(shards, mesh=mesh, in_specs=in_specs, out_specs=out_specs, check_vma=False)
```

```python
import functools

import jax
import jax.numpy as jnp
import numpy as np
from jax import lax
from jax.experimental import pallas as pl
from jax.experimental.pallas import tpu as pltpu
from jax.sharding import PartitionSpec as P

HEAD_DIM = 64
STEP = 10


EPS = 1e-05
CLIP = 0.01
LR = 0.03
LR_GAIN = 0.5
BETA_ONE = 0.9
BETA_TWO = 0.95
ADAM_EPS = 1e-08
DECAY = 0.1
NEG = -1e30
FLOAT = jnp.float32
HALF = jnp.bfloat16
LANES = 128
ROWS = 1024
VMEM_LIMIT = 56 * 2**20
TILE = 512
CHUNK = 256
MESH = pl.DeviceIdType.MESH
SMALL = pl.CostEstimate(flops=2**20, bytes_accessed=2**20, transcendentals=0)

TURN = (0, 2, 1, 3)


def swap(value, axis, bit):
    pairs = [(i, i ^ bit) for i in range(lax.axis_size(axis))]
    return lax.ppermute(value, axis, pairs)


def normed(values, gain):
    return values * lax.rsqrt(jnp.mean(values * values, axis=-1, keepdims=True) + EPS) * gain


def tables(length, width):
    inverse = np.float32(10000.0) ** (-np.arange(0, width, 2, dtype=np.float32) / np.float32(width))
    angle = inverse[:, None] * np.arange(length, dtype=np.float32)[None, :]
    return jnp.asarray(np.cos(angle)), jnp.asarray(np.sin(angle))


def block_of(full, k):
    rows = full.shape[0] // lax.axis_size("dp")
    own = lax.axis_index("dp")
    return lax.dynamic_slice(full, ((own ^ k) * rows, 0), (rows, full.shape[1]))


def scatter_first(full):
    if lax.axis_size("dp") != 8:
        return []
    leaves = jnp.concatenate([block_of(full, k + 1) for k in (0, 2, 4, 6)], axis=0)
    return [swap(leaves, "dp", 1)]


def scatter_middle(full, parts):
    if lax.axis_size("dp") != 8:
        return full, []
    rows = full.shape[0] // 8
    sums = [
        block_of(full, 2 * n).astype(FLOAT) + parts[0][n * rows : (n + 1) * rows].astype(FLOAT)
        for n in range(4)
    ]
    return sums[0], [total.astype(HALF) for total in sums[1:]]


def scatter_last(total, leaves):
    if lax.axis_size("dp") != 8:
        return lax.psum_scatter(total.astype(FLOAT), "dp", scatter_dimension=0, tiled=True)
    for n, leave in enumerate(leaves):
        total = total + swap(leave, "dp", 2 * n + 2).astype(FLOAT)
    return total


def peers_of(own, rank, bits, axis):
    if axis == "dp":
        return [(own ^ k, rank) for k in bits]
    return [(own, rank ^ k) for k in bits]


def greet(peers):
    barrier = pltpu.get_barrier_semaphore()
    for peer in peers:
        pl.semaphore_signal(barrier, inc=1, device_id=peer, device_id_type=MESH)
    pl.semaphore_wait(barrier, len(peers))


def spread_kernel(
    vocab, seqs, micro, numbers, gains, every, ids, all_gains, extra, every_gain, send, recv
):
    own, rank = lax.axis_index("dp"), lax.axis_index("tensor")
    peers = peers_of(own, rank, range(1, 8), "dp")
    greet(peers)
    every[0] = numbers[...]
    every_gain[0] = gains[...]
    copies = []
    for k in range(1, 8):
        for n, (source, target) in enumerate(((numbers, every), (gains, every_gain))):
            copies.append(
                pltpu.make_async_remote_copy(
                    src_ref=source,
                    dst_ref=target.at[k],
                    send_sem=send.at[n, k],
                    recv_sem=recv.at[n, k],
                    device_id=peers[k - 1],
                    device_id_type=MESH,
                )
            )
            copies[-1].start()
    for copy in copies:
        copy.wait()
    lines = ids.shape[0] // (32 * seqs)
    for p in range(4):
        shard = rank ^ TURN[p]
        for k in range(8):
            for j in range(seqs):
                local = every[k, pl.ds((j * 4 + shard) * lines, lines), :] - rank * vocab
                local = jnp.where((local >= 0) & (local < vocab), local, vocab)
                ids[pl.ds(((p * 8 + k) * seqs + j) * lines, lines), :] = local
    total = numbers.shape[0] - 8
    total = sum(every[k, total : total + 1, :].astype(FLOAT) for k in range(8))
    weights = 1.0 / jnp.maximum(total, 1.0)
    id_rows = (numbers.shape[0] - 8) // 3
    entries = vocab // 2
    low = rank * vocab + (own % 2) * entries
    extra[...] = jnp.zeros_like(extra)
    for k in (0, 1):
        order = every[k, 3 * id_rows : 3 * id_rows + 1, :]
        for j in range(seqs):
            weight = sum(
                jnp.where(order[:, micro + m : micro + m + 1] == j, weights[:, m : m + 1], 0.0)
                for m in range(micro)
            )
            for p in range(4):
                row = (j * 4 + (rank ^ TURN[p])) * lines
                for r in range(lines):
                    place = (((k * 4 + p) * seqs + j) * lines + r) * LANES
                    counted = every[k, pl.ds(2 * id_rows + row + r, 1), :].astype(FLOAT)
                    aim = every[k, pl.ds(id_rows + row + r, 1), :] - low
                    aim = jnp.where((aim >= 0) & (aim < entries), aim, -1).astype(FLOAT)
                    extra[0:1, place : place + LANES] = counted * weight
                    extra[1:2, place : place + LANES] = aim
                    extra[2:3, place : place + LANES] = counted
    width = all_gains.shape[1] // 8
    for b in range(8):
        all_gains[:, b * width : (b + 1) * width] = every_gain[own ^ b][:, :width]


def spread(numbers, gains, seqs, length, micro, vocab, width):
    vmem = pl.BlockSpec(memory_space=pltpu.VMEM)
    return pl.pallas_call(
        functools.partial(spread_kernel, vocab, seqs, micro),
        in_specs=[vmem] * 2,
        out_specs=[vmem] * 4,
        out_shape=[
            jax.ShapeDtypeStruct((8, *numbers.shape), numbers.dtype),
            jax.ShapeDtypeStruct((8 * seqs * length // LANES, LANES), jnp.int32),
            jax.ShapeDtypeStruct((8, 8 * width), FLOAT),
            jax.ShapeDtypeStruct((8, 2 * seqs * length), FLOAT),
        ],
        scratch_shapes=[
            pltpu.VMEM((8, *gains.shape), FLOAT),
            pltpu.SemaphoreType.DMA((2, 8)),
            pltpu.SemaphoreType.DMA((2, 8)),
        ],
        compiler_params=pltpu.CompilerParams(collective_id=1, has_side_effects=True),
        cost_estimate=SMALL,
        name="spread",
    )(numbers, gains)


def total_kernel(blocks, out, first, summed, second, send, recv):
    own, rank = lax.axis_index("dp"), lax.axis_index("tensor")
    near = peers_of(own, rank, range(1, 4), "tensor")
    far = peers_of(own, rank, range(1, 8), "dp")
    greet(near + far)
    copies = []
    for k in range(1, 4):
        copy = pltpu.make_async_remote_copy(
            src_ref=blocks,
            dst_ref=first.at[k - 1],
            send_sem=send.at[k - 1],
            recv_sem=recv.at[k - 1],
            device_id=near[k - 1],
            device_id_type=MESH,
        )
        copy.start()
        copies.append(copy)
    for copy in copies:
        copy.wait()
    summed[...] = (blocks[...] + first[0]) + (first[1] + first[2])
    copies = []
    for k in range(1, 8):
        copy = pltpu.make_async_remote_copy(
            src_ref=summed.at[k],
            dst_ref=second.at[k],
            send_sem=send.at[2 + k],
            recv_sem=recv.at[2 + k],
            device_id=far[k - 1],
            device_id_type=MESH,
        )
        copy.start()
        copies.append(copy)
    for copy in copies:
        copy.wait()
    second[0] = summed[0]
    pairs = [second[k] + second[k + 1] for k in (0, 2, 4, 6)]
    out[...] = (pairs[0] + pairs[1]) + (pairs[2] + pairs[3])


def total_over_devices(blocks):
    shape = blocks.shape
    return pl.pallas_call(
        total_kernel,
        in_specs=[pl.BlockSpec(memory_space=pltpu.VMEM)],
        out_specs=pl.BlockSpec(memory_space=pltpu.VMEM),
        out_shape=jax.ShapeDtypeStruct(shape[1:], FLOAT),
        scratch_shapes=[
            pltpu.VMEM((3, *shape), FLOAT),
            pltpu.VMEM(shape, FLOAT),
            pltpu.VMEM(shape, FLOAT),
            pltpu.SemaphoreType.DMA((10,)),
            pltpu.SemaphoreType.DMA((10,)),
        ],
        compiler_params=pltpu.CompilerParams(collective_id=2, has_side_effects=True),
        name="total",
    )(blocks)


def tensor_gather(block):
    half = jnp.concatenate([block, swap(block, "tensor", 2)], axis=0)
    return jnp.concatenate([half, swap(half, "tensor", 1)], axis=0)


def tensor_scatter(full):
    half = full.shape[0] // 2
    quarter = half // 2
    both = full[:half] + swap(full[half:], "tensor", 1)
    there = swap(both[quarter:].astype(HALF), "tensor", 2)
    return both[:quarter] + there.astype(FLOAT)


def lookup_kernel(ids, turned, out, table, corner, rows):
    count = rows.shape[0]
    width, vocab = turned.shape

    @pl.when(pl.program_id(0) == 0)
    def _():
        corner[...] = jnp.zeros_like(corner)
        for v in range(0, vocab, LANES):
            some = min(LANES, vocab - v)
            corner[:width, :some] = turned[:, v : v + some].astype(HALF).astype(FLOAT)
            if some < LANES:
                corner[:width, some:] = jnp.zeros((width, LANES - some), FLOAT)
            table[v : v + LANES, :] = corner[...].T
        if vocab % LANES == 0:
            table[vocab:, :] = jnp.zeros((LANES, LANES), FLOAT)

    def body(i, carry):
        for u in range(16):
            r = i * 16 + u
            rows[pl.ds(r, 1), :] = table[pl.ds(ids[0, 0, r], 1), :]
        return carry

    lax.fori_loop(0, count // 16, body, 0)
    out[...] = rows[:, : out.shape[1]].astype(HALF)


def lookup(turned, ids):
    count = ids.shape[0]
    width, vocab = turned.shape
    padded = (vocab // LANES + 1) * LANES
    return pl.pallas_call(
        lookup_kernel,
        grid=(count // ROWS,),
        in_specs=[
            pl.BlockSpec((1, 1, ROWS), lambda i: (i, 0, 0), memory_space=pltpu.SMEM),
            pl.BlockSpec(turned.shape, lambda i: (0, 0), pipeline_mode=pl.Buffered(1)),
        ],
        out_specs=pl.BlockSpec((ROWS, width), lambda i: (i, 0)),
        out_shape=jax.ShapeDtypeStruct((count, width), HALF),
        scratch_shapes=[
            pltpu.VMEM((padded, LANES), FLOAT),
            pltpu.VMEM((LANES, LANES), FLOAT),
            pltpu.VMEM((ROWS, LANES), FLOAT),
        ],
        compiler_params=pltpu.CompilerParams(vmem_limit_bytes=VMEM_LIMIT),
        cost_estimate=SMALL,
        name="lookup",
    )(ids.reshape(count // ROWS, 1, ROWS), turned)


def collect_kernel(waits, ids, grads, *refs):
    out, squares, rows, *sums = refs[waits:]
    step = pl.program_id(0)
    count = rows.shape[0]
    width, vocab = out.shape

    @pl.when(step == 0)
    def _():
        rows[...] = jnp.zeros_like(rows)
        for total in sums:
            total[...] = jnp.zeros_like(total)

    rows[:, :width] = grads[...].astype(FLOAT)

    def body(i, carry):
        for u in range(16):
            r = i * 16 + u
            total = sums[u % len(sums)]
            place = pl.ds(ids[0, 0, r], 1)
            total[place, :] = total[place, :] + rows[pl.ds(r, 1), :]
        return carry

    lax.fori_loop(0, count // 16, body, 0)

    @pl.when(step == pl.num_programs(0) - 1)
    def _():
        squared = jnp.zeros((8, LANES), FLOAT)
        for v in range(0, vocab, LANES):
            some = min(LANES, vocab - v)
            total = sums[0][v : v + some, :]
            for other in sums[1:]:
                total = total + other[v : v + some, :]
            for r in range(0, some, 8):
                squared = squared + total[r : r + 8, :] * total[r : r + 8, :]
            if some < LANES:
                total = jnp.concatenate([total, jnp.zeros((LANES - some, LANES), FLOAT)], axis=0)
            out[:, v : v + some] = total.T[:width, :some]
        squares[...] = squared


def collect(grads, ids, vocab, before):
    count = ids.shape[0]
    width = grads.shape[1]
    padded = (vocab // LANES + 1) * LANES
    return pl.pallas_call(
        functools.partial(collect_kernel, len(before)),
        grid=(count // ROWS,),
        in_specs=[
            pl.BlockSpec((1, 1, ROWS), lambda i: (i, 0, 0), memory_space=pltpu.SMEM),
            pl.BlockSpec((ROWS, width), lambda i: (i, 0)),
        ]
        + [pl.BlockSpec(memory_space=pl.ANY)] * len(before),
        out_specs=[
            pl.BlockSpec((width, vocab), lambda i: (0, 0)),
            pl.BlockSpec((8, LANES), lambda i: (0, 0)),
        ],
        out_shape=[
            jax.ShapeDtypeStruct((width, vocab), FLOAT),
            jax.ShapeDtypeStruct((8, LANES), FLOAT),
        ],
        scratch_shapes=[pltpu.VMEM((ROWS, LANES), FLOAT)]
        + [pltpu.VMEM((padded, LANES), FLOAT)] * 8,
        compiler_params=pltpu.CompilerParams(vmem_limit_bytes=VMEM_LIMIT),
        cost_estimate=SMALL,
        name="collect",
    )(ids.reshape(count // ROWS, 1, ROWS), grads, *before)


def edge_of(vocab):
    return vocab - (pl.cdiv(vocab, TILE) - 1) * TILE


def each_tile(vocab, work):
    last = edge_of(vocab)
    if last == TILE:
        work(TILE)
    else:
        step, steps = pl.program_id(0), pl.num_programs(0)
        pl.when(step < steps - 1)(lambda: work(TILE))
        pl.when(step == steps - 1)(lambda: work(last))


def turned_rows(rows):
    return jnp.concatenate([rows] * (LANES // 8), axis=0).T


def scan_kernel(vocab, norm, weight, target, logits, stats, turned, peak, total, hit, aims):
    step = pl.program_id(0)
    rows = norm.shape[0]

    @pl.when(step == 0)
    def _():
        peak[...] = jnp.full_like(peak, NEG)
        total[...] = jnp.zeros_like(total)
        hit[...] = jnp.zeros_like(hit)
        aims[...] = turned_rows(target[...])
        for r in range(0, rows, CHUNK):
            turned[:, r : r + CHUNK] = norm[r : r + CHUNK, :].T

    def work(width):
        lane = lax.broadcasted_iota(jnp.int32, (CHUNK, LANES), 1)
        for r in range(0, rows, CHUNK):
            part = pl.ds(r, CHUNK)
            value = jnp.dot(norm[part, :], weight[...], preferred_element_type=FLOAT)
            logits[part, :] = value
            aim = aims[part, 1:2].astype(jnp.int32) - step * TILE
            slabs, found = [], hit[part, :]
            for c in range(0, width, LANES):
                slab = value[:, c : c + LANES]
                if c + LANES > width:
                    slab = jnp.where(lane < width - c, slab, NEG)
                slabs.append(slab)
                found = found + jnp.where(lane == aim - c, slab, 0.0)
            hit[part, :] = found
            before = peak[part, :]
            top = functools.reduce(jnp.maximum, slabs, before)
            added = total[part, :] * jnp.exp(before - top)
            for slab in slabs:
                added = added + jnp.exp(slab - top)
            total[part, :] = added
            peak[part, :] = top

    each_tile(vocab, work)

    @pl.when(step == pl.num_programs(0) - 1)
    def _():
        top = jnp.max(peak[...], axis=1, keepdims=True)
        added = jnp.sum(total[...] * jnp.exp(peak[...] - top), axis=1, keepdims=True)
        found = jnp.sum(hit[...], axis=1, keepdims=True)
        lane = lax.broadcasted_iota(jnp.int32, (rows, LANES), 1)
        joined = jnp.where(lane == 0, top, jnp.where(lane == 1, added, found))
        stats[...] = joined.T[:8, :]


def head_scan(norm, weight, extra):
    rows, depth = norm.shape
    vocab = weight.shape[1]
    return pl.pallas_call(
        functools.partial(scan_kernel, vocab),
        grid=(pl.cdiv(vocab, TILE),),
        in_specs=[
            pl.BlockSpec((rows, depth), lambda i: (0, 0), pipeline_mode=pl.Buffered(1)),
            pl.BlockSpec((depth, TILE), lambda i: (0, i)),
            pl.BlockSpec((8, rows), lambda i: (0, 0)),
        ],
        out_specs=[
            pl.BlockSpec((rows, TILE), lambda i: (0, i)),
            pl.BlockSpec((8, rows), lambda i: (0, 0)),
            pl.BlockSpec((depth, rows), lambda i: (0, 0), pipeline_mode=pl.Buffered(1)),
        ],
        out_shape=[
            jax.ShapeDtypeStruct((rows, vocab), FLOAT),
            jax.ShapeDtypeStruct((8, rows), FLOAT),
            jax.ShapeDtypeStruct((depth, rows), HALF),
        ],
        scratch_shapes=[pltpu.VMEM((rows, LANES), FLOAT)] * 4,
        compiler_params=pltpu.CompilerParams(vmem_limit_bytes=VMEM_LIMIT),
        cost_estimate=SMALL,
        name="head_scan",
    )(norm, weight, extra)


def grad_kernel(vocab, turned, weight, info, logits, grad, out, total, slope, columns):
    step = pl.program_id(0)
    rows = logits.shape[0]

    @pl.when(step == 0)
    def _():
        columns[...] = turned_rows(info[...])
        total[...] = jnp.zeros_like(total)

    def work(width):
        lane = lax.broadcasted_iota(jnp.int32, (CHUNK, TILE), 1)
        table = weight[...]
        if width < TILE:
            table = jnp.where(lax.broadcasted_iota(jnp.int32, table.shape, 1) < width, table, 0.0)
        for r in range(0, rows, CHUNK):
            part = pl.ds(r, CHUNK)
            aim = columns[part, 3:4].astype(jnp.int32) - step * TILE
            value = jnp.exp(logits[part, :] - columns[part, 0:1])
            value = (value - jnp.where(lane == aim, 1.0, 0.0)) * columns[part, 2:3]
            if width < TILE:
                value = jnp.where(lane < width, value, 0.0)
            value = value.astype(HALF)
            slope[part, :] = value
            total[part, :] = total[part, :] + lax.dot_general(
                value, table, (((1,), (1,)), ((), ())), preferred_element_type=FLOAT
            )
        grad[...] = jnp.dot(turned[...], slope[...], preferred_element_type=FLOAT).astype(HALF)

    each_tile(vocab, work)

    @pl.when(step == pl.num_programs(0) - 1)
    def _():
        for r in range(0, rows, CHUNK):
            out[pl.ds(r, CHUNK), :] = total[pl.ds(r, CHUNK), :].astype(HALF)


def head_grad(turned, weight, info, logits):
    depth, rows = turned.shape
    vocab = weight.shape[1]
    return pl.pallas_call(
        functools.partial(grad_kernel, vocab),
        grid=(pl.cdiv(vocab, TILE),),
        in_specs=[
            pl.BlockSpec((depth, rows), lambda i: (0, 0), pipeline_mode=pl.Buffered(1)),
            pl.BlockSpec((depth, TILE), lambda i: (0, i)),
            pl.BlockSpec((8, rows), lambda i: (0, 0)),
            pl.BlockSpec((rows, TILE), lambda i: (0, i)),
        ],
        out_specs=[
            pl.BlockSpec((depth, TILE), lambda i: (0, i)),
            pl.BlockSpec((rows, depth), lambda i: (0, 0), pipeline_mode=pl.Buffered(1)),
        ],
        out_shape=[
            jax.ShapeDtypeStruct((depth, vocab), HALF),
            jax.ShapeDtypeStruct((rows, depth), HALF),
        ],
        scratch_shapes=[
            pltpu.VMEM((rows, depth), FLOAT),
            pltpu.VMEM((rows, TILE), HALF),
            pltpu.VMEM((rows, LANES), FLOAT),
        ],
        compiler_params=pltpu.CompilerParams(vmem_limit_bytes=VMEM_LIMIT),
        cost_estimate=SMALL,
        name="head_grad",
    )(turned, weight, info, logits)


def turn_rows(low, high, cosine, sine):
    return low * cosine - high * sine, high * cosine + low * sine


def reach(block, share, longest):
    back = -(-(longest - 1) // share)
    return max(0, block - back) * share


def seen(first, low, high, place):
    keys = low + lax.broadcasted_iota(jnp.int32, (high - low, first.shape[1]), 0)
    queries = place + lax.broadcasted_iota(jnp.int32, (high - low, first.shape[1]), 1)
    return (keys >= first) & (keys <= queries)


def attend_kernel(base, qkv, cosine, sine, first, attended, kept, log_total):
    seq = pl.program_id(1)
    blocks = base.shape[0]
    length = cosine.shape[1]
    share = length // blocks
    half = HEAD_DIM // 2

    def spot(i):
        return pl.ds(pl.multiple_of(base[i] + seq * share, share), share)

    for i in range(blocks):
        at = pl.ds(i * share, share)
        turns = (cosine[:, at], sine[:, at])
        for c in (0, 1):
            top = c * HEAD_DIM
            low, high = turn_rows(
                qkv[top : top + half, spot(i)], qkv[top + half : top + HEAD_DIM, spot(i)], *turns
            )
            kept[0, top : top + half, at] = low.astype(HALF)
            kept[0, top + half : top + HEAD_DIM, at] = high.astype(HALF)
        kept[0, 2 * HEAD_DIM :, at] = qkv[2 * HEAD_DIM :, spot(i)].astype(HALF)
    key = kept[0, HEAD_DIM : 2 * HEAD_DIM, :].T
    for i in range(blocks):
        low, high = reach(i, share, length // 2), (i + 1) * share
        at = pl.ds(i * share, share)
        scores = jnp.dot(
            key[low:high, :], kept[0, :HEAD_DIM, at], preferred_element_type=FLOAT
        ) * (HEAD_DIM**-0.5)
        scores = jnp.where(seen(first[0, :, at][:1], low, high, i * share), scores, NEG)
        peak = jnp.max(scores, axis=0, keepdims=True)
        expo = jnp.exp(scores - peak)
        summed = jnp.sum(expo, axis=0, keepdims=True)
        probs = (expo * (1.0 / summed)).astype(HALF)
        value = kept[0, 2 * HEAD_DIM :, low:high]
        attended[:, spot(i)] = jnp.dot(value, probs, preferred_element_type=FLOAT).astype(HALF)
        log_total[0, 0, :, at] = jnp.broadcast_to(peak + jnp.log(summed), (8, share))


def attend(base, qkv, cosine, sine, first):
    seqs, length = first.shape[0], first.shape[2]
    heads = qkv.shape[0] // (3 * HEAD_DIM)
    tokens = qkv.shape[1]
    return pl.pallas_call(
        attend_kernel,
        grid=(heads, seqs),
        in_specs=[
            pl.BlockSpec(memory_space=pltpu.SMEM),
            pl.BlockSpec((3 * HEAD_DIM, tokens), lambda h, j: (h, 0)),
            pl.BlockSpec(cosine.shape, lambda h, j: (0, 0)),
            pl.BlockSpec(sine.shape, lambda h, j: (0, 0)),
            pl.BlockSpec((1, 8, length), lambda h, j: (j, 0, 0)),
        ],
        out_specs=[
            pl.BlockSpec((HEAD_DIM, tokens), lambda h, j: (h, 0)),
            pl.BlockSpec((1, 3 * HEAD_DIM, length), lambda h, j: (j, h, 0)),
            pl.BlockSpec((1, 1, 8, length), lambda h, j: (j, h, 0, 0)),
        ],
        out_shape=[
            jax.ShapeDtypeStruct((heads * HEAD_DIM, tokens), HALF),
            jax.ShapeDtypeStruct((seqs, heads * 3 * HEAD_DIM, length), HALF),
            jax.ShapeDtypeStruct((seqs, heads, 8, length), FLOAT),
        ],
        compiler_params=pltpu.CompilerParams(vmem_limit_bytes=VMEM_LIMIT),
        cost_estimate=SMALL,
        name="attend",
    )(base, qkv, cosine, sine, first)


def attend_back_kernel(waits, base, kept, log_total, slope, cosine, sine, first, *refs):
    d_qkv, d_key, d_value = refs[waits:]
    seq = pl.program_id(1)
    blocks = base.shape[0]
    length = cosine.shape[1]
    share = length // blocks
    half = HEAD_DIM // 2
    scale = HEAD_DIM**-0.5

    def spot(i):
        return pl.ds(pl.multiple_of(base[i] + seq * share, share), share)

    def put(part, i, low, high):
        at = pl.ds(i * share, share)
        d_low, d_high = turn_rows(low, high, cosine[:, at], -sine[:, at])
        top = part * HEAD_DIM
        d_qkv[top : top + half, spot(i)] = d_low.astype(HALF)
        d_qkv[top + half : top + HEAD_DIM, spot(i)] = d_high.astype(HALF)

    query = kept[0, :HEAD_DIM, :].T
    key = kept[0, HEAD_DIM : 2 * HEAD_DIM, :].T
    value = kept[0, 2 * HEAD_DIM :, :].T
    d_key[...] = jnp.zeros_like(d_key)
    d_value[...] = jnp.zeros_like(d_value)
    for i in range(blocks):
        low, high = reach(i, share, length // 2), (i + 1) * share
        at = pl.ds(i * share, share)
        turned = slope[:, spot(i)]
        scores = jnp.dot(
            key[low:high, :], kept[0, :HEAD_DIM, at], preferred_element_type=FLOAT
        ) * scale
        scores = jnp.where(seen(first[0, :, at][:1], low, high, i * share), scores, NEG)
        probs = jnp.exp(scores - log_total[0, 0, :1, at])
        d_probs = jnp.dot(value[low:high, :], turned, preferred_element_type=FLOAT)
        centre = jnp.sum(probs * d_probs, axis=0, keepdims=True)
        d_scores = (probs * (d_probs - centre)).astype(HALF)
        d_value[low:high, :] += jnp.dot(probs.astype(HALF), turned.T, preferred_element_type=FLOAT)
        d_key[low:high, :] += jnp.dot(
            d_scores, query[i * share : (i + 1) * share, :], preferred_element_type=FLOAT
        )
        d_query = scale * jnp.dot(
            kept[0, HEAD_DIM : 2 * HEAD_DIM, low:high], d_scores, preferred_element_type=FLOAT
        )
        put(0, i, d_query[:half, :], d_query[half:, :])
    for i in range(blocks):
        rows = pl.ds(i * share, share)
        turned = scale * d_key[rows, :].T
        put(1, i, turned[:half, :], turned[half:, :])
        d_qkv[2 * HEAD_DIM :, spot(i)] = d_value[rows, :].T.astype(HALF)


def attend_back(base, kept, log_total, slope, cosine, sine, first, before):
    seqs, length = first.shape[0], first.shape[2]
    tokens = slope.shape[1]
    heads = slope.shape[0] // HEAD_DIM
    return pl.pallas_call(
        functools.partial(attend_back_kernel, len(before)),
        grid=(heads, seqs),
        in_specs=[
            pl.BlockSpec(memory_space=pltpu.SMEM),
            pl.BlockSpec((1, 3 * HEAD_DIM, length), lambda h, j: (j, h, 0)),
            pl.BlockSpec((1, 1, 8, length), lambda h, j: (j, h, 0, 0)),
            pl.BlockSpec((HEAD_DIM, tokens), lambda h, j: (h, 0)),
            pl.BlockSpec(cosine.shape, lambda h, j: (0, 0)),
            pl.BlockSpec(sine.shape, lambda h, j: (0, 0)),
            pl.BlockSpec((1, 8, length), lambda h, j: (j, 0, 0)),
        ]
        + [pl.BlockSpec(memory_space=pl.ANY)] * len(before),
        out_specs=pl.BlockSpec((3 * HEAD_DIM, tokens), lambda h, j: (h, 0)),
        out_shape=jax.ShapeDtypeStruct((heads * 3 * HEAD_DIM, tokens), HALF),
        scratch_shapes=[pltpu.VMEM((length, HEAD_DIM), FLOAT)] * 2,
        compiler_params=pltpu.CompilerParams(vmem_limit_bytes=VMEM_LIMIT),
        cost_estimate=SMALL,
        name="attend_back",
    )(base, kept, log_total, slope, cosine, sine, first, *before)


def near_and_far(own, rank):
    return (own, rank ^ 1), (own, rank ^ 2)


def remote(source, target, send, recv, n, peer):
    return pltpu.make_async_remote_copy(
        src_ref=source,
        dst_ref=target,
        send_sem=send.at[n],
        recv_sem=recv.at[n],
        device_id=peer,
        device_id_type=MESH,
    )


class Boundary:
    COUNT = 6

    def __init__(self, own, rank, send, recv, parts, rows):
        self.near, self.far = near_and_far(own, rank)
        self.send, self.recv, self.parts = send, recv, parts
        self.rows = [pl.ds(h * rows, rows) for h in range(parts)]
        self.copies = []

    def copy(self, source, target, n, h, peer):
        made = remote(source, target, self.send, self.recv, n * self.parts + h, peer)
        made.start()
        self.copies.append(made)
        return made

    def sums(self, make, partial, beside, away, come):
        later, crossing = {}, []

        def part(p, h):
            partial[p, self.rows[h], :] = make(p, h).astype(HALF)

        def leave(p, h):
            part(2 + p, h)
            at = self.rows[h]
            later[p, h] = self.copy(partial.at[2 + p, at], beside.at[p, at], p, h, self.near)

        def pair(p, h):
            at = self.rows[h]
            later[p, h].wait_recv()
            return partial[p, at, :].astype(FLOAT) + beside[p, at, :].astype(FLOAT)

        for h, at in enumerate(self.rows):
            leave(1, h)
            part(1, h)
            away[at, :] = pair(1, h).astype(HALF)
            crossing.append(self.copy(away.at[at], come.at[at], 2, h, self.far))
        for h in range(self.parts):
            leave(0, h)
        for h in range(self.parts):
            part(0, h)
        for h, at in enumerate(self.rows):
            total = pair(0, h)
            crossing[h].wait_recv()
            yield h, at, total + come[at, :].astype(FLOAT)

    def give(self, full, h):
        at = self.rows[h]
        self.crossed = getattr(self, "crossed", [])
        self.crossed.append(self.copy(full.at[0, at], full.at[1, at], 3, h, self.far))
        self.beside = getattr(self, "beside", [])
        self.beside.append(self.copy(full.at[0, at], full.at[2, at], 4, h, self.near))

    def pass_on(self, full):
        arrived = []
        for h, at in enumerate(self.rows):
            self.crossed[h].wait_recv()
            arrived.append(self.copy(full.at[1, at], full.at[3, at], 5, h, self.near))
        for copy in self.beside + arrived:
            copy.wait_recv()

    def end(self):
        for copy in self.copies:
            copy.wait_send()


def turned_product(left, right):
    return lax.dot_general(left, right, (((0,), (1,)), ((), ())), preferred_element_type=FLOAT)


def columns_of(array, p, h, parts):
    step = array.shape[1] // (4 * parts)
    return array[:, (p * parts + h) * step : (p * parts + h + 1) * step]


def rows_of(index, width):
    return pl.ds(pl.multiple_of(index * width, width), width)


def forward_kernel(parts, gathers, attended, both, stream, gain, *refs):
    blocks, refs = refs[:gathers], refs[gathers:]
    if gathers:
        out, full, feed_w, weight, partial, beside, away, come, send, recv = refs
    else:
        out, full, weight, partial, beside, away, come, send, recv = refs
    own, rank = lax.axis_index("dp"), lax.axis_index("tensor")
    near, far = near_and_far(own, rank)
    others = {k: (own ^ k, rank) for k in (1, 2)} if gathers else {}
    greet([near, far, *others.values()])
    edge = Boundary(own, rank, send, recv, parts, stream.shape[0] // parts)
    moved = {}

    def move(source, k, n, peer):
        copy = remote(source, feed_w.at[rows_of(own ^ k, width)], send, recv, n, peer)
        copy.start()
        edge.copies.append(copy)
        return copy

    if gathers:
        mine, four, six = blocks
        width, base = mine.shape[0], Boundary.COUNT * parts
        moved[2] = move(mine, 0, base, others[2])
        for n, (k, block) in enumerate(((0, mine), (4, four), (6, six))):
            moved[k + 1] = move(block, k, base + 1 + n, others[1])
            feed_w[rows_of(own ^ k, width), :] = block[...]
    weight[...] = both[:, both.shape[1] - weight.shape[1] :]

    def make(p, h):
        return turned_product(columns_of(attended, p, h, parts), weight[...])

    for h, at, total in edge.sums(make, partial, beside, away, come):
        total = stream[at, :] + total
        out[at, :] = total
        full[0, at, :] = normed(total, gain[...]).astype(HALF)
        edge.give(full, h)
    if gathers:
        moved[2].wait_recv()
        moved[3] = move(feed_w.at[rows_of(own ^ 2, width)], 2, base + 4, others[1])
    edge.pass_on(full)
    for k in (1, 5, 7, 3) if gathers else ():
        moved[k].wait_recv()
    edge.end()


def forward_boundary(attended, both, stream, gain, blocks):
    rows, depth = stream.shape
    parts = 2
    vmem = pl.BlockSpec(memory_space=pltpu.VMEM)
    scratch = exchange_scratch(rows, depth, parts)[:4]
    semaphores = Boundary.COUNT * parts + 5
    results = pl.pallas_call(
        functools.partial(forward_kernel, parts, len(blocks)),
        in_specs=[vmem] * (4 + len(blocks)),
        out_specs=[vmem] * (3 if blocks else 2),
        out_shape=[
            jax.ShapeDtypeStruct((rows, depth), FLOAT),
            jax.ShapeDtypeStruct((4, rows, depth), HALF),
        ]
        + [jax.ShapeDtypeStruct((8 * b.shape[0], b.shape[1]), HALF) for b in blocks[:1]],
        scratch_shapes=[pltpu.VMEM((depth, attended.shape[0]), HALF)]
        + scratch
        + [pltpu.SemaphoreType.DMA((semaphores,))] * 2,
        compiler_params=pltpu.CompilerParams(
            collective_id=3, has_side_effects=True, vmem_limit_bytes=VMEM_LIMIT
        ),
        cost_estimate=SMALL,
        name="forward_boundary",
    )(attended, both, stream, gain, *blocks)
    return (results[0], results[1].reshape(4 * rows, depth), *results[2:])


def normed_slope(grad, values, gain):
    root = lax.rsqrt(jnp.mean(values * values, axis=-1, keepdims=True) + EPS)
    unit = values * root
    inner = grad * gain
    middle = jnp.mean(inner * unit, axis=-1, keepdims=True)
    return root * (inner - unit * middle), jnp.sum(grad * unit, axis=0, keepdims=True)


def wide_forward_kernel(
    norm, weight, stream, gain, out, full, partial, beside, away, come, send, recv
):
    own, rank = lax.axis_index("dp"), lax.axis_index("tensor")
    near, far = near_and_far(own, rank)
    other = (own ^ 1, rank)
    greet([near, far, other])
    parts = 2
    edge = Boundary(own, rank, send, recv, parts, stream.shape[0] // parts)
    crossed, moved, last = [], [], []
    ffn = weight.shape[1] // 3

    def make(p, h):
        both = jnp.dot(
            norm[p, edge.rows[h], :], weight[:, : 2 * ffn], preferred_element_type=FLOAT
        )
        gate, up = both[:, :ffn], both[:, ffn:]
        hidden = (gate * (1.0 / (1.0 + jnp.exp(-gate))) * up).astype(HALF)
        return across(hidden, weight[:, 2 * ffn :])

    for h, at, total in edge.sums(make, partial, beside, away, come):
        total = stream[at, :] + total
        out[at, :] = total
        full[0, 0, at, :] = normed(total, gain[...]).astype(HALF)
        mine = full.at[0, 0, at]
        crossed.append(edge.copy(mine, full.at[0, 1, at], 3, h, far))
        moved.append(edge.copy(mine, full.at[1, 0, at], 4, h, other))
        last.append(edge.copy(mine, full.at[0, 2, at], 5, h, near))
    early, late = edge.rows
    crossed[0].wait_recv()
    one = edge.copy(full.at[0, 1, early], full.at[1, 1, early], 6, 0, other)
    last.append(edge.copy(full.at[0, 1, early], full.at[0, 3, early], 7, 0, near))
    moved[0].wait_recv()
    last.append(edge.copy(full.at[1, 0, early], full.at[1, 2, early], 8, 0, near))
    moved[1].wait_recv()
    two = edge.copy(full.at[1, 0, late], full.at[1, 1, late], 6, 1, far)
    last.append(edge.copy(full.at[1, 0, late], full.at[1, 2, late], 8, 1, near))
    crossed[1].wait_recv()
    last.append(edge.copy(full.at[0, 1, late], full.at[0, 3, late], 7, 1, near))
    one.wait_recv()
    last.append(edge.copy(full.at[1, 1, early], full.at[1, 3, early], 9, 0, near))
    two.wait_recv()
    last.append(edge.copy(full.at[1, 1, late], full.at[1, 3, late], 9, 1, near))
    for copy in last:
        copy.wait_recv()
    edge.end()


def wide_forward(norm, weight, stream, gain):
    rows, depth = stream.shape
    vmem = pl.BlockSpec(memory_space=pltpu.VMEM)
    out, full = pl.pallas_call(
        wide_forward_kernel,
        in_specs=[vmem] * 4,
        out_specs=[vmem] * 2,
        out_shape=[
            jax.ShapeDtypeStruct((rows, depth), FLOAT),
            jax.ShapeDtypeStruct((2, 4, rows, depth), HALF),
        ],
        scratch_shapes=exchange_scratch(rows, depth, 2)[:4] + [pltpu.SemaphoreType.DMA((20,))] * 2,
        compiler_params=pltpu.CompilerParams(
            collective_id=9, has_side_effects=True, vmem_limit_bytes=VMEM_LIMIT
        ),
        cost_estimate=SMALL,
        name="wide_forward",
    )(norm.reshape(4, rows, depth), weight, stream, gain)
    return out, full.reshape(8 * rows, depth)


def wide_backward_kernel(partial, stream, gain, out, g_gain, full, beside, leave, come, send, recv):
    own, rank = lax.axis_index("dp"), lax.axis_index("tensor")
    near, far = near_and_far(own, rank)
    other = (own ^ 1, rank)
    greet([near, far, other])
    parts = 2
    edge = Boundary(own, rank, send, recv, parts, stream.shape[0] // parts)
    early, late = edge.rows
    first = {}
    for n, (y, p) in enumerate(((1, 1), (1, 0), (0, 1), (0, 0))):
        for h, at in enumerate(edge.rows):
            first[y, p, h] = edge.copy(
                partial.at[y, 2 + p, at], beside.at[y, p, at], 5 + n, h, near
            )

    def pair(y, p, h):
        at = edge.rows[h]
        first[y, p, h].wait_recv()
        return partial[y, p, at, :].astype(FLOAT) + beside[y, p, at, :].astype(FLOAT)

    leave[1, 1, early, :] = pair(1, 1, 0).astype(HALF)
    by_other = edge.copy(leave.at[1, 1, early], come.at[1, 1, early], 9, 0, other)
    leave[1, 1, late, :] = pair(1, 1, 1).astype(HALF)
    by_far = edge.copy(leave.at[1, 1, late], come.at[1, 1, late], 9, 1, far)
    leave[1, 0, early, :] = pair(1, 0, 0).astype(HALF)
    other_early = edge.copy(leave.at[1, 0, early], come.at[1, 0, early], 0, 0, other)
    leave[0, 1, late, :] = pair(0, 1, 1).astype(HALF)
    far_late = edge.copy(leave.at[0, 1, late], come.at[0, 1, late], 1, 1, far)
    far_early_sum, other_late_sum = pair(0, 1, 0), pair(1, 0, 1)
    by_other.wait_recv()
    leave[0, 1, early, :] = (far_early_sum + come[1, 1, early, :].astype(FLOAT)).astype(HALF)
    far_early = edge.copy(leave.at[0, 1, early], come.at[0, 1, early], 1, 0, far)
    by_far.wait_recv()
    leave[1, 0, late, :] = (other_late_sum + come[1, 1, late, :].astype(FLOAT)).astype(HALF)
    other_late = edge.copy(leave.at[1, 0, late], come.at[1, 0, late], 0, 1, other)
    g_gain[...] = jnp.zeros_like(g_gain)
    for h, waits in ((0, (other_early, far_early)), (1, (far_late, other_late))):
        at = edge.rows[h]
        total = pair(0, 0, h)
        for copy in waits:
            copy.wait_recv()
        total = total + come[1, 0, at, :].astype(FLOAT) + come[0, 1, at, :].astype(FLOAT)
        slope, by_gain = normed_slope(total, stream[at, :], gain[...])
        g_gain[:1, :] = g_gain[:1, :] + by_gain
        out[at, :] = slope
        full[0, at, :] = slope.astype(HALF)
        edge.crossed = getattr(edge, "crossed", [])
        edge.crossed.append(edge.copy(full.at[0, at], full.at[1, at], 2, h, far))
        edge.beside = getattr(edge, "beside", [])
        edge.beside.append(edge.copy(full.at[0, at], full.at[2, at], 3, h, near))
    arrived = []
    for h, at in enumerate(edge.rows):
        edge.crossed[h].wait_recv()
        arrived.append(edge.copy(full.at[1, at], full.at[3, at], 4, h, near))
    for copy in edge.beside + arrived:
        copy.wait_recv()
    edge.end()


def wide_backward(partial, stream, gain):
    rows, depth = stream.shape
    vmem = pl.BlockSpec(memory_space=pltpu.VMEM)
    out, g_gain, full = pl.pallas_call(
        wide_backward_kernel,
        in_specs=[vmem] * 3,
        out_specs=[vmem] * 3,
        out_shape=[
            jax.ShapeDtypeStruct((rows, depth), FLOAT),
            jax.ShapeDtypeStruct((8, depth), FLOAT),
            jax.ShapeDtypeStruct((4, rows, depth), HALF),
        ],
        scratch_shapes=[pltpu.VMEM((2, 2, rows, depth), HALF)] * 3
        + [pltpu.SemaphoreType.DMA((20,))] * 2,
        compiler_params=pltpu.CompilerParams(
            collective_id=4, has_side_effects=True, vmem_limit_bytes=VMEM_LIMIT
        ),
        cost_estimate=SMALL,
        name="wide_backward",
    )(partial.reshape(2, 4, rows, depth), stream, gain)
    return out, g_gain[:1], full.reshape(4 * rows, depth)


def exchange_scratch(rows, depth, parts):
    return [
        pltpu.VMEM((4, rows, depth), HALF),
        pltpu.VMEM((2, rows, depth), HALF),
        pltpu.VMEM((rows, depth), HALF),
        pltpu.VMEM((rows, depth), HALF),
        pltpu.SemaphoreType.DMA((Boundary.COUNT * parts,)),
        pltpu.SemaphoreType.DMA((Boundary.COUNT * parts,)),
    ]


def backward_kernel(
    parts, norm, later, weight, stream, gain, prior, out, g_gain, full, grad, partial, beside, away, come, kept, send, recv
):
    own, rank = lax.axis_index("dp"), lax.axis_index("tensor")
    greet(list(near_and_far(own, rank)))
    edge = Boundary(own, rank, send, recv, parts, stream.shape[0] // parts)
    ffn = weight.shape[1] // 3

    def make(p, h):
        at = edge.rows[h]
        both = jnp.dot(norm[p, at, :], weight[:, : 2 * ffn], preferred_element_type=FLOAT)
        d_hidden = jnp.dot(later[p, at, :], weight[:, 2 * ffn :], preferred_element_type=FLOAT)
        gate, up = both[:, :ffn], both[:, ffn:]
        open_part = 1.0 / (1.0 + jnp.exp(-gate))
        passed = gate * open_part
        d_gate = (d_hidden * up * (open_part * (1.0 + gate * (1.0 - open_part)))).astype(HALF)
        d_up = (d_hidden * passed).astype(HALF)
        kept[p, at, :ffn] = d_gate
        kept[p, at, ffn : 2 * ffn] = d_up
        kept[p, at, 2 * ffn :] = (passed * up).astype(HALF)
        return across(d_gate, weight[:, :ffn]) + across(d_up, weight[:, ffn : 2 * ffn])

    g_gain[...] = jnp.zeros_like(g_gain)
    for h, at, total in edge.sums(make, partial, beside, away, come):
        slope, by_gain = normed_slope(total, stream[at, :], gain[...])
        slope = slope + prior[at, :]
        g_gain[:1, :] = g_gain[:1, :] + by_gain
        out[at, :] = slope
        full[0, at, :] = slope.astype(HALF)
        edge.give(full, h)
    for left, low, high in ((norm, 0, 2 * ffn), (later, 2 * ffn, 3 * ffn)):
        turned = [left[p].T for p in range(4)]
        for c in range(low, high, CHUNK):
            total = jnp.dot(turned[0], kept[0, :, c : c + CHUNK], preferred_element_type=FLOAT)
            for p in (1, 2, 3):
                total = total + jnp.dot(
                    turned[p], kept[p, :, c : c + CHUNK], preferred_element_type=FLOAT
                )
            grad[:, c : c + CHUNK] = total.astype(HALF)
    edge.pass_on(full)
    edge.end()


def backward_boundary(norm, later, weight, stream, gain, prior):
    rows, depth = stream.shape
    parts = 2
    vmem = pl.BlockSpec(memory_space=pltpu.VMEM)
    scratch = exchange_scratch(rows, depth, parts)
    out, g_gain, full, grad = pl.pallas_call(
        functools.partial(backward_kernel, parts),
        in_specs=[vmem] * 6,
        out_specs=[vmem] * 4,
        out_shape=[
            jax.ShapeDtypeStruct((rows, depth), FLOAT),
            jax.ShapeDtypeStruct((8, depth), FLOAT),
            jax.ShapeDtypeStruct((4, rows, depth), HALF),
            jax.ShapeDtypeStruct(weight.shape, HALF),
        ],
        scratch_shapes=scratch[:4] + [pltpu.VMEM((4, rows, weight.shape[1]), HALF)] + scratch[4:],
        compiler_params=pltpu.CompilerParams(
            collective_id=5, has_side_effects=True, vmem_limit_bytes=VMEM_LIMIT
        ),
        cost_estimate=SMALL,
        name="backward_boundary",
    )(norm.reshape(4, rows, depth), later.reshape(4, rows, depth), weight, stream, gain, prior)
    return out, g_gain[:1], full.reshape(4 * rows, depth), grad


def start_kernel(
    ids, turned, gain, block, feed, stays, leaves, stream, full, weights, four, six, pair, *refs
):
    table, corner, rows, out, near, cross, come, send, recv, local = refs
    own, rank = lax.axis_index("dp"), lax.axis_index("tensor")
    beside, across = near_and_far(own, rank)
    far = [(own ^ k, rank) for k in range(1, 8)]
    greet([beside, across] + far)
    width, vocab = turned.shape
    count = rows.shape[0]
    copies, beside_of, across_of, far_of = [], {}, {}, {}

    def begin(source, target, n, peer):
        copy = remote(source, target, send, recv, n, peer)
        copy.start()
        copies.append(copy)
        return copy

    def place(k):
        return pl.ds(pl.multiple_of((own ^ k) * width, width), width)

    weights_of = {}
    for k in (1, 2, 4, 6):
        weights_of[k] = begin(block, weights.at[place(0)], 35 + k, far[k - 1])
    weights[place(0), :] = block[...]
    bit = own % 2
    line = pl.ds(pl.multiple_of(bit * width, width), width)
    aside = begin(leaves, pair.at[line], 43, far[0])
    own_line = pltpu.make_async_copy(stays, pair.at[line], local)
    own_line.start()
    corner[...] = jnp.zeros_like(corner)
    for v in range(0, vocab, LANES):
        some = min(LANES, vocab - v)
        corner[:width, :some] = turned[:, v : v + some].astype(HALF).astype(FLOAT)
        if some < LANES:
            corner[:width, some:] = jnp.zeros((width, LANES - some), FLOAT)
        table[v : v + LANES, :] = corner[...].T
    if vocab % LANES == 0:
        table[vocab:, :] = jnp.zeros((LANES, LANES), FLOAT)

    def fetch(place):
        def body(i, carry):
            for u in range(16):
                r = i * 16 + u
                rows[pl.ds(r, 1), :] = table[pl.ds(ids[place * count + r], 1), :]
            return carry

        lax.fori_loop(0, count // 16, body, 0)

    for p in (3, 2):
        for k in range(8):
            fetch(p * 8 + k)
            out[p, k] = rows[:, :width].astype(HALF)
            beside_of[p - 2, k] = begin(out.at[p, k], near.at[p - 2, k], (p - 2) * 8 + k, beside)
    for k in (2, 4, 6):
        weights_of[k].wait_recv()
        weights_of[k + 1] = begin(weights.at[place(k)], weights.at[place(k)], 36 + k, far[0])
    sixth = begin(feed, six, 45, far[5])
    order = (7, 6, 5, 4, 3, 2, 1, 0)
    for k in order:
        fetch(8 + k)
        beside_of[1, k].wait_recv()
        total = rows[:, :width] + near[1, k].astype(FLOAT)
        out[1, k] = total.astype(HALF)
        across_of[k] = begin(out.at[1, k], cross.at[k], 16 + k, across)
    for k in order:
        fetch(k)
        beside_of[0, k].wait_recv()
        total = rows[:, :width] + near[0, k].astype(FLOAT)
        across_of[k].wait_recv()
        out[0, k] = (total + cross[k].astype(FLOAT)).astype(HALF)
        if k:
            far_of[k] = begin(out.at[0, k], come.at[k], 24 + k, far[k - 1])
    fourth = begin(feed, four, 44, far[3])
    come[0] = out[0, 0]
    for k in order[:-1]:
        far_of[k].wait_recv()
    for b in range(8):
        stream[:, b * width : (b + 1) * width] = come[own ^ b].astype(FLOAT)
    full[0] = normed(stream[...], gain[...]).astype(HALF)
    one = begin(full.at[0], full.at[1], 32, across)
    two = begin(full.at[0], full.at[2], 33, beside)
    one.wait_recv()
    three = begin(full.at[1], full.at[3], 34, beside)
    two.wait_recv()
    three.wait_recv()
    for k in (1, 3, 5, 7):
        weights_of[k].wait_recv()
    aside.wait_recv()
    fourth.wait_recv()
    sixth.wait_recv()
    own_line.wait()
    for copy in copies:
        copy.wait_send()


def start_rows(ids, turned, gain, block, feed, stays, leaves):
    width, vocab = turned.shape
    rows = ids.shape[0] // 32
    padded = (vocab // LANES + 1) * LANES
    vmem = pl.BlockSpec(memory_space=pltpu.VMEM)
    whole = pl.BlockSpec(memory_space=pl.ANY)
    stream, full, weights, four, six, pair = pl.pallas_call(
        start_kernel,
        in_specs=[pl.BlockSpec(memory_space=pltpu.SMEM), vmem, vmem, vmem, vmem, whole, whole],
        out_specs=[vmem] * 5 + [whole],
        out_shape=[
            jax.ShapeDtypeStruct((rows, 8 * width), FLOAT),
            jax.ShapeDtypeStruct((4, rows, 8 * width), HALF),
            jax.ShapeDtypeStruct((8 * width, block.shape[1]), HALF),
            jax.ShapeDtypeStruct(feed.shape, HALF),
            jax.ShapeDtypeStruct(feed.shape, HALF),
            jax.ShapeDtypeStruct((2 * width, stays.shape[1]), HALF),
        ],
        scratch_shapes=[
            pltpu.VMEM((padded, LANES), FLOAT),
            pltpu.VMEM((LANES, LANES), FLOAT),
            pltpu.VMEM((rows, LANES), FLOAT),
            pltpu.VMEM((4, 8, rows, width), HALF),
            pltpu.VMEM((2, 8, rows, width), HALF),
            pltpu.VMEM((8, rows, width), HALF),
            pltpu.VMEM((8, rows, width), HALF),
            pltpu.SemaphoreType.DMA((46,)),
            pltpu.SemaphoreType.DMA((46,)),
            pltpu.SemaphoreType.DMA,
        ],
        compiler_params=pltpu.CompilerParams(
            collective_id=6, has_side_effects=True, vmem_limit_bytes=VMEM_LIMIT
        ),
        cost_estimate=SMALL,
        name="start_rows",
    )(ids, turned, gain, block, feed, stays, leaves)
    return stream, full.reshape(4 * rows, 8 * width), weights, four, six, pair


def end_kernel(parts, waits, d_qkv, weight, stream, gain, prior, gain_one, gain_two, apart, *refs):
    rows, g_gain, arrived, partial, beside, away, come, leave, mine, summed, first, second, send, recv = refs[waits:]
    own, rank = lax.axis_index("dp"), lax.axis_index("tensor")
    near, across = near_and_far(own, rank)
    far = [(own ^ k, rank) for k in range(1, 8)]
    greet([near, across, (own, rank ^ 3)] + far)
    edge = Boundary(own, rank, send, recv, parts, stream.shape[0] // parts)
    aside = remote(apart, arrived, send, recv, Boundary.COUNT * parts, far[0])
    aside.start()
    edge.copies.append(aside)
    width = rows.shape[3]
    gain_zero = jnp.zeros_like(gain[...])
    mine[...] = jnp.zeros_like(mine)

    def make(p, h):
        return turned_product(columns_of(d_qkv, p, h, parts), weight[:, : d_qkv.shape[0]])

    for h, at, total in edge.sums(make, partial, beside, away, come):
        slope, by_gain = normed_slope(total, stream[at, :], gain[...])
        slope = slope + prior[at, :]
        gain_zero = gain_zero + by_gain
        for b in range(8):
            leave[b, at, :] = slope[:, b * width : (b + 1) * width].astype(HALF)
    base = Boundary.COUNT * parts
    far_of, last = {}, []

    def begin(source, target, n, peer):
        copy = remote(source, target, send, recv, base + n, peer)
        copy.start()
        edge.copies.append(copy)
        return copy

    order = (7, 6, 5, 4, 3, 2, 1)
    for k in order:
        far_of[k] = begin(leave.at[own ^ k], rows.at[0, k], k, far[k - 1])
    rows[0, 0] = leave[own]
    for b in range(8):
        for n, line in enumerate((gain_zero, gain_one[...], gain_two[...])):
            mine[own ^ b, n : n + 1, :width] = line[:, b * width : (b + 1) * width]
    gains_of = [
        begin(mine, first.at[n - 1], 31 + n, (own, rank ^ n)) for n in (1, 2, 3)
    ]
    crossed = {}
    for k in (0, 1, 2, 3, 4, 5, 6, 7):
        if k:
            far_of[k].wait_recv()
        crossed[k] = begin(rows.at[0, k], rows.at[1, k], 8 + k, across)
        last.append(begin(rows.at[0, k], rows.at[2, k], 16 + k, near))
    for copy in gains_of:
        copy.wait_recv()
    summed[...] = (mine[...] + first[0]) + (first[1] + first[2])
    gains_of = [begin(summed.at[k], second.at[k], 34 + k, far[k - 1]) for k in range(1, 8)]
    for k in (0, 1, 2, 3, 4, 5, 6, 7):
        crossed[k].wait_recv()
        last.append(begin(rows.at[1, k], rows.at[3, k], 24 + k, near))
    for copy in last + gains_of:
        copy.wait_recv()
    second[0] = summed[0]
    pairs = [second[k] + second[k + 1] for k in (0, 2, 4, 6)]
    g_gain[...] = (pairs[0] + pairs[1]) + (pairs[2] + pairs[3])
    aside.wait_recv()
    edge.end()


def end_rows(d_qkv, weight, stream, gain, prior, gain_one, gain_two, apart, width, before):
    rows, depth = stream.shape
    parts = 2
    vmem = pl.BlockSpec(memory_space=pltpu.VMEM)
    semaphores = Boundary.COUNT * parts + 42
    whole = pl.BlockSpec(memory_space=pl.ANY)
    out, g_gain, arrived = pl.pallas_call(
        functools.partial(end_kernel, parts, len(before)),
        in_specs=[vmem] * 7 + [whole] * (1 + len(before)),
        out_specs=[vmem] * 2 + [whole],
        out_shape=[
            jax.ShapeDtypeStruct((4, 8, rows, width), HALF),
            jax.ShapeDtypeStruct((8, LANES), FLOAT),
            jax.ShapeDtypeStruct(apart.shape, HALF),
        ],
        scratch_shapes=exchange_scratch(rows, depth, parts)[:4]
        + [
            pltpu.VMEM((8, rows, width), HALF),
            pltpu.VMEM((8, 8, LANES), FLOAT),
            pltpu.VMEM((8, 8, LANES), FLOAT),
            pltpu.VMEM((3, 8, 8, LANES), FLOAT),
            pltpu.VMEM((8, 8, LANES), FLOAT),
            pltpu.SemaphoreType.DMA((semaphores,)),
            pltpu.SemaphoreType.DMA((semaphores,)),
        ],
        compiler_params=pltpu.CompilerParams(
            collective_id=7, has_side_effects=True, vmem_limit_bytes=VMEM_LIMIT
        ),
        cost_estimate=SMALL,
        name="end_rows",
    )(d_qkv, weight, stream, gain, prior, gain_one, gain_two, apart, *before)
    return out.reshape(-1, width), g_gain[:3, :width], arrived


def merge_kernel(scan, extra, joined, mine, every, send, recv):
    own, rank = lax.axis_index("dp"), lax.axis_index("tensor")
    turns = [(a, b) for a in (0, 1) for b in range(4)][1:]
    peers = [(own ^ a, rank ^ b) for a, b in turns]
    greet(peers)
    tokens = scan.shape[1] // 2
    share = tokens // 4
    mine[...] = jnp.zeros_like(mine)
    mine[0:3, :] = scan[0:3, :tokens]
    mine[3:6, :] = scan[0:3, tokens:]
    copies = []
    for n, peer in enumerate(peers):
        copies.append(remote(mine, every.at[n], send, recv, n, peer))
        copies[-1].start()
    joined[...] = jnp.zeros_like(joined)
    joined[2:4, :] = extra[:2, :]
    for copy in copies:
        copy.wait()
    for y in (0, 1):
        for p in range(4):
            terms = {(0, 0): mine[3 * y : 3 * y + 3, p * share : (p + 1) * share]}
            for n, (a, b) in enumerate(turns):
                q = TURN.index(TURN[p] ^ b)
                terms[a, b] = every[n, 3 * (y ^ a) : 3 * (y ^ a) + 3, q * share : (q + 1) * share]
            peak = functools.reduce(jnp.maximum, [term[0:1] for term in terms.values()])
            sums, hits = [], []
            for a in (0, 1):
                for b in (0, 2):
                    pair = (terms[a, b], terms[a, b ^ 1])
                    sums.append(sum(term[1:2] * jnp.exp(term[0:1] - peak) for term in pair))
                    hits.append(pair[0][2:3] + pair[1][2:3])
            at = pl.ds(y * tokens + p * share, share)
            joined[0:1, at] = peak + jnp.log((sums[0] + sums[1]) + (sums[2] + sums[3]))
            joined[1:2, at] = (hits[0] + hits[1]) + (hits[2] + hits[3])


def merge_scans(scan, extra):
    vmem = pl.BlockSpec(memory_space=pltpu.VMEM)
    shape = (8, scan.shape[1] // 2)
    return pl.pallas_call(
        merge_kernel,
        in_specs=[vmem] * 2,
        out_specs=vmem,
        out_shape=jax.ShapeDtypeStruct(scan.shape, FLOAT),
        scratch_shapes=[
            pltpu.VMEM(shape, FLOAT),
            pltpu.VMEM((7, *shape), FLOAT),
            pltpu.SemaphoreType.DMA((7,)),
            pltpu.SemaphoreType.DMA((7,)),
        ],
        compiler_params=pltpu.CompilerParams(collective_id=8, has_side_effects=True),
        name="merge_scans",
    )(scan, extra)


def across(left, right):
    return lax.dot_general(left, right, (((1,), (1,)), ((), ())), preferred_element_type=FLOAT)


def product(left, right, over_left, over_right):
    return lax.dot_general(
        left, right, (((over_left,), (over_right,)), ((), ())), preferred_element_type=FLOAT
    )


def adam(weight, grad, first, second, rate, decay):
    first = BETA_ONE * first + (1.0 - BETA_ONE) * grad
    second = BETA_TWO * second + (1.0 - BETA_TWO) * grad * grad
    first_hat = first / (1.0 - BETA_ONE**STEP)
    second_hat = second / (1.0 - BETA_TWO**STEP)
    weight = weight - rate * (first_hat / (jnp.sqrt(second_hat) + ADAM_EPS) + decay * weight)
    return (weight, first, second, weight.astype(HALF))


def update_kernel(counts, factor, *refs):
    arrays = len(counts)
    inputs, outputs = refs[: 3 * arrays + sum(counts)], refs[3 * arrays + sum(counts) :]
    grads = inputs[3 * arrays :]
    for n in range(arrays):
        weight, first, second = inputs[3 * n : 3 * n + 3]
        low = 0
        for grad in grads[: counts[n]]:
            high = low + grad.shape[-1]
            at = (Ellipsis, slice(low, high))
            results = adam(
                weight[at], grad[...].astype(FLOAT) * factor[0], first[at], second[at], LR, DECAY
            )
            for out, result in zip(outputs[4 * n : 4 * n + 4], results):
                out[at] = result
            low = high
        grads = grads[counts[n] :]


def update(arrays, factor):
    rows = arrays[0][0].shape[0]
    steps = rows // 16 if rows % 16 == 0 else 1

    def block(array):
        zeros = (0,) * (array.ndim - 1)
        return pl.BlockSpec((array.shape[0] // steps, *array.shape[1:]), lambda i: (i, *zeros))

    inputs = [array for entry in arrays for array in entry[:3]]
    grads = [grad for entry in arrays for grad in entry[3]]
    outs = [
        jax.ShapeDtypeStruct(entry[0].shape, kind)
        for entry in arrays
        for kind in (FLOAT, FLOAT, FLOAT, HALF)
    ]
    results = pl.pallas_call(
        functools.partial(update_kernel, tuple(len(entry[3]) for entry in arrays)),
        grid=(steps,),
        in_specs=[pl.BlockSpec(memory_space=pltpu.SMEM)] + [block(a) for a in inputs + grads],
        out_specs=[block(a) for a in outs],
        out_shape=outs,
        compiler_params=pltpu.CompilerParams(vmem_limit_bytes=VMEM_LIMIT),
        cost_estimate=SMALL,
        name="update",
    )(factor.reshape(1), *inputs, *grads)
    return [results[4 * n : 4 * n + 4] for n in range(len(arrays))]


def shards(
    token_ids,
    targets,
    segments,
    completion,
    micro_order,
    *state,
):
    weights, means, squares_in = state[:7], state[7:14], state[14:21]
    embedding, attn_in, attn_out, ffn_in, ffn_out, head_table, norm_gains = weights
    group = lax.axis_size("dp")
    parts = lax.axis_size("tensor")
    own, rank = lax.axis_index("dp"), lax.axis_index("tensor")
    vocab, width = embedding.shape
    start = rank * vocab
    seqs, length = token_ids.shape
    micro = micro_order.shape[1]
    share = length // parts
    turn = jnp.array(TURN, jnp.int32)
    dp_order = own ^ jnp.arange(group, dtype=jnp.int32)
    tensor_order = rank ^ turn
    tensor_order_natural = rank ^ jnp.arange(parts, dtype=jnp.int32)
    ffn = ffn_out.shape[0]
    qkv_width = attn_in.shape[1]

    attn_block = jnp.concatenate([attn_in, attn_out.T], axis=1).astype(HALF)
    ffn_block = jnp.concatenate([ffn_in.reshape(width, -1), ffn_out.T], axis=1).astype(HALF)
    bit = own % 2
    entries = vocab // 2
    low_half, high_half = head_table[:, :entries].astype(HALF), head_table[:, entries:].astype(HALF)
    stays = jnp.where(bit == 0, low_half, high_half)
    leaves = jnp.where(bit == 0, high_half, low_half)
    lines = [[i for i in range(group) if i % 2 == odd] for odd in (0, 1)]

    picked_rows = micro_order[0]
    takes_seq = picked_rows[:, None] == jnp.arange(seqs)[None, :]
    local_counts = jnp.sum(jnp.where(takes_seq, jnp.sum(completion, axis=1)[None, :], 0), axis=1)
    id_rows = seqs * length // LANES
    packed = jnp.concatenate(
        [
            token_ids.reshape(-1),
            targets.reshape(-1),
            completion.reshape(-1),
            jnp.pad(jnp.concatenate([local_counts, picked_rows]), (0, 8 * LANES - 2 * micro)),
        ]
    ).reshape(3 * id_rows + 8, LANES)
    gains = jnp.pad(norm_gains.astype(HALF).astype(FLOAT), ((0, 5), (0, LANES - width)))
    if group == 8:
        packed, every_id, gains, extra = spread(
            packed, gains, seqs, length, micro, vocab, width
        )
        every_id = every_id.reshape(-1)
    else:
        packed, gains = lax.all_gather(packed, "dp"), lax.all_gather(gains, "dp")
        packed = jnp.take(packed, dp_order, axis=0)
        every_id = packed[:, :id_rows].reshape(group, seqs, parts, share)
        every_id = jnp.take(every_id, tensor_order, axis=2)
        every_id = every_id.transpose(2, 0, 1, 3).reshape(-1) - start
        every_id = jnp.where((every_id >= 0) & (every_id < vocab), every_id, vocab)
        gains = gains.transpose(1, 0, 2)[:, :, :width].reshape(8, -1)
    packed, leaves = lax.optimization_barrier((packed, leaves))
    gains = gains[:3]
    numbers = packed[:, 3 * id_rows, : 2 * micro]
    counts = jnp.sum(numbers[:, :micro].astype(FLOAT), axis=0)

    def both_order(values):
        values = values.reshape(seqs, parts, share)
        values = jnp.where(rank % 2 == 1, values[:, [1, 0, 3, 2]], values)
        values = jnp.where(rank // 2 == 1, values[:, [2, 3, 0, 1]], values)
        return values[:, list(TURN)].transpose(1, 0, 2).reshape(-1)

    if group != 8:
        rows_extra = []
        for k in (0, 1):
            its_flags = packed[k, 2 * id_rows : 3 * id_rows].reshape(seqs, length).astype(FLOAT)
            its_order = numbers[k, micro:]
            takes = (its_order[None, :] == jnp.arange(seqs)[:, None]).astype(FLOAT)
            its_scale = its_flags * jnp.sum(takes / jnp.maximum(counts, 1.0), axis=1)[:, None]
            aims = packed[k, id_rows : 2 * id_rows].reshape(seqs, length) - start - bit * entries
            aims = jnp.where((aims >= 0) & (aims < entries), aims, -1).astype(FLOAT)
            rows_extra.append(jnp.stack([both_order(its_scale), both_order(aims), both_order(its_flags)]))
        extra = jnp.pad(jnp.concatenate(rows_extra, axis=1), ((0, 5), (0, 0)))

    own_segment = segments[:, :, None] == jnp.arange(8, dtype=jnp.int32)
    sizes = jnp.sum(own_segment.astype(jnp.int32), axis=1)
    begins = jnp.cumsum(sizes, axis=1) - sizes
    first = jnp.sum(jnp.where(own_segment, begins[:, None, :], 0), axis=2)
    first = jnp.broadcast_to(first[:, None, :], (seqs, 8, length))
    base = turn[tensor_order_natural] * (seqs * share)
    cosine, sine = tables(length, HEAD_DIM)

    if group == 8:
        stream0, attn_norm, attn_w, ffn_four, ffn_six, head_rows = start_rows(
            every_id, embedding.T, gains[:1], attn_block, ffn_block, stays, leaves
        )
        ffn_blocks = [ffn_block, ffn_four, ffn_six]
    else:
        rows = lookup(embedding.T, every_id).reshape(parts, group, seqs * share, width)
        rows = rows[:2] + swap(rows[2:], "tensor", 1)
        rows = rows[0] + swap(rows[1], "tensor", 2)
        rows = lax.all_to_all(jnp.take(rows, dp_order, axis=0), "dp", 0, 0)
        stream0 = rows.transpose(1, 0, 2).reshape(seqs * share, -1).astype(FLOAT)
        attn_norm = tensor_gather(normed(stream0, gains[0]).astype(HALF))

        attn_w = lax.all_gather(attn_block, "dp", axis=0, tiled=True)
        came = swap(leaves, "dp", 1)
        head_rows = jnp.concatenate(
            [jnp.where(bit == 0, stays, came), jnp.where(bit == 0, came, stays)], axis=0
        )
        ffn_blocks = []
    head_b = lax.all_gather(head_rows, "dp", axis=0, tiled=True, axis_index_groups=lines)
    attn_in_b, attn_out_b = attn_w[:, :qkv_width], attn_w[:, qkv_width:]
    qkv = product(attn_in_b, attn_norm, 0, 1)
    attended, kept, log_sums = attend(base, qkv, cosine, sine, first)
    stream1, ffn_norm, *ffn_w = forward_boundary(
        attended, attn_w, stream0, gains[1:2], ffn_blocks
    )
    ffn_w = ffn_w[0] if ffn_w else lax.all_gather(ffn_block, "dp", axis=0, tiled=True)
    stream2, final_norm = wide_forward(ffn_norm, ffn_w, stream1, gains[2:])

    logits, scan, final_turned = head_scan(final_norm, head_b, extra)
    info = merge_scans(scan, extra)
    tokens = seqs * length
    seq_loss = jnp.sum(
        ((info[0, :tokens] - info[1, :tokens]) * extra[2, :tokens]).reshape(parts, seqs, share),
        axis=(0, 2),
    )
    g_head, d_final = head_grad(final_turned, head_b, info, logits)
    g_head = lax.psum_scatter(
        g_head, "dp", scatter_dimension=0, tiled=True, axis_index_groups=lines
    )
    g_stays = jnp.where(bit == 0, g_head[:width], g_head[width:])
    g_leaves = jnp.where(bit == 0, g_head[width:], g_head[:width])

    d_stream2, g_gain2, d_branch2 = wide_backward(d_final, stream2, gains[2:])
    d_stream1, g_gain1, d_branch1, g_ffn = backward_boundary(
        ffn_norm, d_branch2, ffn_w, stream1, gains[1:2], d_stream2
    )
    g_ffn_parts = scatter_first(g_ffn)
    d_attended = product(attn_out_b, d_branch1, 0, 1).astype(HALF)
    d_qkv = attend_back(base, kept, log_sums, d_attended, cosine, sine, first, [])
    if group == 8:
        rows, g_gains, g_came = end_rows(
            d_qkv,
            attn_w,
            stream0,
            gains[:1],
            d_stream1,
            g_gain1,
            g_gain2,
            g_leaves,
            width,
            [],
        )
    else:
        d_norm = tensor_scatter(product(d_qkv, attn_in_b, 0, 1))
        d_part, g_gain0 = normed_slope(d_norm, stream0, gains[:1])
        rows = (d_stream1 + d_part).astype(HALF)
        rows = rows.reshape(seqs * share, group, width).transpose(1, 0, 2)
        rows = jnp.take(lax.all_to_all(rows, "dp", 0, 0), dp_order, axis=0)
        rows = tensor_gather(rows[None]).reshape(-1, width)
        g_came = swap(g_leaves, "dp", 1)
        gain_sum = jnp.concatenate([g_gain0, g_gain1, g_gain2]).reshape(3, group, width)
        g_gains = jnp.take(lax.psum(gain_sum, ("dp", "tensor")), own, axis=1)
    g_head = [jnp.where(bit == 0, g_stays, g_came), jnp.where(bit == 0, g_came, g_stays)]
    rows, g_ffn, d_qkv = lax.optimization_barrier((rows, g_ffn, d_qkv))
    g_ffn, g_ffn_leaves = scatter_middle(g_ffn, g_ffn_parts)
    g_attn_in = product(attn_norm, d_qkv, 0, 1).astype(HALF)
    g_attn_out = product(d_branch1, attended, 0, 1).astype(HALF)
    g_attn = jnp.concatenate([g_attn_in, g_attn_out], axis=1)
    g_attn_parts = scatter_first(g_attn)
    g_embed, squares = collect(rows, every_id, vocab, g_ffn_leaves + [g_attn])
    squares, g_attn, g_ffn = lax.optimization_barrier((squares, g_attn, g_ffn))
    g_attn, g_attn_leaves = scatter_middle(g_attn, g_attn_parts)
    g_ffn = scatter_last(g_ffn, g_ffn_leaves)
    g_attn = scatter_last(g_attn, g_attn_leaves)

    owner = (rank == 0).astype(FLOAT)
    squared = jnp.sum(squares) + owner * jnp.sum(g_gains * g_gains)
    for part in (g_attn, g_ffn, *g_head):
        squared = squared + jnp.sum(part.astype(FLOAT) ** 2)
    losses = jnp.sum(jnp.where(takes_seq, seq_loss[None, :], 0.0), axis=1) * owner
    if group == 8:
        sums = jnp.pad(jnp.concatenate([squared[None], losses]), (0, 8 * LANES - 1 - micro))
        sums = total_over_devices(jnp.broadcast_to(sums.reshape(1, 8, LANES), (8, 8, LANES)))
        squared, loss_sums = sums[0, 0], sums[0, 1 : 1 + micro]
    else:
        squared, loss_sums = lax.psum((squared, losses), ("dp", "tensor"))
    grad_norm = jnp.sqrt(squared)
    factor = CLIP / jnp.maximum(grad_norm, CLIP)
    g_parts = (
        [g_embed],
        [g_attn[:, :qkv_width]],
        [g_attn[:, qkv_width:].T],
        [g_ffn[:, : 2 * ffn].reshape(ffn_in.shape)],
        [g_ffn[:, 2 * ffn :]],
        g_head,
    )
    arrays = []
    for place in range(6):
        entry = (weights[place], means[place], squares_in[place])
        if place in (0, 4):
            entry = tuple(array.T for array in entry)
        arrays.append((*entry, g_parts[place]))
    updated = []
    for place, results in enumerate(update(arrays, factor)):
        updated.extend(result.T if place in (0, 4) else result for result in results)
    updated.extend(adam(norm_gains, g_gains * factor, means[6], squares_in[6], LR_GAIN, 0.0))
    return (jnp.stack([loss_sums, counts]), grad_norm, *updated)


def solution(mesh):
    in_specs = (
        P("dp", None),
        P("dp", None),
        P("dp", None),
        P("dp", None),
        P("dp", None),
        P("tensor", "dp"),
        P("dp", "tensor"),
        P("tensor", "dp"),
        P("dp", None, "tensor"),
        P("tensor", "dp"),
        P("dp", "tensor"),
        P(None, "dp"),
        P("tensor", "dp"),
        P("dp", "tensor"),
        P("tensor", "dp"),
        P("dp", None, "tensor"),
        P("tensor", "dp"),
        P("dp", "tensor"),
        P(None, "dp"),
        P("tensor", "dp"),
        P("dp", "tensor"),
        P("tensor", "dp"),
        P("dp", None, "tensor"),
        P("tensor", "dp"),
        P("dp", "tensor"),
        P(None, "dp"),
    )
    out_specs = (
        P(),
        P(),
        P("tensor", "dp"),
        P("tensor", "dp"),
        P("tensor", "dp"),
        P("tensor", "dp"),
        P("dp", "tensor"),
        P("dp", "tensor"),
        P("dp", "tensor"),
        P("dp", "tensor"),
        P("tensor", "dp"),
        P("tensor", "dp"),
        P("tensor", "dp"),
        P("tensor", "dp"),
        P("dp", None, "tensor"),
        P("dp", None, "tensor"),
        P("dp", None, "tensor"),
        P("dp", None, "tensor"),
        P("tensor", "dp"),
        P("tensor", "dp"),
        P("tensor", "dp"),
        P("tensor", "dp"),
        P("dp", "tensor"),
        P("dp", "tensor"),
        P("dp", "tensor"),
        P("dp", "tensor"),
        P(None, "dp"),
        P(None, "dp"),
        P(None, "dp"),
        P(None, "dp"),
    )
    return jax.shard_map(shards, mesh=mesh, in_specs=in_specs, out_specs=out_specs, check_vma=False)
```

```python
import functools

import jax
import jax.numpy as jnp
import numpy as np
from jax import lax
from jax.experimental import pallas as pl
from jax.experimental.pallas import tpu as pltpu
from jax.sharding import PartitionSpec as P

HEAD_DIM = 64
STEP = 10


EPS = 1e-05
CLIP = 0.01
LR = 0.03
LR_GAIN = 0.5
BETA_ONE = 0.9
BETA_TWO = 0.95
ADAM_EPS = 1e-08
DECAY = 0.1
NEG = -1e30
FLOAT = jnp.float32
HALF = jnp.bfloat16
LANES = 128
ROWS = 1024
VMEM_LIMIT = 56 * 2**20
TILE = 512
CHUNK = 256
MESH = pl.DeviceIdType.MESH
SMALL = pl.CostEstimate(flops=2**20, bytes_accessed=2**20, transcendentals=0)

TURN = (0, 2, 1, 3)


def swap(value, axis, bit):
    pairs = [(i, i ^ bit) for i in range(lax.axis_size(axis))]
    return lax.ppermute(value, axis, pairs)


def normed(values, gain):
    return values * lax.rsqrt(jnp.mean(values * values, axis=-1, keepdims=True) + EPS) * gain


def tables(length, width):
    inverse = np.float32(10000.0) ** (-np.arange(0, width, 2, dtype=np.float32) / np.float32(width))
    angle = inverse[:, None] * np.arange(length, dtype=np.float32)[None, :]
    return jnp.asarray(np.cos(angle)), jnp.asarray(np.sin(angle))


def block_of(full, k):
    rows = full.shape[0] // lax.axis_size("dp")
    own = lax.axis_index("dp")
    return lax.dynamic_slice(full, ((own ^ k) * rows, 0), (rows, full.shape[1]))


def scatter_first(full):
    if lax.axis_size("dp") != 8:
        return []
    leaves = jnp.concatenate([block_of(full, k + 1) for k in (0, 2, 4, 6)], axis=0)
    return [swap(leaves, "dp", 1)]


def scatter_middle(full, parts):
    if lax.axis_size("dp") != 8:
        return full, []
    rows = full.shape[0] // 8
    sums = [
        block_of(full, 2 * n).astype(FLOAT) + parts[0][n * rows : (n + 1) * rows].astype(FLOAT)
        for n in range(4)
    ]
    return sums[0], [total.astype(HALF) for total in sums[1:]]


def scatter_last(total, leaves):
    if lax.axis_size("dp") != 8:
        return lax.psum_scatter(total.astype(FLOAT), "dp", scatter_dimension=0, tiled=True)
    for n, leave in enumerate(leaves):
        total = total + swap(leave, "dp", 2 * n + 2).astype(FLOAT)
    return total


def peers_of(own, rank, bits, axis):
    if axis == "dp":
        return [(own ^ k, rank) for k in bits]
    return [(own, rank ^ k) for k in bits]


def greet(peers):
    barrier = pltpu.get_barrier_semaphore()
    for peer in peers:
        pl.semaphore_signal(barrier, inc=1, device_id=peer, device_id_type=MESH)
    pl.semaphore_wait(barrier, len(peers))


def spread_kernel(
    vocab, seqs, micro, numbers, gains, every, ids, all_gains, extra, every_gain, send, recv
):
    own, rank = lax.axis_index("dp"), lax.axis_index("tensor")
    peers = peers_of(own, rank, range(1, 8), "dp")
    greet(peers)
    every[0] = numbers[...]
    every_gain[0] = gains[...]
    copies = []
    for k in range(1, 8):
        for n, (source, target) in enumerate(((numbers, every), (gains, every_gain))):
            copies.append(
                pltpu.make_async_remote_copy(
                    src_ref=source,
                    dst_ref=target.at[k],
                    send_sem=send.at[n, k],
                    recv_sem=recv.at[n, k],
                    device_id=peers[k - 1],
                    device_id_type=MESH,
                )
            )
            copies[-1].start()
    for copy in copies:
        copy.wait()
    lines = ids.shape[0] // (32 * seqs)
    for p in range(4):
        shard = rank ^ TURN[p]
        for k in range(8):
            for j in range(seqs):
                local = every[k, pl.ds((j * 4 + shard) * lines, lines), :] - rank * vocab
                local = jnp.where((local >= 0) & (local < vocab), local, vocab)
                ids[pl.ds(((p * 8 + k) * seqs + j) * lines, lines), :] = local
    total = numbers.shape[0] - 8
    total = sum(every[k, total : total + 1, :].astype(FLOAT) for k in range(8))
    weights = 1.0 / jnp.maximum(total, 1.0)
    id_rows = (numbers.shape[0] - 8) // 3
    entries = vocab // 2
    low = rank * vocab + (own % 2) * entries
    extra[...] = jnp.zeros_like(extra)
    for k in (0, 1):
        order = every[k, 3 * id_rows : 3 * id_rows + 1, :]
        for j in range(seqs):
            weight = sum(
                jnp.where(order[:, micro + m : micro + m + 1] == j, weights[:, m : m + 1], 0.0)
                for m in range(micro)
            )
            for p in range(4):
                row = (j * 4 + (rank ^ TURN[p])) * lines
                for r in range(lines):
                    place = (((k * 4 + p) * seqs + j) * lines + r) * LANES
                    counted = every[k, pl.ds(2 * id_rows + row + r, 1), :].astype(FLOAT)
                    aim = every[k, pl.ds(id_rows + row + r, 1), :] - low
                    aim = jnp.where((aim >= 0) & (aim < entries), aim, -1).astype(FLOAT)
                    extra[0:1, place : place + LANES] = counted * weight
                    extra[1:2, place : place + LANES] = aim
                    extra[2:3, place : place + LANES] = counted
    width = all_gains.shape[1] // 8
    for b in range(8):
        all_gains[:, b * width : (b + 1) * width] = every_gain[own ^ b][:, :width]


def spread(numbers, gains, seqs, length, micro, vocab, width):
    vmem = pl.BlockSpec(memory_space=pltpu.VMEM)
    return pl.pallas_call(
        functools.partial(spread_kernel, vocab, seqs, micro),
        in_specs=[vmem] * 2,
        out_specs=[vmem] * 4,
        out_shape=[
            jax.ShapeDtypeStruct((8, *numbers.shape), numbers.dtype),
            jax.ShapeDtypeStruct((8 * seqs * length // LANES, LANES), jnp.int32),
            jax.ShapeDtypeStruct((8, 8 * width), FLOAT),
            jax.ShapeDtypeStruct((8, 2 * seqs * length), FLOAT),
        ],
        scratch_shapes=[
            pltpu.VMEM((8, *gains.shape), FLOAT),
            pltpu.SemaphoreType.DMA((2, 8)),
            pltpu.SemaphoreType.DMA((2, 8)),
        ],
        compiler_params=pltpu.CompilerParams(collective_id=1, has_side_effects=True),
        cost_estimate=SMALL,
        name="spread",
    )(numbers, gains)


def total_kernel(blocks, out, first, summed, second, send, recv):
    own, rank = lax.axis_index("dp"), lax.axis_index("tensor")
    near = peers_of(own, rank, range(1, 4), "tensor")
    far = peers_of(own, rank, range(1, 8), "dp")
    greet(near + far)
    copies = []
    for k in range(1, 4):
        copy = pltpu.make_async_remote_copy(
            src_ref=blocks,
            dst_ref=first.at[k - 1],
            send_sem=send.at[k - 1],
            recv_sem=recv.at[k - 1],
            device_id=near[k - 1],
            device_id_type=MESH,
        )
        copy.start()
        copies.append(copy)
    for copy in copies:
        copy.wait()
    summed[...] = (blocks[...] + first[0]) + (first[1] + first[2])
    copies = []
    for k in range(1, 8):
        copy = pltpu.make_async_remote_copy(
            src_ref=summed.at[k],
            dst_ref=second.at[k],
            send_sem=send.at[2 + k],
            recv_sem=recv.at[2 + k],
            device_id=far[k - 1],
            device_id_type=MESH,
        )
        copy.start()
        copies.append(copy)
    for copy in copies:
        copy.wait()
    second[0] = summed[0]
    pairs = [second[k] + second[k + 1] for k in (0, 2, 4, 6)]
    out[...] = (pairs[0] + pairs[1]) + (pairs[2] + pairs[3])


def total_over_devices(blocks):
    shape = blocks.shape
    return pl.pallas_call(
        total_kernel,
        in_specs=[pl.BlockSpec(memory_space=pltpu.VMEM)],
        out_specs=pl.BlockSpec(memory_space=pltpu.VMEM),
        out_shape=jax.ShapeDtypeStruct(shape[1:], FLOAT),
        scratch_shapes=[
            pltpu.VMEM((3, *shape), FLOAT),
            pltpu.VMEM(shape, FLOAT),
            pltpu.VMEM(shape, FLOAT),
            pltpu.SemaphoreType.DMA((10,)),
            pltpu.SemaphoreType.DMA((10,)),
        ],
        compiler_params=pltpu.CompilerParams(collective_id=2, has_side_effects=True),
        name="total",
    )(blocks)


def tensor_gather(block):
    half = jnp.concatenate([block, swap(block, "tensor", 2)], axis=0)
    return jnp.concatenate([half, swap(half, "tensor", 1)], axis=0)


def tensor_scatter(full):
    half = full.shape[0] // 2
    quarter = half // 2
    both = full[:half] + swap(full[half:], "tensor", 1)
    there = swap(both[quarter:].astype(HALF), "tensor", 2)
    return both[:quarter] + there.astype(FLOAT)


def lookup_kernel(ids, turned, out, table, corner, rows):
    count = rows.shape[0]
    width, vocab = turned.shape

    @pl.when(pl.program_id(0) == 0)
    def _():
        corner[...] = jnp.zeros_like(corner)
        for v in range(0, vocab, LANES):
            some = min(LANES, vocab - v)
            corner[:width, :some] = turned[:, v : v + some].astype(HALF).astype(FLOAT)
            if some < LANES:
                corner[:width, some:] = jnp.zeros((width, LANES - some), FLOAT)
            table[v : v + LANES, :] = corner[...].T
        if vocab % LANES == 0:
            table[vocab:, :] = jnp.zeros((LANES, LANES), FLOAT)

    def body(i, carry):
        for u in range(16):
            r = i * 16 + u
            rows[pl.ds(r, 1), :] = table[pl.ds(ids[0, 0, r], 1), :]
        return carry

    lax.fori_loop(0, count // 16, body, 0)
    out[...] = rows[:, : out.shape[1]].astype(HALF)


def lookup(turned, ids):
    count = ids.shape[0]
    width, vocab = turned.shape
    padded = (vocab // LANES + 1) * LANES
    return pl.pallas_call(
        lookup_kernel,
        grid=(count // ROWS,),
        in_specs=[
            pl.BlockSpec((1, 1, ROWS), lambda i: (i, 0, 0), memory_space=pltpu.SMEM),
            pl.BlockSpec(turned.shape, lambda i: (0, 0), pipeline_mode=pl.Buffered(1)),
        ],
        out_specs=pl.BlockSpec((ROWS, width), lambda i: (i, 0)),
        out_shape=jax.ShapeDtypeStruct((count, width), HALF),
        scratch_shapes=[
            pltpu.VMEM((padded, LANES), FLOAT),
            pltpu.VMEM((LANES, LANES), FLOAT),
            pltpu.VMEM((ROWS, LANES), FLOAT),
        ],
        compiler_params=pltpu.CompilerParams(vmem_limit_bytes=VMEM_LIMIT),
        cost_estimate=SMALL,
        name="lookup",
    )(ids.reshape(count // ROWS, 1, ROWS), turned)


def collect_kernel(ids, grads, out, squares, rows, *sums):
    step = pl.program_id(0)
    count = rows.shape[0]
    width, vocab = out.shape

    @pl.when(step == 0)
    def _():
        rows[...] = jnp.zeros_like(rows)
        for total in sums:
            total[...] = jnp.zeros_like(total)

    rows[:, :width] = grads[...].astype(FLOAT)

    def body(i, carry):
        for u in range(16):
            r = i * 16 + u
            total = sums[u % len(sums)]
            place = pl.ds(ids[0, 0, r], 1)
            total[place, :] = total[place, :] + rows[pl.ds(r, 1), :]
        return carry

    lax.fori_loop(0, count // 16, body, 0)

    @pl.when(step == pl.num_programs(0) - 1)
    def _():
        squared = jnp.zeros((8, LANES), FLOAT)
        for v in range(0, vocab, LANES):
            some = min(LANES, vocab - v)
            total = sums[0][v : v + some, :]
            for other in sums[1:]:
                total = total + other[v : v + some, :]
            for r in range(0, some, 8):
                squared = squared + total[r : r + 8, :] * total[r : r + 8, :]
            if some < LANES:
                total = jnp.concatenate([total, jnp.zeros((LANES - some, LANES), FLOAT)], axis=0)
            out[:, v : v + some] = total.T[:width, :some]
        squares[...] = squared


def collect(grads, ids, vocab):
    count = ids.shape[0]
    width = grads.shape[1]
    padded = (vocab // LANES + 1) * LANES
    return pl.pallas_call(
        collect_kernel,
        grid=(count // ROWS,),
        in_specs=[
            pl.BlockSpec((1, 1, ROWS), lambda i: (i, 0, 0), memory_space=pltpu.SMEM),
            pl.BlockSpec((ROWS, width), lambda i: (i, 0)),
        ],
        out_specs=[
            pl.BlockSpec((width, vocab), lambda i: (0, 0)),
            pl.BlockSpec((8, LANES), lambda i: (0, 0)),
        ],
        out_shape=[
            jax.ShapeDtypeStruct((width, vocab), FLOAT),
            jax.ShapeDtypeStruct((8, LANES), FLOAT),
        ],
        scratch_shapes=[pltpu.VMEM((ROWS, LANES), FLOAT)]
        + [pltpu.VMEM((padded, LANES), FLOAT)] * 8,
        compiler_params=pltpu.CompilerParams(vmem_limit_bytes=VMEM_LIMIT),
        cost_estimate=SMALL,
        name="collect",
    )(ids.reshape(count // ROWS, 1, ROWS), grads)


def edge_of(vocab):
    return vocab - (pl.cdiv(vocab, TILE) - 1) * TILE


def each_tile(vocab, work):
    last = edge_of(vocab)
    if last == TILE:
        work(TILE)
    else:
        step, steps = pl.program_id(0), pl.num_programs(0)
        pl.when(step < steps - 1)(lambda: work(TILE))
        pl.when(step == steps - 1)(lambda: work(last))


def turned_rows(rows):
    return jnp.concatenate([rows] * (LANES // 8), axis=0).T


def scan_kernel(vocab, norm, weight, target, logits, stats, turned, peak, total, hit, aims):
    step = pl.program_id(0)
    rows = norm.shape[0]

    @pl.when(step == 0)
    def _():
        peak[...] = jnp.full_like(peak, NEG)
        total[...] = jnp.zeros_like(total)
        hit[...] = jnp.zeros_like(hit)
        aims[...] = turned_rows(target[...])
        for r in range(0, rows, CHUNK):
            turned[:, r : r + CHUNK] = norm[r : r + CHUNK, :].T

    def work(width):
        lane = lax.broadcasted_iota(jnp.int32, (CHUNK, LANES), 1)
        for r in range(0, rows, CHUNK):
            part = pl.ds(r, CHUNK)
            value = jnp.dot(norm[part, :], weight[...], preferred_element_type=FLOAT)
            logits[part, :] = value
            aim = aims[part, 1:2].astype(jnp.int32) - step * TILE
            slabs, found = [], hit[part, :]
            for c in range(0, width, LANES):
                slab = value[:, c : c + LANES]
                if c + LANES > width:
                    slab = jnp.where(lane < width - c, slab, NEG)
                slabs.append(slab)
                found = found + jnp.where(lane == aim - c, slab, 0.0)
            hit[part, :] = found
            before = peak[part, :]
            top = functools.reduce(jnp.maximum, slabs, before)
            added = total[part, :] * jnp.exp(before - top)
            for slab in slabs:
                added = added + jnp.exp(slab - top)
            total[part, :] = added
            peak[part, :] = top

    each_tile(vocab, work)

    @pl.when(step == pl.num_programs(0) - 1)
    def _():
        top = jnp.max(peak[...], axis=1, keepdims=True)
        added = jnp.sum(total[...] * jnp.exp(peak[...] - top), axis=1, keepdims=True)
        found = jnp.sum(hit[...], axis=1, keepdims=True)
        lane = lax.broadcasted_iota(jnp.int32, (rows, LANES), 1)
        joined = jnp.where(lane == 0, top, jnp.where(lane == 1, added, found))
        stats[...] = joined.T[:8, :]


def head_scan(norm, weight, extra):
    rows, depth = norm.shape
    vocab = weight.shape[1]
    return pl.pallas_call(
        functools.partial(scan_kernel, vocab),
        grid=(pl.cdiv(vocab, TILE),),
        in_specs=[
            pl.BlockSpec((rows, depth), lambda i: (0, 0), pipeline_mode=pl.Buffered(1)),
            pl.BlockSpec((depth, TILE), lambda i: (0, i)),
            pl.BlockSpec((8, rows), lambda i: (0, 0)),
        ],
        out_specs=[
            pl.BlockSpec((rows, TILE), lambda i: (0, i)),
            pl.BlockSpec((8, rows), lambda i: (0, 0)),
            pl.BlockSpec((depth, rows), lambda i: (0, 0), pipeline_mode=pl.Buffered(1)),
        ],
        out_shape=[
            jax.ShapeDtypeStruct((rows, vocab), FLOAT),
            jax.ShapeDtypeStruct((8, rows), FLOAT),
            jax.ShapeDtypeStruct((depth, rows), HALF),
        ],
        scratch_shapes=[pltpu.VMEM((rows, LANES), FLOAT)] * 4,
        compiler_params=pltpu.CompilerParams(vmem_limit_bytes=VMEM_LIMIT),
        cost_estimate=SMALL,
        name="head_scan",
    )(norm, weight, extra)


def grad_kernel(vocab, turned, weight, info, logits, grad, out, total, slope, columns):
    step = pl.program_id(0)
    rows = logits.shape[0]

    @pl.when(step == 0)
    def _():
        columns[...] = turned_rows(info[...])
        total[...] = jnp.zeros_like(total)

    def work(width):
        lane = lax.broadcasted_iota(jnp.int32, (CHUNK, TILE), 1)
        table = weight[...]
        if width < TILE:
            table = jnp.where(lax.broadcasted_iota(jnp.int32, table.shape, 1) < width, table, 0.0)
        for r in range(0, rows, CHUNK):
            part = pl.ds(r, CHUNK)
            aim = columns[part, 3:4].astype(jnp.int32) - step * TILE
            value = jnp.exp(logits[part, :] - columns[part, 0:1])
            value = (value - jnp.where(lane == aim, 1.0, 0.0)) * columns[part, 2:3]
            if width < TILE:
                value = jnp.where(lane < width, value, 0.0)
            value = value.astype(HALF)
            slope[part, :] = value
            total[part, :] = total[part, :] + lax.dot_general(
                value, table, (((1,), (1,)), ((), ())), preferred_element_type=FLOAT
            )
        grad[...] = jnp.dot(turned[...], slope[...], preferred_element_type=FLOAT).astype(HALF)

    each_tile(vocab, work)

    @pl.when(step == pl.num_programs(0) - 1)
    def _():
        for r in range(0, rows, CHUNK):
            out[pl.ds(r, CHUNK), :] = total[pl.ds(r, CHUNK), :].astype(HALF)


def head_grad(turned, weight, info, logits):
    depth, rows = turned.shape
    vocab = weight.shape[1]
    return pl.pallas_call(
        functools.partial(grad_kernel, vocab),
        grid=(pl.cdiv(vocab, TILE),),
        in_specs=[
            pl.BlockSpec((depth, rows), lambda i: (0, 0), pipeline_mode=pl.Buffered(1)),
            pl.BlockSpec((depth, TILE), lambda i: (0, i)),
            pl.BlockSpec((8, rows), lambda i: (0, 0)),
            pl.BlockSpec((rows, TILE), lambda i: (0, i)),
        ],
        out_specs=[
            pl.BlockSpec((depth, TILE), lambda i: (0, i)),
            pl.BlockSpec((rows, depth), lambda i: (0, 0), pipeline_mode=pl.Buffered(1)),
        ],
        out_shape=[
            jax.ShapeDtypeStruct((depth, vocab), HALF),
            jax.ShapeDtypeStruct((rows, depth), HALF),
        ],
        scratch_shapes=[
            pltpu.VMEM((rows, depth), FLOAT),
            pltpu.VMEM((rows, TILE), HALF),
            pltpu.VMEM((rows, LANES), FLOAT),
        ],
        compiler_params=pltpu.CompilerParams(vmem_limit_bytes=VMEM_LIMIT),
        cost_estimate=SMALL,
        name="head_grad",
    )(turned, weight, info, logits)


def turn_rows(low, high, cosine, sine):
    return low * cosine - high * sine, high * cosine + low * sine


def reach(block, share, longest):
    back = -(-(longest - 1) // share)
    return max(0, block - back) * share


def seen(first, low, high, place):
    keys = low + lax.broadcasted_iota(jnp.int32, (high - low, first.shape[1]), 0)
    queries = place + lax.broadcasted_iota(jnp.int32, (high - low, first.shape[1]), 1)
    return (keys >= first) & (keys <= queries)


def attend_kernel(base, qkv, cosine, sine, first, attended, kept, log_total):
    seq = pl.program_id(1)
    blocks = base.shape[0]
    length = cosine.shape[1]
    share = length // blocks
    half = HEAD_DIM // 2

    def spot(i):
        return pl.ds(pl.multiple_of(base[i] + seq * share, share), share)

    for i in range(blocks):
        at = pl.ds(i * share, share)
        turns = (cosine[:, at], sine[:, at])
        for c in (0, 1):
            top = c * HEAD_DIM
            low, high = turn_rows(
                qkv[top : top + half, spot(i)], qkv[top + half : top + HEAD_DIM, spot(i)], *turns
            )
            kept[0, top : top + half, at] = low.astype(HALF)
            kept[0, top + half : top + HEAD_DIM, at] = high.astype(HALF)
        kept[0, 2 * HEAD_DIM :, at] = qkv[2 * HEAD_DIM :, spot(i)].astype(HALF)
    key = kept[0, HEAD_DIM : 2 * HEAD_DIM, :].T
    for i in range(blocks):
        low, high = reach(i, share, length // 2), (i + 1) * share
        at = pl.ds(i * share, share)
        scores = jnp.dot(
            key[low:high, :], kept[0, :HEAD_DIM, at], preferred_element_type=FLOAT
        ) * (HEAD_DIM**-0.5)
        scores = jnp.where(seen(first[0, :, at][:1], low, high, i * share), scores, NEG)
        peak = jnp.max(scores, axis=0, keepdims=True)
        expo = jnp.exp(scores - peak)
        summed = jnp.sum(expo, axis=0, keepdims=True)
        probs = (expo * (1.0 / summed)).astype(HALF)
        value = kept[0, 2 * HEAD_DIM :, low:high]
        attended[:, spot(i)] = jnp.dot(value, probs, preferred_element_type=FLOAT).astype(HALF)
        log_total[0, 0, :, at] = jnp.broadcast_to(peak + jnp.log(summed), (8, share))


def attend(base, qkv, cosine, sine, first):
    seqs, length = first.shape[0], first.shape[2]
    heads = qkv.shape[0] // (3 * HEAD_DIM)
    tokens = qkv.shape[1]
    return pl.pallas_call(
        attend_kernel,
        grid=(heads, seqs),
        in_specs=[
            pl.BlockSpec(memory_space=pltpu.SMEM),
            pl.BlockSpec((3 * HEAD_DIM, tokens), lambda h, j: (h, 0)),
            pl.BlockSpec(cosine.shape, lambda h, j: (0, 0)),
            pl.BlockSpec(sine.shape, lambda h, j: (0, 0)),
            pl.BlockSpec((1, 8, length), lambda h, j: (j, 0, 0)),
        ],
        out_specs=[
            pl.BlockSpec((HEAD_DIM, tokens), lambda h, j: (h, 0)),
            pl.BlockSpec((1, 3 * HEAD_DIM, length), lambda h, j: (j, h, 0)),
            pl.BlockSpec((1, 1, 8, length), lambda h, j: (j, h, 0, 0)),
        ],
        out_shape=[
            jax.ShapeDtypeStruct((heads * HEAD_DIM, tokens), HALF),
            jax.ShapeDtypeStruct((seqs, heads * 3 * HEAD_DIM, length), HALF),
            jax.ShapeDtypeStruct((seqs, heads, 8, length), FLOAT),
        ],
        compiler_params=pltpu.CompilerParams(vmem_limit_bytes=VMEM_LIMIT),
        cost_estimate=SMALL,
        name="attend",
    )(base, qkv, cosine, sine, first)


def attend_back_kernel(waits, base, kept, log_total, slope, cosine, sine, first, *refs):
    d_qkv, d_key, d_value = refs[waits:]
    seq = pl.program_id(1)
    blocks = base.shape[0]
    length = cosine.shape[1]
    share = length // blocks
    half = HEAD_DIM // 2
    scale = HEAD_DIM**-0.5

    def spot(i):
        return pl.ds(pl.multiple_of(base[i] + seq * share, share), share)

    def put(part, i, low, high):
        at = pl.ds(i * share, share)
        d_low, d_high = turn_rows(low, high, cosine[:, at], -sine[:, at])
        top = part * HEAD_DIM
        d_qkv[top : top + half, spot(i)] = d_low.astype(HALF)
        d_qkv[top + half : top + HEAD_DIM, spot(i)] = d_high.astype(HALF)

    query = kept[0, :HEAD_DIM, :].T
    key = kept[0, HEAD_DIM : 2 * HEAD_DIM, :].T
    value = kept[0, 2 * HEAD_DIM :, :].T
    d_key[...] = jnp.zeros_like(d_key)
    d_value[...] = jnp.zeros_like(d_value)
    for i in range(blocks):
        low, high = reach(i, share, length // 2), (i + 1) * share
        at = pl.ds(i * share, share)
        turned = slope[:, spot(i)]
        scores = jnp.dot(
            key[low:high, :], kept[0, :HEAD_DIM, at], preferred_element_type=FLOAT
        ) * scale
        scores = jnp.where(seen(first[0, :, at][:1], low, high, i * share), scores, NEG)
        probs = jnp.exp(scores - log_total[0, 0, :1, at])
        d_probs = jnp.dot(value[low:high, :], turned, preferred_element_type=FLOAT)
        centre = jnp.sum(probs * d_probs, axis=0, keepdims=True)
        d_scores = (probs * (d_probs - centre)).astype(HALF)
        d_value[low:high, :] += jnp.dot(probs.astype(HALF), turned.T, preferred_element_type=FLOAT)
        d_key[low:high, :] += jnp.dot(
            d_scores, query[i * share : (i + 1) * share, :], preferred_element_type=FLOAT
        )
        d_query = scale * jnp.dot(
            kept[0, HEAD_DIM : 2 * HEAD_DIM, low:high], d_scores, preferred_element_type=FLOAT
        )
        put(0, i, d_query[:half, :], d_query[half:, :])
    for i in range(blocks):
        rows = pl.ds(i * share, share)
        turned = scale * d_key[rows, :].T
        put(1, i, turned[:half, :], turned[half:, :])
        d_qkv[2 * HEAD_DIM :, spot(i)] = d_value[rows, :].T.astype(HALF)


def attend_back(base, kept, log_total, slope, cosine, sine, first, before):
    seqs, length = first.shape[0], first.shape[2]
    tokens = slope.shape[1]
    heads = slope.shape[0] // HEAD_DIM
    return pl.pallas_call(
        functools.partial(attend_back_kernel, len(before)),
        grid=(heads, seqs),
        in_specs=[
            pl.BlockSpec(memory_space=pltpu.SMEM),
            pl.BlockSpec((1, 3 * HEAD_DIM, length), lambda h, j: (j, h, 0)),
            pl.BlockSpec((1, 1, 8, length), lambda h, j: (j, h, 0, 0)),
            pl.BlockSpec((HEAD_DIM, tokens), lambda h, j: (h, 0)),
            pl.BlockSpec(cosine.shape, lambda h, j: (0, 0)),
            pl.BlockSpec(sine.shape, lambda h, j: (0, 0)),
            pl.BlockSpec((1, 8, length), lambda h, j: (j, 0, 0)),
        ]
        + [pl.BlockSpec(memory_space=pl.ANY)] * len(before),
        out_specs=pl.BlockSpec((3 * HEAD_DIM, tokens), lambda h, j: (h, 0)),
        out_shape=jax.ShapeDtypeStruct((heads * 3 * HEAD_DIM, tokens), HALF),
        scratch_shapes=[pltpu.VMEM((length, HEAD_DIM), FLOAT)] * 2,
        compiler_params=pltpu.CompilerParams(vmem_limit_bytes=VMEM_LIMIT),
        cost_estimate=SMALL,
        name="attend_back",
    )(base, kept, log_total, slope, cosine, sine, first, *before)


def near_and_far(own, rank):
    return (own, rank ^ 1), (own, rank ^ 2)


def remote(source, target, send, recv, n, peer):
    return pltpu.make_async_remote_copy(
        src_ref=source,
        dst_ref=target,
        send_sem=send.at[n],
        recv_sem=recv.at[n],
        device_id=peer,
        device_id_type=MESH,
    )


class Boundary:
    COUNT = 6

    def __init__(self, own, rank, send, recv, parts, rows):
        self.near, self.far = near_and_far(own, rank)
        self.send, self.recv, self.parts = send, recv, parts
        self.rows = [pl.ds(h * rows, rows) for h in range(parts)]
        self.copies = []

    def copy(self, source, target, n, h, peer):
        made = remote(source, target, self.send, self.recv, n * self.parts + h, peer)
        made.start()
        self.copies.append(made)
        return made

    def sums(self, make, partial, beside, away, come):
        later, crossing = {}, []

        def part(p, h):
            partial[p, self.rows[h], :] = make(p, h).astype(HALF)

        def leave(p, h):
            part(2 + p, h)
            at = self.rows[h]
            later[p, h] = self.copy(partial.at[2 + p, at], beside.at[p, at], p, h, self.near)

        def pair(p, h):
            at = self.rows[h]
            later[p, h].wait_recv()
            return partial[p, at, :].astype(FLOAT) + beside[p, at, :].astype(FLOAT)

        for h, at in enumerate(self.rows):
            leave(1, h)
            part(1, h)
            away[at, :] = pair(1, h).astype(HALF)
            crossing.append(self.copy(away.at[at], come.at[at], 2, h, self.far))
        for h in range(self.parts):
            leave(0, h)
        for h in range(self.parts):
            part(0, h)
        for h, at in enumerate(self.rows):
            total = pair(0, h)
            crossing[h].wait_recv()
            yield h, at, total + come[at, :].astype(FLOAT)

    def give(self, full, h):
        at = self.rows[h]
        self.crossed = getattr(self, "crossed", [])
        self.crossed.append(self.copy(full.at[0, at], full.at[1, at], 3, h, self.far))
        self.beside = getattr(self, "beside", [])
        self.beside.append(self.copy(full.at[0, at], full.at[2, at], 4, h, self.near))

    def pass_on(self, full):
        arrived = []
        for h, at in enumerate(self.rows):
            self.crossed[h].wait_recv()
            arrived.append(self.copy(full.at[1, at], full.at[3, at], 5, h, self.near))
        for copy in self.beside + arrived:
            copy.wait_recv()

    def end(self):
        for copy in self.copies:
            copy.wait_send()


def turned_product(left, right):
    return lax.dot_general(left, right, (((0,), (1,)), ((), ())), preferred_element_type=FLOAT)


def columns_of(array, p, h, parts):
    step = array.shape[1] // (4 * parts)
    return array[:, (p * parts + h) * step : (p * parts + h + 1) * step]


def rows_of(index, width):
    return pl.ds(pl.multiple_of(index * width, width), width)


def forward_kernel(parts, gathers, attended, both, stream, gain, *refs):
    blocks, refs = refs[:gathers], refs[gathers:]
    if gathers:
        out, full, feed_w, weight, partial, beside, away, come, send, recv = refs
    else:
        out, full, weight, partial, beside, away, come, send, recv = refs
    own, rank = lax.axis_index("dp"), lax.axis_index("tensor")
    near, far = near_and_far(own, rank)
    others = {k: (own ^ k, rank) for k in (1, 2, 6)} if gathers else {}
    greet([near, far, *others.values()])
    edge = Boundary(own, rank, send, recv, parts, stream.shape[0] // parts)
    moved = {}

    def move(source, k, n, peer):
        copy = remote(source, feed_w.at[rows_of(own ^ k, width)], send, recv, n, peer)
        copy.start()
        edge.copies.append(copy)
        return copy

    if gathers:
        mine, four = blocks
        width, base = mine.shape[0], Boundary.COUNT * parts
        for n, k in enumerate((2, 6)):
            moved[k] = move(mine, 0, base + n, others[k])
        moved[1] = move(mine, 0, base + 2, others[1])
        moved[5] = move(four, 4, base + 3, others[1])
        feed_w[rows_of(own, width), :] = mine[...]
        feed_w[rows_of(own ^ 4, width), :] = four[...]
    weight[...] = both[:, both.shape[1] - weight.shape[1] :]

    def make(p, h):
        return turned_product(columns_of(attended, p, h, parts), weight[...])

    for h, at, total in edge.sums(make, partial, beside, away, come):
        total = stream[at, :] + total
        out[at, :] = total
        full[0, at, :] = normed(total, gain[1:2, :]).astype(HALF)
        edge.give(full, h)
    if gathers:
        for n, k in enumerate((2, 6)):
            moved[k].wait_recv()
            moved[k + 1] = move(feed_w.at[rows_of(own ^ k, width)], k, base + 4 + n, others[1])
    edge.pass_on(full)
    for k in (1, 5, 3, 7) if gathers else ():
        moved[k].wait_recv()
    edge.end()


def forward_boundary(attended, both, stream, gain, blocks):
    rows, depth = stream.shape
    parts = 2
    vmem = pl.BlockSpec(memory_space=pltpu.VMEM)
    scratch = exchange_scratch(rows, depth, parts)[:4]
    semaphores = Boundary.COUNT * parts + 6
    results = pl.pallas_call(
        functools.partial(forward_kernel, parts, len(blocks)),
        in_specs=[vmem] * (4 + len(blocks)),
        out_specs=[vmem] * (3 if blocks else 2),
        out_shape=[
            jax.ShapeDtypeStruct((rows, depth), FLOAT),
            jax.ShapeDtypeStruct((4, rows, depth), HALF),
        ]
        + [jax.ShapeDtypeStruct((8 * b.shape[0], b.shape[1]), HALF) for b in blocks[:1]],
        scratch_shapes=[pltpu.VMEM((depth, attended.shape[0]), HALF)]
        + scratch
        + [pltpu.SemaphoreType.DMA((semaphores,))] * 2,
        compiler_params=pltpu.CompilerParams(
            collective_id=3, has_side_effects=True, vmem_limit_bytes=VMEM_LIMIT
        ),
        cost_estimate=SMALL,
        name="forward_boundary",
    )(attended, both, stream, gain, *blocks)
    return (results[0], results[1].reshape(4 * rows, depth), *results[2:])


def normed_slope(grad, values, gain):
    root = lax.rsqrt(jnp.mean(values * values, axis=-1, keepdims=True) + EPS)
    unit = values * root
    inner = grad * gain
    middle = jnp.mean(inner * unit, axis=-1, keepdims=True)
    return root * (inner - unit * middle), jnp.sum(grad * unit, axis=0, keepdims=True)


def wide_forward_kernel(
    norm, weight, stream, gain, out, full, partial, beside, away, come, send, recv
):
    own, rank = lax.axis_index("dp"), lax.axis_index("tensor")
    near, far = near_and_far(own, rank)
    other = (own ^ 1, rank)
    greet([near, far, other])
    parts = 2
    edge = Boundary(own, rank, send, recv, parts, stream.shape[0] // parts)
    crossed, moved, last = [], [], []
    ffn = weight.shape[1] // 3

    def make(p, h):
        both = jnp.dot(
            norm[p, edge.rows[h], :], weight[:, : 2 * ffn], preferred_element_type=FLOAT
        )
        gate, up = both[:, :ffn], both[:, ffn:]
        hidden = (gate * (1.0 / (1.0 + jnp.exp(-gate))) * up).astype(HALF)
        return across(hidden, weight[:, 2 * ffn :])

    for h, at, total in edge.sums(make, partial, beside, away, come):
        total = stream[at, :] + total
        out[at, :] = total
        full[0, 0, at, :] = normed(total, gain[2:3, :]).astype(HALF)
        mine = full.at[0, 0, at]
        crossed.append(edge.copy(mine, full.at[0, 1, at], 3, h, far))
        moved.append(edge.copy(mine, full.at[1, 0, at], 4, h, other))
        last.append(edge.copy(mine, full.at[0, 2, at], 5, h, near))
    early, late = edge.rows
    crossed[0].wait_recv()
    one = edge.copy(full.at[0, 1, early], full.at[1, 1, early], 6, 0, other)
    last.append(edge.copy(full.at[0, 1, early], full.at[0, 3, early], 7, 0, near))
    moved[0].wait_recv()
    last.append(edge.copy(full.at[1, 0, early], full.at[1, 2, early], 8, 0, near))
    moved[1].wait_recv()
    two = edge.copy(full.at[1, 0, late], full.at[1, 1, late], 6, 1, far)
    last.append(edge.copy(full.at[1, 0, late], full.at[1, 2, late], 8, 1, near))
    crossed[1].wait_recv()
    last.append(edge.copy(full.at[0, 1, late], full.at[0, 3, late], 7, 1, near))
    one.wait_recv()
    last.append(edge.copy(full.at[1, 1, early], full.at[1, 3, early], 9, 0, near))
    two.wait_recv()
    last.append(edge.copy(full.at[1, 1, late], full.at[1, 3, late], 9, 1, near))
    for copy in last:
        copy.wait_recv()
    edge.end()


def wide_forward(norm, weight, stream, gain):
    rows, depth = stream.shape
    vmem = pl.BlockSpec(memory_space=pltpu.VMEM)
    out, full = pl.pallas_call(
        wide_forward_kernel,
        in_specs=[vmem] * 4,
        out_specs=[vmem] * 2,
        out_shape=[
            jax.ShapeDtypeStruct((rows, depth), FLOAT),
            jax.ShapeDtypeStruct((2, 4, rows, depth), HALF),
        ],
        scratch_shapes=exchange_scratch(rows, depth, 2)[:4] + [pltpu.SemaphoreType.DMA((20,))] * 2,
        compiler_params=pltpu.CompilerParams(
            collective_id=9, has_side_effects=True, vmem_limit_bytes=VMEM_LIMIT
        ),
        cost_estimate=SMALL,
        name="wide_forward",
    )(norm.reshape(4, rows, depth), weight, stream, gain)
    return out, full.reshape(8 * rows, depth)


def wide_backward_kernel(partial, stream, gain, out, g_gain, full, beside, leave, come, send, recv):
    own, rank = lax.axis_index("dp"), lax.axis_index("tensor")
    near, far = near_and_far(own, rank)
    other = (own ^ 1, rank)
    greet([near, far, other])
    parts = 2
    edge = Boundary(own, rank, send, recv, parts, stream.shape[0] // parts)
    early, late = edge.rows
    first = {}
    for n, (y, p) in enumerate(((1, 1), (1, 0), (0, 1), (0, 0))):
        for h, at in enumerate(edge.rows):
            first[y, p, h] = edge.copy(
                partial.at[y, 2 + p, at], beside.at[y, p, at], 5 + n, h, near
            )

    def pair(y, p, h):
        at = edge.rows[h]
        first[y, p, h].wait_recv()
        return partial[y, p, at, :].astype(FLOAT) + beside[y, p, at, :].astype(FLOAT)

    leave[1, 1, early, :] = pair(1, 1, 0).astype(HALF)
    by_other = edge.copy(leave.at[1, 1, early], come.at[1, 1, early], 9, 0, other)
    leave[1, 1, late, :] = pair(1, 1, 1).astype(HALF)
    by_far = edge.copy(leave.at[1, 1, late], come.at[1, 1, late], 9, 1, far)
    leave[1, 0, early, :] = pair(1, 0, 0).astype(HALF)
    other_early = edge.copy(leave.at[1, 0, early], come.at[1, 0, early], 0, 0, other)
    leave[0, 1, late, :] = pair(0, 1, 1).astype(HALF)
    far_late = edge.copy(leave.at[0, 1, late], come.at[0, 1, late], 1, 1, far)
    far_early_sum, other_late_sum = pair(0, 1, 0), pair(1, 0, 1)
    by_other.wait_recv()
    leave[0, 1, early, :] = (far_early_sum + come[1, 1, early, :].astype(FLOAT)).astype(HALF)
    far_early = edge.copy(leave.at[0, 1, early], come.at[0, 1, early], 1, 0, far)
    by_far.wait_recv()
    leave[1, 0, late, :] = (other_late_sum + come[1, 1, late, :].astype(FLOAT)).astype(HALF)
    other_late = edge.copy(leave.at[1, 0, late], come.at[1, 0, late], 0, 1, other)
    g_gain[...] = jnp.zeros_like(g_gain)
    for h, waits in ((0, (other_early, far_early)), (1, (far_late, other_late))):
        at = edge.rows[h]
        total = pair(0, 0, h)
        for copy in waits:
            copy.wait_recv()
        total = total + come[1, 0, at, :].astype(FLOAT) + come[0, 1, at, :].astype(FLOAT)
        slope, by_gain = normed_slope(total, stream[at, :], gain[2:3, :])
        g_gain[:1, :] = g_gain[:1, :] + by_gain
        out[at, :] = slope
        full[0, at, :] = slope.astype(HALF)
        edge.crossed = getattr(edge, "crossed", [])
        edge.crossed.append(edge.copy(full.at[0, at], full.at[1, at], 2, h, far))
        edge.beside = getattr(edge, "beside", [])
        edge.beside.append(edge.copy(full.at[0, at], full.at[2, at], 3, h, near))
    arrived = []
    for h, at in enumerate(edge.rows):
        edge.crossed[h].wait_recv()
        arrived.append(edge.copy(full.at[1, at], full.at[3, at], 4, h, near))
    for copy in edge.beside + arrived:
        copy.wait_recv()
    edge.end()


def wide_backward(partial, stream, gain):
    rows, depth = stream.shape
    vmem = pl.BlockSpec(memory_space=pltpu.VMEM)
    out, g_gain, full = pl.pallas_call(
        wide_backward_kernel,
        in_specs=[vmem] * 3,
        out_specs=[vmem] * 3,
        out_shape=[
            jax.ShapeDtypeStruct((rows, depth), FLOAT),
            jax.ShapeDtypeStruct((8, depth), FLOAT),
            jax.ShapeDtypeStruct((4, rows, depth), HALF),
        ],
        scratch_shapes=[pltpu.VMEM((2, 2, rows, depth), HALF)] * 3
        + [pltpu.SemaphoreType.DMA((20,))] * 2,
        compiler_params=pltpu.CompilerParams(
            collective_id=4, has_side_effects=True, vmem_limit_bytes=VMEM_LIMIT
        ),
        cost_estimate=SMALL,
        name="wide_backward",
    )(partial.reshape(2, 4, rows, depth), stream, gain)
    return out, g_gain, full.reshape(4 * rows, depth)


def exchange_scratch(rows, depth, parts):
    return [
        pltpu.VMEM((4, rows, depth), HALF),
        pltpu.VMEM((2, rows, depth), HALF),
        pltpu.VMEM((rows, depth), HALF),
        pltpu.VMEM((rows, depth), HALF),
        pltpu.SemaphoreType.DMA((Boundary.COUNT * parts,)),
        pltpu.SemaphoreType.DMA((Boundary.COUNT * parts,)),
    ]


def backward_kernel(
    parts, norm, later, weight, stream, gain, prior, out, g_gain, full, grad, partial, beside, away, come, kept, send, recv
):
    own, rank = lax.axis_index("dp"), lax.axis_index("tensor")
    greet(list(near_and_far(own, rank)))
    edge = Boundary(own, rank, send, recv, parts, stream.shape[0] // parts)
    ffn = weight.shape[1] // 3

    def make(p, h):
        at = edge.rows[h]
        both = jnp.dot(norm[p, at, :], weight[:, : 2 * ffn], preferred_element_type=FLOAT)
        d_hidden = jnp.dot(later[p, at, :], weight[:, 2 * ffn :], preferred_element_type=FLOAT)
        gate, up = both[:, :ffn], both[:, ffn:]
        open_part = 1.0 / (1.0 + jnp.exp(-gate))
        passed = gate * open_part
        d_gate = (d_hidden * up * (open_part * (1.0 + gate * (1.0 - open_part)))).astype(HALF)
        d_up = (d_hidden * passed).astype(HALF)
        kept[p, at, :ffn] = d_gate
        kept[p, at, ffn : 2 * ffn] = d_up
        kept[p, at, 2 * ffn :] = (passed * up).astype(HALF)
        return across(d_gate, weight[:, :ffn]) + across(d_up, weight[:, ffn : 2 * ffn])

    g_gain[...] = jnp.zeros_like(g_gain)
    for h, at, total in edge.sums(make, partial, beside, away, come):
        slope, by_gain = normed_slope(total, stream[at, :], gain[1:2, :])
        slope = slope + prior[at, :]
        g_gain[:1, :] = g_gain[:1, :] + by_gain
        out[at, :] = slope
        full[0, at, :] = slope.astype(HALF)
        edge.give(full, h)
    for left, low, high in ((norm, 0, 2 * ffn), (later, 2 * ffn, 3 * ffn)):
        turned = [left[p].T for p in range(4)]
        for c in range(low, high, CHUNK):
            total = jnp.dot(turned[0], kept[0, :, c : c + CHUNK], preferred_element_type=FLOAT)
            for p in (1, 2, 3):
                total = total + jnp.dot(
                    turned[p], kept[p, :, c : c + CHUNK], preferred_element_type=FLOAT
                )
            grad[:, c : c + CHUNK] = total.astype(HALF)
    edge.pass_on(full)
    edge.end()


def backward_boundary(norm, later, weight, stream, gain, prior):
    rows, depth = stream.shape
    parts = 2
    vmem = pl.BlockSpec(memory_space=pltpu.VMEM)
    scratch = exchange_scratch(rows, depth, parts)
    out, g_gain, full, grad = pl.pallas_call(
        functools.partial(backward_kernel, parts),
        in_specs=[vmem] * 6,
        out_specs=[vmem] * 4,
        out_shape=[
            jax.ShapeDtypeStruct((rows, depth), FLOAT),
            jax.ShapeDtypeStruct((8, depth), FLOAT),
            jax.ShapeDtypeStruct((4, rows, depth), HALF),
            jax.ShapeDtypeStruct(weight.shape, HALF),
        ],
        scratch_shapes=scratch[:4] + [pltpu.VMEM((4, rows, weight.shape[1]), HALF)] + scratch[4:],
        compiler_params=pltpu.CompilerParams(
            collective_id=5, has_side_effects=True, vmem_limit_bytes=VMEM_LIMIT
        ),
        cost_estimate=SMALL,
        name="backward_boundary",
    )(norm.reshape(4, rows, depth), later.reshape(4, rows, depth), weight, stream, gain, prior)
    return out, g_gain, full.reshape(4 * rows, depth), grad


def start_kernel(
    ids, turned, gain, block, feed, stays, leaves, stream, full, weights, four, pair, *refs
):
    table, corner, rows, out, near, cross, come, send, recv, local = refs
    own, rank = lax.axis_index("dp"), lax.axis_index("tensor")
    beside, across = near_and_far(own, rank)
    far = [(own ^ k, rank) for k in range(1, 8)]
    greet([beside, across] + far)
    width, vocab = turned.shape
    count = rows.shape[0]
    copies, beside_of, across_of, far_of = [], {}, {}, {}

    def begin(source, target, n, peer):
        copy = remote(source, target, send, recv, n, peer)
        copy.start()
        copies.append(copy)
        return copy

    def place(k):
        return pl.ds(pl.multiple_of((own ^ k) * width, width), width)

    weights_of = {}
    for k in (1, 2, 4, 6):
        weights_of[k] = begin(block, weights.at[place(0)], 35 + k, far[k - 1])
    weights[place(0), :] = block[...]
    bit = own % 2
    line = pl.ds(pl.multiple_of(bit * width, width), width)
    aside = begin(leaves, pair.at[line], 43, far[0])
    own_line = pltpu.make_async_copy(stays, pair.at[line], local)
    own_line.start()
    corner[...] = jnp.zeros_like(corner)
    for v in range(0, vocab, LANES):
        some = min(LANES, vocab - v)
        corner[:width, :some] = turned[:, v : v + some].astype(HALF).astype(FLOAT)
        if some < LANES:
            corner[:width, some:] = jnp.zeros((width, LANES - some), FLOAT)
        table[v : v + LANES, :] = corner[...].T
    if vocab % LANES == 0:
        table[vocab:, :] = jnp.zeros((LANES, LANES), FLOAT)

    def fetch(place):
        def body(i, carry):
            for u in range(16):
                r = i * 16 + u
                rows[pl.ds(r, 1), :] = table[pl.ds(ids[place * count + r], 1), :]
            return carry

        lax.fori_loop(0, count // 16, body, 0)

    for p in (3, 2):
        for k in range(8):
            fetch(p * 8 + k)
            out[p, k] = rows[:, :width].astype(HALF)
            beside_of[p - 2, k] = begin(out.at[p, k], near.at[p - 2, k], (p - 2) * 8 + k, beside)
    for k in (2, 4, 6):
        weights_of[k].wait_recv()
        weights_of[k + 1] = begin(weights.at[place(k)], weights.at[place(k)], 36 + k, far[0])
    order = (7, 6, 5, 4, 3, 2, 1, 0)
    for k in order:
        fetch(8 + k)
        beside_of[1, k].wait_recv()
        total = rows[:, :width] + near[1, k].astype(FLOAT)
        out[1, k] = total.astype(HALF)
        across_of[k] = begin(out.at[1, k], cross.at[k], 16 + k, across)
    for k in order:
        fetch(k)
        beside_of[0, k].wait_recv()
        total = rows[:, :width] + near[0, k].astype(FLOAT)
        across_of[k].wait_recv()
        out[0, k] = (total + cross[k].astype(FLOAT)).astype(HALF)
        if k:
            far_of[k] = begin(out.at[0, k], come.at[k], 24 + k, far[k - 1])
    fourth = begin(feed, four, 44, far[3])
    come[0] = out[0, 0]
    for k in order[:-1]:
        far_of[k].wait_recv()
    for b in range(8):
        stream[:, b * width : (b + 1) * width] = come[own ^ b].astype(FLOAT)
    full[0] = normed(stream[...], gain[0:1, :]).astype(HALF)
    one = begin(full.at[0], full.at[1], 32, across)
    two = begin(full.at[0], full.at[2], 33, beside)
    one.wait_recv()
    three = begin(full.at[1], full.at[3], 34, beside)
    two.wait_recv()
    three.wait_recv()
    for k in (1, 3, 5, 7):
        weights_of[k].wait_recv()
    aside.wait_recv()
    fourth.wait_recv()
    own_line.wait()
    for copy in copies:
        copy.wait_send()


def start_rows(ids, turned, gain, block, feed, stays, leaves):
    width, vocab = turned.shape
    rows = ids.shape[0] // 32
    padded = (vocab // LANES + 1) * LANES
    vmem = pl.BlockSpec(memory_space=pltpu.VMEM)
    whole = pl.BlockSpec(memory_space=pl.ANY)
    stream, full, weights, four, pair = pl.pallas_call(
        start_kernel,
        in_specs=[pl.BlockSpec(memory_space=pltpu.SMEM), vmem, vmem, vmem, vmem, whole, whole],
        out_specs=[vmem] * 4 + [whole],
        out_shape=[
            jax.ShapeDtypeStruct((rows, 8 * width), FLOAT),
            jax.ShapeDtypeStruct((4, rows, 8 * width), HALF),
            jax.ShapeDtypeStruct((8 * width, block.shape[1]), HALF),
            jax.ShapeDtypeStruct(feed.shape, HALF),
            jax.ShapeDtypeStruct((2 * width, stays.shape[1]), HALF),
        ],
        scratch_shapes=[
            pltpu.VMEM((padded, LANES), FLOAT),
            pltpu.VMEM((LANES, LANES), FLOAT),
            pltpu.VMEM((rows, LANES), FLOAT),
            pltpu.VMEM((4, 8, rows, width), HALF),
            pltpu.VMEM((2, 8, rows, width), HALF),
            pltpu.VMEM((8, rows, width), HALF),
            pltpu.VMEM((8, rows, width), HALF),
            pltpu.SemaphoreType.DMA((45,)),
            pltpu.SemaphoreType.DMA((45,)),
            pltpu.SemaphoreType.DMA,
        ],
        compiler_params=pltpu.CompilerParams(
            collective_id=6, has_side_effects=True, vmem_limit_bytes=VMEM_LIMIT
        ),
        cost_estimate=SMALL,
        name="start_rows",
    )(ids, turned, gain, block, feed, stays, leaves)
    return stream, full.reshape(4 * rows, 8 * width), weights, four, pair


def end_kernel(parts, waits, d_qkv, weight, stream, gain, prior, gain_one, gain_two, apart, *refs):
    rows, g_gain, arrived, partial, beside, away, come, leave, mine, summed, first, second, send, recv = refs[waits:]
    own, rank = lax.axis_index("dp"), lax.axis_index("tensor")
    near, across = near_and_far(own, rank)
    far = [(own ^ k, rank) for k in range(1, 8)]
    greet([near, across, (own, rank ^ 3)] + far)
    edge = Boundary(own, rank, send, recv, parts, stream.shape[0] // parts)
    aside = remote(apart, arrived, send, recv, Boundary.COUNT * parts, far[0])
    aside.start()
    edge.copies.append(aside)
    width = rows.shape[3]
    gain_zero = jnp.zeros_like(gain[0:1, :])
    mine[...] = jnp.zeros_like(mine)

    def make(p, h):
        return turned_product(columns_of(d_qkv, p, h, parts), weight[:, : d_qkv.shape[0]])

    for h, at, total in edge.sums(make, partial, beside, away, come):
        slope, by_gain = normed_slope(total, stream[at, :], gain[0:1, :])
        slope = slope + prior[at, :]
        gain_zero = gain_zero + by_gain
        for b in range(8):
            leave[b, at, :] = slope[:, b * width : (b + 1) * width].astype(HALF)
    base = Boundary.COUNT * parts
    far_of, last = {}, []

    def begin(source, target, n, peer):
        copy = remote(source, target, send, recv, base + n, peer)
        copy.start()
        edge.copies.append(copy)
        return copy

    order = (7, 6, 5, 4, 3, 2, 1)
    for k in order:
        far_of[k] = begin(leave.at[own ^ k], rows.at[0, k], k, far[k - 1])
    rows[0, 0] = leave[own]
    for b in range(8):
        for n, line in enumerate((gain_zero, gain_one[0:1, :], gain_two[0:1, :])):
            mine[own ^ b, n : n + 1, :width] = line[:, b * width : (b + 1) * width]
    gains_of = [
        begin(mine, first.at[n - 1], 31 + n, (own, rank ^ n)) for n in (1, 2, 3)
    ]
    crossed = {}
    for k in (0, 1, 2, 3, 4, 5, 6, 7):
        if k:
            far_of[k].wait_recv()
        crossed[k] = begin(rows.at[0, k], rows.at[1, k], 8 + k, across)
        last.append(begin(rows.at[0, k], rows.at[2, k], 16 + k, near))
    for copy in gains_of:
        copy.wait_recv()
    summed[...] = (mine[...] + first[0]) + (first[1] + first[2])
    gains_of = [begin(summed.at[k], second.at[k], 34 + k, far[k - 1]) for k in range(1, 8)]
    for k in (0, 1, 2, 3, 4, 5, 6, 7):
        crossed[k].wait_recv()
        last.append(begin(rows.at[1, k], rows.at[3, k], 24 + k, near))
    for copy in last + gains_of:
        copy.wait_recv()
    second[0] = summed[0]
    pairs = [second[k] + second[k + 1] for k in (0, 2, 4, 6)]
    g_gain[...] = (pairs[0] + pairs[1]) + (pairs[2] + pairs[3])
    aside.wait_recv()
    edge.end()


def end_rows(d_qkv, weight, stream, gain, prior, gain_one, gain_two, apart, width, before):
    rows, depth = stream.shape
    parts = 2
    vmem = pl.BlockSpec(memory_space=pltpu.VMEM)
    semaphores = Boundary.COUNT * parts + 42
    whole = pl.BlockSpec(memory_space=pl.ANY)
    out, g_gain, arrived = pl.pallas_call(
        functools.partial(end_kernel, parts, len(before)),
        in_specs=[vmem] * 7 + [whole] * (1 + len(before)),
        out_specs=[vmem] * 2 + [whole],
        out_shape=[
            jax.ShapeDtypeStruct((4, 8, rows, width), HALF),
            jax.ShapeDtypeStruct((8, LANES), FLOAT),
            jax.ShapeDtypeStruct(apart.shape, HALF),
        ],
        scratch_shapes=exchange_scratch(rows, depth, parts)[:4]
        + [
            pltpu.VMEM((8, rows, width), HALF),
            pltpu.VMEM((8, 8, LANES), FLOAT),
            pltpu.VMEM((8, 8, LANES), FLOAT),
            pltpu.VMEM((3, 8, 8, LANES), FLOAT),
            pltpu.VMEM((8, 8, LANES), FLOAT),
            pltpu.SemaphoreType.DMA((semaphores,)),
            pltpu.SemaphoreType.DMA((semaphores,)),
        ],
        compiler_params=pltpu.CompilerParams(
            collective_id=7, has_side_effects=True, vmem_limit_bytes=VMEM_LIMIT
        ),
        cost_estimate=SMALL,
        name="end_rows",
    )(d_qkv, weight, stream, gain, prior, gain_one, gain_two, apart, *before)
    return out.reshape(-1, width), g_gain[:3, :width], arrived


def merge_kernel(scan, extra, joined, mine, every, send, recv):
    own, rank = lax.axis_index("dp"), lax.axis_index("tensor")
    turns = [(a, b) for a in (0, 1) for b in range(4)][1:]
    peers = [(own ^ a, rank ^ b) for a, b in turns]
    greet(peers)
    tokens = scan.shape[1] // 2
    share = tokens // 4
    mine[...] = jnp.zeros_like(mine)
    mine[0:3, :] = scan[0:3, :tokens]
    mine[3:6, :] = scan[0:3, tokens:]
    copies = []
    for n, peer in enumerate(peers):
        copies.append(remote(mine, every.at[n], send, recv, n, peer))
        copies[-1].start()
    joined[...] = jnp.zeros_like(joined)
    joined[2:4, :] = extra[:2, :]
    for copy in copies:
        copy.wait()
    for y in (0, 1):
        for p in range(4):
            terms = {(0, 0): mine[3 * y : 3 * y + 3, p * share : (p + 1) * share]}
            for n, (a, b) in enumerate(turns):
                q = TURN.index(TURN[p] ^ b)
                terms[a, b] = every[n, 3 * (y ^ a) : 3 * (y ^ a) + 3, q * share : (q + 1) * share]
            peak = functools.reduce(jnp.maximum, [term[0:1] for term in terms.values()])
            sums, hits = [], []
            for a in (0, 1):
                for b in (0, 2):
                    pair = (terms[a, b], terms[a, b ^ 1])
                    sums.append(sum(term[1:2] * jnp.exp(term[0:1] - peak) for term in pair))
                    hits.append(pair[0][2:3] + pair[1][2:3])
            at = pl.ds(y * tokens + p * share, share)
            joined[0:1, at] = peak + jnp.log((sums[0] + sums[1]) + (sums[2] + sums[3]))
            joined[1:2, at] = (hits[0] + hits[1]) + (hits[2] + hits[3])


def merge_scans(scan, extra):
    vmem = pl.BlockSpec(memory_space=pltpu.VMEM)
    shape = (8, scan.shape[1] // 2)
    return pl.pallas_call(
        merge_kernel,
        in_specs=[vmem] * 2,
        out_specs=vmem,
        out_shape=jax.ShapeDtypeStruct(scan.shape, FLOAT),
        scratch_shapes=[
            pltpu.VMEM(shape, FLOAT),
            pltpu.VMEM((7, *shape), FLOAT),
            pltpu.SemaphoreType.DMA((7,)),
            pltpu.SemaphoreType.DMA((7,)),
        ],
        compiler_params=pltpu.CompilerParams(collective_id=8, has_side_effects=True),
        name="merge_scans",
    )(scan, extra)


def across(left, right):
    return lax.dot_general(left, right, (((1,), (1,)), ((), ())), preferred_element_type=FLOAT)


def product(left, right, over_left, over_right):
    return lax.dot_general(
        left, right, (((over_left,), (over_right,)), ((), ())), preferred_element_type=FLOAT
    )


def adam(weight, grad, first, second, rate, decay):
    first = BETA_ONE * first + (1.0 - BETA_ONE) * grad
    second = BETA_TWO * second + (1.0 - BETA_TWO) * grad * grad
    first_hat = first / (1.0 - BETA_ONE**STEP)
    second_hat = second / (1.0 - BETA_TWO**STEP)
    weight = weight - rate * (first_hat / (jnp.sqrt(second_hat) + ADAM_EPS) + decay * weight)
    return (weight, first, second, weight.astype(HALF))


def update_kernel(counts, factor, *refs):
    arrays = len(counts)
    inputs, outputs = refs[: 3 * arrays + sum(counts)], refs[3 * arrays + sum(counts) :]
    grads = inputs[3 * arrays :]
    for n in range(arrays):
        weight, first, second = inputs[3 * n : 3 * n + 3]
        low = 0
        for grad in grads[: counts[n]]:
            high = low + grad.shape[-1]
            at = (Ellipsis, slice(low, high))
            results = adam(
                weight[at], grad[...].astype(FLOAT) * factor[0], first[at], second[at], LR, DECAY
            )
            for out, result in zip(outputs[4 * n : 4 * n + 4], results):
                out[at] = result
            low = high
        grads = grads[counts[n] :]


def update(arrays, factor):
    rows = arrays[0][0].shape[0]
    steps = rows // 16 if rows % 16 == 0 else 1

    def block(array):
        zeros = (0,) * (array.ndim - 1)
        return pl.BlockSpec((array.shape[0] // steps, *array.shape[1:]), lambda i: (i, *zeros))

    inputs = [array for entry in arrays for array in entry[:3]]
    grads = [grad for entry in arrays for grad in entry[3]]
    outs = [
        jax.ShapeDtypeStruct(entry[0].shape, kind)
        for entry in arrays
        for kind in (FLOAT, FLOAT, FLOAT, HALF)
    ]
    results = pl.pallas_call(
        functools.partial(update_kernel, tuple(len(entry[3]) for entry in arrays)),
        grid=(steps,),
        in_specs=[pl.BlockSpec(memory_space=pltpu.SMEM)] + [block(a) for a in inputs + grads],
        out_specs=[block(a) for a in outs],
        out_shape=outs,
        compiler_params=pltpu.CompilerParams(vmem_limit_bytes=VMEM_LIMIT),
        cost_estimate=SMALL,
        name="update",
    )(factor.reshape(1), *inputs, *grads)
    return [results[4 * n : 4 * n + 4] for n in range(len(arrays))]


def shards(
    token_ids,
    targets,
    segments,
    completion,
    micro_order,
    *state,
):
    weights, means, squares_in = state[:7], state[7:14], state[14:21]
    embedding, attn_in, attn_out, ffn_in, ffn_out, head_table, norm_gains = weights
    group = lax.axis_size("dp")
    parts = lax.axis_size("tensor")
    own, rank = lax.axis_index("dp"), lax.axis_index("tensor")
    vocab, width = embedding.shape
    start = rank * vocab
    seqs, length = token_ids.shape
    micro = micro_order.shape[1]
    share = length // parts
    turn = jnp.array(TURN, jnp.int32)
    dp_order = own ^ jnp.arange(group, dtype=jnp.int32)
    tensor_order = rank ^ turn
    tensor_order_natural = rank ^ jnp.arange(parts, dtype=jnp.int32)
    ffn = ffn_out.shape[0]
    qkv_width = attn_in.shape[1]

    attn_block = jnp.concatenate([attn_in, attn_out.T], axis=1).astype(HALF)
    ffn_block = jnp.concatenate([ffn_in.reshape(width, -1), ffn_out.T], axis=1).astype(HALF)
    bit = own % 2
    entries = vocab // 2
    low_half, high_half = head_table[:, :entries], head_table[:, entries:]
    stays = jnp.where(bit == 0, low_half, high_half).astype(HALF)
    leaves = jnp.where(bit == 0, high_half, low_half).astype(HALF)
    lines = [[i for i in range(group) if i % 2 == odd] for odd in (0, 1)]

    picked_rows = micro_order[0]
    takes_seq = picked_rows[:, None] == jnp.arange(seqs)[None, :]
    local_counts = jnp.sum(jnp.where(takes_seq, jnp.sum(completion, axis=1)[None, :], 0), axis=1)
    id_rows = seqs * length // LANES
    packed = jnp.concatenate(
        [
            token_ids.reshape(-1),
            targets.reshape(-1),
            completion.reshape(-1),
            jnp.pad(jnp.concatenate([local_counts, picked_rows]), (0, 8 * LANES - 2 * micro)),
        ]
    ).reshape(3 * id_rows + 8, LANES)
    gains = jnp.pad(norm_gains.astype(HALF).astype(FLOAT), ((0, 5), (0, LANES - width)))
    if group == 8:
        packed, every_id, gains, extra = spread(
            packed, gains, seqs, length, micro, vocab, width
        )
        every_id = every_id.reshape(-1)
    else:
        packed, gains = lax.all_gather(packed, "dp"), lax.all_gather(gains, "dp")
        packed = jnp.take(packed, dp_order, axis=0)
        every_id = packed[:, :id_rows].reshape(group, seqs, parts, share)
        every_id = jnp.take(every_id, tensor_order, axis=2)
        every_id = every_id.transpose(2, 0, 1, 3).reshape(-1) - start
        every_id = jnp.where((every_id >= 0) & (every_id < vocab), every_id, vocab)
        gains = gains.transpose(1, 0, 2)[:, :, :width].reshape(8, -1)
    packed, leaves = lax.optimization_barrier((packed, leaves))
    numbers = packed[:, 3 * id_rows, : 2 * micro]
    counts = jnp.sum(numbers[:, :micro].astype(FLOAT), axis=0)

    def both_order(values):
        values = values.reshape(seqs, parts, share)
        values = jnp.where(rank % 2 == 1, values[:, [1, 0, 3, 2]], values)
        values = jnp.where(rank // 2 == 1, values[:, [2, 3, 0, 1]], values)
        return values[:, list(TURN)].transpose(1, 0, 2).reshape(-1)

    if group != 8:
        rows_extra = []
        for k in (0, 1):
            its_flags = packed[k, 2 * id_rows : 3 * id_rows].reshape(seqs, length).astype(FLOAT)
            its_order = numbers[k, micro:]
            takes = (its_order[None, :] == jnp.arange(seqs)[:, None]).astype(FLOAT)
            its_scale = its_flags * jnp.sum(takes / jnp.maximum(counts, 1.0), axis=1)[:, None]
            aims = packed[k, id_rows : 2 * id_rows].reshape(seqs, length) - start - bit * entries
            aims = jnp.where((aims >= 0) & (aims < entries), aims, -1).astype(FLOAT)
            rows_extra.append(jnp.stack([both_order(its_scale), both_order(aims), both_order(its_flags)]))
        extra = jnp.pad(jnp.concatenate(rows_extra, axis=1), ((0, 5), (0, 0)))

    own_segment = segments[:, :, None] == jnp.arange(8, dtype=jnp.int32)
    sizes = jnp.sum(own_segment.astype(jnp.int32), axis=1)
    begins = jnp.cumsum(sizes, axis=1) - sizes
    first = jnp.sum(jnp.where(own_segment, begins[:, None, :], 0), axis=2)
    first = jnp.broadcast_to(first[:, None, :], (seqs, 8, length))
    base = turn[tensor_order_natural] * (seqs * share)
    cosine, sine = tables(length, HEAD_DIM)

    if group == 8:
        stream0, attn_norm, attn_w, ffn_four, head_rows = start_rows(
            every_id, embedding.T, gains, attn_block, ffn_block, stays, leaves
        )
        ffn_blocks = [ffn_block, ffn_four]
    else:
        rows = lookup(embedding.T, every_id).reshape(parts, group, seqs * share, width)
        rows = rows[:2] + swap(rows[2:], "tensor", 1)
        rows = rows[0] + swap(rows[1], "tensor", 2)
        rows = lax.all_to_all(jnp.take(rows, dp_order, axis=0), "dp", 0, 0)
        stream0 = rows.transpose(1, 0, 2).reshape(seqs * share, -1).astype(FLOAT)
        attn_norm = tensor_gather(normed(stream0, gains[0]).astype(HALF))

        attn_w = lax.all_gather(attn_block, "dp", axis=0, tiled=True)
        came = swap(leaves, "dp", 1)
        head_rows = jnp.concatenate(
            [jnp.where(bit == 0, stays, came), jnp.where(bit == 0, came, stays)], axis=0
        )
        ffn_blocks = []
    head_b = lax.all_gather(head_rows, "dp", axis=0, tiled=True, axis_index_groups=lines)
    attn_in_b, attn_out_b = attn_w[:, :qkv_width], attn_w[:, qkv_width:]
    qkv = product(attn_in_b, attn_norm, 0, 1)
    attended, kept, log_sums = attend(base, qkv, cosine, sine, first)
    stream1, ffn_norm, *ffn_w = forward_boundary(
        attended, attn_w, stream0, gains, ffn_blocks
    )
    ffn_w = ffn_w[0] if ffn_w else lax.all_gather(ffn_block, "dp", axis=0, tiled=True)
    stream2, final_norm = wide_forward(ffn_norm, ffn_w, stream1, gains)

    logits, scan, final_turned = head_scan(final_norm, head_b, extra)
    info = merge_scans(scan, extra)
    tokens = seqs * length
    seq_loss = jnp.sum(
        ((info[0, :tokens] - info[1, :tokens]) * extra[2, :tokens]).reshape(parts, seqs, share),
        axis=(0, 2),
    )
    g_head, d_final = head_grad(final_turned, head_b, info, logits)
    g_head = lax.psum_scatter(
        g_head, "dp", scatter_dimension=0, tiled=True, axis_index_groups=lines
    )
    g_stays = jnp.where(bit == 0, g_head[:width], g_head[width:])
    g_leaves = jnp.where(bit == 0, g_head[width:], g_head[:width])

    d_stream2, g_gain2, d_branch2 = wide_backward(d_final, stream2, gains)
    d_stream1, g_gain1, d_branch1, g_ffn = backward_boundary(
        ffn_norm, d_branch2, ffn_w, stream1, gains, d_stream2
    )
    g_ffn_parts = scatter_first(g_ffn)
    d_attended = product(attn_out_b, d_branch1, 0, 1).astype(HALF)
    d_qkv = attend_back(base, kept, log_sums, d_attended, cosine, sine, first, [])
    g_attn_in = product(attn_norm, d_qkv, 0, 1).astype(HALF)
    g_attn_out = product(d_branch1, attended, 0, 1).astype(HALF)
    g_attn = jnp.concatenate([g_attn_in, g_attn_out], axis=1)
    g_attn_parts = scatter_first(g_attn)
    d_qkv, g_ffn = lax.optimization_barrier((d_qkv, g_ffn))
    g_ffn, g_ffn_leaves = scatter_middle(g_ffn, g_ffn_parts)
    if group == 8:
        rows, g_gains, g_came = end_rows(
            d_qkv,
            attn_w,
            stream0,
            gains,
            d_stream1,
            g_gain1,
            g_gain2,
            g_leaves,
            width,
            g_ffn_leaves,
        )
    else:
        d_norm = tensor_scatter(product(d_qkv, attn_in_b, 0, 1))
        d_part, g_gain0 = normed_slope(d_norm, stream0, gains[0:1])
        rows = (d_stream1 + d_part).astype(HALF)
        rows = rows.reshape(seqs * share, group, width).transpose(1, 0, 2)
        rows = jnp.take(lax.all_to_all(rows, "dp", 0, 0), dp_order, axis=0)
        rows = tensor_gather(rows[None]).reshape(-1, width)
        g_came = swap(g_leaves, "dp", 1)
        gain_sum = jnp.concatenate([g_gain0, g_gain1[:1], g_gain2[:1]]).reshape(3, group, width)
        g_gains = jnp.take(lax.psum(gain_sum, ("dp", "tensor")), own, axis=1)
    g_head = [jnp.where(bit == 0, g_stays, g_came), jnp.where(bit == 0, g_came, g_stays)]
    rows, g_ffn, g_attn = lax.optimization_barrier((rows, g_ffn, g_attn))
    g_ffn = scatter_last(g_ffn, g_ffn_leaves)
    g_attn, g_attn_leaves = scatter_middle(g_attn, g_attn_parts)
    last_id, g_ffn, *g_attn_leaves = lax.optimization_barrier((every_id, g_ffn, *g_attn_leaves))
    g_embed, squares = collect(rows, last_id, vocab)
    squares, g_attn = lax.optimization_barrier((squares, g_attn))
    g_attn = scatter_last(g_attn, g_attn_leaves)

    owner = (rank == 0).astype(FLOAT)
    squared = jnp.sum(squares) + owner * jnp.sum(g_gains * g_gains)
    for part in (g_attn, g_ffn, *g_head):
        squared = squared + jnp.sum(part.astype(FLOAT) ** 2)
    losses = jnp.sum(jnp.where(takes_seq, seq_loss[None, :], 0.0), axis=1) * owner
    if group == 8:
        sums = jnp.pad(jnp.concatenate([squared[None], losses]), (0, 8 * LANES - 1 - micro))
        sums = total_over_devices(jnp.broadcast_to(sums.reshape(1, 8, LANES), (8, 8, LANES)))
        squared, loss_sums = sums[0, 0], sums[0, 1 : 1 + micro]
    else:
        squared, loss_sums = lax.psum((squared, losses), ("dp", "tensor"))
    grad_norm = jnp.sqrt(squared)
    factor = CLIP / jnp.maximum(grad_norm, CLIP)
    g_parts = (
        [g_embed],
        [g_attn[:, :qkv_width]],
        [g_attn[:, qkv_width:].T],
        [g_ffn[:, : 2 * ffn].reshape(ffn_in.shape)],
        [g_ffn[:, 2 * ffn :]],
        g_head,
    )
    arrays = []
    for place in range(6):
        entry = (weights[place], means[place], squares_in[place])
        if place in (0, 4):
            entry = tuple(array.T for array in entry)
        arrays.append((*entry, g_parts[place]))
    updated = []
    for place, results in enumerate(update(arrays, factor)):
        updated.extend(result.T if place in (0, 4) else result for result in results)
    updated.extend(adam(norm_gains, g_gains * factor, means[6], squares_in[6], LR_GAIN, 0.0))
    return (jnp.stack([loss_sums, counts]), grad_norm, *updated)


def solution(mesh):
    in_specs = (
        P("dp", None),
        P("dp", None),
        P("dp", None),
        P("dp", None),
        P("dp", None),
        P("tensor", "dp"),
        P("dp", "tensor"),
        P("tensor", "dp"),
        P("dp", None, "tensor"),
        P("tensor", "dp"),
        P("dp", "tensor"),
        P(None, "dp"),
        P("tensor", "dp"),
        P("dp", "tensor"),
        P("tensor", "dp"),
        P("dp", None, "tensor"),
        P("tensor", "dp"),
        P("dp", "tensor"),
        P(None, "dp"),
        P("tensor", "dp"),
        P("dp", "tensor"),
        P("tensor", "dp"),
        P("dp", None, "tensor"),
        P("tensor", "dp"),
        P("dp", "tensor"),
        P(None, "dp"),
    )
    out_specs = (
        P(),
        P(),
        P("tensor", "dp"),
        P("tensor", "dp"),
        P("tensor", "dp"),
        P("tensor", "dp"),
        P("dp", "tensor"),
        P("dp", "tensor"),
        P("dp", "tensor"),
        P("dp", "tensor"),
        P("tensor", "dp"),
        P("tensor", "dp"),
        P("tensor", "dp"),
        P("tensor", "dp"),
        P("dp", None, "tensor"),
        P("dp", None, "tensor"),
        P("dp", None, "tensor"),
        P("dp", None, "tensor"),
        P("tensor", "dp"),
        P("tensor", "dp"),
        P("tensor", "dp"),
        P("tensor", "dp"),
        P("dp", "tensor"),
        P("dp", "tensor"),
        P("dp", "tensor"),
        P("dp", "tensor"),
        P(None, "dp"),
        P(None, "dp"),
        P(None, "dp"),
        P(None, "dp"),
    )
    return jax.shard_map(shards, mesh=mesh, in_specs=in_specs, out_specs=out_specs, check_vma=False)
```

```python
import functools

import jax
import jax.numpy as jnp
import numpy as np
from jax import lax
from jax.experimental import pallas as pl
from jax.experimental.pallas import tpu as pltpu
from jax.sharding import PartitionSpec as P

HEAD_DIM = 64
STEP = 10


EPS = 1e-05
CLIP = 0.01
LR = 0.03
LR_GAIN = 0.5
BETA_ONE = 0.9
BETA_TWO = 0.95
ADAM_EPS = 1e-08
DECAY = 0.1
NEG = -1e30
FLOAT = jnp.float32
HALF = jnp.bfloat16
LANES = 128
ROWS = 1024
VMEM_LIMIT = 56 * 2**20
TILE = 512
CHUNK = 256
MESH = pl.DeviceIdType.MESH
SMALL = pl.CostEstimate(flops=2**20, bytes_accessed=2**20, transcendentals=0)

TURN = (0, 2, 1, 3)


def swap(value, axis, bit):
    pairs = [(i, i ^ bit) for i in range(lax.axis_size(axis))]
    return lax.ppermute(value, axis, pairs)


def normed(values, gain):
    return values * lax.rsqrt(jnp.mean(values * values, axis=-1, keepdims=True) + EPS) * gain


def tables(length, width):
    inverse = np.float32(10000.0) ** (-np.arange(0, width, 2, dtype=np.float32) / np.float32(width))
    angle = inverse[:, None] * np.arange(length, dtype=np.float32)[None, :]
    return jnp.asarray(np.cos(angle)), jnp.asarray(np.sin(angle))


def block_of(full, k):
    rows = full.shape[0] // lax.axis_size("dp")
    own = lax.axis_index("dp")
    return lax.dynamic_slice(full, ((own ^ k) * rows, 0), (rows, full.shape[1]))


def scatter_first(full):
    if lax.axis_size("dp") != 8:
        return []
    leaves = jnp.concatenate([block_of(full, k + 1) for k in (0, 2, 4, 6)], axis=0)
    return [swap(leaves, "dp", 1)]


def scatter_middle(full, parts):
    if lax.axis_size("dp") != 8:
        return full, []
    rows = full.shape[0] // 8
    sums = [
        block_of(full, 2 * n).astype(FLOAT) + parts[0][n * rows : (n + 1) * rows].astype(FLOAT)
        for n in range(4)
    ]
    return sums[0], [total.astype(HALF) for total in sums[1:]]


def scatter_last(total, leaves):
    if lax.axis_size("dp") != 8:
        return lax.psum_scatter(total.astype(FLOAT), "dp", scatter_dimension=0, tiled=True)
    for n, leave in enumerate(leaves):
        total = total + swap(leave, "dp", 2 * n + 2).astype(FLOAT)
    return total


def peers_of(own, rank, bits, axis):
    if axis == "dp":
        return [(own ^ k, rank) for k in bits]
    return [(own, rank ^ k) for k in bits]


def greet(peers):
    barrier = pltpu.get_barrier_semaphore()
    for peer in peers:
        pl.semaphore_signal(barrier, inc=1, device_id=peer, device_id_type=MESH)
    pl.semaphore_wait(barrier, len(peers))


def spread_kernel(
    vocab, seqs, micro, numbers, gains, every, ids, all_gains, extra, every_gain, send, recv
):
    own, rank = lax.axis_index("dp"), lax.axis_index("tensor")
    peers = peers_of(own, rank, range(1, 8), "dp")
    greet(peers)
    every[0] = numbers[...]
    every_gain[0] = gains[...]
    copies = []
    for k in range(1, 8):
        for n, (source, target) in enumerate(((numbers, every), (gains, every_gain))):
            copies.append(
                pltpu.make_async_remote_copy(
                    src_ref=source,
                    dst_ref=target.at[k],
                    send_sem=send.at[n, k],
                    recv_sem=recv.at[n, k],
                    device_id=peers[k - 1],
                    device_id_type=MESH,
                )
            )
            copies[-1].start()
    for copy in copies:
        copy.wait()
    lines = ids.shape[0] // (32 * seqs)
    for p in range(4):
        shard = rank ^ TURN[p]
        for k in range(8):
            for j in range(seqs):
                local = every[k, pl.ds((j * 4 + shard) * lines, lines), :] - rank * vocab
                local = jnp.where((local >= 0) & (local < vocab), local, vocab)
                ids[pl.ds(((p * 8 + k) * seqs + j) * lines, lines), :] = local
    total = numbers.shape[0] - 8
    total = sum(every[k, total : total + 1, :].astype(FLOAT) for k in range(8))
    weights = 1.0 / jnp.maximum(total, 1.0)
    id_rows = (numbers.shape[0] - 8) // 3
    entries = vocab // 2
    low = rank * vocab + (own % 2) * entries
    extra[...] = jnp.zeros_like(extra)
    for k in (0, 1):
        order = every[k, 3 * id_rows : 3 * id_rows + 1, :]
        for j in range(seqs):
            weight = sum(
                jnp.where(order[:, micro + m : micro + m + 1] == j, weights[:, m : m + 1], 0.0)
                for m in range(micro)
            )
            for p in range(4):
                row = (j * 4 + (rank ^ TURN[p])) * lines
                for r in range(lines):
                    place = (((k * 4 + p) * seqs + j) * lines + r) * LANES
                    counted = every[k, pl.ds(2 * id_rows + row + r, 1), :].astype(FLOAT)
                    aim = every[k, pl.ds(id_rows + row + r, 1), :] - low
                    aim = jnp.where((aim >= 0) & (aim < entries), aim, -1).astype(FLOAT)
                    extra[0:1, place : place + LANES] = counted * weight
                    extra[1:2, place : place + LANES] = aim
                    extra[2:3, place : place + LANES] = counted
    width = all_gains.shape[1] // 8
    for b in range(8):
        all_gains[:, b * width : (b + 1) * width] = every_gain[own ^ b][:, :width]


def spread(numbers, gains, seqs, length, micro, vocab, width):
    vmem = pl.BlockSpec(memory_space=pltpu.VMEM)
    return pl.pallas_call(
        functools.partial(spread_kernel, vocab, seqs, micro),
        in_specs=[vmem] * 2,
        out_specs=[vmem] * 4,
        out_shape=[
            jax.ShapeDtypeStruct((8, *numbers.shape), numbers.dtype),
            jax.ShapeDtypeStruct((8 * seqs * length // LANES, LANES), jnp.int32),
            jax.ShapeDtypeStruct((8, 8 * width), FLOAT),
            jax.ShapeDtypeStruct((8, 2 * seqs * length), FLOAT),
        ],
        scratch_shapes=[
            pltpu.VMEM((8, *gains.shape), FLOAT),
            pltpu.SemaphoreType.DMA((2, 8)),
            pltpu.SemaphoreType.DMA((2, 8)),
        ],
        compiler_params=pltpu.CompilerParams(collective_id=1, has_side_effects=True),
        cost_estimate=SMALL,
        name="spread",
    )(numbers, gains)


def total_kernel(blocks, out, first, summed, second, send, recv):
    own, rank = lax.axis_index("dp"), lax.axis_index("tensor")
    near = peers_of(own, rank, range(1, 4), "tensor")
    far = peers_of(own, rank, range(1, 8), "dp")
    greet(near + far)
    copies = []
    for k in range(1, 4):
        copy = pltpu.make_async_remote_copy(
            src_ref=blocks,
            dst_ref=first.at[k - 1],
            send_sem=send.at[k - 1],
            recv_sem=recv.at[k - 1],
            device_id=near[k - 1],
            device_id_type=MESH,
        )
        copy.start()
        copies.append(copy)
    for copy in copies:
        copy.wait()
    summed[...] = (blocks[...] + first[0]) + (first[1] + first[2])
    copies = []
    for k in range(1, 8):
        copy = pltpu.make_async_remote_copy(
            src_ref=summed.at[k],
            dst_ref=second.at[k],
            send_sem=send.at[2 + k],
            recv_sem=recv.at[2 + k],
            device_id=far[k - 1],
            device_id_type=MESH,
        )
        copy.start()
        copies.append(copy)
    for copy in copies:
        copy.wait()
    second[0] = summed[0]
    pairs = [second[k] + second[k + 1] for k in (0, 2, 4, 6)]
    out[...] = (pairs[0] + pairs[1]) + (pairs[2] + pairs[3])


def total_over_devices(blocks):
    shape = blocks.shape
    return pl.pallas_call(
        total_kernel,
        in_specs=[pl.BlockSpec(memory_space=pltpu.VMEM)],
        out_specs=pl.BlockSpec(memory_space=pltpu.VMEM),
        out_shape=jax.ShapeDtypeStruct(shape[1:], FLOAT),
        scratch_shapes=[
            pltpu.VMEM((3, *shape), FLOAT),
            pltpu.VMEM(shape, FLOAT),
            pltpu.VMEM(shape, FLOAT),
            pltpu.SemaphoreType.DMA((10,)),
            pltpu.SemaphoreType.DMA((10,)),
        ],
        compiler_params=pltpu.CompilerParams(collective_id=2, has_side_effects=True),
        name="total",
    )(blocks)


def tensor_gather(block):
    half = jnp.concatenate([block, swap(block, "tensor", 2)], axis=0)
    return jnp.concatenate([half, swap(half, "tensor", 1)], axis=0)


def tensor_scatter(full):
    half = full.shape[0] // 2
    quarter = half // 2
    both = full[:half] + swap(full[half:], "tensor", 1)
    there = swap(both[quarter:].astype(HALF), "tensor", 2)
    return both[:quarter] + there.astype(FLOAT)


def lookup_kernel(ids, turned, out, table, corner, rows):
    count = rows.shape[0]
    width, vocab = turned.shape

    @pl.when(pl.program_id(0) == 0)
    def _():
        corner[...] = jnp.zeros_like(corner)
        for v in range(0, vocab, LANES):
            some = min(LANES, vocab - v)
            corner[:width, :some] = turned[:, v : v + some].astype(HALF).astype(FLOAT)
            if some < LANES:
                corner[:width, some:] = jnp.zeros((width, LANES - some), FLOAT)
            table[v : v + LANES, :] = corner[...].T
        if vocab % LANES == 0:
            table[vocab:, :] = jnp.zeros((LANES, LANES), FLOAT)

    def body(i, carry):
        for u in range(16):
            r = i * 16 + u
            rows[pl.ds(r, 1), :] = table[pl.ds(ids[0, 0, r], 1), :]
        return carry

    lax.fori_loop(0, count // 16, body, 0)
    out[...] = rows[:, : out.shape[1]].astype(HALF)


def lookup(turned, ids):
    count = ids.shape[0]
    width, vocab = turned.shape
    padded = (vocab // LANES + 1) * LANES
    return pl.pallas_call(
        lookup_kernel,
        grid=(count // ROWS,),
        in_specs=[
            pl.BlockSpec((1, 1, ROWS), lambda i: (i, 0, 0), memory_space=pltpu.SMEM),
            pl.BlockSpec(turned.shape, lambda i: (0, 0), pipeline_mode=pl.Buffered(1)),
        ],
        out_specs=pl.BlockSpec((ROWS, width), lambda i: (i, 0)),
        out_shape=jax.ShapeDtypeStruct((count, width), HALF),
        scratch_shapes=[
            pltpu.VMEM((padded, LANES), FLOAT),
            pltpu.VMEM((LANES, LANES), FLOAT),
            pltpu.VMEM((ROWS, LANES), FLOAT),
        ],
        compiler_params=pltpu.CompilerParams(vmem_limit_bytes=VMEM_LIMIT),
        cost_estimate=SMALL,
        name="lookup",
    )(ids.reshape(count // ROWS, 1, ROWS), turned)


def collect_kernel(ids, grads, out, squares, rows, *sums):
    step = pl.program_id(0)
    count = rows.shape[0]
    width, vocab = out.shape

    @pl.when(step == 0)
    def _():
        rows[...] = jnp.zeros_like(rows)
        for total in sums:
            total[...] = jnp.zeros_like(total)

    rows[:, :width] = grads[...].astype(FLOAT)

    def body(i, carry):
        for u in range(16):
            r = i * 16 + u
            total = sums[u % len(sums)]
            place = pl.ds(ids[0, 0, r], 1)
            total[place, :] = total[place, :] + rows[pl.ds(r, 1), :]
        return carry

    lax.fori_loop(0, count // 16, body, 0)

    @pl.when(step == pl.num_programs(0) - 1)
    def _():
        squared = jnp.zeros((8, LANES), FLOAT)
        for v in range(0, vocab, LANES):
            some = min(LANES, vocab - v)
            total = sums[0][v : v + some, :]
            for other in sums[1:]:
                total = total + other[v : v + some, :]
            for r in range(0, some, 8):
                squared = squared + total[r : r + 8, :] * total[r : r + 8, :]
            if some < LANES:
                total = jnp.concatenate([total, jnp.zeros((LANES - some, LANES), FLOAT)], axis=0)
            out[:, v : v + some] = total.T[:width, :some]
        squares[...] = squared


def collect(grads, ids, vocab):
    count = ids.shape[0]
    width = grads.shape[1]
    padded = (vocab // LANES + 1) * LANES
    return pl.pallas_call(
        collect_kernel,
        grid=(count // ROWS,),
        in_specs=[
            pl.BlockSpec((1, 1, ROWS), lambda i: (i, 0, 0), memory_space=pltpu.SMEM),
            pl.BlockSpec((ROWS, width), lambda i: (i, 0)),
        ],
        out_specs=[
            pl.BlockSpec((width, vocab), lambda i: (0, 0)),
            pl.BlockSpec((8, LANES), lambda i: (0, 0)),
        ],
        out_shape=[
            jax.ShapeDtypeStruct((width, vocab), FLOAT),
            jax.ShapeDtypeStruct((8, LANES), FLOAT),
        ],
        scratch_shapes=[pltpu.VMEM((ROWS, LANES), FLOAT)]
        + [pltpu.VMEM((padded, LANES), FLOAT)] * 8,
        compiler_params=pltpu.CompilerParams(vmem_limit_bytes=VMEM_LIMIT),
        cost_estimate=SMALL,
        name="collect",
    )(ids.reshape(count // ROWS, 1, ROWS), grads)


def edge_of(vocab):
    return vocab - (pl.cdiv(vocab, TILE) - 1) * TILE


def each_tile(vocab, work):
    last = edge_of(vocab)
    if last == TILE:
        work(TILE)
    else:
        step, steps = pl.program_id(0), pl.num_programs(0)
        pl.when(step < steps - 1)(lambda: work(TILE))
        pl.when(step == steps - 1)(lambda: work(last))


def turned_rows(rows):
    return jnp.concatenate([rows] * (LANES // 8), axis=0).T


def scan_kernel(vocab, norm, weight, target, logits, stats, turned, peak, total, hit, aims):
    step = pl.program_id(0)
    rows = norm.shape[0]

    @pl.when(step == 0)
    def _():
        peak[...] = jnp.full_like(peak, NEG)
        total[...] = jnp.zeros_like(total)
        hit[...] = jnp.zeros_like(hit)
        aims[...] = turned_rows(target[...])
        for r in range(0, rows, CHUNK):
            turned[:, r : r + CHUNK] = norm[r : r + CHUNK, :].T

    def work(width):
        lane = lax.broadcasted_iota(jnp.int32, (CHUNK, LANES), 1)
        for r in range(0, rows, CHUNK):
            part = pl.ds(r, CHUNK)
            value = jnp.dot(norm[part, :], weight[...], preferred_element_type=FLOAT)
            logits[part, :] = value
            aim = aims[part, 1:2].astype(jnp.int32) - step * TILE
            slabs, found = [], hit[part, :]
            for c in range(0, width, LANES):
                slab = value[:, c : c + LANES]
                if c + LANES > width:
                    slab = jnp.where(lane < width - c, slab, NEG)
                slabs.append(slab)
                found = found + jnp.where(lane == aim - c, slab, 0.0)
            hit[part, :] = found
            before = peak[part, :]
            top = functools.reduce(jnp.maximum, slabs, before)
            added = total[part, :] * jnp.exp(before - top)
            for slab in slabs:
                added = added + jnp.exp(slab - top)
            total[part, :] = added
            peak[part, :] = top

    each_tile(vocab, work)

    @pl.when(step == pl.num_programs(0) - 1)
    def _():
        top = jnp.max(peak[...], axis=1, keepdims=True)
        added = jnp.sum(total[...] * jnp.exp(peak[...] - top), axis=1, keepdims=True)
        found = jnp.sum(hit[...], axis=1, keepdims=True)
        lane = lax.broadcasted_iota(jnp.int32, (rows, LANES), 1)
        joined = jnp.where(lane == 0, top, jnp.where(lane == 1, added, found))
        stats[...] = joined.T[:8, :]


def head_scan(norm, weight, extra):
    rows, depth = norm.shape
    vocab = weight.shape[1]
    return pl.pallas_call(
        functools.partial(scan_kernel, vocab),
        grid=(pl.cdiv(vocab, TILE),),
        in_specs=[
            pl.BlockSpec((rows, depth), lambda i: (0, 0), pipeline_mode=pl.Buffered(1)),
            pl.BlockSpec((depth, TILE), lambda i: (0, i)),
            pl.BlockSpec((8, rows), lambda i: (0, 0)),
        ],
        out_specs=[
            pl.BlockSpec((rows, TILE), lambda i: (0, i)),
            pl.BlockSpec((8, rows), lambda i: (0, 0)),
            pl.BlockSpec((depth, rows), lambda i: (0, 0), pipeline_mode=pl.Buffered(1)),
        ],
        out_shape=[
            jax.ShapeDtypeStruct((rows, vocab), FLOAT),
            jax.ShapeDtypeStruct((8, rows), FLOAT),
            jax.ShapeDtypeStruct((depth, rows), HALF),
        ],
        scratch_shapes=[pltpu.VMEM((rows, LANES), FLOAT)] * 4,
        compiler_params=pltpu.CompilerParams(vmem_limit_bytes=VMEM_LIMIT),
        cost_estimate=SMALL,
        name="head_scan",
    )(norm, weight, extra)


def grad_kernel(vocab, turned, weight, info, logits, grad, out, total, slope, columns):
    step = pl.program_id(0)
    rows = logits.shape[0]

    @pl.when(step == 0)
    def _():
        columns[...] = turned_rows(info[...])
        total[...] = jnp.zeros_like(total)

    def work(width):
        lane = lax.broadcasted_iota(jnp.int32, (CHUNK, TILE), 1)
        table = weight[...]
        if width < TILE:
            table = jnp.where(lax.broadcasted_iota(jnp.int32, table.shape, 1) < width, table, 0.0)
        for r in range(0, rows, CHUNK):
            part = pl.ds(r, CHUNK)
            aim = columns[part, 3:4].astype(jnp.int32) - step * TILE
            value = jnp.exp(logits[part, :] - columns[part, 0:1])
            value = (value - jnp.where(lane == aim, 1.0, 0.0)) * columns[part, 2:3]
            if width < TILE:
                value = jnp.where(lane < width, value, 0.0)
            value = value.astype(HALF)
            slope[part, :] = value
            total[part, :] = total[part, :] + lax.dot_general(
                value, table, (((1,), (1,)), ((), ())), preferred_element_type=FLOAT
            )
        grad[...] = jnp.dot(turned[...], slope[...], preferred_element_type=FLOAT).astype(HALF)

    each_tile(vocab, work)

    @pl.when(step == pl.num_programs(0) - 1)
    def _():
        for r in range(0, rows, CHUNK):
            out[pl.ds(r, CHUNK), :] = total[pl.ds(r, CHUNK), :].astype(HALF)


def head_grad(turned, weight, info, logits):
    depth, rows = turned.shape
    vocab = weight.shape[1]
    return pl.pallas_call(
        functools.partial(grad_kernel, vocab),
        grid=(pl.cdiv(vocab, TILE),),
        in_specs=[
            pl.BlockSpec((depth, rows), lambda i: (0, 0), pipeline_mode=pl.Buffered(1)),
            pl.BlockSpec((depth, TILE), lambda i: (0, i)),
            pl.BlockSpec((8, rows), lambda i: (0, 0)),
            pl.BlockSpec((rows, TILE), lambda i: (0, i)),
        ],
        out_specs=[
            pl.BlockSpec((depth, TILE), lambda i: (0, i)),
            pl.BlockSpec((rows, depth), lambda i: (0, 0), pipeline_mode=pl.Buffered(1)),
        ],
        out_shape=[
            jax.ShapeDtypeStruct((depth, vocab), HALF),
            jax.ShapeDtypeStruct((rows, depth), HALF),
        ],
        scratch_shapes=[
            pltpu.VMEM((rows, depth), FLOAT),
            pltpu.VMEM((rows, TILE), HALF),
            pltpu.VMEM((rows, LANES), FLOAT),
        ],
        compiler_params=pltpu.CompilerParams(vmem_limit_bytes=VMEM_LIMIT),
        cost_estimate=SMALL,
        name="head_grad",
    )(turned, weight, info, logits)


def turn_rows(low, high, cosine, sine):
    return low * cosine - high * sine, high * cosine + low * sine


def reach(block, share, longest):
    back = -(-(longest - 1) // share)
    return max(0, block - back) * share


def seen(first, low, high, place):
    keys = low + lax.broadcasted_iota(jnp.int32, (high - low, first.shape[1]), 0)
    queries = place + lax.broadcasted_iota(jnp.int32, (high - low, first.shape[1]), 1)
    return (keys >= first) & (keys <= queries)


def attend_kernel(base, qkv, cosine, sine, first, attended, kept, log_total):
    seq = pl.program_id(1)
    blocks = base.shape[0]
    length = cosine.shape[1]
    share = length // blocks
    half = HEAD_DIM // 2

    def spot(i):
        return pl.ds(pl.multiple_of(base[i] + seq * share, share), share)

    for i in range(blocks):
        at = pl.ds(i * share, share)
        turns = (cosine[:, at], sine[:, at])
        for c in (0, 1):
            top = c * HEAD_DIM
            low, high = turn_rows(
                qkv[top : top + half, spot(i)], qkv[top + half : top + HEAD_DIM, spot(i)], *turns
            )
            kept[0, top : top + half, at] = low.astype(HALF)
            kept[0, top + half : top + HEAD_DIM, at] = high.astype(HALF)
        kept[0, 2 * HEAD_DIM :, at] = qkv[2 * HEAD_DIM :, spot(i)].astype(HALF)
    key = kept[0, HEAD_DIM : 2 * HEAD_DIM, :].T
    for i in range(blocks):
        low, high = reach(i, share, length // 2), (i + 1) * share
        at = pl.ds(i * share, share)
        scores = jnp.dot(
            key[low:high, :], kept[0, :HEAD_DIM, at], preferred_element_type=FLOAT
        ) * (HEAD_DIM**-0.5)
        scores = jnp.where(seen(first[0, :, at][:1], low, high, i * share), scores, NEG)
        peak = jnp.max(scores, axis=0, keepdims=True)
        expo = jnp.exp(scores - peak)
        summed = jnp.sum(expo, axis=0, keepdims=True)
        probs = (expo * (1.0 / summed)).astype(HALF)
        value = kept[0, 2 * HEAD_DIM :, low:high]
        attended[:, spot(i)] = jnp.dot(value, probs, preferred_element_type=FLOAT).astype(HALF)
        log_total[0, 0, :, at] = jnp.broadcast_to(peak + jnp.log(summed), (8, share))


def attend(base, qkv, cosine, sine, first):
    seqs, length = first.shape[0], first.shape[2]
    heads = qkv.shape[0] // (3 * HEAD_DIM)
    tokens = qkv.shape[1]
    return pl.pallas_call(
        attend_kernel,
        grid=(heads, seqs),
        in_specs=[
            pl.BlockSpec(memory_space=pltpu.SMEM),
            pl.BlockSpec((3 * HEAD_DIM, tokens), lambda h, j: (h, 0)),
            pl.BlockSpec(cosine.shape, lambda h, j: (0, 0)),
            pl.BlockSpec(sine.shape, lambda h, j: (0, 0)),
            pl.BlockSpec((1, 8, length), lambda h, j: (j, 0, 0)),
        ],
        out_specs=[
            pl.BlockSpec((HEAD_DIM, tokens), lambda h, j: (h, 0)),
            pl.BlockSpec((1, 3 * HEAD_DIM, length), lambda h, j: (j, h, 0)),
            pl.BlockSpec((1, 1, 8, length), lambda h, j: (j, h, 0, 0)),
        ],
        out_shape=[
            jax.ShapeDtypeStruct((heads * HEAD_DIM, tokens), HALF),
            jax.ShapeDtypeStruct((seqs, heads * 3 * HEAD_DIM, length), HALF),
            jax.ShapeDtypeStruct((seqs, heads, 8, length), FLOAT),
        ],
        compiler_params=pltpu.CompilerParams(vmem_limit_bytes=VMEM_LIMIT),
        cost_estimate=SMALL,
        name="attend",
    )(base, qkv, cosine, sine, first)


def attend_back_kernel(waits, base, kept, log_total, slope, cosine, sine, first, *refs):
    d_qkv, d_key, d_value = refs[waits:]
    seq = pl.program_id(1)
    blocks = base.shape[0]
    length = cosine.shape[1]
    share = length // blocks
    half = HEAD_DIM // 2
    scale = HEAD_DIM**-0.5

    def spot(i):
        return pl.ds(pl.multiple_of(base[i] + seq * share, share), share)

    def put(part, i, low, high):
        at = pl.ds(i * share, share)
        d_low, d_high = turn_rows(low, high, cosine[:, at], -sine[:, at])
        top = part * HEAD_DIM
        d_qkv[top : top + half, spot(i)] = d_low.astype(HALF)
        d_qkv[top + half : top + HEAD_DIM, spot(i)] = d_high.astype(HALF)

    query = kept[0, :HEAD_DIM, :].T
    key = kept[0, HEAD_DIM : 2 * HEAD_DIM, :].T
    value = kept[0, 2 * HEAD_DIM :, :].T
    d_key[...] = jnp.zeros_like(d_key)
    d_value[...] = jnp.zeros_like(d_value)
    for i in range(blocks):
        low, high = reach(i, share, length // 2), (i + 1) * share
        at = pl.ds(i * share, share)
        turned = slope[:, spot(i)]
        scores = jnp.dot(
            key[low:high, :], kept[0, :HEAD_DIM, at], preferred_element_type=FLOAT
        ) * scale
        scores = jnp.where(seen(first[0, :, at][:1], low, high, i * share), scores, NEG)
        probs = jnp.exp(scores - log_total[0, 0, :1, at])
        d_probs = jnp.dot(value[low:high, :], turned, preferred_element_type=FLOAT)
        centre = jnp.sum(probs * d_probs, axis=0, keepdims=True)
        d_scores = (probs * (d_probs - centre)).astype(HALF)
        d_value[low:high, :] += jnp.dot(probs.astype(HALF), turned.T, preferred_element_type=FLOAT)
        d_key[low:high, :] += jnp.dot(
            d_scores, query[i * share : (i + 1) * share, :], preferred_element_type=FLOAT
        )
        d_query = scale * jnp.dot(
            kept[0, HEAD_DIM : 2 * HEAD_DIM, low:high], d_scores, preferred_element_type=FLOAT
        )
        put(0, i, d_query[:half, :], d_query[half:, :])
    for i in range(blocks):
        rows = pl.ds(i * share, share)
        turned = scale * d_key[rows, :].T
        put(1, i, turned[:half, :], turned[half:, :])
        d_qkv[2 * HEAD_DIM :, spot(i)] = d_value[rows, :].T.astype(HALF)


def attend_back(base, kept, log_total, slope, cosine, sine, first, before):
    seqs, length = first.shape[0], first.shape[2]
    tokens = slope.shape[1]
    heads = slope.shape[0] // HEAD_DIM
    return pl.pallas_call(
        functools.partial(attend_back_kernel, len(before)),
        grid=(heads, seqs),
        in_specs=[
            pl.BlockSpec(memory_space=pltpu.SMEM),
            pl.BlockSpec((1, 3 * HEAD_DIM, length), lambda h, j: (j, h, 0)),
            pl.BlockSpec((1, 1, 8, length), lambda h, j: (j, h, 0, 0)),
            pl.BlockSpec((HEAD_DIM, tokens), lambda h, j: (h, 0)),
            pl.BlockSpec(cosine.shape, lambda h, j: (0, 0)),
            pl.BlockSpec(sine.shape, lambda h, j: (0, 0)),
            pl.BlockSpec((1, 8, length), lambda h, j: (j, 0, 0)),
        ]
        + [pl.BlockSpec(memory_space=pl.ANY)] * len(before),
        out_specs=pl.BlockSpec((3 * HEAD_DIM, tokens), lambda h, j: (h, 0)),
        out_shape=jax.ShapeDtypeStruct((heads * 3 * HEAD_DIM, tokens), HALF),
        scratch_shapes=[pltpu.VMEM((length, HEAD_DIM), FLOAT)] * 2,
        compiler_params=pltpu.CompilerParams(vmem_limit_bytes=VMEM_LIMIT),
        cost_estimate=SMALL,
        name="attend_back",
    )(base, kept, log_total, slope, cosine, sine, first, *before)


def near_and_far(own, rank):
    return (own, rank ^ 1), (own, rank ^ 2)


def remote(source, target, send, recv, n, peer):
    return pltpu.make_async_remote_copy(
        src_ref=source,
        dst_ref=target,
        send_sem=send.at[n],
        recv_sem=recv.at[n],
        device_id=peer,
        device_id_type=MESH,
    )


class Boundary:
    COUNT = 6

    def __init__(self, own, rank, send, recv, parts, rows):
        self.near, self.far = near_and_far(own, rank)
        self.send, self.recv, self.parts = send, recv, parts
        self.rows = [pl.ds(h * rows, rows) for h in range(parts)]
        self.copies = []

    def copy(self, source, target, n, h, peer):
        made = remote(source, target, self.send, self.recv, n * self.parts + h, peer)
        made.start()
        self.copies.append(made)
        return made

    def sums(self, make, partial, beside, away, come):
        later, crossing = {}, []

        def part(p, h):
            partial[p, self.rows[h], :] = make(p, h).astype(HALF)

        def leave(p, h):
            part(2 + p, h)
            at = self.rows[h]
            later[p, h] = self.copy(partial.at[2 + p, at], beside.at[p, at], p, h, self.near)

        def pair(p, h):
            at = self.rows[h]
            later[p, h].wait_recv()
            return partial[p, at, :].astype(FLOAT) + beside[p, at, :].astype(FLOAT)

        for h, at in enumerate(self.rows):
            leave(1, h)
            part(1, h)
            away[at, :] = pair(1, h).astype(HALF)
            crossing.append(self.copy(away.at[at], come.at[at], 2, h, self.far))
        for h in range(self.parts):
            leave(0, h)
        for h in range(self.parts):
            part(0, h)
        for h, at in enumerate(self.rows):
            total = pair(0, h)
            crossing[h].wait_recv()
            yield h, at, total + come[at, :].astype(FLOAT)

    def give(self, full, h):
        at = self.rows[h]
        self.crossed = getattr(self, "crossed", [])
        self.crossed.append(self.copy(full.at[0, at], full.at[1, at], 3, h, self.far))
        self.beside = getattr(self, "beside", [])
        self.beside.append(self.copy(full.at[0, at], full.at[2, at], 4, h, self.near))

    def pass_on(self, full):
        arrived = []
        for h, at in enumerate(self.rows):
            self.crossed[h].wait_recv()
            arrived.append(self.copy(full.at[1, at], full.at[3, at], 5, h, self.near))
        for copy in self.beside + arrived:
            copy.wait_recv()

    def end(self):
        for copy in self.copies:
            copy.wait_send()


def turned_product(left, right):
    return lax.dot_general(left, right, (((0,), (1,)), ((), ())), preferred_element_type=FLOAT)


def columns_of(array, p, h, parts):
    step = array.shape[1] // (4 * parts)
    return array[:, (p * parts + h) * step : (p * parts + h + 1) * step]


def rows_of(index, width):
    return pl.ds(pl.multiple_of(index * width, width), width)


def forward_kernel(parts, gathers, attended, both, stream, gain, *refs):
    blocks, refs = refs[:gathers], refs[gathers:]
    if gathers:
        out, full, feed_w, weight, partial, beside, away, come, send, recv = refs
    else:
        out, full, weight, partial, beside, away, come, send, recv = refs
    own, rank = lax.axis_index("dp"), lax.axis_index("tensor")
    near, far = near_and_far(own, rank)
    others = {k: (own ^ k, rank) for k in (1, 2, 6)} if gathers else {}
    greet([near, far, *others.values()])
    edge = Boundary(own, rank, send, recv, parts, stream.shape[0] // parts)
    moved = {}

    def move(source, k, n, peer):
        copy = remote(source, feed_w.at[rows_of(own ^ k, width)], send, recv, n, peer)
        copy.start()
        edge.copies.append(copy)
        return copy

    if gathers:
        mine, four = blocks
        width, base = mine.shape[0], Boundary.COUNT * parts
        for n, k in enumerate((2, 6)):
            moved[k] = move(mine, 0, base + n, others[k])
        moved[1] = move(mine, 0, base + 2, others[1])
        moved[5] = move(four, 4, base + 3, others[1])
        feed_w[rows_of(own, width), :] = mine[...]
        feed_w[rows_of(own ^ 4, width), :] = four[...]
    weight[...] = both[:, both.shape[1] - weight.shape[1] :]

    def make(p, h):
        return turned_product(columns_of(attended, p, h, parts), weight[...])

    for h, at, total in edge.sums(make, partial, beside, away, come):
        total = stream[at, :] + total
        out[at, :] = total
        full[0, at, :] = normed(total, gain[1:2, :]).astype(HALF)
        edge.give(full, h)
    if gathers:
        for n, k in enumerate((2, 6)):
            moved[k].wait_recv()
            moved[k + 1] = move(feed_w.at[rows_of(own ^ k, width)], k, base + 4 + n, others[1])
    edge.pass_on(full)
    for k in (1, 5, 3, 7) if gathers else ():
        moved[k].wait_recv()
    edge.end()


def forward_boundary(attended, both, stream, gain, blocks):
    rows, depth = stream.shape
    parts = 2
    vmem = pl.BlockSpec(memory_space=pltpu.VMEM)
    scratch = exchange_scratch(rows, depth, parts)[:4]
    semaphores = Boundary.COUNT * parts + 6
    results = pl.pallas_call(
        functools.partial(forward_kernel, parts, len(blocks)),
        in_specs=[vmem] * (4 + len(blocks)),
        out_specs=[vmem] * (3 if blocks else 2),
        out_shape=[
            jax.ShapeDtypeStruct((rows, depth), FLOAT),
            jax.ShapeDtypeStruct((4, rows, depth), HALF),
        ]
        + [jax.ShapeDtypeStruct((8 * b.shape[0], b.shape[1]), HALF) for b in blocks[:1]],
        scratch_shapes=[pltpu.VMEM((depth, attended.shape[0]), HALF)]
        + scratch
        + [pltpu.SemaphoreType.DMA((semaphores,))] * 2,
        compiler_params=pltpu.CompilerParams(
            collective_id=3, has_side_effects=True, vmem_limit_bytes=VMEM_LIMIT
        ),
        cost_estimate=SMALL,
        name="forward_boundary",
    )(attended, both, stream, gain, *blocks)
    return (results[0], results[1].reshape(4 * rows, depth), *results[2:])


def normed_slope(grad, values, gain):
    root = lax.rsqrt(jnp.mean(values * values, axis=-1, keepdims=True) + EPS)
    unit = values * root
    inner = grad * gain
    middle = jnp.mean(inner * unit, axis=-1, keepdims=True)
    return root * (inner - unit * middle), jnp.sum(grad * unit, axis=0, keepdims=True)


def wide_forward_kernel(
    norm, weight, stream, gain, out, full, partial, beside, away, come, send, recv
):
    own, rank = lax.axis_index("dp"), lax.axis_index("tensor")
    near, far = near_and_far(own, rank)
    other = (own ^ 1, rank)
    greet([near, far, other])
    parts = 2
    edge = Boundary(own, rank, send, recv, parts, stream.shape[0] // parts)
    crossed, moved, last = [], [], []
    ffn = weight.shape[1] // 3

    def make(p, h):
        both = jnp.dot(
            norm[p, edge.rows[h], :], weight[:, : 2 * ffn], preferred_element_type=FLOAT
        )
        gate, up = both[:, :ffn], both[:, ffn:]
        hidden = (gate * (1.0 / (1.0 + jnp.exp(-gate))) * up).astype(HALF)
        return across(hidden, weight[:, 2 * ffn :])

    for h, at, total in edge.sums(make, partial, beside, away, come):
        total = stream[at, :] + total
        out[at, :] = total
        full[0, 0, at, :] = normed(total, gain[2:3, :]).astype(HALF)
        mine = full.at[0, 0, at]
        crossed.append(edge.copy(mine, full.at[0, 1, at], 3, h, far))
        moved.append(edge.copy(mine, full.at[1, 0, at], 4, h, other))
        last.append(edge.copy(mine, full.at[0, 2, at], 5, h, near))
    early, late = edge.rows
    crossed[0].wait_recv()
    one = edge.copy(full.at[0, 1, early], full.at[1, 1, early], 6, 0, other)
    last.append(edge.copy(full.at[0, 1, early], full.at[0, 3, early], 7, 0, near))
    moved[0].wait_recv()
    last.append(edge.copy(full.at[1, 0, early], full.at[1, 2, early], 8, 0, near))
    moved[1].wait_recv()
    two = edge.copy(full.at[1, 0, late], full.at[1, 1, late], 6, 1, far)
    last.append(edge.copy(full.at[1, 0, late], full.at[1, 2, late], 8, 1, near))
    crossed[1].wait_recv()
    last.append(edge.copy(full.at[0, 1, late], full.at[0, 3, late], 7, 1, near))
    one.wait_recv()
    last.append(edge.copy(full.at[1, 1, early], full.at[1, 3, early], 9, 0, near))
    two.wait_recv()
    last.append(edge.copy(full.at[1, 1, late], full.at[1, 3, late], 9, 1, near))
    for copy in last:
        copy.wait_recv()
    edge.end()


def wide_forward(norm, weight, stream, gain):
    rows, depth = stream.shape
    vmem = pl.BlockSpec(memory_space=pltpu.VMEM)
    out, full = pl.pallas_call(
        wide_forward_kernel,
        in_specs=[vmem] * 4,
        out_specs=[vmem] * 2,
        out_shape=[
            jax.ShapeDtypeStruct((rows, depth), FLOAT),
            jax.ShapeDtypeStruct((2, 4, rows, depth), HALF),
        ],
        scratch_shapes=exchange_scratch(rows, depth, 2)[:4] + [pltpu.SemaphoreType.DMA((20,))] * 2,
        compiler_params=pltpu.CompilerParams(
            collective_id=9, has_side_effects=True, vmem_limit_bytes=VMEM_LIMIT
        ),
        cost_estimate=SMALL,
        name="wide_forward",
    )(norm.reshape(4, rows, depth), weight, stream, gain)
    return out, full.reshape(8 * rows, depth)


def wide_backward_kernel(partial, stream, gain, out, g_gain, full, beside, leave, come, send, recv):
    own, rank = lax.axis_index("dp"), lax.axis_index("tensor")
    near, far = near_and_far(own, rank)
    other = (own ^ 1, rank)
    greet([near, far, other])
    parts = 2
    edge = Boundary(own, rank, send, recv, parts, stream.shape[0] // parts)
    early, late = edge.rows
    first = {}
    for n, (y, p) in enumerate(((1, 1), (1, 0), (0, 1), (0, 0))):
        for h, at in enumerate(edge.rows):
            first[y, p, h] = edge.copy(
                partial.at[y, 2 + p, at], beside.at[y, p, at], 5 + n, h, near
            )

    def pair(y, p, h):
        at = edge.rows[h]
        first[y, p, h].wait_recv()
        return partial[y, p, at, :].astype(FLOAT) + beside[y, p, at, :].astype(FLOAT)

    leave[1, 1, early, :] = pair(1, 1, 0).astype(HALF)
    by_other = edge.copy(leave.at[1, 1, early], come.at[1, 1, early], 9, 0, other)
    leave[1, 1, late, :] = pair(1, 1, 1).astype(HALF)
    by_far = edge.copy(leave.at[1, 1, late], come.at[1, 1, late], 9, 1, far)
    leave[1, 0, early, :] = pair(1, 0, 0).astype(HALF)
    other_early = edge.copy(leave.at[1, 0, early], come.at[1, 0, early], 0, 0, other)
    leave[0, 1, late, :] = pair(0, 1, 1).astype(HALF)
    far_late = edge.copy(leave.at[0, 1, late], come.at[0, 1, late], 1, 1, far)
    far_early_sum, other_late_sum = pair(0, 1, 0), pair(1, 0, 1)
    by_other.wait_recv()
    leave[0, 1, early, :] = (far_early_sum + come[1, 1, early, :].astype(FLOAT)).astype(HALF)
    far_early = edge.copy(leave.at[0, 1, early], come.at[0, 1, early], 1, 0, far)
    by_far.wait_recv()
    leave[1, 0, late, :] = (other_late_sum + come[1, 1, late, :].astype(FLOAT)).astype(HALF)
    other_late = edge.copy(leave.at[1, 0, late], come.at[1, 0, late], 0, 1, other)
    g_gain[...] = jnp.zeros_like(g_gain)
    for h, waits in ((0, (other_early, far_early)), (1, (far_late, other_late))):
        at = edge.rows[h]
        total = pair(0, 0, h)
        for copy in waits:
            copy.wait_recv()
        total = total + come[1, 0, at, :].astype(FLOAT) + come[0, 1, at, :].astype(FLOAT)
        slope, by_gain = normed_slope(total, stream[at, :], gain[2:3, :])
        g_gain[:1, :] = g_gain[:1, :] + by_gain
        out[at, :] = slope
        full[0, at, :] = slope.astype(HALF)
        edge.crossed = getattr(edge, "crossed", [])
        edge.crossed.append(edge.copy(full.at[0, at], full.at[1, at], 2, h, far))
        edge.beside = getattr(edge, "beside", [])
        edge.beside.append(edge.copy(full.at[0, at], full.at[2, at], 3, h, near))
    arrived = []
    for h, at in enumerate(edge.rows):
        edge.crossed[h].wait_recv()
        arrived.append(edge.copy(full.at[1, at], full.at[3, at], 4, h, near))
    for copy in edge.beside + arrived:
        copy.wait_recv()
    edge.end()


def wide_backward(partial, stream, gain):
    rows, depth = stream.shape
    vmem = pl.BlockSpec(memory_space=pltpu.VMEM)
    out, g_gain, full = pl.pallas_call(
        wide_backward_kernel,
        in_specs=[vmem] * 3,
        out_specs=[vmem] * 3,
        out_shape=[
            jax.ShapeDtypeStruct((rows, depth), FLOAT),
            jax.ShapeDtypeStruct((8, depth), FLOAT),
            jax.ShapeDtypeStruct((4, rows, depth), HALF),
        ],
        scratch_shapes=[pltpu.VMEM((2, 2, rows, depth), HALF)] * 3
        + [pltpu.SemaphoreType.DMA((20,))] * 2,
        compiler_params=pltpu.CompilerParams(
            collective_id=4, has_side_effects=True, vmem_limit_bytes=VMEM_LIMIT
        ),
        cost_estimate=SMALL,
        name="wide_backward",
    )(partial.reshape(2, 4, rows, depth), stream, gain)
    return out, g_gain, full.reshape(4 * rows, depth)


def exchange_scratch(rows, depth, parts):
    return [
        pltpu.VMEM((4, rows, depth), HALF),
        pltpu.VMEM((2, rows, depth), HALF),
        pltpu.VMEM((rows, depth), HALF),
        pltpu.VMEM((rows, depth), HALF),
        pltpu.SemaphoreType.DMA((Boundary.COUNT * parts,)),
        pltpu.SemaphoreType.DMA((Boundary.COUNT * parts,)),
    ]


def backward_kernel(
    parts, norm, later, weight, stream, gain, prior, out, g_gain, full, grad, partial, beside, away, come, kept, send, recv
):
    own, rank = lax.axis_index("dp"), lax.axis_index("tensor")
    greet(list(near_and_far(own, rank)))
    edge = Boundary(own, rank, send, recv, parts, stream.shape[0] // parts)
    ffn = weight.shape[1] // 3

    def make(p, h):
        at = edge.rows[h]
        both = jnp.dot(norm[p, at, :], weight[:, : 2 * ffn], preferred_element_type=FLOAT)
        d_hidden = jnp.dot(later[p, at, :], weight[:, 2 * ffn :], preferred_element_type=FLOAT)
        gate, up = both[:, :ffn], both[:, ffn:]
        open_part = 1.0 / (1.0 + jnp.exp(-gate))
        passed = gate * open_part
        d_gate = (d_hidden * up * (open_part * (1.0 + gate * (1.0 - open_part)))).astype(HALF)
        d_up = (d_hidden * passed).astype(HALF)
        kept[p, at, :ffn] = d_gate
        kept[p, at, ffn : 2 * ffn] = d_up
        kept[p, at, 2 * ffn :] = (passed * up).astype(HALF)
        return across(d_gate, weight[:, :ffn]) + across(d_up, weight[:, ffn : 2 * ffn])

    g_gain[...] = jnp.zeros_like(g_gain)
    for h, at, total in edge.sums(make, partial, beside, away, come):
        slope, by_gain = normed_slope(total, stream[at, :], gain[1:2, :])
        slope = slope + prior[at, :]
        g_gain[:1, :] = g_gain[:1, :] + by_gain
        out[at, :] = slope
        full[0, at, :] = slope.astype(HALF)
        edge.give(full, h)
    for left, low, high in ((norm, 0, 2 * ffn), (later, 2 * ffn, 3 * ffn)):
        turned = [left[p].T for p in range(4)]
        for c in range(low, high, CHUNK):
            total = jnp.dot(turned[0], kept[0, :, c : c + CHUNK], preferred_element_type=FLOAT)
            for p in (1, 2, 3):
                total = total + jnp.dot(
                    turned[p], kept[p, :, c : c + CHUNK], preferred_element_type=FLOAT
                )
            grad[:, c : c + CHUNK] = total.astype(HALF)
    edge.pass_on(full)
    edge.end()


def backward_boundary(norm, later, weight, stream, gain, prior):
    rows, depth = stream.shape
    parts = 2
    vmem = pl.BlockSpec(memory_space=pltpu.VMEM)
    scratch = exchange_scratch(rows, depth, parts)
    out, g_gain, full, grad = pl.pallas_call(
        functools.partial(backward_kernel, parts),
        in_specs=[vmem] * 6,
        out_specs=[vmem] * 4,
        out_shape=[
            jax.ShapeDtypeStruct((rows, depth), FLOAT),
            jax.ShapeDtypeStruct((8, depth), FLOAT),
            jax.ShapeDtypeStruct((4, rows, depth), HALF),
            jax.ShapeDtypeStruct(weight.shape, HALF),
        ],
        scratch_shapes=scratch[:4] + [pltpu.VMEM((4, rows, weight.shape[1]), HALF)] + scratch[4:],
        compiler_params=pltpu.CompilerParams(
            collective_id=5, has_side_effects=True, vmem_limit_bytes=VMEM_LIMIT
        ),
        cost_estimate=SMALL,
        name="backward_boundary",
    )(norm.reshape(4, rows, depth), later.reshape(4, rows, depth), weight, stream, gain, prior)
    return out, g_gain, full.reshape(4 * rows, depth), grad


def start_kernel(
    ids, turned, gain, block, feed, stays, leaves, stream, full, weights, four, pair, *refs
):
    table, corner, rows, out, near, cross, come, send, recv, local = refs
    own, rank = lax.axis_index("dp"), lax.axis_index("tensor")
    beside, across = near_and_far(own, rank)
    far = [(own ^ k, rank) for k in range(1, 8)]
    greet([beside, across] + far)
    width, vocab = turned.shape
    count = rows.shape[0]
    copies, beside_of, across_of, far_of = [], {}, {}, {}

    def begin(source, target, n, peer):
        copy = remote(source, target, send, recv, n, peer)
        copy.start()
        copies.append(copy)
        return copy

    def place(k):
        return pl.ds(pl.multiple_of((own ^ k) * width, width), width)

    weights_of = {}
    for k in (1, 2, 4, 6):
        weights_of[k] = begin(block, weights.at[place(0)], 35 + k, far[k - 1])
    weights[place(0), :] = block[...]
    bit = own % 2
    line = pl.ds(pl.multiple_of(bit * width, width), width)
    aside = begin(leaves, pair.at[line], 43, far[0])
    own_line = pltpu.make_async_copy(stays, pair.at[line], local)
    own_line.start()
    corner[...] = jnp.zeros_like(corner)
    for v in range(0, vocab, LANES):
        some = min(LANES, vocab - v)
        corner[:width, :some] = turned[:, v : v + some].astype(HALF).astype(FLOAT)
        if some < LANES:
            corner[:width, some:] = jnp.zeros((width, LANES - some), FLOAT)
        table[v : v + LANES, :] = corner[...].T
    if vocab % LANES == 0:
        table[vocab:, :] = jnp.zeros((LANES, LANES), FLOAT)

    def fetch(place):
        def body(i, carry):
            for u in range(16):
                r = i * 16 + u
                rows[pl.ds(r, 1), :] = table[pl.ds(ids[place * count + r], 1), :]
            return carry

        lax.fori_loop(0, count // 16, body, 0)

    for p in (3, 2):
        for k in range(8):
            fetch(p * 8 + k)
            out[p, k] = rows[:, :width].astype(HALF)
            beside_of[p - 2, k] = begin(out.at[p, k], near.at[p - 2, k], (p - 2) * 8 + k, beside)
    for k in (2, 4, 6):
        weights_of[k].wait_recv()
        weights_of[k + 1] = begin(weights.at[place(k)], weights.at[place(k)], 36 + k, far[0])
    order = (7, 6, 5, 4, 3, 2, 1, 0)
    for k in order:
        fetch(8 + k)
        beside_of[1, k].wait_recv()
        total = rows[:, :width] + near[1, k].astype(FLOAT)
        out[1, k] = total.astype(HALF)
        across_of[k] = begin(out.at[1, k], cross.at[k], 16 + k, across)
    for k in order:
        fetch(k)
        beside_of[0, k].wait_recv()
        total = rows[:, :width] + near[0, k].astype(FLOAT)
        across_of[k].wait_recv()
        out[0, k] = (total + cross[k].astype(FLOAT)).astype(HALF)
        if k:
            far_of[k] = begin(out.at[0, k], come.at[k], 24 + k, far[k - 1])
    fourth = begin(feed, four, 44, far[3])
    come[0] = out[0, 0]
    for k in order[:-1]:
        far_of[k].wait_recv()
    for b in range(8):
        stream[:, b * width : (b + 1) * width] = come[own ^ b].astype(FLOAT)
    full[0] = normed(stream[...], gain[0:1, :]).astype(HALF)
    one = begin(full.at[0], full.at[1], 32, across)
    two = begin(full.at[0], full.at[2], 33, beside)
    one.wait_recv()
    three = begin(full.at[1], full.at[3], 34, beside)
    two.wait_recv()
    three.wait_recv()
    for k in (1, 3, 5, 7):
        weights_of[k].wait_recv()
    aside.wait_recv()
    fourth.wait_recv()
    own_line.wait()
    for copy in copies:
        copy.wait_send()


def start_rows(ids, turned, gain, block, feed, stays, leaves):
    width, vocab = turned.shape
    rows = ids.shape[0] // 32
    padded = (vocab // LANES + 1) * LANES
    vmem = pl.BlockSpec(memory_space=pltpu.VMEM)
    whole = pl.BlockSpec(memory_space=pl.ANY)
    stream, full, weights, four, pair = pl.pallas_call(
        start_kernel,
        in_specs=[pl.BlockSpec(memory_space=pltpu.SMEM), vmem, vmem, vmem, vmem, whole, whole],
        out_specs=[vmem] * 4 + [whole],
        out_shape=[
            jax.ShapeDtypeStruct((rows, 8 * width), FLOAT),
            jax.ShapeDtypeStruct((4, rows, 8 * width), HALF),
            jax.ShapeDtypeStruct((8 * width, block.shape[1]), HALF),
            jax.ShapeDtypeStruct(feed.shape, HALF),
            jax.ShapeDtypeStruct((2 * width, stays.shape[1]), HALF),
        ],
        scratch_shapes=[
            pltpu.VMEM((padded, LANES), FLOAT),
            pltpu.VMEM((LANES, LANES), FLOAT),
            pltpu.VMEM((rows, LANES), FLOAT),
            pltpu.VMEM((4, 8, rows, width), HALF),
            pltpu.VMEM((2, 8, rows, width), HALF),
            pltpu.VMEM((8, rows, width), HALF),
            pltpu.VMEM((8, rows, width), HALF),
            pltpu.SemaphoreType.DMA((45,)),
            pltpu.SemaphoreType.DMA((45,)),
            pltpu.SemaphoreType.DMA,
        ],
        compiler_params=pltpu.CompilerParams(
            collective_id=6, has_side_effects=True, vmem_limit_bytes=VMEM_LIMIT
        ),
        cost_estimate=SMALL,
        name="start_rows",
    )(ids, turned, gain, block, feed, stays, leaves)
    return stream, full.reshape(4 * rows, 8 * width), weights, four, pair


def end_kernel(parts, waits, d_qkv, weight, stream, gain, prior, gain_one, gain_two, apart, *refs):
    rows, g_gain, arrived, partial, beside, away, come, leave, mine, summed, first, second, send, recv = refs[waits:]
    own, rank = lax.axis_index("dp"), lax.axis_index("tensor")
    near, across = near_and_far(own, rank)
    far = [(own ^ k, rank) for k in range(1, 8)]
    greet([near, across, (own, rank ^ 3)] + far)
    edge = Boundary(own, rank, send, recv, parts, stream.shape[0] // parts)
    aside = remote(apart, arrived, send, recv, Boundary.COUNT * parts, far[0])
    aside.start()
    edge.copies.append(aside)
    width = rows.shape[3]
    gain_zero = jnp.zeros_like(gain[0:1, :])
    mine[...] = jnp.zeros_like(mine)

    def make(p, h):
        return turned_product(columns_of(d_qkv, p, h, parts), weight[:, : d_qkv.shape[0]])

    for h, at, total in edge.sums(make, partial, beside, away, come):
        slope, by_gain = normed_slope(total, stream[at, :], gain[0:1, :])
        slope = slope + prior[at, :]
        gain_zero = gain_zero + by_gain
        for b in range(8):
            leave[b, at, :] = slope[:, b * width : (b + 1) * width].astype(HALF)
    base = Boundary.COUNT * parts
    far_of, last = {}, []

    def begin(source, target, n, peer):
        copy = remote(source, target, send, recv, base + n, peer)
        copy.start()
        edge.copies.append(copy)
        return copy

    order = (7, 6, 5, 4, 3, 2, 1)
    for k in order:
        far_of[k] = begin(leave.at[own ^ k], rows.at[0, k], k, far[k - 1])
    rows[0, 0] = leave[own]
    for b in range(8):
        for n, line in enumerate((gain_zero, gain_one[0:1, :], gain_two[0:1, :])):
            mine[own ^ b, n : n + 1, :width] = line[:, b * width : (b + 1) * width]
    gains_of = [
        begin(mine, first.at[n - 1], 31 + n, (own, rank ^ n)) for n in (1, 2, 3)
    ]
    crossed = {}
    for k in (0, 1, 7, 6, 5, 4, 3, 2):
        if k:
            far_of[k].wait_recv()
        crossed[k] = begin(rows.at[0, k], rows.at[1, k], 8 + k, across)
        last.append(begin(rows.at[0, k], rows.at[2, k], 16 + k, near))
    for copy in gains_of:
        copy.wait_recv()
    summed[...] = (mine[...] + first[0]) + (first[1] + first[2])
    gains_of = [begin(summed.at[k], second.at[k], 34 + k, far[k - 1]) for k in range(1, 8)]
    for k in (0, 1, 7, 6, 5, 4, 3, 2):
        crossed[k].wait_recv()
        last.append(begin(rows.at[1, k], rows.at[3, k], 24 + k, near))
    for copy in last + gains_of:
        copy.wait_recv()
    second[0] = summed[0]
    pairs = [second[k] + second[k + 1] for k in (0, 2, 4, 6)]
    g_gain[...] = (pairs[0] + pairs[1]) + (pairs[2] + pairs[3])
    aside.wait_recv()
    edge.end()


def end_rows(d_qkv, weight, stream, gain, prior, gain_one, gain_two, apart, width, before):
    rows, depth = stream.shape
    parts = 2
    vmem = pl.BlockSpec(memory_space=pltpu.VMEM)
    semaphores = Boundary.COUNT * parts + 42
    whole = pl.BlockSpec(memory_space=pl.ANY)
    out, g_gain, arrived = pl.pallas_call(
        functools.partial(end_kernel, parts, len(before)),
        in_specs=[vmem] * 7 + [whole] * (1 + len(before)),
        out_specs=[vmem] * 2 + [whole],
        out_shape=[
            jax.ShapeDtypeStruct((4, 8, rows, width), HALF),
            jax.ShapeDtypeStruct((8, LANES), FLOAT),
            jax.ShapeDtypeStruct(apart.shape, HALF),
        ],
        scratch_shapes=exchange_scratch(rows, depth, parts)[:4]
        + [
            pltpu.VMEM((8, rows, width), HALF),
            pltpu.VMEM((8, 8, LANES), FLOAT),
            pltpu.VMEM((8, 8, LANES), FLOAT),
            pltpu.VMEM((3, 8, 8, LANES), FLOAT),
            pltpu.VMEM((8, 8, LANES), FLOAT),
            pltpu.SemaphoreType.DMA((semaphores,)),
            pltpu.SemaphoreType.DMA((semaphores,)),
        ],
        compiler_params=pltpu.CompilerParams(
            collective_id=7, has_side_effects=True, vmem_limit_bytes=VMEM_LIMIT
        ),
        cost_estimate=SMALL,
        name="end_rows",
    )(d_qkv, weight, stream, gain, prior, gain_one, gain_two, apart, *before)
    return out.reshape(-1, width), g_gain[:3, :width], arrived


def merge_kernel(scan, extra, joined, mine, every, send, recv):
    own, rank = lax.axis_index("dp"), lax.axis_index("tensor")
    turns = [(a, b) for a in (0, 1) for b in range(4)][1:]
    peers = [(own ^ a, rank ^ b) for a, b in turns]
    greet(peers)
    tokens = scan.shape[1] // 2
    share = tokens // 4
    mine[...] = jnp.zeros_like(mine)
    mine[0:3, :] = scan[0:3, :tokens]
    mine[3:6, :] = scan[0:3, tokens:]
    copies = []
    for n, peer in enumerate(peers):
        copies.append(remote(mine, every.at[n], send, recv, n, peer))
        copies[-1].start()
    joined[...] = jnp.zeros_like(joined)
    joined[2:4, :] = extra[:2, :]
    for copy in copies:
        copy.wait()
    for y in (0, 1):
        for p in range(4):
            terms = {(0, 0): mine[3 * y : 3 * y + 3, p * share : (p + 1) * share]}
            for n, (a, b) in enumerate(turns):
                q = TURN.index(TURN[p] ^ b)
                terms[a, b] = every[n, 3 * (y ^ a) : 3 * (y ^ a) + 3, q * share : (q + 1) * share]
            peak = functools.reduce(jnp.maximum, [term[0:1] for term in terms.values()])
            sums, hits = [], []
            for a in (0, 1):
                for b in (0, 2):
                    pair = (terms[a, b], terms[a, b ^ 1])
                    sums.append(sum(term[1:2] * jnp.exp(term[0:1] - peak) for term in pair))
                    hits.append(pair[0][2:3] + pair[1][2:3])
            at = pl.ds(y * tokens + p * share, share)
            joined[0:1, at] = peak + jnp.log((sums[0] + sums[1]) + (sums[2] + sums[3]))
            joined[1:2, at] = (hits[0] + hits[1]) + (hits[2] + hits[3])


def merge_scans(scan, extra):
    vmem = pl.BlockSpec(memory_space=pltpu.VMEM)
    shape = (8, scan.shape[1] // 2)
    return pl.pallas_call(
        merge_kernel,
        in_specs=[vmem] * 2,
        out_specs=vmem,
        out_shape=jax.ShapeDtypeStruct(scan.shape, FLOAT),
        scratch_shapes=[
            pltpu.VMEM(shape, FLOAT),
            pltpu.VMEM((7, *shape), FLOAT),
            pltpu.SemaphoreType.DMA((7,)),
            pltpu.SemaphoreType.DMA((7,)),
        ],
        compiler_params=pltpu.CompilerParams(collective_id=8, has_side_effects=True),
        name="merge_scans",
    )(scan, extra)


def across(left, right):
    return lax.dot_general(left, right, (((1,), (1,)), ((), ())), preferred_element_type=FLOAT)


def product(left, right, over_left, over_right):
    return lax.dot_general(
        left, right, (((over_left,), (over_right,)), ((), ())), preferred_element_type=FLOAT
    )


def adam(weight, grad, first, second, rate, decay):
    first = BETA_ONE * first + (1.0 - BETA_ONE) * grad
    second = BETA_TWO * second + (1.0 - BETA_TWO) * grad * grad
    first_hat = first / (1.0 - BETA_ONE**STEP)
    second_hat = second / (1.0 - BETA_TWO**STEP)
    weight = weight - rate * (first_hat / (jnp.sqrt(second_hat) + ADAM_EPS) + decay * weight)
    return (weight, first, second, weight.astype(HALF))


def update_kernel(counts, factor, *refs):
    arrays = len(counts)
    inputs, outputs = refs[: 3 * arrays + sum(counts)], refs[3 * arrays + sum(counts) :]
    grads = inputs[3 * arrays :]
    for n in range(arrays):
        weight, first, second = inputs[3 * n : 3 * n + 3]
        low = 0
        for grad in grads[: counts[n]]:
            high = low + grad.shape[-1]
            at = (Ellipsis, slice(low, high))
            results = adam(
                weight[at], grad[...].astype(FLOAT) * factor[0], first[at], second[at], LR, DECAY
            )
            for out, result in zip(outputs[4 * n : 4 * n + 4], results):
                out[at] = result
            low = high
        grads = grads[counts[n] :]


def update(arrays, factor):
    rows = arrays[0][0].shape[0]
    steps = rows // 16 if rows % 16 == 0 else 1

    def block(array):
        zeros = (0,) * (array.ndim - 1)
        return pl.BlockSpec((array.shape[0] // steps, *array.shape[1:]), lambda i: (i, *zeros))

    inputs = [array for entry in arrays for array in entry[:3]]
    grads = [grad for entry in arrays for grad in entry[3]]
    outs = [
        jax.ShapeDtypeStruct(entry[0].shape, kind)
        for entry in arrays
        for kind in (FLOAT, FLOAT, FLOAT, HALF)
    ]
    results = pl.pallas_call(
        functools.partial(update_kernel, tuple(len(entry[3]) for entry in arrays)),
        grid=(steps,),
        in_specs=[pl.BlockSpec(memory_space=pltpu.SMEM)] + [block(a) for a in inputs + grads],
        out_specs=[block(a) for a in outs],
        out_shape=outs,
        compiler_params=pltpu.CompilerParams(vmem_limit_bytes=VMEM_LIMIT),
        cost_estimate=SMALL,
        name="update",
    )(factor.reshape(1), *inputs, *grads)
    return [results[4 * n : 4 * n + 4] for n in range(len(arrays))]


def shards(
    token_ids,
    targets,
    segments,
    completion,
    micro_order,
    *state,
):
    weights, means, squares_in = state[:7], state[7:14], state[14:21]
    embedding, attn_in, attn_out, ffn_in, ffn_out, head_table, norm_gains = weights
    group = lax.axis_size("dp")
    parts = lax.axis_size("tensor")
    own, rank = lax.axis_index("dp"), lax.axis_index("tensor")
    vocab, width = embedding.shape
    start = rank * vocab
    seqs, length = token_ids.shape
    micro = micro_order.shape[1]
    share = length // parts
    turn = jnp.array(TURN, jnp.int32)
    dp_order = own ^ jnp.arange(group, dtype=jnp.int32)
    tensor_order = rank ^ turn
    tensor_order_natural = rank ^ jnp.arange(parts, dtype=jnp.int32)
    ffn = ffn_out.shape[0]
    qkv_width = attn_in.shape[1]

    attn_block = jnp.concatenate([attn_in, attn_out.T], axis=1).astype(HALF)
    ffn_block = jnp.concatenate([ffn_in.reshape(width, -1), ffn_out.T], axis=1).astype(HALF)
    bit = own % 2
    entries = vocab // 2
    low_half, high_half = head_table[:, :entries], head_table[:, entries:]
    stays = jnp.where(bit == 0, low_half, high_half).astype(HALF)
    leaves = jnp.where(bit == 0, high_half, low_half).astype(HALF)
    lines = [[i for i in range(group) if i % 2 == odd] for odd in (0, 1)]

    picked_rows = micro_order[0]
    takes_seq = picked_rows[:, None] == jnp.arange(seqs)[None, :]
    local_counts = jnp.sum(jnp.where(takes_seq, jnp.sum(completion, axis=1)[None, :], 0), axis=1)
    id_rows = seqs * length // LANES
    packed = jnp.concatenate(
        [
            token_ids.reshape(-1),
            targets.reshape(-1),
            completion.reshape(-1),
            jnp.pad(jnp.concatenate([local_counts, picked_rows]), (0, 8 * LANES - 2 * micro)),
        ]
    ).reshape(3 * id_rows + 8, LANES)
    gains = jnp.pad(norm_gains.astype(HALF).astype(FLOAT), ((0, 5), (0, LANES - width)))
    if group == 8:
        packed, every_id, gains, extra = spread(
            packed, gains, seqs, length, micro, vocab, width
        )
        every_id = every_id.reshape(-1)
    else:
        packed, gains = lax.all_gather(packed, "dp"), lax.all_gather(gains, "dp")
        packed = jnp.take(packed, dp_order, axis=0)
        every_id = packed[:, :id_rows].reshape(group, seqs, parts, share)
        every_id = jnp.take(every_id, tensor_order, axis=2)
        every_id = every_id.transpose(2, 0, 1, 3).reshape(-1) - start
        every_id = jnp.where((every_id >= 0) & (every_id < vocab), every_id, vocab)
        gains = gains.transpose(1, 0, 2)[:, :, :width].reshape(8, -1)
    packed, leaves = lax.optimization_barrier((packed, leaves))
    numbers = packed[:, 3 * id_rows, : 2 * micro]
    counts = jnp.sum(numbers[:, :micro].astype(FLOAT), axis=0)

    def both_order(values):
        values = values.reshape(seqs, parts, share)
        values = jnp.where(rank % 2 == 1, values[:, [1, 0, 3, 2]], values)
        values = jnp.where(rank // 2 == 1, values[:, [2, 3, 0, 1]], values)
        return values[:, list(TURN)].transpose(1, 0, 2).reshape(-1)

    if group != 8:
        rows_extra = []
        for k in (0, 1):
            its_flags = packed[k, 2 * id_rows : 3 * id_rows].reshape(seqs, length).astype(FLOAT)
            its_order = numbers[k, micro:]
            takes = (its_order[None, :] == jnp.arange(seqs)[:, None]).astype(FLOAT)
            its_scale = its_flags * jnp.sum(takes / jnp.maximum(counts, 1.0), axis=1)[:, None]
            aims = packed[k, id_rows : 2 * id_rows].reshape(seqs, length) - start - bit * entries
            aims = jnp.where((aims >= 0) & (aims < entries), aims, -1).astype(FLOAT)
            rows_extra.append(jnp.stack([both_order(its_scale), both_order(aims), both_order(its_flags)]))
        extra = jnp.pad(jnp.concatenate(rows_extra, axis=1), ((0, 5), (0, 0)))

    own_segment = segments[:, :, None] == jnp.arange(8, dtype=jnp.int32)
    sizes = jnp.sum(own_segment.astype(jnp.int32), axis=1)
    begins = jnp.cumsum(sizes, axis=1) - sizes
    first = jnp.sum(jnp.where(own_segment, begins[:, None, :], 0), axis=2)
    first = jnp.broadcast_to(first[:, None, :], (seqs, 8, length))
    base = turn[tensor_order_natural] * (seqs * share)
    cosine, sine = tables(length, HEAD_DIM)

    if group == 8:
        stream0, attn_norm, attn_w, ffn_four, head_rows = start_rows(
            every_id, embedding.T, gains, attn_block, ffn_block, stays, leaves
        )
        ffn_blocks = [ffn_block, ffn_four]
    else:
        rows = lookup(embedding.T, every_id).reshape(parts, group, seqs * share, width)
        rows = rows[:2] + swap(rows[2:], "tensor", 1)
        rows = rows[0] + swap(rows[1], "tensor", 2)
        rows = lax.all_to_all(jnp.take(rows, dp_order, axis=0), "dp", 0, 0)
        stream0 = rows.transpose(1, 0, 2).reshape(seqs * share, -1).astype(FLOAT)
        attn_norm = tensor_gather(normed(stream0, gains[0]).astype(HALF))

        attn_w = lax.all_gather(attn_block, "dp", axis=0, tiled=True)
        came = swap(leaves, "dp", 1)
        head_rows = jnp.concatenate(
            [jnp.where(bit == 0, stays, came), jnp.where(bit == 0, came, stays)], axis=0
        )
        ffn_blocks = []
    head_b = lax.all_gather(head_rows, "dp", axis=0, tiled=True, axis_index_groups=lines)
    attn_in_b, attn_out_b = attn_w[:, :qkv_width], attn_w[:, qkv_width:]
    qkv = product(attn_in_b, attn_norm, 0, 1)
    attended, kept, log_sums = attend(base, qkv, cosine, sine, first)
    stream1, ffn_norm, *ffn_w = forward_boundary(
        attended, attn_w, stream0, gains, ffn_blocks
    )
    ffn_w = ffn_w[0] if ffn_w else lax.all_gather(ffn_block, "dp", axis=0, tiled=True)
    stream2, final_norm = wide_forward(ffn_norm, ffn_w, stream1, gains)

    logits, scan, final_turned = head_scan(final_norm, head_b, extra)
    info = merge_scans(scan, extra)
    tokens = seqs * length
    seq_loss = jnp.sum(
        ((info[0, :tokens] - info[1, :tokens]) * extra[2, :tokens]).reshape(parts, seqs, share),
        axis=(0, 2),
    )
    g_head, d_final = head_grad(final_turned, head_b, info, logits)
    g_head = lax.psum_scatter(
        g_head, "dp", scatter_dimension=0, tiled=True, axis_index_groups=lines
    )
    g_stays = jnp.where(bit == 0, g_head[:width], g_head[width:])
    g_leaves = jnp.where(bit == 0, g_head[width:], g_head[:width])

    d_stream2, g_gain2, d_branch2 = wide_backward(d_final, stream2, gains)
    d_stream1, g_gain1, d_branch1, g_ffn = backward_boundary(
        ffn_norm, d_branch2, ffn_w, stream1, gains, d_stream2
    )
    g_ffn_parts = scatter_first(g_ffn)
    d_attended = product(attn_out_b, d_branch1, 0, 1).astype(HALF)
    d_qkv = attend_back(base, kept, log_sums, d_attended, cosine, sine, first, [])
    g_attn_in = product(attn_norm, d_qkv, 0, 1).astype(HALF)
    g_attn_out = product(d_branch1, attended, 0, 1).astype(HALF)
    g_attn = jnp.concatenate([g_attn_in, g_attn_out], axis=1)
    g_attn_parts = scatter_first(g_attn)
    d_qkv, g_ffn = lax.optimization_barrier((d_qkv, g_ffn))
    g_ffn, g_ffn_leaves = scatter_middle(g_ffn, g_ffn_parts)
    if group == 8:
        rows, g_gains, g_came = end_rows(
            d_qkv,
            attn_w,
            stream0,
            gains,
            d_stream1,
            g_gain1,
            g_gain2,
            g_leaves,
            width,
            g_ffn_leaves,
        )
    else:
        d_norm = tensor_scatter(product(d_qkv, attn_in_b, 0, 1))
        d_part, g_gain0 = normed_slope(d_norm, stream0, gains[0:1])
        rows = (d_stream1 + d_part).astype(HALF)
        rows = rows.reshape(seqs * share, group, width).transpose(1, 0, 2)
        rows = jnp.take(lax.all_to_all(rows, "dp", 0, 0), dp_order, axis=0)
        rows = tensor_gather(rows[None]).reshape(-1, width)
        g_came = swap(g_leaves, "dp", 1)
        gain_sum = jnp.concatenate([g_gain0, g_gain1[:1], g_gain2[:1]]).reshape(3, group, width)
        g_gains = jnp.take(lax.psum(gain_sum, ("dp", "tensor")), own, axis=1)
    g_head = [jnp.where(bit == 0, g_stays, g_came), jnp.where(bit == 0, g_came, g_stays)]
    rows, g_ffn, g_attn = lax.optimization_barrier((rows, g_ffn, g_attn))
    g_ffn = scatter_last(g_ffn, g_ffn_leaves)
    g_attn, g_attn_leaves = scatter_middle(g_attn, g_attn_parts)
    last_id, g_ffn, *g_attn_leaves = lax.optimization_barrier((every_id, g_ffn, *g_attn_leaves))
    g_embed, squares = collect(rows, last_id, vocab)
    squares, g_attn = lax.optimization_barrier((squares, g_attn))
    g_attn = scatter_last(g_attn, g_attn_leaves)

    owner = (rank == 0).astype(FLOAT)
    squared = jnp.sum(squares) + owner * jnp.sum(g_gains * g_gains)
    for part in (g_attn, g_ffn, *g_head):
        squared = squared + jnp.sum(part.astype(FLOAT) ** 2)
    losses = jnp.sum(jnp.where(takes_seq, seq_loss[None, :], 0.0), axis=1) * owner
    if group == 8:
        sums = jnp.pad(jnp.concatenate([squared[None], losses]), (0, 8 * LANES - 1 - micro))
        sums = total_over_devices(jnp.broadcast_to(sums.reshape(1, 8, LANES), (8, 8, LANES)))
        squared, loss_sums = sums[0, 0], sums[0, 1 : 1 + micro]
    else:
        squared, loss_sums = lax.psum((squared, losses), ("dp", "tensor"))
    grad_norm = jnp.sqrt(squared)
    factor = CLIP / jnp.maximum(grad_norm, CLIP)
    g_parts = (
        [g_embed],
        [g_attn[:, :qkv_width]],
        [g_attn[:, qkv_width:].T],
        [g_ffn[:, : 2 * ffn].reshape(ffn_in.shape)],
        [g_ffn[:, 2 * ffn :]],
        g_head,
    )
    arrays = []
    for place in range(6):
        entry = (weights[place], means[place], squares_in[place])
        if place in (0, 4):
            entry = tuple(array.T for array in entry)
        arrays.append((*entry, g_parts[place]))
    updated = []
    for place, results in enumerate(update(arrays, factor)):
        updated.extend(result.T if place in (0, 4) else result for result in results)
    updated.extend(adam(norm_gains, g_gains * factor, means[6], squares_in[6], LR_GAIN, 0.0))
    return (jnp.stack([loss_sums, counts]), grad_norm, *updated)


def solution(mesh):
    in_specs = (
        P("dp", None),
        P("dp", None),
        P("dp", None),
        P("dp", None),
        P("dp", None),
        P("tensor", "dp"),
        P("dp", "tensor"),
        P("tensor", "dp"),
        P("dp", None, "tensor"),
        P("tensor", "dp"),
        P("dp", "tensor"),
        P(None, "dp"),
        P("tensor", "dp"),
        P("dp", "tensor"),
        P("tensor", "dp"),
        P("dp", None, "tensor"),
        P("tensor", "dp"),
        P("dp", "tensor"),
        P(None, "dp"),
        P("tensor", "dp"),
        P("dp", "tensor"),
        P("tensor", "dp"),
        P("dp", None, "tensor"),
        P("tensor", "dp"),
        P("dp", "tensor"),
        P(None, "dp"),
    )
    out_specs = (
        P(),
        P(),
        P("tensor", "dp"),
        P("tensor", "dp"),
        P("tensor", "dp"),
        P("tensor", "dp"),
        P("dp", "tensor"),
        P("dp", "tensor"),
        P("dp", "tensor"),
        P("dp", "tensor"),
        P("tensor", "dp"),
        P("tensor", "dp"),
        P("tensor", "dp"),
        P("tensor", "dp"),
        P("dp", None, "tensor"),
        P("dp", None, "tensor"),
        P("dp", None, "tensor"),
        P("dp", None, "tensor"),
        P("tensor", "dp"),
        P("tensor", "dp"),
        P("tensor", "dp"),
        P("tensor", "dp"),
        P("dp", "tensor"),
        P("dp", "tensor"),
        P("dp", "tensor"),
        P("dp", "tensor"),
        P(None, "dp"),
        P(None, "dp"),
        P(None, "dp"),
        P(None, "dp"),
    )
    return jax.shard_map(shards, mesh=mesh, in_specs=in_specs, out_specs=out_specs, check_vma=False)
```
